128 devices in a mesh: dp: 32 (over z_lo, y, x), mp: 4 (over z_hi, core).
Axes of the slice: x: 4, y: 4, z: 4 (z_hi: 2, z_lo: 2; z = z_hi * 2 + z_lo), core: 2. Of those that a mesh axis runs over, the one named last changes fastest.
Arguments:
- tokens: bfloat16 [65536, 1024], P('dp'), may hold values from -6 to 6
- cotangent: bfloat16 [65536, 1024], P('dp'), may hold values from -6 to 6
- segments: int32 [32, 2048], P('dp'), may hold values from 0 to 2, never falling along the last dimension, each value on 1 to 1568 neighbouring positions
- padding: int32 [32, 2048], P('dp'), may hold values 0 or 1
- positions: int32 [3, 32, 2048], P(None, 'dp'), may hold values from 0 to 15
- ln1_gain: float32 [1024], replicated, may hold values from 0.5 to 1.5
- ln1_bias: float32 [1024], replicated, may hold values from -1.5 to 1.5
- w_qkv: bfloat16 [3, 1024, 1024], P(None, None, 'mp'), may hold values from -0.1875 to 0.1875
- b_qkv: float32 [3, 1024], P(None, 'mp'), may hold values from -1.5 to 1.5
- w_out: bfloat16 [1024, 1024], P('mp'), may hold values from -1.5 to 1.5
- b_out: float32 [1024], replicated, may hold values from -3 to 3
- ln2_gain: float32 [1024], replicated, may hold values from 0.5 to 1.5
- ln2_bias: float32 [1024], replicated, may hold values from -3 to 3
- w_up: bfloat16 [1024, 4096], P(None, 'mp'), may hold values from -0.1875 to 0.1875
- b_up: float32 [4096], P('mp'), may hold values from -3 to 3
- w_down: bfloat16 [4096, 1024], P('mp'), may hold values from -0.09375 to 0.09375
- b_down: float32 [1024], replicated, may hold values from -3 to 3
Outputs:
- mixed: bfloat16 [65536, 1024], P(('dp', 'mp'))
- input_grad: float32 [65536, 1024], P(('dp', 'mp'))
- grad_ln1_gain: float32 [1024], replicated
- grad_ln1_bias: float32 [1024], replicated
- grad_w_qkv: float32 [3, 1024, 1024], P(None, None, 'mp')
- grad_b_qkv: float32 [3, 1024], P(None, 'mp')
- grad_w_out: float32 [1024, 1024], P('mp')
- grad_b_out: float32 [1024], replicated
- grad_ln2_gain: float32 [1024], replicated
- grad_ln2_bias: float32 [1024], replicated
- grad_w_up: float32 [1024, 4096], P(None, 'mp')
- grad_b_up: float32 [4096], P('mp')
- grad_w_down: float32 [4096, 1024], P('mp')
- grad_b_down: float32 [1024], replicated
The draws below stay inside these ranges and needn't reach their ends.
Inputs may be any that keep to these rules, and one draw needn't show every extreme that they name: `segments`: within a pack the numbers never fall; a clip has 1 to min(1568, 2048) tokens, and some clip of every pack has exactly that many.
All inputs are finite; a program needn't handle non-finite values. No bound on the sum of `padding` on one device may be relied on, other than what follows from the above.
Results may differ from the reference program's by a relative error of at most 0.0095.
Values may be sent and summed in bfloat16 or wider, within the bound.
No kernel may reach another device: no remote copies, remote signals or barrier semaphores. Data moves between devices by JAX's collectives and lax.ppermute only.
A program may use at most 256 MiB of HBM per device.

```python
import math
import jax
import jax.numpy as jnp
import numpy as np
from jax import lax

D = 1024
HEADS = 16
HEAD_DIM = 64
FF = 4096
TOK_DEV = 2048
CLIP = 1568
PACKS = 32
TOKENS = 65536


def touch_ends(entries, own_key, least, largest):
    place = [jax.random.randint(jax.random.fold_in(own_key, axis), (), 0, length) for axis, length in enumerate(entries.shape)]
    longest = entries.shape.index(max(entries.shape))
    beside = place[:longest] + [(place[longest] + 1) % entries.shape[longest]] + place[longest + 1:]
    return entries.at[tuple(place)].set(least).at[tuple(beside)].set(largest)


def steps_of(own_key, shape, split, least, largest):
    level = 1.0
    for axis_at, shards_of in split:
        draws = jax.random.uniform(jax.random.fold_in(jax.random.fold_in(own_key, 6), axis_at), (shards_of,), jnp.float32, least / len(split), largest / len(split))
        level = level * jnp.repeat(jnp.exp(draws), shape[axis_at] // shards_of).reshape((-1,) + (1,) * (len(shape) - 1 - axis_at))
    return level


def profile(count, total, limit, lean):
    loads = [(1 << 20) // math.isqrt(standing ** lean) + 1 for standing in range(2, count + 1)]
    rest, holding = total - limit - (count - 1), [1] * (count - 1)
    while rest > 0:
        free = [i for i in range(count - 1) if holding[i] < limit]
        whole, remaining = sum([loads[i] for i in free]), rest
        for i in free:
            extra = min(limit - holding[i], max(1, remaining * loads[i] // whole), rest)
            holding[i] = holding[i] + extra
            rest = rest - extra
    return np.array([limit] + holding)


def uneven_parts(rng, amount, total, most, lean):
    if amount == 2:
        one = jax.random.randint(rng, (), max(1, total - most), min(most, total - 1) + 1)
        return jnp.stack([one, total - one])
    sizes = jnp.asarray(profile(amount, total, most, lean), jnp.int32)
    couples = (amount - 1) // 2
    giver, taker = sizes[1:1 + 2 * couples:2], sizes[2:2 + 2 * couples:2]
    room = jnp.minimum(giver - 1, most - taker)
    moved = jax.random.randint(jax.random.fold_in(rng, 1), (couples,), 0, 1 << 20) % (room + 1)
    sizes = sizes.at[1:1 + 2 * couples:2].set(giver - moved).at[2:2 + 2 * couples:2].set(taker + moved)
    return sizes[jax.random.permutation(jax.random.fold_in(rng, 2), amount)]


def centred(stream_key, extent, width, limit, pieces=(), held_as=jnp.bfloat16):
    array = width * jax.random.normal(stream_key, extent, jnp.float32)
    if pieces:
        array = array * steps_of(stream_key, extent, pieces, -0.22, 0.18)
    return jnp.clip(array, -limit, limit).astype(held_as)


def setup_inputs(seed: int = 0) -> dict:
    arg_keys = jax.random.split(jax.random.key(seed), 18)
    return {
        "tokens": centred(arg_keys[0], (TOKENS, D), 1.0, 6.0, ((0, 32),)),
        "cotangent": centred(arg_keys[1], (TOKENS, D), 1.0, 6.0, ((0, 32),)),
        "segments": jax.vmap(lambda own: jnp.searchsorted(jnp.cumsum(uneven_parts(own, TOK_DEV // CLIP + 2, TOK_DEV, min(CLIP, TOK_DEV), 0)), jnp.arange(TOK_DEV), side="right"))(jax.random.split(arg_keys[2], PACKS)).reshape((PACKS, TOK_DEV)).astype(jnp.int32),
        "padding": touch_ends((jax.random.randint(arg_keys[3], (PACKS, TOK_DEV), 0, 16) < 1).astype(jnp.int32), jax.random.fold_in(arg_keys[3], 1), 0, 1),
        "positions": touch_ends(jax.random.randint(arg_keys[4], (3, PACKS, TOK_DEV), 0, 16), jax.random.fold_in(arg_keys[4], 1), 0, 15).astype(jnp.int32),
        "ln1_gain": jnp.clip(1.0 + 0.1 * jax.random.normal(arg_keys[5], (D,), jnp.float32), 0.5, 1.5),
        "ln1_bias": centred(arg_keys[6], (D,), 0.25, 1.5, (), jnp.float32),
        "w_qkv": centred(arg_keys[7], (3, D, D), D ** -0.5, 0.1875, ((2, 4),)),
        "b_qkv": centred(arg_keys[8], (3, D), 0.25, 1.5, ((1, 4),), jnp.float32),
        "w_out": centred(arg_keys[9], (D, D), (max(16, D * 16 // min(CLIP, TOK_DEV))) ** -0.5, 1.5, ((0, 4),)),
        "b_out": centred(arg_keys[10], (D,), 0.5, 3.0, (), jnp.float32),
        "ln2_gain": jnp.clip(1.0 + 0.1 * jax.random.normal(arg_keys[11], (D,), jnp.float32), 0.5, 1.5),
        "ln2_bias": centred(arg_keys[12], (D,), 0.5, 3.0, (), jnp.float32),
        "w_up": centred(arg_keys[13], (D, FF), D ** -0.5, 0.1875, ((1, 4),)),
        "b_up": centred(arg_keys[14], (FF,), 0.5, 3.0, ((0, 4),), jnp.float32),
        "w_down": centred(arg_keys[15], (FF, D), FF ** -0.5, 0.09375, ((0, 4),)),
        "b_down": centred(arg_keys[16], (D,), 0.5, 3.0, (), jnp.float32),
    }


epsilon = 1e-06
highest = lax.Precision.HIGHEST

@jax.custom_vjp
def low(v):
    return lax.optimization_barrier(v.astype(jnp.bfloat16)).astype(jnp.float32)

@jax.custom_vjp
def low_back(v):
    return v

def low_keep(v):
    return (low(v), None)

def low_pass(kept, grad):
    return (grad,)

def back_keep(v):
    return (v, None)

def back_low(kept, grad):
    return (low(grad),)
low.defvjp(low_keep, low_pass)
low_back.defvjp(back_keep, back_low)

def layer_norm(values, gain, shift):
    center = lax.optimization_barrier(jnp.mean(values, axis=-1, keepdims=True))
    shifted = values - center
    spread = lax.optimization_barrier(jnp.mean(shifted * shifted, axis=-1, keepdims=True))
    return shifted * lax.rsqrt(spread + epsilon) * gain + shift

def rope_tables(places, head_dim):
    pair_count = head_dim // 6
    section_size = 2 * pair_count
    feature_ids = jnp.arange(head_dim)
    section_of = feature_ids // section_size
    place_in = feature_ids % section_size
    frequency = jnp.exp(-math.log(10000.0) * (place_in % pair_count).astype(jnp.float32) / pair_count)
    coordinate = jnp.zeros((places.shape[1], head_dim), jnp.float32)
    for section_id in range(3):
        coordinate = coordinate + jnp.where((section_of == section_id)[None, :], places[section_id][:, None].astype(jnp.float32), 0.0)
    angles = coordinate * frequency[None, :]
    rotated = (section_of < 3)[None, :]
    return (jnp.where(rotated, jnp.cos(angles), 1.0), jnp.where(rotated, jnp.sin(angles), 0.0))

def rope_turn(head_dim):
    pair_count = head_dim // 6
    section_size = 2 * pair_count
    source = jnp.arange(head_dim)[:, None]
    target = jnp.arange(head_dim)[None, :]
    leading = target % section_size < pair_count
    partner = jnp.where(leading, target + pair_count, target - pair_count)
    chosen = (source == partner) & (target // section_size < 3)
    return jnp.where(chosen, jnp.where(leading, -1.0, 1.0), 0.0).astype(jnp.float32)

def rotate(values, cosines, sines, rotate_map):
    turned = jnp.einsum('lhd,de->lhe', values, rotate_map, precision=highest)
    return values * cosines[:, None, :] + turned * sines[:, None, :]

def forward(params, inputs, cosines, sines, rotate_map, allowed):
    gain_one, bias_one, w_qkv, b_qkv, w_out, b_out, gain_two, bias_two, w_up, b_up, w_down, b_down = params
    seq_length = inputs.shape[0]
    scale = 1.0 / math.sqrt(HEAD_DIM)
    normed_one = low(layer_norm(inputs, gain_one, bias_one))
    projected = low_back(jnp.einsum('ld,cde->cle', normed_one, w_qkv, precision=highest) + b_qkv[:, None, :])
    queries = low(rotate(projected[0].reshape(seq_length, HEADS, HEAD_DIM), cosines, sines, rotate_map))
    keys_low = low(rotate(projected[1].reshape(seq_length, HEADS, HEAD_DIM), cosines, sines, rotate_map))
    values_low = low(projected[2].reshape(seq_length, HEADS, HEAD_DIM))

    def one_head(parts):
        head_queries, head_keys, head_values = parts
        raw_scores = low_back(jnp.dot(head_queries, head_keys.T, precision=highest))
        scores = jnp.where(allowed, raw_scores * scale, -1e+30)
        probs = jax.nn.softmax(scores, axis=-1)
        return jnp.dot(low(probs), head_values, precision=highest)
    attended = lax.map(jax.checkpoint(one_head), (queries.transpose(1, 0, 2), keys_low.transpose(1, 0, 2), values_low.transpose(1, 0, 2)))
    heads_out = low_back(low(attended.transpose(1, 0, 2).reshape(seq_length, D)))
    branch = low_back(jnp.dot(heads_out, w_out, precision=highest) + b_out)
    middle = inputs + branch
    normed_two = low(layer_norm(middle, gain_two, bias_two))
    hidden_pre = low_back(jnp.dot(normed_two, w_up, precision=highest) + b_up)
    activation = low(jax.nn.gelu(hidden_pre, approximate=False))
    return middle + jnp.dot(activation, w_down, precision=highest) + b_down

def reference(tokens, cotangent, segments, padding, positions, ln1_gain, ln1_bias, w_qkv, b_qkv, w_out, b_out, ln2_gain, ln2_bias, w_up, b_up, w_down, b_down):
    params = tuple((item.astype(jnp.float32) for item in (ln1_gain, ln1_bias, w_qkv, b_qkv, w_out, b_out, ln2_gain, ln2_bias, w_up, b_up, w_down, b_down)))
    rotate_map = rope_turn(HEAD_DIM)
    token_packs = tokens.reshape(PACKS, TOK_DEV, D)
    grad_packs = cotangent.reshape(PACKS, TOK_DEV, D)
    place_packs = positions.transpose(1, 0, 2)
    token_ids = jnp.arange(TOK_DEV)

    def one_pack(sums, item):
        pack_tokens, pack_grad, pack_segments, pack_padding, pack_places = item
        cosines, sines = rope_tables(pack_places, HEAD_DIM)
        allowed = (pack_segments[:, None] == pack_segments[None, :]) & ((pack_padding[None, :] == 0) | (token_ids[:, None] == token_ids[None, :]))

        def run(weights, inputs):
            return forward(weights, inputs, cosines, sines, rotate_map, allowed)
        output, pull = jax.vjp(run, params, pack_tokens.astype(jnp.float32))
        grads, grad_inputs = pull(pack_grad.astype(jnp.float32))
        sums = tuple((left + right for left, right in zip(sums, grads)))
        return (sums, (output.astype(jnp.bfloat16), grad_inputs))
    zeros = tuple((jnp.zeros_like(item) for item in params))
    sums, (outputs, grad_inputs) = lax.scan(one_pack, zeros, (token_packs, grad_packs, segments, padding, place_packs))
    return (outputs.reshape(TOKENS, D), grad_inputs.reshape(TOKENS, D), sums[0], sums[1], sums[2], sums[3], sums[4], sums[5], sums[6], sums[7], sums[8], sums[9], sums[10], sums[11])
```

```python
import functools
import math

import jax
import jax.numpy as jnp
from jax import lax
from jax.experimental import pallas as pl
from jax.experimental.pallas import tpu as pltpu
from jax.sharding import Mesh
from jax.sharding import PartitionSpec as P

HEAD_DIM = 64
HEADS = 4
WIDTH = HEADS * HEAD_DIM
AUG = 128
TILE = 256
MIB = 1 << 20
DP = ("zl", "y", "x")
MP = ("zh", "c")
EVERY = ("zl", "y", "x", "zh", "c")

epsilon = 1e-06
NEG = -1e30
bf16 = jnp.bfloat16
f32 = jnp.float32


def dot_nn(a, b):
    return lax.dot_general(a, b, (((1,), (0,)), ((), ())), preferred_element_type=f32)


def dot_nt(a, b):
    return lax.dot_general(a, b, (((1,), (1,)), ((), ())), preferred_element_type=f32)


def dot_tn(a, b):
    return lax.dot_general(a, b, (((0,), (0,)), ((), ())), preferred_element_type=f32)


def normalized(values):
    center = jnp.mean(values, axis=-1, keepdims=True)
    shifted = values - center
    spread = jnp.mean(shifted * shifted, axis=-1, keepdims=True)
    inverse = lax.rsqrt(spread + epsilon)
    return shifted * inverse, inverse


def norm_back(hat, inverse, gain, grad):
    scaled = grad * gain
    return inverse * (
        scaled
        - jnp.mean(scaled, axis=-1, keepdims=True)
        - hat * jnp.mean(scaled * hat, axis=-1, keepdims=True)
    )


def turned(x, low, high):
    width = x.shape[1]
    pair = HEAD_DIM // 6
    return pltpu.roll(x, width - pair, 1) * low + pltpu.roll(x, pair, 1) * high


def three_parts(x):
    first = x.astype(bf16).astype(f32)
    rest = x - first
    second = rest.astype(bf16).astype(f32)
    return first, second, rest - second


def params(limit, axes=1):
    return pltpu.CompilerParams(
        dimension_semantics=("arbitrary",) * axes, vmem_limit_bytes=limit * MIB
    )


def whole(shape):
    return pl.BlockSpec(shape, lambda *_: (0,) * len(shape))


def qkv_kernel(
    tok, w, b, gain, shift, cos, low, high, key_extra, query_extra,
    h1, k_aug, v_aug, q_aug_t, q_out, k_t, v_t,
):
    hat, _ = normalized(tok[...].astype(f32))
    normed = (hat * gain[...] + shift[...]).astype(bf16)
    h1[...] = normed
    q = dot_nn(normed, w[0]) + b[0:1, :]
    k = dot_nn(normed, w[1]) + b[1:2, :]
    v = dot_nn(normed, w[2]) + b[2:3, :]
    q = (q * cos[...] + turned(q, low[...], high[...])) * (1.0 / math.sqrt(HEAD_DIM))
    k = k * cos[...] + turned(k, low[...], high[...])
    q_out[...] = q.astype(bf16)
    q_turned = q.T.astype(bf16)
    k_t[...] = k.T.astype(bf16)
    v_t[...] = v.T.astype(bf16)
    lane = lax.broadcasted_iota(jnp.int32, (TILE, AUG), 1)
    ones = jnp.where((lane >= HEAD_DIM) & (lane < HEAD_DIM + 3), 1.0, 0.0)
    extra = key_extra[...].astype(f32)
    for h in range(HEADS):
        at = h // 2 * AUG
        k_pair, v_pair = k[:, at : at + AUG], v[:, at : at + AUG]
        if h % 2:
            k_pair, v_pair = pltpu.roll(k_pair, HEAD_DIM, 1), pltpu.roll(v_pair, HEAD_DIM, 1)
        k_aug[:, h * AUG : (h + 1) * AUG] = jnp.where(lane < HEAD_DIM, k_pair, extra).astype(bf16)
        v_aug[:, h * AUG : (h + 1) * AUG] = jnp.where(lane < HEAD_DIM, v_pair, ones).astype(bf16)
        q_aug_t[h * AUG : h * AUG + HEAD_DIM, :] = q_turned[h * HEAD_DIM : (h + 1) * HEAD_DIM, :]
        q_aug_t[h * AUG + HEAD_DIM : (h + 1) * AUG, :] = query_extra[...]


def project(tokens, w, b, gain, shift, cos, low, high, key_extra, query_extra):
    length, width = tokens.shape
    tiles = length // TILE

    def rows(columns):
        return pl.BlockSpec((TILE, columns), lambda i: (i, 0))

    def columns(count):
        return pl.BlockSpec((count, TILE), lambda i: (0, i))

    out = jax.ShapeDtypeStruct
    return pl.pallas_call(
        qkv_kernel,
        grid=(tiles,),
        in_specs=[
            rows(width), whole(w.shape), whole(b.shape), whole((1, width)), whole((1, width)),
            rows(WIDTH), rows(WIDTH), rows(WIDTH), rows(AUG), columns(AUG - HEAD_DIM),
        ],
        out_specs=[
            rows(width), rows(HEADS * AUG), rows(HEADS * AUG), columns(HEADS * AUG), rows(WIDTH),
            columns(WIDTH), columns(WIDTH),
        ],
        out_shape=[
            out((length, width), bf16), out((length, HEADS * AUG), bf16),
            out((length, HEADS * AUG), bf16), out((HEADS * AUG, length), bf16),
            out((length, WIDTH), bf16), out((WIDTH, length), bf16), out((WIDTH, length), bf16),
        ],
        compiler_params=params(40),
        cost_estimate=pl.CostEstimate(
            flops=6 * length * width * WIDTH, bytes_accessed=20 * MIB, transcendentals=0
        ),
        name="project",
    )(tokens, w, b, gain, shift, cos, low, high, key_extra, query_extra)


def attend_kernel(info, k_aug, v_t, q_aug_t, k_t, pad, o, o_t, lse, top, total, acc, *, part):
    tile = 2 * pl.program_id(0) + part
    tiles = pl.num_programs(0) * 2
    padded = pad[0:1, :] > 0
    for h in range(HEADS):
        q_h = q_aug_t[h * AUG : h * AUG + HEAD_DIM, :].astype(f32)
        k_h = k_t[h * HEAD_DIM : (h + 1) * HEAD_DIM, :].astype(f32)
        own = jnp.sum(q_h * k_h, axis=0, keepdims=True)
        top[h : h + 1, :] = jnp.where(padded, own, -3e38)
        total[h : h + 1, :] = jnp.where(padded, 1.0, 0.0)
    here = pl.ds(pl.multiple_of(tile * TILE, TILE), TILE)
    acc[...] = jnp.where(padded, v_t[:, here].astype(f32), 0.0)

    def step(j, _):
        keys = pl.ds(pl.multiple_of(j * TILE, TILE), TILE)
        for h in range(HEADS):
            feat = slice(h * HEAD_DIM, (h + 1) * HEAD_DIM)
            wide = slice(h * AUG, (h + 1) * AUG)
            scores = dot_nn(k_aug[keys, wide], q_aug_t[wide, :])
            old = top[h : h + 1, :]
            new = jnp.maximum(old, jnp.max(scores, axis=0, keepdims=True))
            probs = jnp.exp(scores - new)
            fade = jnp.exp(old - new)
            top[h : h + 1, :] = new
            total[h : h + 1, :] = total[h : h + 1, :] * fade + jnp.sum(probs, axis=0, keepdims=True)
            acc[feat, :] = acc[feat, :] * fade + dot_nn(v_t[feat, keys], probs.astype(bf16))
        return 0

    lax.fori_loop(info[tile], info[tiles + tile], step, 0)
    for h in range(HEADS):
        feat = slice(h * HEAD_DIM, (h + 1) * HEAD_DIM)
        acc[feat, :] = acc[feat, :] / total[h : h + 1, :]
    lse[...] = jnp.zeros_like(lse)
    lse[0:HEADS, :] = top[0:HEADS, :] + jnp.log(total[0:HEADS, :])
    turned_o = acc[...]
    o_t[...] = turned_o.astype(bf16)
    o[...] = turned_o.T.astype(bf16)


def attend(part, info, k_aug, v_t, q_aug_t, k_t, pad):
    length = k_aug.shape[0]
    half = length // 2

    def columns(count):
        return pl.BlockSpec((count, TILE), lambda i, *_: (0, 2 * i + part))

    def packed(count):
        return pl.BlockSpec((count, TILE), lambda i, *_: (0, i))

    out = jax.ShapeDtypeStruct
    return pl.pallas_call(
        functools.partial(attend_kernel, part=part),
        grid_spec=pltpu.PrefetchScalarGridSpec(
            num_scalar_prefetch=1,
            grid=(half // TILE,),
            in_specs=[
                whole(k_aug.shape), whole(v_t.shape), columns(HEADS * AUG), columns(WIDTH),
                columns(8),
            ],
            out_specs=[
                pl.BlockSpec((TILE, WIDTH), lambda i, *_: (i, 0)), packed(WIDTH), packed(8),
            ],
            scratch_shapes=[
                pltpu.VMEM((8, TILE), f32), pltpu.VMEM((8, TILE), f32), pltpu.VMEM((WIDTH, TILE), f32),
            ],
        ),
        out_shape=[out((half, WIDTH), bf16), out((WIDTH, half), bf16), out((8, half), f32)],
        compiler_params=params(32),
        cost_estimate=pl.CostEstimate(
            flops=12 * half * length * WIDTH, bytes_accessed=6 * MIB, transcendentals=0
        ),
        name="attend",
    )(info, k_aug, v_t, q_aug_t, k_t, pad)


def gelu_parts(u):
    size = jnp.abs(u)
    t = 1.0 / (1.0 + (0.3275911 / math.sqrt(2.0)) * size)
    bell = jnp.exp(-0.5 * (u * u))
    poly = 0.5 * 1.061405429
    for c in (-1.453152027, 1.421413741, -0.284496736, 0.254829592):
        poly = poly * t + 0.5 * c
    tail = poly * t * bell
    below = jnp.where(u >= 0, 1.0 - tail, tail)
    return u * below, below + u * bell * (1.0 / math.sqrt(2.0 * math.pi))


def mlp_kernel(
    info, tok, cot, o_0, o_1, o_2, o_3, w_0, w_1, w_2, w_3, b_out, gain, shift, w_up, b_up, w_down,
    x2, h2, act, du, mlp, dh2, db_up,
):
    i = pl.program_id(0)
    mid = tok[...].astype(f32) + b_out[...]
    for o_j, w_j in ((o_0, w_0), (o_1, w_1), (o_2, w_2), (o_3, w_3)):
        mid = mid + dot_nn(o_j[...], w_j[...])

    @pl.when(i == 0)
    def _():
        x2[...] = mid
        db_up[...] = jnp.zeros_like(db_up)

    hat, _ = normalized(mid)
    normed = (hat * gain[...] + shift[...]).astype(bf16)
    h2[...] = normed
    u = dot_nn(normed, w_up[...]) + b_up[...]
    grad_act = dot_nt(cot[...], w_down[...])
    value, slope = gelu_parts(u)
    value = value.astype(bf16)
    grad = (grad_act * slope).astype(bf16)
    act[...] = value
    du[...] = grad
    db_up[0:1, :] += jnp.sum(grad.astype(f32), axis=0, keepdims=True)
    mlp[0] = dot_nn(value, w_down[...]).astype(bf16)
    dh2[0] = dot_nt(grad, w_up[...]).astype(bf16)


def mlp(part, info, me_at, tokens, cotangent, o_parts, w_parts, b_out, gain, shift, w_up, b_up, w_down):
    length, width = tokens.shape
    half = length // 2
    hidden = w_up.shape[1]
    owners = half // TILE

    def owner(i, info):
        return jnp.bitwise_xor(info[me_at], i)

    def rows(columns):
        return pl.BlockSpec((TILE, columns), lambda i, info: (2 * owner(i, info) + part, 0))

    def packed(columns):
        return pl.BlockSpec((TILE, columns), lambda i, info: (owner(i, info), 0))

    def relative(columns):
        return pl.BlockSpec((1, TILE, columns), lambda i, info: (i, 0, 0))

    out = jax.ShapeDtypeStruct
    return pl.pallas_call(
        mlp_kernel,
        grid_spec=pltpu.PrefetchScalarGridSpec(
            num_scalar_prefetch=1,
            grid=(owners,),
            in_specs=[rows(width), rows(width)]
            + [packed(WIDTH)] * 4
            + [whole((WIDTH, width))] * 4
            + [whole((1, width))] * 3
            + [whole(w_up.shape), whole((1, hidden)), whole(w_down.shape)],
            out_specs=[
                whole((TILE, width)), packed(width), packed(hidden), packed(hidden),
                relative(width), relative(width), whole((8, hidden)),
            ],
        ),
        out_shape=[
            out((TILE, width), f32), out((half, width), bf16), out((half, hidden), bf16),
            out((half, hidden), bf16), out((owners, TILE, width), bf16),
            out((owners, TILE, width), bf16), out((8, hidden), f32),
        ],
        compiler_params=params(56),
        cost_estimate=pl.CostEstimate(
            flops=10 * half * width * hidden, bytes_accessed=20 * MIB, transcendentals=0
        ),
        name="mlp",
    )(info, tokens, cotangent, *o_parts, *w_parts, b_out, gain, shift, w_up, b_up, w_down)


def mlp_weights_kernel(h2_a, h2_b, du_a, du_b, act_a, act_b, cot_a, cot_b, out, up, down):
    i = pl.program_id(0)

    @pl.when(i == 0)
    def _():
        up[...] = jnp.zeros_like(up)
        down[...] = jnp.zeros_like(down)

    up[...] += dot_tn(h2_a[...], du_a[...]) + dot_tn(h2_b[...], du_b[...])
    down[...] += dot_tn(act_a[...], cot_a[...]) + dot_tn(act_b[...], cot_b[...])

    @pl.when(i == pl.num_programs(0) - 1)
    def _():
        out[0] = up[...].astype(bf16)
        out[1] = down[...].astype(bf16)


def mlp_weights(h2, du, act, cotangent):
    half, width = h2[0].shape
    hidden = du[0].shape[1]

    def packed(columns):
        return pl.BlockSpec((TILE, columns), lambda i: (i, 0))

    def rows(part):
        return pl.BlockSpec((TILE, width), lambda i: (2 * i + part, 0))

    return pl.pallas_call(
        mlp_weights_kernel,
        grid=(half // TILE,),
        in_specs=[packed(width)] * 2 + [packed(hidden)] * 4 + [rows(0), rows(1)],
        out_specs=whole((2, width, hidden)),
        out_shape=jax.ShapeDtypeStruct((2, width, hidden), bf16),
        scratch_shapes=[pltpu.VMEM((width, hidden), f32), pltpu.VMEM((hidden, width), f32)],
        compiler_params=params(56),
        cost_estimate=pl.CostEstimate(
            flops=8 * half * width * hidden, bytes_accessed=20 * MIB, transcendentals=0
        ),
        name="mlp_weights",
    )(*h2, *du, *act, cotangent, cotangent)


def middle_kernel(
    info, here, there, x2, cot, gain, w_0, w_1, w_2, w_3, dx2, g, d_0, d_1, d_2, d_3, small
):
    grad = here[...].astype(f32) + there[...].astype(f32)
    hat, inverse = normalized(x2[...])
    dy = cot[...].astype(f32)
    full = dy + norm_back(hat, inverse, gain[...], grad)
    dx2[...] = full
    low = full.astype(bf16)
    g[...] = low
    small[...] = jnp.zeros_like(small)
    small[0:1, :] = jnp.sum(grad * hat, axis=0, keepdims=True)
    small[1:2, :] = jnp.sum(grad, axis=0, keepdims=True)
    small[2:3, :] = jnp.sum(low.astype(f32), axis=0, keepdims=True)
    small[3:4, :] = jnp.sum(dy, axis=0, keepdims=True)
    for d_j, w_j in ((d_0, w_0), (d_1, w_1), (d_2, w_2), (d_3, w_3)):
        d_j[...] = dot_nt(low, w_j[...]).astype(bf16)


def middle(part, info, me_at, here, there, x2, cotangent, gain, w_parts):
    width = x2.shape[1]
    out = jax.ShapeDtypeStruct
    own = whole((TILE, width))
    return pl.pallas_call(
        middle_kernel,
        grid_spec=pltpu.PrefetchScalarGridSpec(
            num_scalar_prefetch=1,
            grid=(1,),
            in_specs=[
                own, own, own,
                pl.BlockSpec((TILE, width), lambda i, info: (2 * info[me_at] + part, 0)),
                whole((1, width)),
            ]
            + [whole((WIDTH, width))] * 4,
            out_specs=[own, own] + [whole((TILE, WIDTH))] * 4 + [whole((8, width))],
        ),
        out_shape=[out((TILE, width), f32), out((TILE, width), bf16)]
        + [out((TILE, WIDTH), bf16)] * 4
        + [out((8, width), f32)],
        compiler_params=params(40),
        cost_estimate=pl.CostEstimate(
            flops=2 * TILE * width * width, bytes_accessed=8 * MIB, transcendentals=0
        ),
        name="middle",
    )(info, here, there, x2, cotangent, gain, *w_parts)


def out_weights_kernel(info, *refs):
    out = refs[-1]
    g_a, g_b = refs[-3], refs[-2]
    for j in range(4):
        total = dot_tn(refs[j][...], g_a[...]) + dot_tn(refs[4 + j][...], g_b[...])
        out[j] = total.astype(bf16)


def out_weights(info, me_at, o_a, o_b, g_a, g_b):
    width = g_a.shape[1]
    own = pl.BlockSpec((TILE, WIDTH), lambda i, info: (info[me_at], 0))
    return pl.pallas_call(
        out_weights_kernel,
        grid_spec=pltpu.PrefetchScalarGridSpec(
            num_scalar_prefetch=1,
            grid=(1,),
            in_specs=[own] * 8 + [whole((TILE, width))] * 2,
            out_specs=whole((4, WIDTH, width)),
        ),
        out_shape=jax.ShapeDtypeStruct((4, WIDTH, width), bf16),
        compiler_params=params(40),
        cost_estimate=pl.CostEstimate(
            flops=4 * TILE * width * width, bytes_accessed=6 * MIB, transcendentals=0
        ),
        name="out_weights",
    )(info, *o_a, *o_b, g_a, g_b)


def attend_back_kernel(
    info, k_aug, v_aug, k_t, q_aug_t, q, v_t, o_t, lse, pad, do, cos, low, high, dk_in, dv_in,
    dq_out, dk, dv, q_side, do_side, q_lanes, do_lanes, dq_t, *, part, me_at, first,
):
    i = pl.program_id(0)
    tiles = pl.num_programs(0) * 2
    tile = 2 * jnp.bitwise_xor(info[me_at], i) + part

    @pl.when(i == 0)
    def _():
        if first:
            dk[...] = jnp.zeros_like(dk)
            dv[...] = jnp.zeros_like(dv)
        else:
            dk[...] = dk_in[...]
            dv[...] = dv_in[...]

    here = pl.ds(pl.multiple_of(tile * TILE, TILE), TILE)
    do_here = do[...]
    q_here = q[...]
    do_t = do_here.astype(f32).T
    k_here = k_t[:, here].astype(f32)
    padded = pad[0:1, :]
    row = lax.broadcasted_iota(jnp.int32, (AUG - HEAD_DIM, TILE), 0)
    lane = lax.broadcasted_iota(jnp.int32, (TILE, WIDTH), 1) // HEAD_DIM
    dk_parts, dv_parts = [], []
    for h in range(HEADS):
        feat = slice(h * HEAD_DIM, (h + 1) * HEAD_DIM)
        at = h * AUG
        q_h = q_aug_t[at : at + HEAD_DIM, :]
        do_h = do_t[feat, :]
        delta = jnp.sum(do_h * o_t[feat, :].astype(f32), axis=0, keepdims=True)
        lse_h = lse[h : h + 1, :]
        one, two, three = three_parts(-lse_h)
        extra = q_aug_t[at + HEAD_DIM : at + AUG, :].astype(f32)
        extra = jnp.where(row == 4, one, jnp.where(row == 5, two, jnp.where(row == 6, three, extra)))
        q_side[at : at + HEAD_DIM, :] = q_h
        q_side[at + HEAD_DIM : at + AUG, :] = extra.astype(bf16)
        one, two, three = three_parts(-delta)
        extra = jnp.where(row == 0, one, jnp.where(row == 1, two, jnp.where(row == 2, three, 0.0)))
        do_side[at : at + HEAD_DIM, :] = do_h.astype(bf16)
        do_side[at + HEAD_DIM : at + AUG, :] = extra.astype(bf16)
        q_lanes[h] = jnp.where(lane == h, q_here, jnp.zeros_like(q_here))
        do_lanes[h] = jnp.where(lane == h, do_here, jnp.zeros_like(do_here))
        q_h = q_h.astype(f32)
        k_h = k_here[feat, :]
        p_own = padded * jnp.exp(jnp.sum(q_h * k_h, axis=0, keepdims=True) - lse_h)
        dp_own = jnp.sum(do_h * v_t[feat, :].astype(f32), axis=0, keepdims=True)
        ds_own = p_own * (dp_own - delta)
        dq_t[feat, :] = ds_own * k_h
        dk_parts.append(ds_own * q_h)
        dv_parts.append(p_own * do_h)
    dk[here, :] += jnp.concatenate(dk_parts, axis=0).T
    dv[here, :] += jnp.concatenate(dv_parts, axis=0).T

    def step(j, _):
        keys = pl.ds(pl.multiple_of(j * TILE, TILE), TILE)
        dk_new, dv_new = dk[keys, :], dv[keys, :]
        for h in range(HEADS):
            feat = slice(h * HEAD_DIM, (h + 1) * HEAD_DIM)
            wide = slice(h * AUG, (h + 1) * AUG)
            probs = jnp.exp(dot_nn(k_aug[keys, wide], q_side[wide, :]))
            ds = (probs * dot_nn(v_aug[keys, wide], do_side[wide, :])).astype(bf16)
            dv_new = dv_new + dot_nn(probs.astype(bf16), do_lanes[h])
            dk_new = dk_new + dot_nn(ds, q_lanes[h])
            dq_t[feat, :] += dot_nn(k_t[feat, keys], ds)
        dk[keys, :] = dk_new
        dv[keys, :] = dv_new
        return 0

    lax.fori_loop(info[tile], info[tiles + tile], step, 0)
    dq = dq_t[...].T * (1.0 / math.sqrt(HEAD_DIM))
    dq_out[...] = (dq * cos[...] - turned(dq, low[...], high[...])).astype(bf16)


def attend_back(part, info, me_at, k_aug, v_aug, k_t, q_aug_t, q, v_t, o_t, lse, pad, do, tables, dk, dv):
    length = k_aug.shape[0]
    half = length // 2

    def owner(i, info):
        return jnp.bitwise_xor(info[me_at], i)

    def rows(columns):
        return pl.BlockSpec((TILE, columns), lambda i, info: (2 * owner(i, info) + part, 0))

    def columns(count):
        return pl.BlockSpec((count, TILE), lambda i, info: (0, 2 * owner(i, info) + part))

    def packed(count):
        return pl.BlockSpec((count, TILE), lambda i, info: (0, owner(i, info)))

    out = jax.ShapeDtypeStruct
    first = dk is None
    if first:
        dk = dv = jnp.zeros((8, WIDTH), f32)
    return pl.pallas_call(
        functools.partial(attend_back_kernel, part=part, me_at=me_at, first=first),
        grid_spec=pltpu.PrefetchScalarGridSpec(
            num_scalar_prefetch=1,
            grid=(half // TILE,),
            in_specs=[
                whole(k_aug.shape), whole(v_aug.shape), whole(k_t.shape), columns(HEADS * AUG),
                rows(WIDTH), columns(WIDTH), packed(WIDTH), packed(8), columns(8),
                pl.BlockSpec((None, TILE, WIDTH), lambda i, info: (i, 0, 0)),
                rows(WIDTH), rows(WIDTH), rows(WIDTH), whole(dk.shape), whole(dv.shape),
            ],
            out_specs=[
                pl.BlockSpec((TILE, WIDTH), lambda i, info: (owner(i, info), 0)),
                whole((length, WIDTH)), whole((length, WIDTH)),
            ],
            scratch_shapes=[
                pltpu.VMEM((HEADS * AUG, TILE), bf16), pltpu.VMEM((HEADS * AUG, TILE), bf16),
                pltpu.VMEM((HEADS, TILE, WIDTH), bf16), pltpu.VMEM((HEADS, TILE, WIDTH), bf16),
                pltpu.VMEM((WIDTH, TILE), f32),
            ],
        ),
        out_shape=[out((half, WIDTH), bf16), out((length, WIDTH), f32), out((length, WIDTH), f32)],
        compiler_params=params(56),
        cost_estimate=pl.CostEstimate(
            flops=32 * half * length * WIDTH, bytes_accessed=16 * MIB, transcendentals=0
        ),
        name="attend_back",
    )(info, k_aug, v_aug, k_t, q_aug_t, q, v_t, o_t, lse, pad, do, *tables, dk, dv)


def project_back_kernel(
    info, tok, h1, dq_a, dq_b, dk, dv, cos, low, high, w,
    dh1, grad_w, grad_b, small, acc,
):
    i = pl.program_id(0)

    @pl.when(i == 0)
    def _():
        acc[...] = jnp.zeros_like(acc)
        grad_b[...] = jnp.zeros_like(grad_b)
        small[...] = jnp.zeros_like(small)

    dq = jnp.where(i % 2 == 0, dq_a[...], dq_b[...])
    dk_here = dk[...]
    dk_low = (dk_here * cos[...] - turned(dk_here, low[...], high[...])).astype(bf16)
    dv_low = dv[...].astype(bf16)
    normed = h1[...]
    grad = None
    for c, part in enumerate((dq, dk_low, dv_low)):
        acc[c] += dot_tn(normed, part)
        grad_b[c : c + 1, :] += jnp.sum(part.astype(f32), axis=0, keepdims=True)
        term = dot_nt(part, w[c])
        grad = term if grad is None else grad + term
    hat, _ = normalized(tok[...].astype(f32))
    small[0:1, :] += jnp.sum(grad * hat, axis=0, keepdims=True)
    small[1:2, :] += jnp.sum(grad, axis=0, keepdims=True)
    dh1[0] = grad.astype(bf16)

    @pl.when(i == pl.num_programs(0) - 1)
    def _():
        grad_w[...] = acc[...].astype(bf16)


def project_back(info, me_at, tokens, h1, dq_a, dq_b, dk, dv, tables, w):
    length, width = tokens.shape
    tiles = length // TILE

    def rows(columns):
        return pl.BlockSpec(
            (TILE, columns),
            lambda i, info: (2 * jnp.bitwise_xor(info[me_at], i // 2) + i % 2, 0),
        )

    def packed(columns):
        return pl.BlockSpec(
            (TILE, columns), lambda i, info: (jnp.bitwise_xor(info[me_at], i // 2), 0)
        )

    out = jax.ShapeDtypeStruct
    return pl.pallas_call(
        project_back_kernel,
        grid_spec=pltpu.PrefetchScalarGridSpec(
            num_scalar_prefetch=1,
            grid=(tiles,),
            in_specs=[
                rows(width), rows(width), packed(WIDTH), packed(WIDTH), rows(WIDTH), rows(WIDTH),
                rows(WIDTH), rows(WIDTH), rows(WIDTH), whole(w.shape),
            ],
            out_specs=[
                pl.BlockSpec((1, TILE, width), lambda i, info: (i // 2, i % 2, 0)),
                whole(w.shape), whole((8, WIDTH)), whole((8, width)),
            ],
            scratch_shapes=[pltpu.VMEM(w.shape, f32)],
        ),
        out_shape=[
            out((tiles // 2, 2 * TILE, width), bf16), out(w.shape, bf16), out((8, WIDTH), f32),
            out((8, width), f32),
        ],
        compiler_params=params(48),
        cost_estimate=pl.CostEstimate(
            flops=12 * length * width * WIDTH, bytes_accessed=20 * MIB, transcendentals=0
        ),
        name="project_back",
    )(info, tokens, h1, dq_a, dq_b, dk, dv, *tables, w)


def finish_kernel(info, here, there, tok, gain, dx2_a, dx2_b, out):
    grad = here[...].astype(f32) + there[...].astype(f32)
    hat, inverse = normalized(tok[...].astype(f32))
    dx2 = jnp.where(pl.program_id(0) == 0, dx2_a[...], dx2_b[...])
    out[...] = dx2 + norm_back(hat, inverse, gain[...], grad)


def finish(info, me_at, here, there, tokens, gain, dx2_a, dx2_b):
    width = tokens.shape[1]
    share = here.shape[0]
    rows = pl.BlockSpec((TILE, width), lambda i, info: (i, 0))
    return pl.pallas_call(
        finish_kernel,
        grid_spec=pltpu.PrefetchScalarGridSpec(
            num_scalar_prefetch=1,
            grid=(share // TILE,),
            in_specs=[
                rows, rows,
                pl.BlockSpec((TILE, width), lambda i, info: (2 * info[me_at] + i, 0)),
                whole((1, width)), whole((TILE, width)), whole((TILE, width)),
            ],
            out_specs=rows,
        ),
        out_shape=jax.ShapeDtypeStruct((share, width), f32),
        compiler_params=params(32),
        name="finish",
    )(info, here, there, tokens, gain, dx2_a, dx2_b)


def swap(array, axis, bit=1):
    size = lax.axis_size(axis)
    if size == 1:
        return jnp.zeros_like(array)
    return lax.ppermute(array, axis, [(i, i ^ bit) for i in range(size)])


def swap_both(array):
    return lax.ppermute(array, MP, [(i, i ^ 3) for i in range(4)])


def added_on_arrival(parts):
    other = swap(jnp.concatenate([parts[1:2], parts[3:4]]), "c")
    keep = parts[0].astype(f32) + other[0].astype(f32)
    give = (parts[2].astype(f32) + other[1].astype(f32)).astype(bf16)
    return keep.astype(bf16), swap(give, "zh")


def everywhere(vectors, over_group):
    for axis in DP:
        for bit in (1, 2):
            if lax.axis_size(axis) > bit:
                vectors = vectors + swap(vectors, axis, bit)
    shared = vectors[:over_group]
    for axis in MP:
        shared = shared + swap(shared, axis)
    return shared, vectors[over_group:]


def summed_over_packs(rows):
    length, width = rows.shape
    group = lax.axis_size(("y", "x"))
    blocks = rows.reshape(group, length // group, width)
    blocks = lax.all_to_all(blocks, ("y", "x"), 0, 0, tiled=True)
    total = jnp.sum(blocks.astype(f32), axis=0).astype(bf16)
    if lax.axis_size("zl") > 1:
        total = (total.astype(f32) + swap(total, "zl").astype(f32)).astype(bf16)
    blocks = jnp.broadcast_to(total[None], (group,) + total.shape)
    blocks = lax.all_to_all(blocks, ("y", "x"), 0, 0, tiled=True)
    return blocks.reshape(length, width).astype(f32)


def rope_tables(places):
    pair = HEAD_DIM // 6
    feature = jnp.arange(HEAD_DIM)
    section = feature // (2 * pair)
    place_in = feature % (2 * pair)
    frequency = jnp.exp(-math.log(10000.0) * (place_in % pair).astype(f32) / pair)
    coordinate = jnp.zeros((places.shape[1], HEAD_DIM), f32)
    for s in range(3):
        coordinate = coordinate + jnp.where(
            (section == s)[None, :], places[s][:, None].astype(f32), 0.0
        )
    angles = coordinate * frequency[None, :]
    turns = (section < 3)[None, :]
    leading = (place_in < pair)[None, :]
    cos = jnp.where(turns, jnp.cos(angles), 1.0)
    sin = jnp.where(turns, jnp.sin(angles), 0.0)
    low = jnp.where(leading, -sin, 0.0)
    high = jnp.where(leading, 0.0, sin)
    return tuple(jnp.tile(table, (1, HEADS)) for table in (cos, low, high))


def mask_parts(segments, padding):
    length = segments.shape[0]
    tiles = length // TILE
    ids = jnp.arange(3)
    same = segments[:, None] == ids[None, :]
    columns = [
        jnp.where(padding[:, None] != 0, NEG, 0.0),
        jnp.where(same, 0.0, NEG),
        jnp.ones((length, 3), f32),
        jnp.zeros((length, AUG - HEAD_DIM - 7), f32),
    ]
    key_extra = jnp.concatenate([jnp.zeros((length, HEAD_DIM), f32)] + columns, axis=1).astype(bf16)
    query_extra = jnp.concatenate(
        [
            jnp.ones((1, length), f32), same.T.astype(f32),
            jnp.zeros((AUG - HEAD_DIM - 4, length), f32),
        ]
    ).astype(bf16)
    pad = jnp.broadcast_to((padding != 0).astype(f32)[None], (8, length))
    lowest = segments[::TILE]
    highest = segments[TILE - 1 :: TILE]
    begins = jnp.sum((segments[None, :] < lowest[:, None]).astype(jnp.int32), axis=1)
    ends = jnp.sum((segments[None, :] <= highest[:, None]).astype(jnp.int32), axis=1)
    bounds = jnp.concatenate([begins // TILE, (ends + TILE - 1) // TILE])
    return key_extra, query_extra, pad, bounds, 2 * tiles


def local(
    tokens, cotangent, segments, padding, positions, ln1_gain, ln1_bias, w_qkv, b_qkv, w_out, b_out,
    ln2_gain, ln2_bias, w_up, b_up, w_down, b_down,
):
    w_zh = swap(w_out, "zh")
    w_c = swap(w_out, "c")
    w_both = swap(w_zh, "c")
    w_parts = (w_out, w_c, w_zh, w_both)
    gain_one, gain_two = ln1_gain[None], ln2_gain[None]

    key_extra, query_extra, pad, bounds, me_at = mask_parts(segments[0], padding[0])
    info = jnp.concatenate([bounds, lax.axis_index(MP)[None].astype(jnp.int32)])
    tables = rope_tables(positions[:, 0, :])
    h1, k_aug, v_aug, q_aug_t, q, k_t, v_t = project(
        tokens, w_qkv, b_qkv, gain_one, ln1_bias[None], *tables, key_extra, query_extra
    )

    o_parts, o_ts, lses = [], [], []
    for part in range(2):
        o, o_t, lse = attend(part, info, k_aug, v_t, q_aug_t, k_t, pad)
        o_zh = swap(o, "zh")
        o_parts.append((o, swap(o, "c"), o_zh, swap(o_zh, "c")))
        o_ts.append(o_t)
        lses.append(lse)

    x2, h2, act, du, mlp_sum, dh2 = [], [], [], [], [], []
    grad_b_up = 0.0
    for part in range(2):
        x2_own, h2_part, act_part, du_part, mlp_part, dh2_part, db_up = mlp(
            part, info, me_at, tokens, cotangent, o_parts[part], w_parts, b_out[None], gain_two,
            ln2_bias[None], w_up, b_up[None], w_down,
        )
        x2.append(x2_own)
        h2.append(h2_part)
        act.append(act_part)
        du.append(du_part)
        mlp_sum.append(mlp_part)
        dh2.append(added_on_arrival(dh2_part))
        grad_b_up = grad_b_up + db_up[0:1]
    grad_mlp = mlp_weights(h2, du, act, cotangent)

    dx2, g, small, dos = [], [], 0.0, []
    for part in range(2):
        dx2_own, g_own, d_own, d_c, d_zh, d_both, sums = middle(
            part, info, me_at, *dh2[part], x2[part], cotangent, gain_two, w_parts
        )
        dx2.append(dx2_own)
        g.append(g_own)
        small = small + sums[0:4]
        dos.append(jnp.stack([d_own, swap(d_c, "c"), swap(d_zh, "zh"), swap_both(d_both)]))

    dq = []
    dk = dv = None
    for part in range(2):
        dq_part, dk, dv = attend_back(
            part, info, me_at, k_aug, v_aug, k_t, q_aug_t, q, v_t, o_ts[part], lses[part], pad,
            dos[part], tables, dk, dv,
        )
        dq.append(dq_part)

    mixed = jnp.concatenate(
        [
            x2[part] + (here.astype(f32) + there.astype(f32)) + b_down[None]
            for part in range(2)
            for here, there in [added_on_arrival(mlp_sum[part])]
        ]
    ).astype(bf16)
    out_here, out_there = added_on_arrival(
        out_weights(info, me_at, o_parts[0], o_parts[1], g[0], g[1])
    )
    out_sum = (out_here.astype(f32) + out_there.astype(f32)).astype(bf16)
    hidden = w_up.shape[1]
    width = tokens.shape[1]
    grad_mlp = summed_over_packs(grad_mlp.reshape(2 * width, hidden)).reshape(2, width, hidden)
    grad_w_out = summed_over_packs(out_sum)

    dh1, grad_w_qkv, grad_b_qkv, small_one = project_back(
        info, me_at, tokens, h1, dq[0], dq[1], dk, dv, tables, w_qkv
    )
    here, there = added_on_arrival(dh1)
    grad_inputs = finish(info, me_at, here, there, tokens, gain_one, dx2[0], dx2[1])
    grad_w_qkv = summed_over_packs(grad_w_qkv.reshape(3 * width, WIDTH)).reshape(w_qkv.shape)

    shared, split = everywhere(jnp.concatenate([small, grad_b_up]), 4)
    first = jnp.concatenate(
        [small_one[0:2], jnp.pad(grad_b_qkv[0:3], ((0, 0), (0, width - WIDTH)))]
    )
    shared_one, split_one = everywhere(first, 2)
    return (
        mixed, grad_inputs, shared_one[0], shared_one[1], grad_w_qkv, split_one[:, :WIDTH],
        grad_w_out, shared[2], shared[0], shared[1], grad_mlp[0], split[0], grad_mlp[1], shared[3],
    )


def solution(mesh):
    packs = mesh.shape["dp"]
    if packs == 32:
        shape = (2, 4, 4, 2, 2)
    else:
        shape = (1, packs, 1, 2, 2)
    split = Mesh(mesh.devices.reshape(shape), EVERY)
    in_specs = (
        P(DP, None), P(DP, None), P(DP, None), P(DP, None), P(None, DP, None), P(), P(),
        P(None, None, MP), P(None, MP), P(MP, None), P(), P(), P(), P(None, MP), P(MP),
        P(MP, None), P(),
    )
    out_specs = (
        P(EVERY, None), P(EVERY, None), P(), P(), P(None, None, MP), P(None, MP), P(MP, None), P(),
        P(), P(), P(None, MP), P(MP), P(MP, None), P(),
    )
    return jax.shard_map(local, mesh=split, in_specs=in_specs, out_specs=out_specs, check_vma=False)
```

```python
import functools
import math

import jax
import jax.numpy as jnp
import ml_dtypes
import numpy as np
from jax import lax
from jax.experimental import pallas as pl
from jax.experimental.pallas import tpu as pltpu
from jax.sharding import Mesh
from jax.sharding import PartitionSpec as P

HEAD_DIM = 64
HEADS = 4
WIDTH = HEADS * HEAD_DIM
AUG = 128
TILE = 256
PLACES = 64
MIB = 1 << 20
DP = ("zl", "y", "x")
MP = ("zh", "c")
EVERY = ("zl", "y", "x", "zh", "c")

epsilon = 1e-06
NEG = -1e30
bf16 = jnp.bfloat16
f32 = jnp.float32


def dot_nn(a, b):
    return lax.dot_general(a, b, (((1,), (0,)), ((), ())), preferred_element_type=f32)


def dot_nt(a, b):
    return lax.dot_general(a, b, (((1,), (1,)), ((), ())), preferred_element_type=f32)


def dot_tn(a, b):
    return lax.dot_general(a, b, (((0,), (0,)), ((), ())), preferred_element_type=f32)


def normalized(values):
    center = jnp.mean(values, axis=-1, keepdims=True)
    shifted = values - center
    spread = jnp.mean(shifted * shifted, axis=-1, keepdims=True)
    inverse = lax.rsqrt(spread + epsilon)
    return shifted * inverse, inverse


def norm_back(hat, inverse, gain, grad):
    scaled = grad * gain
    return inverse * (
        scaled
        - jnp.mean(scaled, axis=-1, keepdims=True)
        - hat * jnp.mean(scaled * hat, axis=-1, keepdims=True)
    )


def turned(x, low, high):
    width = x.shape[1]
    pair = HEAD_DIM // 6
    return pltpu.roll(x, width - pair, 1) * low + pltpu.roll(x, pair, 1) * high


def three_parts(x):
    first = x.astype(bf16).astype(f32)
    rest = x - first
    second = rest.astype(bf16).astype(f32)
    return first, second, rest - second


def params(limit, axes=1):
    return pltpu.CompilerParams(
        dimension_semantics=("arbitrary",) * axes, vmem_limit_bytes=limit * MIB
    )


def whole(shape):
    return pl.BlockSpec(shape, lambda *_: (0,) * len(shape))


def rope_constants():
    pair = HEAD_DIM // 6
    feature = np.arange(WIDTH) % HEAD_DIM
    section, place = feature // (2 * pair), feature % (2 * pair)
    frequency = np.exp(-math.log(10000.0) * (place % pair) / pair)
    table = np.zeros((PLACES, 3, WIDTH))
    for s in range(3):
        for value in range(16):
            angle = value * frequency
            turns = section == s
            table[s * 16 + value, 0] = np.where(turns, np.cos(angle), 0.0)
            table[s * 16 + value, 1] = np.where(turns & (place < pair), -np.sin(angle), 0.0)
            table[s * 16 + value, 2] = np.where(turns & (place >= pair), np.sin(angle), 0.0)
    table[48, 0] = section == 3
    rest = table.reshape(PLACES, 3 * WIDTH).astype(np.float32)
    parts = []
    for _ in range(3):
        part = rest.astype(ml_dtypes.bfloat16)
        parts.append(part)
        rest = rest - part.astype(np.float32)
    return np.concatenate(parts)


def rope_factors(positions, table):
    row = lax.broadcasted_iota(jnp.int32, (PLACES, TILE), 0)
    where = jnp.where(
        row < 16, positions[0:1, :], jnp.where(row < 32, positions[1:2, :], positions[2:3, :])
    )
    hit = ((where == row % 16) & (row < 48)) | (row == 48)
    hit = jnp.where(hit, 1.0, 0.0)
    hits = jnp.concatenate([hit, hit, hit]).astype(bf16)
    factors = dot_tn(hits, table[...])
    return factors[:, :WIDTH], factors[:, WIDTH : 2 * WIDTH], factors[:, 2 * WIDTH :]


def head_lanes(pair, h):
    return pltpu.roll(pair, HEAD_DIM, 1) if h % 2 else pair


def side_by_side(heads):
    lane = lax.broadcasted_iota(jnp.int32, (TILE, AUG), 1)
    pairs = [
        jnp.where(lane < HEAD_DIM, heads[h], pltpu.roll(heads[h + 1], HEAD_DIM, 1))
        for h in range(0, HEADS, 2)
    ]
    return jnp.concatenate(pairs, axis=1)


def qkv_kernel(tok, w, b, gain, shift, pos, seg, pad, table, q_aug, k_aug, k_aug_t, v_aug, q_out):
    hat, _ = normalized(tok[...].astype(f32))
    normed = (hat * gain[...] + shift[...]).astype(bf16)
    cos, low, high = rope_factors(pos, table)
    q = dot_nn(normed, w[0]) + b[0:1, :]
    k = dot_nn(normed, w[1]) + b[1:2, :]
    v = dot_nn(normed, w[2]) + b[2:3, :]
    q = (q * cos + turned(q, low, high)) * (1.0 / math.sqrt(HEAD_DIM))
    k = k * cos + turned(k, low, high)
    q_out[...] = q.astype(bf16)
    k_t = k.T
    row = lax.broadcasted_iota(jnp.int32, (HEAD_DIM, TILE), 0)
    clip = seg[...]
    same = (row >= 1) & (row < 4) & (clip == row - 1)
    mask = jnp.where((row >= 1) & (row < 4) & (clip != row - 1), NEG, 0.0)
    mask = jnp.where(row == 0, jnp.where(pad[...] != 0, NEG, 0.0), mask)
    k_extra = jnp.where((row >= 4) & (row < 7), 1.0, mask)
    q_extra = jnp.where(same | (row == 0), 1.0, 0.0)
    for h in range(HEADS):
        at = h * AUG
        k_aug_t[at : at + HEAD_DIM, :] = k_t[h * HEAD_DIM : (h + 1) * HEAD_DIM, :].astype(bf16)
        k_aug_t[at + HEAD_DIM : at + AUG, :] = k_extra.astype(bf16)
    blank = jnp.zeros((HEAD_DIM, TILE), f32)
    k_side = jnp.concatenate([blank, k_extra]).T
    q_side = jnp.concatenate([blank, q_extra]).T
    lane = lax.broadcasted_iota(jnp.int32, (TILE, AUG), 1)
    ones = jnp.where((lane >= HEAD_DIM) & (lane < HEAD_DIM + 3), 1.0, 0.0)
    for h in range(HEADS):
        pair = slice(h // 2 * AUG, h // 2 * AUG + AUG)
        wide = slice(h * AUG, (h + 1) * AUG)
        q_aug[:, wide] = jnp.where(lane < HEAD_DIM, head_lanes(q[:, pair], h), q_side).astype(bf16)
        k_aug[:, wide] = jnp.where(lane < HEAD_DIM, head_lanes(k[:, pair], h), k_side).astype(bf16)
        v_aug[:, wide] = jnp.where(lane < HEAD_DIM, head_lanes(v[:, pair], h), ones).astype(bf16)


def project(tokens, w, b, gain, shift, positions, segments, padding, table):
    length, width = tokens.shape
    tiles = length // TILE

    def rows(columns):
        return pl.BlockSpec((TILE, columns), lambda i: (i, 0))

    def columns(count):
        return pl.BlockSpec((count, TILE), lambda i: (0, i))

    out = jax.ShapeDtypeStruct
    wide = out((length, HEADS * AUG), bf16)
    return pl.pallas_call(
        qkv_kernel,
        grid=(tiles,),
        in_specs=[
            rows(width), whole(w.shape), whole(b.shape), whole((1, width)), whole((1, width)),
            columns(3), columns(1), columns(1), whole(table.shape),
        ],
        out_specs=[
            rows(HEADS * AUG), rows(HEADS * AUG), columns(HEADS * AUG), rows(HEADS * AUG),
            rows(WIDTH),
        ],
        out_shape=[
            wide, wide, out((HEADS * AUG, length), bf16), wide, out((length, WIDTH), bf16),
        ],
        compiler_params=params(40),
        cost_estimate=pl.CostEstimate(
            flops=6 * length * width * WIDTH, bytes_accessed=20 * MIB, transcendentals=0
        ),
        name="project",
    )(tokens, w, b, gain, shift, positions, segments, padding, table)


def attend_kernel(
    info, q_aug, k_here, k_aug_t, v_aug, o, q_back_t, own_out, top, acc, held, *, part
):
    tile = 2 * pl.program_id(0) + part
    tiles = pl.num_programs(0) * 2
    begin, end = info[tile], info[tiles + tile]
    lane = lax.broadcasted_iota(jnp.int32, (TILE, AUG), 1)
    padded = k_here[:, HEAD_DIM : HEAD_DIM + 1].astype(f32) < -1.0
    owns = []
    for h in range(HEADS):
        wide = slice(h * AUG, (h + 1) * AUG)
        product = q_aug[:, wide].astype(f32) * k_here[:, wide].astype(f32)
        own = jnp.sum(jnp.where(lane < HEAD_DIM, product, 0.0), axis=1, keepdims=True)
        owns.append(own)
        top[:, wide] = jnp.broadcast_to(jnp.where(padded, own, -3e38), (TILE, AUG))

    def score(j, _):
        keys = pl.ds(pl.multiple_of(j * TILE, TILE), TILE)
        for h in range(HEADS):
            wide = slice(h * AUG, (h + 1) * AUG)
            scores = dot_nn(q_aug[:, wide], k_aug_t[wide, keys])
            held[h, :, keys] = scores
            top[:, wide] = jnp.maximum(
                top[:, wide], jnp.maximum(scores[:, :AUG], scores[:, AUG:])
            )
        return 0

    lax.fori_loop(begin, end, score, 0)
    here = pl.ds(pl.multiple_of(tile * TILE, TILE), TILE)
    raws = []
    for h in range(HEADS):
        wide = slice(h * AUG, (h + 1) * AUG)
        peak = jnp.max(top[:, wide], axis=1, keepdims=True)
        raw = jnp.where(padded, jnp.exp(owns[h] - peak), 0.0)
        raws.append(raw)
        top[:, wide] = jnp.broadcast_to(peak, (TILE, AUG))
        acc[:, wide] = raw * v_aug[here, wide].astype(f32)

    def mix(j, _):
        keys = pl.ds(pl.multiple_of(j * TILE, TILE), TILE)
        for h in range(HEADS):
            wide = slice(h * AUG, (h + 1) * AUG)
            scores, peak = held[h, :, keys], top[:, wide]
            probs = jnp.concatenate(
                [jnp.exp(scores[:, :AUG] - peak), jnp.exp(scores[:, AUG:] - peak)], axis=1
            )
            acc[:, wide] += dot_nn(probs.astype(bf16), v_aug[keys, wide])
        return 0

    lax.fori_loop(begin, end, mix, 0)
    heads = []
    own_all = jnp.zeros((TILE, AUG), f32)
    for h in range(HEADS):
        wide = slice(h * AUG, (h + 1) * AUG)
        mixed = acc[:, wide]
        total = mixed[:, HEAD_DIM : HEAD_DIM + 1]
        heads.append(mixed / total)
        one, two, three = three_parts(-(top[:, h * AUG : h * AUG + 1] + jnp.log(total)))
        back = jnp.where(lane == HEAD_DIM + 4, one, q_aug[:, wide].astype(f32))
        back = jnp.where(lane == HEAD_DIM + 5, two, back)
        back = jnp.where(lane == HEAD_DIM + 6, three, back)
        q_back_t[wide, :] = back.T.astype(bf16)
        own_all = jnp.where(lane == h, raws[h] / total, own_all)
    own_out[...] = own_all
    o[...] = side_by_side(heads).astype(bf16)


def attend(part, info, q_aug, k_aug, k_aug_t, v_aug):
    length = k_aug.shape[0]
    half = length // 2

    def rows(columns):
        return pl.BlockSpec((TILE, columns), lambda i, *_: (2 * i + part, 0))

    def packed(columns):
        return pl.BlockSpec((TILE, columns), lambda i, *_: (i, 0))

    out = jax.ShapeDtypeStruct
    return pl.pallas_call(
        functools.partial(attend_kernel, part=part),
        grid_spec=pltpu.PrefetchScalarGridSpec(
            num_scalar_prefetch=1,
            grid=(half // TILE,),
            in_specs=[
                rows(HEADS * AUG), rows(HEADS * AUG), whole(k_aug_t.shape), whole(v_aug.shape),
            ],
            out_specs=[
                packed(WIDTH), pl.BlockSpec((HEADS * AUG, TILE), lambda i, *_: (0, i)), packed(AUG),
            ],
            scratch_shapes=[
                pltpu.VMEM((TILE, HEADS * AUG), f32), pltpu.VMEM((TILE, HEADS * AUG), f32),
                pltpu.VMEM((HEADS, TILE, length), f32),
            ],
        ),
        out_shape=[
            out((half, WIDTH), bf16), out((HEADS * AUG, half), bf16), out((half, AUG), f32),
        ],
        compiler_params=params(40),
        cost_estimate=pl.CostEstimate(
            flops=24 * half * length * WIDTH, bytes_accessed=6 * MIB, transcendentals=0
        ),
        name="attend",
    )(info, q_aug, k_aug, k_aug_t, v_aug)


def gelu_parts(u):
    size = jnp.abs(u)
    t = 1.0 / (1.0 + (0.3275911 / math.sqrt(2.0)) * size)
    bell = jnp.exp(-0.5 * (u * u))
    poly = 0.5 * 1.061405429
    for c in (-1.453152027, 1.421413741, -0.284496736, 0.254829592):
        poly = poly * t + 0.5 * c
    tail = poly * t * bell
    below = jnp.where(u >= 0, 1.0 - tail, tail)
    return u * below, below + u * bell * (1.0 / math.sqrt(2.0 * math.pi))


def mlp_kernel(
    info, tok, cot, o_all, w_all, b_out, gain, shift, w_up, b_up, w_down,
    x2, h2, act, du, mlp, dh2, db_up,
):
    i = pl.program_id(0)
    mid = tok[...].astype(f32) + b_out[...]
    for j in range(4):
        mid = mid + dot_nn(o_all[j], w_all[j])

    @pl.when(i == 0)
    def _():
        x2[...] = mid
        db_up[...] = jnp.zeros_like(db_up)

    hat, _ = normalized(mid)
    normed = (hat * gain[...] + shift[...]).astype(bf16)
    h2[...] = normed
    u = dot_nn(normed, w_up[...]) + b_up[...]
    grad_act = dot_nt(cot[...], w_down[...])
    value, slope = gelu_parts(u)
    value = value.astype(bf16)
    grad = (grad_act * slope).astype(bf16)
    act[...] = value
    du[...] = grad
    db_up[0:1, :] += jnp.sum(grad.astype(f32), axis=0, keepdims=True)
    mlp[0] = dot_nn(value, w_down[...]).astype(bf16)
    dh2[0] = dot_nt(grad, w_up[...]).astype(bf16)


def mlp(part, info, me_at, tokens, cotangent, o_all, w_all, b_out, gain, shift, w_up, b_up, w_down):
    length, width = tokens.shape
    half = length // 2
    hidden = w_up.shape[1]
    owners = half // TILE

    def owner(i, info):
        return jnp.bitwise_xor(info[me_at], i)

    def rows(columns):
        return pl.BlockSpec((TILE, columns), lambda i, info: (2 * owner(i, info) + part, 0))

    def packed(columns):
        return pl.BlockSpec((TILE, columns), lambda i, info: (owner(i, info), 0))

    def relative(columns):
        return pl.BlockSpec((1, TILE, columns), lambda i, info: (i, 0, 0))

    out = jax.ShapeDtypeStruct
    return pl.pallas_call(
        mlp_kernel,
        grid_spec=pltpu.PrefetchScalarGridSpec(
            num_scalar_prefetch=1,
            grid=(owners,),
            in_specs=[
                rows(width), rows(width),
                pl.BlockSpec((4, TILE, WIDTH), lambda i, info: (0, owner(i, info), 0)),
                whole(w_all.shape),
            ]
            + [whole((1, width))] * 3
            + [whole(w_up.shape), whole((1, hidden)), whole(w_down.shape)],
            out_specs=[
                whole((TILE, width)), packed(width), packed(hidden), packed(hidden),
                relative(width), relative(width), whole((8, hidden)),
            ],
        ),
        out_shape=[
            out((TILE, width), f32), out((half, width), bf16), out((half, hidden), bf16),
            out((half, hidden), bf16), out((owners, TILE, width), bf16),
            out((owners, TILE, width), bf16), out((8, hidden), f32),
        ],
        compiler_params=params(56),
        cost_estimate=pl.CostEstimate(
            flops=20 * half * width * hidden, bytes_accessed=20 * MIB, transcendentals=0
        ),
        name="mlp",
    )(info, tokens, cotangent, o_all, w_all, b_out, gain, shift, w_up, b_up, w_down)


def mlp_weights_kernel(h2_a, h2_b, du_a, du_b, act_a, act_b, cot_a, cot_b, out, up, down):
    i = pl.program_id(0)

    @pl.when(i == 0)
    def _():
        up[...] = jnp.zeros_like(up)
        down[...] = jnp.zeros_like(down)

    up[...] += dot_tn(h2_a[...], du_a[...]) + dot_tn(h2_b[...], du_b[...])
    down[...] += dot_tn(act_a[...], cot_a[...]) + dot_tn(act_b[...], cot_b[...])

    @pl.when(i == pl.num_programs(0) - 1)
    def _():
        out[0] = up[...].astype(bf16)
        out[1] = down[...].astype(bf16)


def mlp_weights(h2, du, act, cotangent):
    half, width = h2[0].shape
    hidden = du[0].shape[1]

    def packed(columns):
        return pl.BlockSpec((TILE, columns), lambda i: (i, 0))

    def rows(part):
        return pl.BlockSpec((TILE, width), lambda i: (2 * i + part, 0))

    return pl.pallas_call(
        mlp_weights_kernel,
        grid=(half // TILE,),
        in_specs=[packed(width)] * 2 + [packed(hidden)] * 4 + [rows(0), rows(1)],
        out_specs=whole((2, width, hidden)),
        out_shape=jax.ShapeDtypeStruct((2, width, hidden), bf16),
        scratch_shapes=[pltpu.VMEM((width, hidden), f32), pltpu.VMEM((hidden, width), f32)],
        compiler_params=params(56),
        cost_estimate=pl.CostEstimate(
            flops=8 * half * width * hidden, bytes_accessed=20 * MIB, transcendentals=0
        ),
        name="mlp_weights",
    )(*h2, *du, *act, cotangent, cotangent)


def middle_kernel(
    info, here, there, x2, cot, gain, w_all, dx2, g, d_0, d_1, d_2, d_3, small, *, me_at
):
    grad = here[...].astype(f32) + there[...].astype(f32)
    hat, inverse = normalized(x2[...])
    dy = cot[...].astype(f32)
    full = dy + norm_back(hat, inverse, gain[...], grad)
    dx2[...] = full
    low = full.astype(bf16)
    g[...] = low
    small[...] = jnp.zeros_like(small)
    small[0:1, :] = jnp.sum(grad * hat, axis=0, keepdims=True)
    small[1:2, :] = jnp.sum(grad, axis=0, keepdims=True)
    small[2:3, :] = jnp.sum(low.astype(f32), axis=0, keepdims=True)
    small[3:4, :] = jnp.sum(dy, axis=0, keepdims=True)
    for j, d_j in enumerate((d_0, d_1, d_2, d_3)):
        d_j[...] = dot_nt(low, w_all[jnp.bitwise_xor(info[me_at], j)]).astype(bf16)


def middle(part, info, me_at, here, there, x2, cotangent, gain, w_all):
    width = x2.shape[1]
    out = jax.ShapeDtypeStruct
    own = whole((TILE, width))
    return pl.pallas_call(
        functools.partial(middle_kernel, me_at=me_at),
        grid_spec=pltpu.PrefetchScalarGridSpec(
            num_scalar_prefetch=1,
            grid=(1,),
            in_specs=[
                own, own, own,
                pl.BlockSpec((TILE, width), lambda i, info: (2 * info[me_at] + part, 0)),
                whole((1, width)), whole(w_all.shape),
            ],
            out_specs=[own, own] + [whole((TILE, WIDTH))] * 4 + [whole((8, width))],
        ),
        out_shape=[out((TILE, width), f32), out((TILE, width), bf16)]
        + [out((TILE, WIDTH), bf16)] * 4
        + [out((8, width), f32)],
        compiler_params=params(40),
        cost_estimate=pl.CostEstimate(
            flops=2 * TILE * width * width, bytes_accessed=8 * MIB, transcendentals=0
        ),
        name="middle",
    )(info, here, there, x2, cotangent, gain, w_all)


def out_weights_kernel(info, o_a, o_b, g_a, g_b, out):
    for j in range(4):
        out[j] = (dot_tn(o_a[j], g_a[...]) + dot_tn(o_b[j], g_b[...])).astype(bf16)


def out_weights(info, me_at, o_a, o_b, g_a, g_b):
    width = g_a.shape[1]
    own = pl.BlockSpec((4, TILE, WIDTH), lambda i, info: (0, info[me_at], 0))
    return pl.pallas_call(
        out_weights_kernel,
        grid_spec=pltpu.PrefetchScalarGridSpec(
            num_scalar_prefetch=1,
            grid=(1,),
            in_specs=[own] * 2 + [whole((TILE, width))] * 2,
            out_specs=whole((4, WIDTH, width)),
        ),
        out_shape=jax.ShapeDtypeStruct((4, WIDTH, width), bf16),
        compiler_params=params(40),
        cost_estimate=pl.CostEstimate(
            flops=4 * TILE * width * width, bytes_accessed=6 * MIB, transcendentals=0
        ),
        name="out_weights",
    )(info, o_a, o_b, g_a, g_b)


def attend_back_kernel(
    info, k_aug, v_aug, q_back_t, q, o, own_in, do, pos, table, dk_in, dv_in,
    dq_out, dk, dv, do_side, q_lanes, do_lanes, dq_wide, *, part, me_at, first,
):
    i = pl.program_id(0)
    tiles = pl.num_programs(0) * 2
    tile = 2 * jnp.bitwise_xor(info[me_at], i) + part

    @pl.when(i == 0)
    def _():
        if first:
            dk[...] = jnp.zeros_like(dk)
            dv[...] = jnp.zeros_like(dv)
        else:
            dk[...] = dk_in[...]
            dv[...] = dv_in[...]

    here = pl.ds(pl.multiple_of(tile * TILE, TILE), TILE)
    do_here, q_here = do[...], q[...]
    do_f, o_f = do_here.astype(f32), o[...].astype(f32)
    lane = lax.broadcasted_iota(jnp.int32, (TILE, AUG), 1)
    head = lax.broadcasted_iota(jnp.int32, (TILE, WIDTH), 1) // HEAD_DIM
    p_wide = jnp.zeros((TILE, WIDTH), f32)
    ds_wide = jnp.zeros((TILE, WIDTH), f32)
    for h in range(HEADS):
        pair = slice(h // 2 * AUG, h // 2 * AUG + AUG)
        wide = slice(h * AUG, (h + 1) * AUG)
        do_h = jnp.where(lane < HEAD_DIM, head_lanes(do_f[:, pair], h), 0.0)
        delta = jnp.sum(do_h * head_lanes(o_f[:, pair], h), axis=1, keepdims=True)
        one, two, three = three_parts(-delta)
        side = jnp.where(lane == HEAD_DIM, one, do_h)
        side = jnp.where(lane == HEAD_DIM + 1, two, side)
        side = jnp.where(lane == HEAD_DIM + 2, three, side)
        do_side[wide, :] = side.T.astype(bf16)
        q_lanes[h] = jnp.where(head == h, q_here, jnp.zeros_like(q_here))
        do_lanes[h] = jnp.where(head == h, do_here, jnp.zeros_like(do_here))
        p_own = own_in[:, h : h + 1]
        dp_own = jnp.sum(do_h * v_aug[here, wide].astype(f32), axis=1, keepdims=True)
        ds_own = p_own * (dp_own - delta)
        dq_wide[:, wide] = ds_own * k_aug[here, wide].astype(f32)
        p_wide = jnp.where(head == h, p_own, p_wide)
        ds_wide = jnp.where(head == h, ds_own, ds_wide)
    dk[here, :] += ds_wide * q_here.astype(f32)
    dv[here, :] += p_wide * do_f

    def step(j, _):
        keys = pl.ds(pl.multiple_of(j * TILE, TILE), TILE)
        dk_new, dv_new = dk[keys, :], dv[keys, :]
        for h in range(HEADS):
            wide = slice(h * AUG, (h + 1) * AUG)
            probs = jnp.exp(dot_nn(k_aug[keys, wide], q_back_t[wide, :]))
            ds = (probs * dot_nn(v_aug[keys, wide], do_side[wide, :])).astype(bf16)
            dv_new = dv_new + dot_nn(probs.astype(bf16), do_lanes[h])
            dk_new = dk_new + dot_nn(ds, q_lanes[h])
            dq_wide[:, wide] += dot_tn(ds, k_aug[keys, wide])
        dk[keys, :] = dk_new
        dv[keys, :] = dv_new
        return 0

    lax.fori_loop(info[tile], info[tiles + tile], step, 0)
    dq = side_by_side([dq_wide[:, h * AUG : (h + 1) * AUG] for h in range(HEADS)])
    dq = dq * (1.0 / math.sqrt(HEAD_DIM))
    cos, low, high = rope_factors(pos, table)
    dq_out[...] = (dq * cos - turned(dq, low, high)).astype(bf16)


def attend_back(
    part, info, me_at, k_aug, v_aug, q_back_t, q, o, own, do, positions, table, dk, dv
):
    length = k_aug.shape[0]
    half = length // 2

    def owner(i, info):
        return jnp.bitwise_xor(info[me_at], i)

    def rows(columns):
        return pl.BlockSpec((TILE, columns), lambda i, info: (2 * owner(i, info) + part, 0))

    def packed(columns):
        return pl.BlockSpec((TILE, columns), lambda i, info: (owner(i, info), 0))

    out = jax.ShapeDtypeStruct
    first = dk is None
    if first:
        dk = dv = jnp.zeros((8, WIDTH), f32)
    return pl.pallas_call(
        functools.partial(attend_back_kernel, part=part, me_at=me_at, first=first),
        grid_spec=pltpu.PrefetchScalarGridSpec(
            num_scalar_prefetch=1,
            grid=(half // TILE,),
            in_specs=[
                whole(k_aug.shape), whole(v_aug.shape),
                pl.BlockSpec((HEADS * AUG, TILE), lambda i, info: (0, owner(i, info))),
                rows(WIDTH), packed(WIDTH), packed(AUG),
                pl.BlockSpec((None, TILE, WIDTH), lambda i, info: (i, 0, 0)),
                pl.BlockSpec((3, TILE), lambda i, info: (0, 2 * owner(i, info) + part)),
                whole(table.shape), whole(dk.shape), whole(dv.shape),
            ],
            out_specs=[packed(WIDTH), whole((length, WIDTH)), whole((length, WIDTH))],
            scratch_shapes=[
                pltpu.VMEM((HEADS * AUG, TILE), bf16), pltpu.VMEM((HEADS, TILE, WIDTH), bf16),
                pltpu.VMEM((HEADS, TILE, WIDTH), bf16), pltpu.VMEM((TILE, HEADS * AUG), f32),
            ],
        ),
        out_shape=[out((half, WIDTH), bf16), out((length, WIDTH), f32), out((length, WIDTH), f32)],
        compiler_params=params(56),
        cost_estimate=pl.CostEstimate(
            flops=72 * half * length * WIDTH, bytes_accessed=16 * MIB, transcendentals=0
        ),
        name="attend_back",
    )(info, k_aug, v_aug, q_back_t, q, o, own, do, positions, table, dk, dv)


def project_back_kernel(
    info, tok, gain, shift, dq_a, dq_b, dk, dv, pos, table, w, dh1, sums, acc, grad_b, small
):
    i = pl.program_id(0)

    @pl.when(i == 0)
    def _():
        acc[...] = jnp.zeros_like(acc)
        grad_b[...] = jnp.zeros_like(grad_b)
        small[...] = jnp.zeros_like(small)

    hat, _ = normalized(tok[...].astype(f32))
    normed = (hat * gain[...] + shift[...]).astype(bf16)
    dq = jnp.where(i % 2 == 0, dq_a[...], dq_b[...])
    dk_here = dk[...]
    cos, low, high = rope_factors(pos, table)
    dk_low = (dk_here * cos - turned(dk_here, low, high)).astype(bf16)
    dv_low = dv[...].astype(bf16)
    width = normed.shape[1]
    grad = None
    for c, part in enumerate((dq, dk_low, dv_low)):
        acc[c * width : (c + 1) * width, :] += dot_tn(normed, part)
        grad_b[c : c + 1, :] += jnp.sum(part.astype(f32), axis=0, keepdims=True)
        term = dot_nt(part, w[c])
        grad = term if grad is None else grad + term
    small[0:1, :] += jnp.sum(grad * hat, axis=0, keepdims=True)
    small[1:2, :] += jnp.sum(grad, axis=0, keepdims=True)
    dh1[0] = grad.astype(bf16)

    @pl.when(i == pl.num_programs(0) - 1)
    def _():
        blocks = sums.shape[0]
        deep = 3 * width // blocks
        extra_rows = sums.shape[1] - deep
        rows = [grad_b[c : c + 1, :] for c in range(3)] + [
            small[v : v + 1, r * WIDTH : (r + 1) * WIDTH]
            for v in range(2)
            for r in range(width // WIDTH)
        ]
        for n in range(blocks):
            sums[n, 0:deep, :] = acc[n * deep : (n + 1) * deep, :].astype(bf16)
            row = lax.broadcasted_iota(jnp.int32, (extra_rows, WIDTH), 0)
            extra = jnp.zeros((extra_rows, WIDTH), f32)
            for m, value in enumerate(rows[n::blocks]):
                one, two, three = three_parts(value)
                extra = jnp.where(row == 2 * m, one, jnp.where(row == 2 * m + 1, two, extra))
            sums[n, deep : deep + extra_rows, :] = extra.astype(bf16)


def project_back(info, me_at, tokens, gain, shift, dq_a, dq_b, dk, dv, positions, table, w, blocks):
    length, width = tokens.shape
    tiles = length // TILE

    def place(i, info):
        return 2 * jnp.bitwise_xor(info[me_at], i // 2) + i % 2

    def rows(columns):
        return pl.BlockSpec((TILE, columns), lambda i, info: (place(i, info), 0))

    def packed(columns):
        return pl.BlockSpec(
            (TILE, columns), lambda i, info: (jnp.bitwise_xor(info[me_at], i // 2), 0)
        )

    out = jax.ShapeDtypeStruct
    vectors = -(-(3 + 2 * width // WIDTH) // blocks)
    sums = (blocks, 3 * width // blocks + -(-vectors // 8) * 16, WIDTH)
    return pl.pallas_call(
        project_back_kernel,
        grid_spec=pltpu.PrefetchScalarGridSpec(
            num_scalar_prefetch=1,
            grid=(tiles,),
            in_specs=[
                rows(width), whole((1, width)), whole((1, width)), packed(WIDTH), packed(WIDTH),
                rows(WIDTH), rows(WIDTH),
                pl.BlockSpec((3, TILE), lambda i, info: (0, place(i, info))), whole(table.shape),
                whole(w.shape),
            ],
            out_specs=[
                pl.BlockSpec((1, TILE, width), lambda i, info: (i // 2, i % 2, 0)), whole(sums),
            ],
            scratch_shapes=[
                pltpu.VMEM((3 * width, WIDTH), f32), pltpu.VMEM((8, WIDTH), f32),
                pltpu.VMEM((8, width), f32),
            ],
        ),
        out_shape=[out((tiles // 2, 2 * TILE, width), bf16), out(sums, bf16)],
        compiler_params=params(48),
        cost_estimate=pl.CostEstimate(
            flops=24 * length * width * WIDTH, bytes_accessed=20 * MIB, transcendentals=0
        ),
        name="project_back",
    )(info, tokens, gain, shift, dq_a, dq_b, dk, dv, positions, table, w)


def finish_kernel(info, here, there, tok, gain, dx2_a, dx2_b, out):
    grad = here[...].astype(f32) + there[...].astype(f32)
    hat, inverse = normalized(tok[...].astype(f32))
    dx2 = jnp.where(pl.program_id(0) == 0, dx2_a[...], dx2_b[...])
    out[...] = dx2 + norm_back(hat, inverse, gain[...], grad)


def finish(info, me_at, here, there, tokens, gain, dx2_a, dx2_b):
    width = tokens.shape[1]
    share = here.shape[0]
    rows = pl.BlockSpec((TILE, width), lambda i, info: (i, 0))
    return pl.pallas_call(
        finish_kernel,
        grid_spec=pltpu.PrefetchScalarGridSpec(
            num_scalar_prefetch=1,
            grid=(share // TILE,),
            in_specs=[
                rows, rows,
                pl.BlockSpec((TILE, width), lambda i, info: (2 * info[me_at] + i, 0)),
                whole((1, width)), whole((TILE, width)), whole((TILE, width)),
            ],
            out_specs=rows,
        ),
        out_shape=jax.ShapeDtypeStruct((share, width), f32),
        compiler_params=params(32),
        name="finish",
    )(info, here, there, tokens, gain, dx2_a, dx2_b)


def swap(array, axis, bit=1):
    size = lax.axis_size(axis)
    if size == 1:
        return jnp.zeros_like(array)
    return lax.ppermute(array, axis, [(i, i ^ bit) for i in range(size)])


def swap_both(array):
    return lax.ppermute(array, MP, [(i, i ^ 3) for i in range(4)])


def added_on_arrival(parts):
    other = swap(jnp.concatenate([parts[1:2], parts[3:4]]), "c")
    keep = parts[0].astype(f32) + other[0].astype(f32)
    give = (parts[2].astype(f32) + other[1].astype(f32)).astype(bf16)
    return keep.astype(bf16), swap(give, "zh")


def after(value, *earlier):
    return lax.optimization_barrier((value, earlier))[0]


def two_parts(value):
    first = value.astype(bf16)
    return first, (value - first.astype(f32)).astype(bf16)


def scattered_sum(rows, axes):
    group = lax.axis_size(axes)
    length, width = rows.shape
    blocks = rows.reshape(group, length // group, width)
    blocks = lax.all_to_all(blocks, axes, 0, 0, tiled=True)
    return jnp.sum(blocks.astype(f32), axis=0).astype(bf16)


def spread(block, axes):
    group = lax.axis_size(axes)
    return lax.all_to_all(
        jnp.broadcast_to(block[None], (group,) + block.shape), axes, 0, 0, tiled=True
    )


def both_sums(total):
    if lax.axis_size("zl") == 1:
        return total
    return (total.astype(f32) + swap(total, "zl").astype(f32)).astype(bf16)


def clip_bounds(segments):
    length = segments.shape[0]
    tiles = length // TILE
    ends = jnp.sum((segments[None, :] < jnp.arange(4)[:, None]).astype(jnp.int32), axis=1)
    first = jnp.arange(tiles) * TILE
    low = jnp.zeros((tiles,), jnp.int32)
    high = jnp.full((tiles,), length, jnp.int32)
    for n in range(1, 3):
        low = jnp.where(ends[n] <= first, ends[n], low)
    for n in (2, 1):
        high = jnp.where(ends[n] >= first + TILE, ends[n], high)
    return jnp.concatenate([low // TILE, (high + TILE - 1) // TILE]), 2 * tiles


def local(
    tokens, cotangent, segments, padding, positions, ln1_gain, ln1_bias, w_qkv, b_qkv, w_out, b_out,
    ln2_gain, ln2_bias, w_up, b_up, w_down, b_down,
):
    width, hidden = w_up.shape
    w_all = lax.all_gather(w_out, MP)
    gain_one, shift_one = ln1_gain[None], ln1_bias[None]
    gain_two, shift_two = ln2_gain[None], ln2_bias[None]
    bounds, me_at = clip_bounds(segments[0])
    info = jnp.concatenate([bounds, lax.axis_index(MP)[None].astype(jnp.int32)])
    table = jnp.asarray(rope_constants())
    places = positions[:, 0, :]
    q_aug, k_aug, k_aug_t, v_aug, q = project(
        tokens, w_qkv, b_qkv, gain_one, shift_one, places, segments, padding, table
    )

    o_0, q_back_0, own_0 = attend(0, info, q_aug, k_aug, k_aug_t, v_aug)
    all_0 = lax.all_gather(o_0, MP)
    o_1, q_back_1, own_1 = attend(1, after(info, o_0, w_all), q_aug, k_aug, k_aug_t, v_aug)
    all_1 = lax.all_gather(o_1, MP)

    def mlp_half(part, info, o_all):
        return mlp(
            part, info, me_at, tokens, cotangent, o_all, w_all, b_out[None], gain_two, shift_two,
            w_up, b_up[None], w_down,
        )

    x2_0, h2_0, act_0, du_0, mlp_0, dh2_0, db_0 = mlp_half(0, info, all_0)
    x2_1, h2_1, act_1, du_1, mlp_1, dh2_1, db_1 = mlp_half(1, after(info, x2_0), all_1)
    here_0, there_0 = added_on_arrival(dh2_0)
    here_1, there_1 = added_on_arrival(dh2_1)
    grad_mlp = mlp_weights((h2_0, h2_1), (du_0, du_1), (act_0, act_1), cotangent)

    def exchanged(d_own, d_c, d_zh, d_both):
        return jnp.stack([d_own, swap(d_c, "c"), swap(d_zh, "zh"), swap_both(d_both)])

    dx2_0, g_0, *d_0, small_0 = middle(
        0, after(info, grad_mlp), me_at, here_0, there_0, x2_0, cotangent, gain_two, w_all
    )
    do_0 = exchanged(*d_0)
    dx2_1, g_1, *d_1, small_1 = middle(
        1, after(info, do_0), me_at, here_1, there_1, x2_1, cotangent, gain_two, w_all
    )
    do_1 = exchanged(*d_1)
    out_parts = out_weights(info, me_at, all_0, all_1, g_0, g_1)

    small = small_0[0:4] + small_1[0:4]
    first, second = two_parts(small.reshape(4, width // AUG, AUG))
    extra = jnp.concatenate([first, second], axis=1)
    extra = jnp.pad(extra, ((0, 0), (0, WIDTH - extra.shape[1]), (0, 0)))
    grad_out = jnp.concatenate([out_parts, extra], axis=2)
    grad_out = lax.psum_scatter(grad_out, MP, scatter_dimension=0, tiled=False)

    mlp_sum = jnp.concatenate([mlp_0, mlp_1], axis=1)
    other = swap(jnp.concatenate([mlp_sum[1:2], mlp_sum[3:4]]), "c")

    part_sum = scattered_sum(grad_mlp.reshape(2 * width, hidden), ("y", "x"))
    dq_0, dk, dv = attend_back(
        0, after(info, out_parts), me_at, k_aug, v_aug, q_back_0, q, o_0, own_0, do_0, places, table,
        None, None,
    )

    part_sum, other = after((part_sum, other), dq_0)
    keep = mlp_sum[0].astype(f32) + other[0].astype(f32)
    give = (mlp_sum[2].astype(f32) + other[1].astype(f32)).astype(bf16)
    part_sum = both_sums(part_sum)
    bias = jnp.concatenate(two_parts((db_0[0] + db_1[0]).reshape(hidden // AUG, AUG)))
    grad_out = jnp.concatenate(
        [
            grad_out[:, :width],
            jnp.concatenate(
                [grad_out[: 2 * width // AUG, width:], bias,
                 jnp.zeros((WIDTH - 2 * (width + hidden) // AUG, AUG), bf16)]
            ),
        ],
        axis=1,
    )
    out_sum = scattered_sum(grad_out, ("y", "x"))
    there = swap(give, "zh")
    dq_1, dk, dv = attend_back(
        1, after(info, part_sum, give, grad_out), me_at, k_aug, v_aug, q_back_1, q, o_1, own_1,
        do_1, places, table, dk, dv,
    )
    grad_mlp = spread(part_sum, ("y", "x")).reshape(2, width, hidden)
    grad_out = spread(both_sums(after(out_sum, dq_1)), ("y", "x")).reshape(WIDTH, width + AUG)
    dh1, sums = project_back(
        after(info, grad_out), me_at, tokens, gain_one, shift_one, dq_0, dq_1, dk, dv, places, table,
        w_qkv, lax.axis_size(DP),
    )
    blocks, deep, _ = sums.shape
    sums = after(sums, grad_mlp)
    sums = spread(scattered_sum(sums.reshape(blocks * deep, WIDTH), DP), DP)
    mixed = (
        jnp.concatenate([x2_0, x2_1]) + (keep + there.astype(f32)) + b_down[None]
    ).astype(bf16)
    here, there = added_on_arrival(dh1)
    grad_inputs = finish(info, me_at, here, there, tokens, gain_one, dx2_0, dx2_1)

    extra = grad_out[:, width:].astype(f32)
    count = width // AUG
    vector = (extra[:count] + extra[count : 2 * count]).reshape(width)
    shared = lax.all_gather(vector, MP)
    count_up = hidden // AUG
    grad_b_up = extra[2 * count : 2 * count + 2 * count_up]
    grad_b_up = (grad_b_up[:count_up] + grad_b_up[count_up:]).reshape(hidden)

    kept = 3 * width // blocks
    grad_qkv = sums[:, :kept].astype(f32).reshape(w_qkv.shape)
    rows = jnp.concatenate(
        [
            sums[:, at].astype(f32) + sums[:, at + 1].astype(f32)
            for at in range(kept, deep, 2)
        ]
    )
    count = width // WIDTH
    ln = rows[3 : 3 + 2 * count]
    ln = ln + swap(ln, "c")
    ln = (ln + swap(ln, "zh")).reshape(2, width)
    return (
        mixed, grad_inputs, ln[0], ln[1], grad_qkv, rows[0:3], grad_out[:, :width].astype(f32),
        shared[2], shared[0], shared[1], grad_mlp[0].astype(f32), grad_b_up,
        grad_mlp[1].astype(f32), shared[3],
    )


def solution(mesh):
    packs = mesh.shape["dp"]
    if packs == 32:
        shape = (2, 4, 4, 2, 2)
    else:
        shape = (1, packs, 1, 2, 2)
    split = Mesh(mesh.devices.reshape(shape), EVERY)
    in_specs = (
        P(DP, None), P(DP, None), P(DP, None), P(DP, None), P(None, DP, None), P(), P(),
        P(None, None, MP), P(None, MP), P(MP, None), P(), P(), P(), P(None, MP), P(MP),
        P(MP, None), P(),
    )
    out_specs = (
        P(EVERY, None), P(EVERY, None), P(), P(), P(None, None, MP), P(None, MP), P(MP, None), P(),
        P(), P(), P(None, MP), P(MP), P(MP, None), P(),
    )
    return jax.shard_map(local, mesh=split, in_specs=in_specs, out_specs=out_specs, check_vma=False)
```

```python
import functools
import math

import jax
import jax.numpy as jnp
import ml_dtypes
import numpy as np
from jax import lax
from jax.experimental import pallas as pl
from jax.experimental.pallas import tpu as pltpu
from jax.sharding import Mesh
from jax.sharding import PartitionSpec as P

HEAD_DIM = 64
HEADS = 4
WIDTH = HEADS * HEAD_DIM
AUG = 128
TILE = 256
PLACES = 64
LIMIT = 56
MIB = 1 << 20
DP = ("zl", "y", "x")
MP = ("zh", "c")
EVERY = ("zl", "y", "x", "zh", "c")

epsilon = 1e-06
NEG = -1e30
bf16 = jnp.bfloat16
f32 = jnp.float32


def dot_nn(a, b):
    return lax.dot_general(a, b, (((1,), (0,)), ((), ())), preferred_element_type=f32)


def dot_nt(a, b):
    return lax.dot_general(a, b, (((1,), (1,)), ((), ())), preferred_element_type=f32)


def dot_tn(a, b):
    return lax.dot_general(a, b, (((0,), (0,)), ((), ())), preferred_element_type=f32)


def normalized(values):
    center = jnp.mean(values, axis=-1, keepdims=True)
    shifted = values - center
    spread = jnp.mean(shifted * shifted, axis=-1, keepdims=True)
    inverse = lax.rsqrt(spread + epsilon)
    return shifted * inverse, inverse


def norm_back(hat, inverse, gain, grad):
    scaled = grad * gain
    return inverse * (
        scaled
        - jnp.mean(scaled, axis=-1, keepdims=True)
        - hat * jnp.mean(scaled * hat, axis=-1, keepdims=True)
    )


def turned(x, low, high):
    width = x.shape[1]
    pair = HEAD_DIM // 6
    return pltpu.roll(x, width - pair, 1) * low + pltpu.roll(x, pair, 1) * high


def three_parts(x):
    first = x.astype(bf16).astype(f32)
    rest = x - first
    second = rest.astype(bf16).astype(f32)
    return first, second, rest - second


def params(limit, axes=1):
    return pltpu.CompilerParams(
        dimension_semantics=("arbitrary",) * axes, vmem_limit_bytes=limit * MIB
    )


def in_order(kernel, inputs, earlier):
    def run(*refs):
        kernel(*refs[:inputs], *refs[inputs + earlier :])

    return run


def unread(arrays):
    return [pl.BlockSpec(memory_space=pl.ANY)] * len(arrays)


def whole(shape):
    return pl.BlockSpec(shape, lambda *_: (0,) * len(shape))


def rope_constants():
    pair = HEAD_DIM // 6
    feature = np.arange(WIDTH) % HEAD_DIM
    section, place = feature // (2 * pair), feature % (2 * pair)
    frequency = np.exp(-math.log(10000.0) * (place % pair) / pair)
    table = np.zeros((PLACES, 3, WIDTH))
    for s in range(3):
        for value in range(16):
            angle = value * frequency
            turns = section == s
            table[s * 16 + value, 0] = np.where(turns, np.cos(angle), 0.0)
            table[s * 16 + value, 1] = np.where(turns & (place < pair), -np.sin(angle), 0.0)
            table[s * 16 + value, 2] = np.where(turns & (place >= pair), np.sin(angle), 0.0)
    table[48, 0] = section == 3
    rest = table.reshape(PLACES, 3 * WIDTH).astype(np.float32)
    parts = []
    for _ in range(3):
        part = rest.astype(ml_dtypes.bfloat16)
        parts.append(part)
        rest = rest - part.astype(np.float32)
    return np.concatenate(parts)


def rope_factors(positions, table):
    row = lax.broadcasted_iota(jnp.int32, (PLACES, TILE), 0)
    where = jnp.where(
        row < 16, positions[0:1, :], jnp.where(row < 32, positions[1:2, :], positions[2:3, :])
    )
    hit = ((where == row % 16) & (row < 48)) | (row == 48)
    hit = jnp.where(hit, 1.0, 0.0)
    hits = jnp.concatenate([hit, hit, hit]).astype(bf16)
    factors = dot_tn(hits, table[...])
    return factors[:, :WIDTH], factors[:, WIDTH : 2 * WIDTH], factors[:, 2 * WIDTH :]


def qkv_kernel(
    tok, w, b, gain, shift, pos, seg, pad, table, k_aug, v_aug, q_aug_t, q_out, k_t, v_t
):
    hat, _ = normalized(tok[...].astype(f32))
    normed = (hat * gain[...] + shift[...]).astype(bf16)
    cos, low, high = rope_factors(pos, table)
    q = dot_nn(normed, w[0]) + b[0:1, :]
    k = dot_nn(normed, w[1]) + b[1:2, :]
    v = dot_nn(normed, w[2]) + b[2:3, :]
    q = (q * cos + turned(q, low, high)) * (1.0 / math.sqrt(HEAD_DIM))
    k = k * cos + turned(k, low, high)
    q_out[...] = q.astype(bf16)
    q_t = q.T.astype(bf16)
    k_t[...] = k.T.astype(bf16)
    v_t[...] = v.T.astype(bf16)
    row = lax.broadcasted_iota(jnp.int32, (HEAD_DIM, TILE), 0)
    clip = seg[...]
    same = (row >= 1) & (row < 4) & (clip == row - 1)
    mask = jnp.where((row >= 1) & (row < 4) & (clip != row - 1), NEG, 0.0)
    mask = jnp.where(row == 0, jnp.where(pad[...] != 0, NEG, 0.0), mask)
    k_extra = jnp.where((row >= 4) & (row < 7), 1.0, mask)
    q_extra = jnp.where(same | (row == 0), 1.0, 0.0).astype(bf16)
    k_side = jnp.concatenate([jnp.zeros((HEAD_DIM, TILE), f32), k_extra]).T
    lane = lax.broadcasted_iota(jnp.int32, (TILE, AUG), 1)
    ones = jnp.where((lane >= HEAD_DIM) & (lane < HEAD_DIM + 3), 1.0, 0.0)
    for h in range(HEADS):
        pair = slice(h // 2 * AUG, h // 2 * AUG + AUG)
        wide = slice(h * AUG, (h + 1) * AUG)
        k_pair, v_pair = k[:, pair], v[:, pair]
        if h % 2:
            k_pair, v_pair = pltpu.roll(k_pair, HEAD_DIM, 1), pltpu.roll(v_pair, HEAD_DIM, 1)
        k_aug[:, wide] = jnp.where(lane < HEAD_DIM, k_pair, k_side).astype(bf16)
        v_aug[:, wide] = jnp.where(lane < HEAD_DIM, v_pair, ones).astype(bf16)
        q_aug_t[h * AUG : h * AUG + HEAD_DIM, :] = q_t[h * HEAD_DIM : (h + 1) * HEAD_DIM, :]
        q_aug_t[h * AUG + HEAD_DIM : (h + 1) * AUG, :] = q_extra


def project(tokens, w, b, gain, shift, positions, segments, padding, table):
    length, width = tokens.shape
    tiles = length // TILE

    def rows(columns):
        return pl.BlockSpec((TILE, columns), lambda i: (i, 0))

    def columns(count):
        return pl.BlockSpec((count, TILE), lambda i: (0, i))

    out = jax.ShapeDtypeStruct
    wide = out((length, HEADS * AUG), bf16)
    flat = out((WIDTH, length), bf16)
    return pl.pallas_call(
        qkv_kernel,
        grid=(tiles,),
        in_specs=[
            rows(width), whole(w.shape), whole(b.shape), whole((1, width)), whole((1, width)),
            columns(3), columns(1), columns(1), whole(table.shape),
        ],
        out_specs=[
            rows(HEADS * AUG), rows(HEADS * AUG), columns(HEADS * AUG), rows(WIDTH), columns(WIDTH),
            columns(WIDTH),
        ],
        out_shape=[
            wide, wide, out((HEADS * AUG, length), bf16), out((length, WIDTH), bf16), flat, flat,
        ],
        compiler_params=params(LIMIT),
        cost_estimate=pl.CostEstimate(
            flops=6 * length * width * WIDTH, bytes_accessed=20 * MIB, transcendentals=0
        ),
        name="project",
    )(tokens, w, b, gain, shift, positions, segments, padding, table)


def attend_kernel(info, k_aug, v_t, q_aug_t, k_t, pad, o, o_t, lse, top, total, acc, *, part):
    tile = 2 * pl.program_id(0) + part
    tiles = pl.num_programs(0) * 2
    padded = pad[...] != 0
    for h in range(HEADS):
        q_h = q_aug_t[h * AUG : h * AUG + HEAD_DIM, :].astype(f32)
        k_h = k_t[h * HEAD_DIM : (h + 1) * HEAD_DIM, :].astype(f32)
        own = jnp.sum(q_h * k_h, axis=0, keepdims=True)
        top[h : h + 1, :] = jnp.where(padded, own, -3e38)
        total[h : h + 1, :] = jnp.where(padded, 1.0, 0.0)
    here = pl.ds(pl.multiple_of(tile * TILE, TILE), TILE)
    acc[...] = jnp.where(padded, v_t[:, here].astype(f32), 0.0)
    feats = [slice(h * HEAD_DIM, (h + 1) * HEAD_DIM) for h in range(HEADS)]
    wides = [slice(h * AUG, (h + 1) * AUG) for h in range(HEADS)]

    def step(j, count):
        keys = pl.ds(pl.multiple_of(j * TILE, TILE), count * TILE)
        scores = [dot_nn(k_aug[keys, wide], q_aug_t[wide, :]) for wide in wides]
        probs, fades = [], []
        for h in range(HEADS):
            old = top[h : h + 1, :]
            new = jnp.maximum(old, jnp.max(scores[h], axis=0, keepdims=True))
            prob = jnp.exp(scores[h] - new)
            fade = jnp.exp(old - new)
            top[h : h + 1, :] = new
            total[h : h + 1, :] = total[h : h + 1, :] * fade + jnp.sum(prob, axis=0, keepdims=True)
            probs.append(prob.astype(bf16))
            fades.append(fade)
        for h, feat in enumerate(feats):
            acc[feat, :] = acc[feat, :] * fades[h] + dot_nn(v_t[feat, keys], probs[h])

    begin, end = info[tile], info[tiles + tile]
    pairs = (end - begin) // 2

    def two(n, _):
        step(begin + 2 * n, 2)
        return 0

    lax.fori_loop(0, pairs, two, 0)

    @pl.when(begin + 2 * pairs < end)
    def _():
        step(end - 1, 1)

    for h, feat in enumerate(feats):
        acc[feat, :] = acc[feat, :] / total[h : h + 1, :]
    lse[...] = jnp.zeros_like(lse)
    lse[0:HEADS, :] = top[0:HEADS, :] + jnp.log(total[0:HEADS, :])
    turned_o = acc[...]
    o_t[...] = turned_o.astype(bf16)
    o[...] = turned_o.T.astype(bf16)


def attend(part, info, k_aug, v_t, q_aug_t, k_t, padding, earlier):
    length = k_aug.shape[0]
    half = length // 2

    def columns(count):
        return pl.BlockSpec((count, TILE), lambda i, *_: (0, 2 * i + part))

    def packed(count):
        return pl.BlockSpec((count, TILE), lambda i, *_: (0, i))

    out = jax.ShapeDtypeStruct
    return pl.pallas_call(
        in_order(functools.partial(attend_kernel, part=part), 6, len(earlier)),
        grid_spec=pltpu.PrefetchScalarGridSpec(
            num_scalar_prefetch=1,
            grid=(half // TILE,),
            in_specs=[
                whole(k_aug.shape), whole(v_t.shape), columns(HEADS * AUG), columns(WIDTH),
                columns(1),
            ]
            + unread(earlier),
            out_specs=[
                pl.BlockSpec((TILE, WIDTH), lambda i, *_: (i, 0)), packed(WIDTH), packed(8),
            ],
            scratch_shapes=[
                pltpu.VMEM((8, TILE), f32), pltpu.VMEM((8, TILE), f32), pltpu.VMEM((WIDTH, TILE), f32),
            ],
        ),
        out_shape=[out((half, WIDTH), bf16), out((WIDTH, half), bf16), out((8, half), f32)],
        compiler_params=params(LIMIT),
        cost_estimate=pl.CostEstimate(
            flops=24 * half * length * WIDTH, bytes_accessed=6 * MIB, transcendentals=0
        ),
        name="attend",
    )(info, k_aug, v_t, q_aug_t, k_t, padding, *earlier)


def gelu_parts(u):
    size = jnp.abs(u)
    t = 1.0 / (1.0 + (0.3275911 / math.sqrt(2.0)) * size)
    bell = jnp.exp(-0.5 * (u * u))
    poly = 0.5 * 1.061405429
    for c in (-1.453152027, 1.421413741, -0.284496736, 0.254829592):
        poly = poly * t + 0.5 * c
    tail = poly * t * bell
    below = jnp.where(u >= 0, 1.0 - tail, tail)
    return u * below, below + u * bell * (1.0 / math.sqrt(2.0 * math.pi))


def mlp_kernel(
    info, tok, cot, o_a, o_b, w_all, b_out, gain, shift, w_up, b_up, w_down,
    x2, h2, act, du, mlp, dh2, db_up, w_out, *, me_at,
):
    i = pl.program_id(0)

    @pl.when(i == 0)
    def _():
        for n, j in enumerate((0, 2, 1, 3)):
            w_out[n * WIDTH : (n + 1) * WIDTH, :] = w_all[jnp.bitwise_xor(info[me_at], j)]
        db_up[...] = jnp.zeros_like(db_up)

    heads = jnp.concatenate([o_a[0], o_a[1], o_b[0], o_b[1]], axis=1)
    mid = tok[...].astype(f32) + b_out[...] + dot_nn(heads, w_out[...])

    @pl.when(i == 0)
    def _():
        x2[...] = mid

    hat, _ = normalized(mid)
    normed = (hat * gain[...] + shift[...]).astype(bf16)
    h2[...] = normed
    u = dot_nn(normed, w_up[...]) + b_up[...]
    grad_act = dot_nt(cot[...], w_down[...])
    value, slope = gelu_parts(u)
    value = value.astype(bf16)
    grad = (grad_act * slope).astype(bf16)
    act[...] = value
    du[...] = grad
    db_up[0:1, :] += jnp.sum(grad.astype(f32), axis=0, keepdims=True)
    mlp[0] = dot_nn(value, w_down[...]).astype(bf16)
    dh2[0] = dot_nt(grad, w_up[...]).astype(bf16)


def mlp(
    part, info, me_at, tokens, cotangent, o_a, o_b, w_all, b_out, gain, shift, w_up, b_up, w_down,
    earlier,
):
    length, width = tokens.shape
    half = length // 2
    hidden = w_up.shape[1]
    owners = half // TILE

    def owner(i, info):
        return jnp.bitwise_xor(info[me_at], i)

    def rows(columns):
        return pl.BlockSpec((TILE, columns), lambda i, info: (2 * owner(i, info) + part, 0))

    def packed(columns):
        return pl.BlockSpec((TILE, columns), lambda i, info: (owner(i, info), 0))

    def relative(columns):
        return pl.BlockSpec((1, TILE, columns), lambda i, info: (i, 0, 0))

    out = jax.ShapeDtypeStruct
    return pl.pallas_call(
        in_order(functools.partial(mlp_kernel, me_at=me_at), 12, len(earlier)),
        grid_spec=pltpu.PrefetchScalarGridSpec(
            num_scalar_prefetch=1,
            grid=(owners,),
            in_specs=[rows(width), rows(width)]
            + [pl.BlockSpec((2, TILE, WIDTH), lambda i, info: (0, owner(i, info), 0))] * 2
            + [whole(w_all.shape)]
            + [whole((1, width))] * 3
            + [whole(w_up.shape), whole((1, hidden)), whole(w_down.shape)]
            + unread(earlier),
            out_specs=[
                whole((TILE, width)), packed(width), packed(hidden), packed(hidden),
                relative(width), relative(width), whole((8, hidden)),
            ],
            scratch_shapes=[pltpu.VMEM((4 * WIDTH, width), bf16)],
        ),
        out_shape=[
            out((TILE, width), f32), out((half, width), bf16), out((half, hidden), bf16),
            out((half, hidden), bf16), out((owners, TILE, width), bf16),
            out((owners, TILE, width), bf16), out((8, hidden), f32),
        ],
        compiler_params=params(LIMIT),
        cost_estimate=pl.CostEstimate(
            flops=20 * half * width * hidden, bytes_accessed=20 * MIB, transcendentals=0
        ),
        name="mlp",
    )(
        info, tokens, cotangent, o_a, o_b, w_all, b_out, gain, shift, w_up, b_up, w_down, *earlier
    )


def weights_kernel(left_a, left_b, right_a, right_b, out):
    left = jnp.concatenate([left_a[...], left_b[...]])
    right = jnp.concatenate([right_a[...], right_b[...]])
    out[...] = dot_tn(left, right).astype(bf16)


def up_weights(h2, du, earlier):
    half, width = h2[0].shape
    hidden = du[0].shape[1]
    return pl.pallas_call(
        in_order(weights_kernel, 4, len(earlier)),
        grid=(width // TILE,),
        in_specs=[pl.BlockSpec((half, TILE), lambda i: (0, i))] * 2
        + [whole((half, hidden))] * 2
        + unread(earlier),
        out_specs=pl.BlockSpec((TILE, hidden), lambda i: (i, 0)),
        out_shape=jax.ShapeDtypeStruct((width, hidden), bf16),
        compiler_params=params(LIMIT),
        cost_estimate=pl.CostEstimate(
            flops=8 * half * width * hidden, bytes_accessed=12 * MIB, transcendentals=0
        ),
        name="up_weights",
    )(*h2, *du, *earlier)


def down_weights_kernel(act_a, act_b, cot, out):
    owners = cot.shape[0] // (2 * TILE)
    rows = [cot[n * TILE : (n + 1) * TILE, :] for p in range(2) for n in range(p, 2 * owners, 2)]
    out[...] = dot_tn(
        jnp.concatenate([act_a[...], act_b[...]]), jnp.concatenate(rows)
    ).astype(bf16)


def down_weights(act, cotangent, earlier):
    half, hidden = act[0].shape
    length, width = cotangent.shape
    return pl.pallas_call(
        in_order(down_weights_kernel, 3, len(earlier)),
        grid=(hidden // TILE,),
        in_specs=[pl.BlockSpec((half, TILE), lambda i: (0, i))] * 2
        + [whole((length, width))]
        + unread(earlier),
        out_specs=pl.BlockSpec((TILE, width), lambda i: (i, 0)),
        out_shape=jax.ShapeDtypeStruct((hidden, width), bf16),
        compiler_params=params(LIMIT),
        cost_estimate=pl.CostEstimate(
            flops=8 * half * width * hidden, bytes_accessed=12 * MIB, transcendentals=0
        ),
        name="down_weights",
    )(*act, cotangent, *earlier)


def middle_kernel(
    info, here, there, x2, cot, gain, w_all, dx2, g, d_0, d_1, d_2, d_3, small, *, me_at
):
    grad = here[...].astype(f32) + there[...].astype(f32)
    hat, inverse = normalized(x2[...])
    dy = cot[...].astype(f32)
    full = dy + norm_back(hat, inverse, gain[...], grad)
    dx2[...] = full
    low = full.astype(bf16)
    g[...] = low
    small[...] = jnp.zeros_like(small)
    small[0:1, :] = jnp.sum(grad * hat, axis=0, keepdims=True)
    small[1:2, :] = jnp.sum(grad, axis=0, keepdims=True)
    small[2:3, :] = jnp.sum(low.astype(f32), axis=0, keepdims=True)
    small[3:4, :] = jnp.sum(dy, axis=0, keepdims=True)
    for j, d_j in enumerate((d_0, d_1, d_2, d_3)):
        d_j[...] = dot_nt(low, w_all[jnp.bitwise_xor(info[me_at], j)]).astype(bf16)


def middle(part, info, me_at, here, there, x2, cotangent, gain, w_all, earlier):
    width = x2.shape[1]
    out = jax.ShapeDtypeStruct
    own = whole((TILE, width))
    return pl.pallas_call(
        in_order(functools.partial(middle_kernel, me_at=me_at), 7, len(earlier)),
        grid_spec=pltpu.PrefetchScalarGridSpec(
            num_scalar_prefetch=1,
            grid=(1,),
            in_specs=[
                own, own, own,
                pl.BlockSpec((TILE, width), lambda i, info: (2 * info[me_at] + part, 0)),
                whole((1, width)), whole(w_all.shape),
            ]
            + unread(earlier),
            out_specs=[own, own] + [whole((TILE, WIDTH))] * 4 + [whole((8, width))],
        ),
        out_shape=[out((TILE, width), f32), out((TILE, width), bf16)]
        + [out((TILE, WIDTH), bf16)] * 4
        + [out((8, width), f32)],
        compiler_params=params(40),
        cost_estimate=pl.CostEstimate(
            flops=2 * TILE * width * width, bytes_accessed=8 * MIB, transcendentals=0
        ),
        name="middle",
    )(info, here, there, x2, cotangent, gain, w_all, *earlier)


def out_weights_kernel(info, oa_a, oa_b, ob_a, ob_b, g_a, g_b, out):
    grad = jnp.concatenate([g_a[...], g_b[...]])
    for j, (first, second, at) in enumerate(
        ((oa_a, ob_a, 0), (oa_b, ob_b, 0), (oa_a, ob_a, 1), (oa_b, ob_b, 1))
    ):
        out[j] = dot_tn(jnp.concatenate([first[at], second[at]]), grad).astype(bf16)


def out_weights(info, me_at, pairs_a, pairs_b, g_a, g_b):
    width = g_a.shape[1]
    own = pl.BlockSpec((2, TILE, WIDTH), lambda i, info: (0, info[me_at], 0))
    return pl.pallas_call(
        out_weights_kernel,
        grid_spec=pltpu.PrefetchScalarGridSpec(
            num_scalar_prefetch=1,
            grid=(1,),
            in_specs=[own] * 4 + [whole((TILE, width))] * 2,
            out_specs=whole((4, WIDTH, width)),
        ),
        out_shape=jax.ShapeDtypeStruct((4, WIDTH, width), bf16),
        compiler_params=params(LIMIT),
        cost_estimate=pl.CostEstimate(
            flops=4 * TILE * width * width, bytes_accessed=6 * MIB, transcendentals=0
        ),
        name="out_weights",
    )(info, *pairs_a, *pairs_b, g_a, g_b)


def attend_back_kernel(
    info, k_aug, v_aug, k_t, q_aug_t, q, v_t, o_t, lse, pad, do, pos, table, dk_in, dv_in,
    dq_out, dk, dv, q_side, do_side, q_lanes, do_lanes, dq_t, *, part, me_at, first,
):
    i = pl.program_id(0)
    tiles = pl.num_programs(0) * 2
    tile = 2 * jnp.bitwise_xor(info[me_at], i) + part

    @pl.when(i == 0)
    def _():
        if first:
            dk[...] = jnp.zeros_like(dk)
            dv[...] = jnp.zeros_like(dv)
        else:
            dk[...] = dk_in[...]
            dv[...] = dv_in[...]

    here = pl.ds(pl.multiple_of(tile * TILE, TILE), TILE)
    do_here, q_here = do[...], q[...]
    do_t = do_here.astype(f32).T
    k_here = k_t[:, here].astype(f32)
    padded = jnp.where(pad[...] != 0, 1.0, 0.0)
    row = lax.broadcasted_iota(jnp.int32, (AUG - HEAD_DIM, TILE), 0)
    lane = lax.broadcasted_iota(jnp.int32, (TILE, WIDTH), 1) // HEAD_DIM
    dk_parts, dv_parts = [], []
    for h in range(HEADS):
        feat = slice(h * HEAD_DIM, (h + 1) * HEAD_DIM)
        at = h * AUG
        q_h = q_aug_t[at : at + HEAD_DIM, :]
        do_h = do_t[feat, :]
        delta = jnp.sum(do_h * o_t[feat, :].astype(f32), axis=0, keepdims=True)
        lse_h = lse[h : h + 1, :]
        one, two, three = three_parts(-lse_h)
        extra = q_aug_t[at + HEAD_DIM : at + AUG, :].astype(f32)
        extra = jnp.where(row == 4, one, jnp.where(row == 5, two, jnp.where(row == 6, three, extra)))
        q_side[at : at + HEAD_DIM, :] = q_h
        q_side[at + HEAD_DIM : at + AUG, :] = extra.astype(bf16)
        one, two, three = three_parts(-delta)
        extra = jnp.where(row == 0, one, jnp.where(row == 1, two, jnp.where(row == 2, three, 0.0)))
        do_side[at : at + HEAD_DIM, :] = do_h.astype(bf16)
        do_side[at + HEAD_DIM : at + AUG, :] = extra.astype(bf16)
        q_lanes[h] = jnp.where(lane == h, q_here, jnp.zeros_like(q_here))
        do_lanes[h] = jnp.where(lane == h, do_here, jnp.zeros_like(do_here))
        q_h = q_h.astype(f32)
        k_h = k_here[feat, :]
        p_own = padded * jnp.exp(jnp.sum(q_h * k_h, axis=0, keepdims=True) - lse_h)
        dp_own = jnp.sum(do_h * v_t[feat, :].astype(f32), axis=0, keepdims=True)
        ds_own = p_own * (dp_own - delta)
        dq_t[feat, :] = ds_own * k_h
        dk_parts.append(ds_own * q_h)
        dv_parts.append(p_own * do_h)
    dk[here, :] += jnp.concatenate(dk_parts, axis=0).T
    dv[here, :] += jnp.concatenate(dv_parts, axis=0).T

    def step(j, _):
        keys = pl.ds(pl.multiple_of(j * TILE, TILE), TILE)
        probs, grads = [], []
        for h in range(HEADS):
            wide = slice(h * AUG, (h + 1) * AUG)
            prob = jnp.exp(dot_nn(k_aug[keys, wide], q_side[wide, :]))
            grad = prob * dot_nn(v_aug[keys, wide], do_side[wide, :])
            probs.append(prob.astype(bf16))
            grads.append(grad.astype(bf16))
        deep = (HEADS * TILE, WIDTH)
        dv[keys, :] += dot_nn(jnp.concatenate(probs, axis=1), do_lanes[...].reshape(deep))
        dk[keys, :] += dot_nn(jnp.concatenate(grads, axis=1), q_lanes[...].reshape(deep))
        for h in range(HEADS):
            feat = slice(h * HEAD_DIM, (h + 1) * HEAD_DIM)
            dq_t[feat, :] += dot_nn(k_t[feat, keys], grads[h])
        return 0

    lax.fori_loop(info[tile], info[tiles + tile], step, 0)
    dq = dq_t[...].T * (1.0 / math.sqrt(HEAD_DIM))
    cos, low, high = rope_factors(pos, table)
    dq_out[...] = (dq * cos - turned(dq, low, high)).astype(bf16)


def attend_back(
    part, info, me_at, k_aug, v_aug, k_t, q_aug_t, q, v_t, o_t, lse, padding, do, positions, table,
    dk, dv, earlier,
):
    length = k_aug.shape[0]
    half = length // 2

    def owner(i, info):
        return jnp.bitwise_xor(info[me_at], i)

    def rows(columns):
        return pl.BlockSpec((TILE, columns), lambda i, info: (2 * owner(i, info) + part, 0))

    def columns(count):
        return pl.BlockSpec((count, TILE), lambda i, info: (0, 2 * owner(i, info) + part))

    def packed(count):
        return pl.BlockSpec((count, TILE), lambda i, info: (0, owner(i, info)))

    out = jax.ShapeDtypeStruct
    first = dk is None
    if first:
        dk = dv = jnp.zeros((8, WIDTH), f32)
    return pl.pallas_call(
        in_order(
            functools.partial(attend_back_kernel, part=part, me_at=me_at, first=first),
            15, len(earlier),
        ),
        grid_spec=pltpu.PrefetchScalarGridSpec(
            num_scalar_prefetch=1,
            grid=(half // TILE,),
            in_specs=[
                whole(k_aug.shape), whole(v_aug.shape), whole(k_t.shape), columns(HEADS * AUG),
                rows(WIDTH), columns(WIDTH), packed(WIDTH), packed(8), columns(1),
                pl.BlockSpec((None, TILE, WIDTH), lambda i, info: (i, 0, 0)), columns(3),
                whole(table.shape), whole(dk.shape), whole(dv.shape),
            ]
            + unread(earlier),
            out_specs=[
                pl.BlockSpec((TILE, WIDTH), lambda i, info: (owner(i, info), 0)),
                whole((length, WIDTH)), whole((length, WIDTH)),
            ],
            scratch_shapes=[
                pltpu.VMEM((HEADS * AUG, TILE), bf16), pltpu.VMEM((HEADS * AUG, TILE), bf16),
                pltpu.VMEM((HEADS, TILE, WIDTH), bf16), pltpu.VMEM((HEADS, TILE, WIDTH), bf16),
                pltpu.VMEM((WIDTH, TILE), f32),
            ],
        ),
        out_shape=[out((half, WIDTH), bf16), out((length, WIDTH), f32), out((length, WIDTH), f32)],
        compiler_params=params(LIMIT),
        cost_estimate=pl.CostEstimate(
            flops=72 * half * length * WIDTH, bytes_accessed=16 * MIB, transcendentals=0
        ),
        name="attend_back",
    )(
        info, k_aug, v_aug, k_t, q_aug_t, q, v_t, o_t, lse, padding, do, positions, table, dk, dv,
        *earlier,
    )


def project_back_kernel(
    info, tok, gain, shift, dq_a, dq_b, dk, dv, pos, table, w, out_sum, early,
    dh1, sums, acc, grad_b, small, w_wide,
):
    i = pl.program_id(0)

    @pl.when(i == 0)
    def _():
        acc[...] = jnp.zeros_like(acc)
        grad_b[...] = jnp.zeros_like(grad_b)
        small[...] = jnp.zeros_like(small)
        for c in range(3):
            w_wide[:, c * WIDTH : (c + 1) * WIDTH] = w[c]

    hat, _ = normalized(tok[...].astype(f32))
    normed = (hat * gain[...] + shift[...]).astype(bf16)
    dq = jnp.where(i % 2 == 0, dq_a[...], dq_b[...])
    dk_here = dk[...]
    cos, low, high = rope_factors(pos, table)
    dk_low = (dk_here * cos - turned(dk_here, low, high)).astype(bf16)
    parts = jnp.concatenate([dq, dk_low, dv[...].astype(bf16)], axis=1)
    acc[...] += dot_tn(normed, parts)
    grad_b[0:1, :] += jnp.sum(parts.astype(f32), axis=0, keepdims=True)
    grad = dot_nt(parts, w_wide[...])
    small[0:1, :] += jnp.sum(grad * hat, axis=0, keepdims=True)
    small[1:2, :] += jnp.sum(grad, axis=0, keepdims=True)
    dh1[0] = grad.astype(bf16)

    @pl.when(i == pl.num_programs(0) - 1)
    def _():
        width = normed.shape[1]
        blocks = sums.shape[0]
        deep = 3 * width // blocks
        extra_at = deep + width // blocks
        extra_rows = sums.shape[1] - extra_at

        def cut(ref, row, count):
            return [ref[row : row + 1, r * WIDTH : (r + 1) * WIDTH] for r in range(count)]

        rows = cut(grad_b, 0, 3)
        for ref, count in ((small, 2), (early, 5)):
            for v in range(count):
                rows += cut(ref, v, width // WIDTH)
        for n in range(blocks):
            for at, length in pieces(n * deep, deep, width):
                c, begin = at // width, at % width
                sums[n, at - n * deep : at - n * deep + length, :] = acc[
                    begin : begin + length, c * WIDTH : (c + 1) * WIDTH
                ].astype(bf16)
            share = width // blocks
            for at, length in pieces(n * share, share, WIDTH):
                c, begin = at // WIDTH, at % WIDTH
                to = deep + at - n * share
                sums[n, to : to + length, :] = out_sum[
                    begin : begin + length, c * WIDTH : (c + 1) * WIDTH
                ]
            row = lax.broadcasted_iota(jnp.int32, (extra_rows, WIDTH), 0)
            extra = jnp.zeros((extra_rows, WIDTH), f32)
            for m, value in enumerate(rows[n::blocks]):
                one, two, _ = three_parts(value)
                extra = jnp.where(row == 2 * m, one, jnp.where(row == 2 * m + 1, two, extra))
            sums[n, extra_at : extra_at + extra_rows, :] = extra.astype(bf16)


def pieces(begin, count, period):
    at, end, cuts = begin, begin + count, []
    while at < end:
        length = min(end - at, period - at % period)
        cuts.append((at, length))
        at += length
    return cuts


def project_back(
    info, me_at, tokens, gain, shift, dq_a, dq_b, dk, dv, positions, table, w, out_sum, early, blocks
):
    length, width = tokens.shape
    tiles = length // TILE

    def place(i, info):
        return 2 * jnp.bitwise_xor(info[me_at], i // 2) + i % 2

    def rows(columns):
        return pl.BlockSpec((TILE, columns), lambda i, info: (place(i, info), 0))

    def packed(columns):
        return pl.BlockSpec(
            (TILE, columns), lambda i, info: (jnp.bitwise_xor(info[me_at], i // 2), 0)
        )

    out = jax.ShapeDtypeStruct
    vectors = -(-(3 + 7 * width // WIDTH) // blocks)
    sums = (blocks, 4 * width // blocks + -(-vectors // 8) * 16, WIDTH)
    return pl.pallas_call(
        project_back_kernel,
        grid_spec=pltpu.PrefetchScalarGridSpec(
            num_scalar_prefetch=1,
            grid=(tiles,),
            in_specs=[
                rows(width), whole((1, width)), whole((1, width)), packed(WIDTH), packed(WIDTH),
                rows(WIDTH), rows(WIDTH),
                pl.BlockSpec((3, TILE), lambda i, info: (0, place(i, info))), whole(table.shape),
                whole(w.shape), whole(out_sum.shape), whole(early.shape),
            ],
            out_specs=[
                pl.BlockSpec((1, TILE, width), lambda i, info: (i // 2, i % 2, 0)), whole(sums),
            ],
            scratch_shapes=[
                pltpu.VMEM((width, 3 * WIDTH), f32), pltpu.VMEM((8, 3 * WIDTH), f32),
                pltpu.VMEM((8, width), f32), pltpu.VMEM((width, 3 * WIDTH), bf16),
            ],
        ),
        out_shape=[out((tiles // 2, 2 * TILE, width), bf16), out(sums, bf16)],
        compiler_params=params(LIMIT),
        cost_estimate=pl.CostEstimate(
            flops=24 * length * width * WIDTH, bytes_accessed=20 * MIB, transcendentals=0
        ),
        name="project_back",
    )(info, tokens, gain, shift, dq_a, dq_b, dk, dv, positions, table, w, out_sum, early)


def finish_kernel(info, here, there, tok, gain, dx2_a, dx2_b, out):
    grad = here[...].astype(f32) + there[...].astype(f32)
    hat, inverse = normalized(tok[...].astype(f32))
    dx2 = jnp.where(pl.program_id(0) == 0, dx2_a[...], dx2_b[...])
    out[...] = dx2 + norm_back(hat, inverse, gain[...], grad)


def finish(info, me_at, here, there, tokens, gain, dx2_a, dx2_b):
    width = tokens.shape[1]
    share = here.shape[0]
    rows = pl.BlockSpec((TILE, width), lambda i, info: (i, 0))
    return pl.pallas_call(
        finish_kernel,
        grid_spec=pltpu.PrefetchScalarGridSpec(
            num_scalar_prefetch=1,
            grid=(share // TILE,),
            in_specs=[
                rows, rows,
                pl.BlockSpec((TILE, width), lambda i, info: (2 * info[me_at] + i, 0)),
                whole((1, width)), whole((TILE, width)), whole((TILE, width)),
            ],
            out_specs=rows,
        ),
        out_shape=jax.ShapeDtypeStruct((share, width), f32),
        compiler_params=params(32),
        name="finish",
    )(info, here, there, tokens, gain, dx2_a, dx2_b)


def swap(array, axis, bit=1):
    size = lax.axis_size(axis)
    if size == 1:
        return jnp.zeros_like(array)
    return lax.ppermute(array, axis, [(i, i ^ bit) for i in range(size)])


def swap_both(array):
    return lax.ppermute(array, MP, [(i, i ^ 3) for i in range(4)])


def scattered_sum(rows, axes):
    group = lax.axis_size(axes)
    length, width = rows.shape
    blocks = rows.reshape(group, length // group, width)
    blocks = lax.all_to_all(blocks, axes, 0, 0, tiled=True)
    return jnp.sum(blocks.astype(f32), axis=0).astype(bf16)


def spread(block, axes):
    group = lax.axis_size(axes)
    return lax.all_to_all(
        jnp.broadcast_to(block[None], (group,) + block.shape), axes, 0, 0, tiled=True
    )


def both_sums(total):
    if lax.axis_size("zl") == 1:
        return total
    return (total.astype(f32) + swap(total, "zl").astype(f32)).astype(bf16)


def clip_bounds(segments):
    length = segments.shape[0]
    tiles = length // TILE
    ends = jnp.sum((segments[None, :] < jnp.arange(4)[:, None]).astype(jnp.int32), axis=1)
    first = jnp.arange(tiles) * TILE
    low = jnp.zeros((tiles,), jnp.int32)
    high = jnp.full((tiles,), length, jnp.int32)
    for n in range(1, 3):
        low = jnp.where(ends[n] <= first, ends[n], low)
    for n in (2, 1):
        high = jnp.where(ends[n] >= first + TILE, ends[n], high)
    return jnp.concatenate([low // TILE, (high + TILE - 1) // TILE]), 2 * tiles


def local(
    tokens, cotangent, segments, padding, positions, ln1_gain, ln1_bias, w_qkv, b_qkv, w_out, b_out,
    ln2_gain, ln2_bias, w_up, b_up, w_down, b_down,
):
    width, hidden = w_up.shape
    w_all = lax.all_gather(w_out, MP)
    gain_one, shift_one = ln1_gain[None], ln1_bias[None]
    gain_two, shift_two = ln2_gain[None], ln2_bias[None]
    bounds, me_at = clip_bounds(segments[0])
    info = jnp.concatenate([bounds, lax.axis_index(MP)[None].astype(jnp.int32)])
    table = jnp.asarray(rope_constants())
    places = positions[:, 0, :]
    k_aug, v_aug, q_aug_t, q, k_t, v_t = project(
        tokens, w_qkv, b_qkv, gain_one, shift_one, places, segments, padding, table
    )

    def everyones(o):
        pair = jnp.stack([o, swap(o, "zh")])
        return pair, swap(pair, "c")

    o_0, o_t_0, lse_0 = attend(0, info, k_aug, v_t, q_aug_t, k_t, padding, ())
    pairs_0 = everyones(o_0)
    o_1, o_t_1, lse_1 = attend(1, info, k_aug, v_t, q_aug_t, k_t, padding, (o_0, w_all))
    pairs_1 = everyones(o_1)

    def mlp_half(part, pairs, earlier):
        return mlp(
            part, info, me_at, tokens, cotangent, *pairs, w_all, b_out[None], gain_two, shift_two,
            w_up, b_up[None], w_down, earlier,
        )

    x2_0, h2_0, act_0, du_0, mlp_0, dh2_0, db_0 = mlp_half(0, pairs_0, (o_1,))
    x2_1, h2_1, act_1, du_1, mlp_1, dh2_1, db_1 = mlp_half(1, pairs_1, (x2_0,))

    def met(parts):
        other = swap(jnp.concatenate([parts[1:2], parts[3:4]]), "c")
        keep = (parts[0].astype(f32) + other[0].astype(f32)).astype(bf16)
        return keep, (parts[2].astype(f32) + other[1].astype(f32)).astype(bf16)

    here_0, give_0 = met(dh2_0)
    there_0 = swap(give_0, "zh")
    grad_down = down_weights((act_0, act_1), cotangent, (give_0,))
    here_1, give_1 = met(dh2_1)
    there_1 = swap(give_1, "zh")
    grad_up = up_weights((h2_0, h2_1), (du_0, du_1), (give_1, grad_down))

    def exchanged(d_own, d_c, d_zh, d_both):
        return jnp.stack([d_own, swap(d_c, "c"), swap(d_zh, "zh"), swap_both(d_both)])

    dx2_0, g_0, *d_0, small_0 = middle(
        0, info, me_at, here_0, there_0, x2_0, cotangent, gain_two, w_all, (grad_up,)
    )
    do_0 = exchanged(*d_0)
    dx2_1, g_1, *d_1, small_1 = middle(
        1, info, me_at, here_1, there_1, x2_1, cotangent, gain_two, w_all, (g_0,)
    )
    do_1 = exchanged(*d_1)
    grad_out = out_weights(info, me_at, pairs_0, pairs_1, g_0, g_1)

    sent = jnp.stack([jnp.concatenate([mlp_0[j], mlp_1[j], grad_out[j]]) for j in (1, 3)])
    other = swap(sent, "c")
    part_sum = scattered_sum(jnp.concatenate([grad_up, grad_down]), ("y", "x"))
    dq_0, dk, dv = attend_back(
        0, info, me_at, k_aug, v_aug, k_t, q_aug_t, q, v_t, o_t_0, lse_0, padding, do_0, places,
        table, None, None, (sent, g_1),
    )

    keep, give = (
        (jnp.concatenate([mlp_0[j], mlp_1[j], grad_out[j]]).astype(f32) + other[n].astype(f32)).astype(
            bf16
        )
        for n, j in enumerate((0, 2))
    )
    there = swap(give, "zh")
    part_sum = both_sums(part_sum)
    dq_1, dk, dv = attend_back(
        1, info, me_at, k_aug, v_aug, k_t, q_aug_t, q, v_t, o_t_1, lse_1, padding, do_1, places,
        table, dk, dv, (give, part_sum, dq_0),
    )
    grad_mlp = spread(part_sum, ("y", "x")).reshape(2, width, hidden)
    received = keep.astype(f32) + there.astype(f32)
    out_sum = received[2 * TILE :].astype(bf16)
    early = jnp.concatenate([(small_0 + small_1)[0:4], (db_0 + db_1)[0:1], jnp.zeros((3, width), f32)])
    dh1, sums = project_back(
        info, me_at, tokens, gain_one, shift_one, dq_0, dq_1, dk, dv, places, table, w_qkv, out_sum,
        early, lax.axis_size(DP),
    )
    blocks, deep, _ = sums.shape
    sums = spread(scattered_sum(sums.reshape(blocks * deep, WIDTH), DP), DP)
    here, give = met(dh1)
    grad_inputs = finish(info, me_at, here, swap(give, "zh"), tokens, gain_one, dx2_0, dx2_1)
    mixed = (jnp.concatenate([x2_0, x2_1]) + received[: 2 * TILE] + b_down[None]).astype(bf16)

    kept, shared = 3 * width // blocks, width // blocks
    grad_qkv = sums[:, :kept].astype(f32).reshape(w_qkv.shape)
    grad_w_out = sums[:, kept : kept + shared].astype(f32).reshape(width // WIDTH, WIDTH, WIDTH)
    grad_w_out = grad_w_out.transpose(1, 0, 2).reshape(WIDTH, width)
    rows = jnp.concatenate(
        [
            sums[:, at].astype(f32) + sums[:, at + 1].astype(f32)
            for at in range(kept + shared, deep, 2)
        ]
    )
    count = width // WIDTH
    group = rows[3 : 3 + 6 * count]
    group = group + swap(group, "c")
    group = (group + swap(group, "zh")).reshape(6, width)
    return (
        mixed, grad_inputs, group[0], group[1], grad_qkv, rows[0:3], grad_w_out, group[4], group[2],
        group[3], grad_mlp[0].astype(f32), rows[3 + 6 * count : 3 + 7 * count].reshape(hidden),
        grad_mlp[1].astype(f32), group[5],
    )


def solution(mesh):
    packs = mesh.shape["dp"]
    if packs == 32:
        shape = (2, 4, 4, 2, 2)
    else:
        shape = (1, packs, 1, 2, 2)
    split = Mesh(mesh.devices.reshape(shape), EVERY)
    in_specs = (
        P(DP, None), P(DP, None), P(DP, None), P(DP, None), P(None, DP, None), P(), P(),
        P(None, None, MP), P(None, MP), P(MP, None), P(), P(), P(), P(None, MP), P(MP),
        P(MP, None), P(),
    )
    out_specs = (
        P(EVERY, None), P(EVERY, None), P(), P(), P(None, None, MP), P(None, MP), P(MP, None), P(),
        P(), P(), P(None, MP), P(MP), P(MP, None), P(),
    )
    return jax.shard_map(local, mesh=split, in_specs=in_specs, out_specs=out_specs, check_vma=False)
```

```python
import functools
import math

import jax
import jax.numpy as jnp
import ml_dtypes
import numpy as np
from jax import lax
from jax.experimental import pallas as pl
from jax.experimental.pallas import tpu as pltpu
from jax.sharding import Mesh
from jax.sharding import PartitionSpec as P

HEAD_DIM = 64
HEADS = 4
WIDTH = HEADS * HEAD_DIM
AUG = 128
TILE = 256
PLACES = 64
LIMIT = 60
MIB = 1 << 20
DP = ("zl", "y", "x")
MP = ("zh", "c")
EVERY = ("zl", "y", "x", "zh", "c")

epsilon = 1e-06
NEG = -1e30
bf16 = jnp.bfloat16
f32 = jnp.float32


def dot_nn(a, b):
    return lax.dot_general(a, b, (((1,), (0,)), ((), ())), preferred_element_type=f32)


def dot_nt(a, b):
    return lax.dot_general(a, b, (((1,), (1,)), ((), ())), preferred_element_type=f32)


def dot_tn(a, b):
    return lax.dot_general(a, b, (((0,), (0,)), ((), ())), preferred_element_type=f32)


def normalized(values):
    center = jnp.mean(values, axis=-1, keepdims=True)
    shifted = values - center
    spread = jnp.mean(shifted * shifted, axis=-1, keepdims=True)
    inverse = lax.rsqrt(spread + epsilon)
    return shifted * inverse, inverse


def norm_back(hat, inverse, gain, grad):
    scaled = grad * gain
    return inverse * (
        scaled
        - jnp.mean(scaled, axis=-1, keepdims=True)
        - hat * jnp.mean(scaled * hat, axis=-1, keepdims=True)
    )


def turned(x, low, high):
    width = x.shape[1]
    pair = HEAD_DIM // 6
    return pltpu.roll(x, width - pair, 1) * low + pltpu.roll(x, pair, 1) * high


def three_parts(x):
    first = x.astype(bf16).astype(f32)
    rest = x - first
    second = rest.astype(bf16).astype(f32)
    return first, second, rest - second


def params(limit, axes=1):
    return pltpu.CompilerParams(
        dimension_semantics=("arbitrary",) * axes, vmem_limit_bytes=limit * MIB
    )


def in_order(kernel, inputs, earlier):
    def run(*refs):
        kernel(*refs[:inputs], *refs[inputs + earlier :])

    return run


def unread(arrays):
    return [pl.BlockSpec(memory_space=pl.ANY)] * len(arrays)


def whole(shape):
    return pl.BlockSpec(shape, lambda *_: (0,) * len(shape))


def clip_range(info, tile, length):
    first, second = info[0], info[1]
    at = tile * TILE
    begin = jnp.where(second <= at, second, jnp.where(first <= at, first, 0))
    end = jnp.where(
        first >= at + TILE, first, jnp.where(second >= at + TILE, second, length)
    )
    return begin // TILE, (end + TILE - 1) // TILE


def rope_constants():
    pair = HEAD_DIM // 6
    feature = np.arange(WIDTH) % HEAD_DIM
    section, place = feature // (2 * pair), feature % (2 * pair)
    frequency = np.exp(-math.log(10000.0) * (place % pair) / pair)
    table = np.zeros((PLACES, 3, WIDTH))
    for s in range(3):
        for value in range(16):
            angle = value * frequency
            turns = section == s
            table[s * 16 + value, 0] = np.where(turns, np.cos(angle), 0.0)
            table[s * 16 + value, 1] = np.where(turns & (place < pair), -np.sin(angle), 0.0)
            table[s * 16 + value, 2] = np.where(turns & (place >= pair), np.sin(angle), 0.0)
    table[48, 0] = section == 3
    rest = table.reshape(PLACES, 3 * WIDTH).astype(np.float32)
    parts = []
    for _ in range(3):
        part = rest.astype(ml_dtypes.bfloat16)
        parts.append(part)
        rest = rest - part.astype(np.float32)
    return np.concatenate(parts)


def rope_factors(positions, table):
    row = lax.broadcasted_iota(jnp.int32, (PLACES, TILE), 0)
    where = jnp.where(
        row < 16, positions[0], jnp.where(row < 32, positions[1], positions[2])
    )
    hit = ((where == row % 16) & (row < 48)) | (row == 48)
    hit = jnp.where(hit, 1.0, 0.0)
    hits = jnp.concatenate([hit, hit, hit]).astype(bf16)
    factors = dot_tn(hits, table[...])
    return factors[:, :WIDTH], factors[:, WIDTH : 2 * WIDTH], factors[:, 2 * WIDTH :]


def qkv_kernel(
    tok, w, b, gain, shift, pos, seg, pad, table, k_aug, v_aug, q_aug_t, q_out, k_t, v_t
):
    hat, _ = normalized(tok[...].astype(f32))
    normed = (hat * gain[...] + shift[...]).astype(bf16)
    cos, low, high = rope_factors(pos, table)
    q = dot_nn(normed, w[0]) + b[0:1, :]
    k = dot_nn(normed, w[1]) + b[1:2, :]
    v = dot_nn(normed, w[2]) + b[2:3, :]
    q = (q * cos + turned(q, low, high)) * (1.0 / math.sqrt(HEAD_DIM))
    k = k * cos + turned(k, low, high)
    q_out[...] = q.astype(bf16)
    q_t = q.T.astype(bf16)
    k_t[...] = k.T.astype(bf16)
    v_t[...] = v.T.astype(bf16)
    row = lax.broadcasted_iota(jnp.int32, (HEAD_DIM, TILE), 0)
    clip = seg[...]
    same = (row >= 1) & (row < 4) & (clip == row - 1)
    mask = jnp.where((row >= 1) & (row < 4) & (clip != row - 1), NEG, 0.0)
    mask = jnp.where(row == 0, jnp.where(pad[...] != 0, NEG, 0.0), mask)
    k_extra = jnp.where((row >= 4) & (row < 7), 1.0, mask)
    q_extra = jnp.where(same | (row == 0), 1.0, 0.0).astype(bf16)
    k_side = jnp.concatenate([jnp.zeros((HEAD_DIM, TILE), f32), k_extra]).T
    lane = lax.broadcasted_iota(jnp.int32, (TILE, AUG), 1)
    ones = jnp.where((lane >= HEAD_DIM) & (lane < HEAD_DIM + 3), 1.0, 0.0)
    for h in range(HEADS):
        pair = slice(h // 2 * AUG, h // 2 * AUG + AUG)
        wide = slice(h * AUG, (h + 1) * AUG)
        k_pair, v_pair = k[:, pair], v[:, pair]
        if h % 2:
            k_pair, v_pair = pltpu.roll(k_pair, HEAD_DIM, 1), pltpu.roll(v_pair, HEAD_DIM, 1)
        k_aug[:, wide] = jnp.where(lane < HEAD_DIM, k_pair, k_side).astype(bf16)
        v_aug[:, wide] = jnp.where(lane < HEAD_DIM, v_pair, ones).astype(bf16)
        q_aug_t[h * AUG : h * AUG + HEAD_DIM, :] = q_t[h * HEAD_DIM : (h + 1) * HEAD_DIM, :]
        q_aug_t[h * AUG + HEAD_DIM : (h + 1) * AUG, :] = q_extra


def project(tokens, w, b, gain, shift, positions, segments, padding, table):
    length, width = tokens.shape
    tiles = length // TILE

    def rows(columns):
        return pl.BlockSpec((TILE, columns), lambda i: (i, 0))

    def columns(count):
        return pl.BlockSpec((count, TILE), lambda i: (0, i))

    out = jax.ShapeDtypeStruct
    wide = out((length, HEADS * AUG), bf16)
    flat = out((WIDTH, length), bf16)
    return pl.pallas_call(
        qkv_kernel,
        grid=(tiles,),
        in_specs=[
            rows(width), whole(w.shape), whole(b.shape), whole((1, width)), whole((1, width)),
            pl.BlockSpec((3, 1, TILE), lambda i: (0, 0, i)), columns(1), columns(1), whole(table.shape),
        ],
        out_specs=[
            rows(HEADS * AUG), rows(HEADS * AUG), columns(HEADS * AUG), rows(WIDTH), columns(WIDTH),
            columns(WIDTH),
        ],
        out_shape=[
            wide, wide, out((HEADS * AUG, length), bf16), out((length, WIDTH), bf16), flat, flat,
        ],
        compiler_params=params(LIMIT),
        cost_estimate=pl.CostEstimate(
            flops=6 * length * width * WIDTH, bytes_accessed=20 * MIB, transcendentals=0
        ),
        name="project",
    )(tokens, w, b, gain, shift, positions, segments, padding, table)


def attend_kernel(info, k_aug, v_t, q_aug_t, k_t, pad, o, o_t, lse, top, total, acc, *, part):
    tile = 2 * pl.program_id(0) + part
    padded = pad[...] != 0
    for h in range(HEADS):
        q_h = q_aug_t[h * AUG : h * AUG + HEAD_DIM, :].astype(f32)
        k_h = k_t[h * HEAD_DIM : (h + 1) * HEAD_DIM, :].astype(f32)
        own = jnp.sum(q_h * k_h, axis=0, keepdims=True)
        top[h : h + 1, :] = jnp.where(padded, own, -3e38)
        total[h : h + 1, :] = jnp.where(padded, 1.0, 0.0)
    here = pl.ds(pl.multiple_of(tile * TILE, TILE), TILE)
    acc[...] = jnp.where(padded, v_t[:, here].astype(f32), 0.0)
    feats = [slice(h * HEAD_DIM, (h + 1) * HEAD_DIM) for h in range(HEADS)]
    wides = [slice(h * AUG, (h + 1) * AUG) for h in range(HEADS)]

    def step(j, count):
        keys = pl.ds(pl.multiple_of(j * TILE, TILE), count * TILE)
        scores = [dot_nn(k_aug[keys, wide], q_aug_t[wide, :]) for wide in wides]
        probs, fades = [], []
        for h in range(HEADS):
            old = top[h : h + 1, :]
            new = jnp.maximum(old, jnp.max(scores[h], axis=0, keepdims=True))
            prob = jnp.exp(scores[h] - new)
            fade = jnp.exp(old - new)
            top[h : h + 1, :] = new
            total[h : h + 1, :] = total[h : h + 1, :] * fade + jnp.sum(prob, axis=0, keepdims=True)
            probs.append(prob.astype(bf16))
            fades.append(fade)
        for h, feat in enumerate(feats):
            acc[feat, :] = acc[feat, :] * fades[h] + dot_nn(v_t[feat, keys], probs[h])

    begin, end = clip_range(info, tile, k_aug.shape[0])
    pairs = (end - begin) // 2

    def two(n, _):
        step(begin + 2 * n, 2)
        return 0

    lax.fori_loop(0, pairs, two, 0)

    @pl.when(begin + 2 * pairs < end)
    def _():
        step(end - 1, 1)

    for h, feat in enumerate(feats):
        acc[feat, :] = acc[feat, :] / total[h : h + 1, :]
    lse[...] = jnp.zeros_like(lse)
    lse[0:HEADS, :] = top[0:HEADS, :] + jnp.log(total[0:HEADS, :])
    turned_o = acc[...]
    o_t[...] = turned_o.astype(bf16)
    o[...] = turned_o.T.astype(bf16)


def attend(part, info, k_aug, v_t, q_aug_t, k_t, padding, earlier):
    length = k_aug.shape[0]
    half = length // 2

    def columns(count):
        return pl.BlockSpec((count, TILE), lambda i, *_: (0, 2 * i + part))

    def packed(count):
        return pl.BlockSpec((count, TILE), lambda i, *_: (0, i))

    out = jax.ShapeDtypeStruct
    return pl.pallas_call(
        in_order(functools.partial(attend_kernel, part=part), 6, len(earlier)),
        grid_spec=pltpu.PrefetchScalarGridSpec(
            num_scalar_prefetch=1,
            grid=(half // TILE,),
            in_specs=[
                whole(k_aug.shape), whole(v_t.shape), columns(HEADS * AUG), columns(WIDTH),
                columns(1),
            ]
            + unread(earlier),
            out_specs=[
                pl.BlockSpec((TILE, WIDTH), lambda i, *_: (i, 0)), packed(WIDTH), packed(8),
            ],
            scratch_shapes=[
                pltpu.VMEM((8, TILE), f32), pltpu.VMEM((8, TILE), f32), pltpu.VMEM((WIDTH, TILE), f32),
            ],
        ),
        out_shape=[out((half, WIDTH), bf16), out((WIDTH, half), bf16), out((8, half), f32)],
        compiler_params=params(LIMIT),
        cost_estimate=pl.CostEstimate(
            flops=24 * half * length * WIDTH, bytes_accessed=6 * MIB, transcendentals=0
        ),
        name="attend",
    )(info, k_aug, v_t, q_aug_t, k_t, padding, *earlier)


def pair_kernel(first, second, out):
    out[0] = first[...]
    out[1] = second[...]


def paired(first, second, earlier):
    shape = (2,) + first.shape
    return pl.pallas_call(
        in_order(pair_kernel, 2, len(earlier)),
        in_specs=[pl.BlockSpec(memory_space=pltpu.VMEM)] * 2 + unread(earlier),
        out_specs=pl.BlockSpec(memory_space=pltpu.VMEM),
        out_shape=jax.ShapeDtypeStruct(shape, first.dtype),
        name="paired",
    )(first, second, *earlier)


def gelu_parts(u):
    size = jnp.abs(u)
    t = 1.0 / (1.0 + (0.3275911 / math.sqrt(2.0)) * size)
    bell = jnp.exp(-0.5 * (u * u))
    poly = 0.5 * 1.061405429
    for c in (-1.453152027, 1.421413741, -0.284496736, 0.254829592):
        poly = poly * t + 0.5 * c
    tail = poly * t * bell
    below = jnp.where(u >= 0, 1.0 - tail, tail)
    return u * below, below + u * bell * (1.0 / math.sqrt(2.0 * math.pi))


def mlp_kernel(
    info, tok, cot, o_a, o_b, w_all, b_out, gain, shift, w_up, b_up, w_down,
    x2, h2, act, du, mlp_sent, mlp_kept, dh2_sent, dh2_kept, db_up, w_out, *, me_at,
):
    i = pl.program_id(0)

    @pl.when(i == 0)
    def _():
        for n, j in enumerate((0, 2, 1, 3)):
            w_out[n * WIDTH : (n + 1) * WIDTH, :] = w_all[jnp.bitwise_xor(info[me_at], j)]
        db_up[...] = jnp.zeros_like(db_up)

    heads = jnp.concatenate([o_a[0], o_a[1], o_b[0], o_b[1]], axis=1)
    mid = tok[...].astype(f32) + b_out[...] + dot_nn(heads, w_out[...])

    @pl.when(i == 2)
    def _():
        x2[...] = mid

    hat, _ = normalized(mid)
    normed = (hat * gain[...] + shift[...]).astype(bf16)
    h2[...] = normed
    u = dot_nn(normed, w_up[...]) + b_up[...]
    grad_act = dot_nt(cot[...], w_down[...])
    value, slope = gelu_parts(u)
    value = value.astype(bf16)
    grad = (grad_act * slope).astype(bf16)
    act[...] = value
    du[...] = grad
    db_up[0:1, :] += jnp.sum(grad.astype(f32), axis=0, keepdims=True)
    mlp_part = dot_nn(value, w_down[...]).astype(bf16)
    dh2_part = dot_nt(grad, w_up[...]).astype(bf16)

    @pl.when(i < 2)
    def _():
        mlp_sent[0] = mlp_part
        dh2_sent[0] = dh2_part

    @pl.when(i >= 2)
    def _():
        mlp_kept[0] = mlp_part
        dh2_kept[0] = dh2_part


def mlp(
    part, info, me_at, tokens, cotangent, o_a, o_b, w_all, b_out, gain, shift, w_up, b_up, w_down,
    earlier,
):
    length, width = tokens.shape
    half = length // 2
    hidden = w_up.shape[1]
    owners = half // TILE

    def owner(i, info):
        return jnp.bitwise_xor(info[me_at], (2 * i + 1) % 5)

    def rows(columns):
        return pl.BlockSpec((TILE, columns), lambda i, info: (2 * owner(i, info) + part, 0))

    def packed(columns):
        return pl.BlockSpec((TILE, columns), lambda i, info: (owner(i, info), 0))

    sent = pl.BlockSpec((1, TILE, width), lambda i, info: (jnp.minimum(i, 1), 0, 0))
    kept = pl.BlockSpec((1, TILE, width), lambda i, info: (jnp.maximum(i - 2, 0), 0, 0))

    out = jax.ShapeDtypeStruct
    return pl.pallas_call(
        in_order(functools.partial(mlp_kernel, me_at=me_at), 12, len(earlier)),
        grid_spec=pltpu.PrefetchScalarGridSpec(
            num_scalar_prefetch=1,
            grid=(owners,),
            in_specs=[rows(width), rows(width)]
            + [pl.BlockSpec((2, TILE, WIDTH), lambda i, info: (0, owner(i, info), 0))] * 2
            + [whole(w_all.shape)]
            + [whole((1, width))] * 3
            + [whole(w_up.shape), whole((1, hidden)), whole(w_down.shape)]
            + unread(earlier),
            out_specs=[
                whole((TILE, width)), packed(width), packed(hidden), packed(hidden),
                sent, kept, sent, kept, whole((8, hidden)),
            ],
            scratch_shapes=[pltpu.VMEM((4 * WIDTH, width), bf16)],
        ),
        out_shape=[
            out((TILE, width), f32), out((half, width), bf16), out((half, hidden), bf16),
            out((half, hidden), bf16),
        ]
        + [out((owners // 2, TILE, width), bf16)] * 4
        + [out((8, hidden), f32)],
        compiler_params=params(LIMIT),
        cost_estimate=pl.CostEstimate(
            flops=20 * half * width * hidden, bytes_accessed=20 * MIB, transcendentals=0
        ),
        name="mlp",
    )(
        info, tokens, cotangent, o_a, o_b, w_all, b_out, gain, shift, w_up, b_up, w_down, *earlier
    )


def up_weights_kernel(left_a, left_b, right_a, right_b, out):
    left = jnp.concatenate([left_a[...], left_b[...]])
    right = jnp.concatenate([right_a[...], right_b[...]])
    out[...] = dot_tn(left, right).astype(bf16)


def up_weights(h2, du, filled, earlier):
    half, width = h2[0].shape
    hidden = du[0].shape[1]
    return pl.pallas_call(
        in_order(up_weights_kernel, 4, 1 + len(earlier)),
        grid=(width // TILE,),
        in_specs=[pl.BlockSpec((half, TILE), lambda i: (0, i))] * 2
        + [whole((half, hidden))] * 2
        + unread((filled,) + earlier),
        out_specs=pl.BlockSpec((TILE, hidden), lambda i: (i, 0)),
        out_shape=jax.ShapeDtypeStruct(filled.shape, bf16),
        input_output_aliases={4: 0},
        compiler_params=params(LIMIT),
        cost_estimate=pl.CostEstimate(
            flops=8 * half * width * hidden, bytes_accessed=12 * MIB, transcendentals=0
        ),
        name="up_weights",
    )(*h2, *du, filled, *earlier)


def down_weights_kernel(act_a, act_b, cot, out):
    owners = cot.shape[0] // (2 * TILE)
    rows = [cot[n * TILE : (n + 1) * TILE, :] for p in range(2) for n in range(p, 2 * owners, 2)]
    out[...] = dot_tn(
        jnp.concatenate([act_a[...], act_b[...]]), jnp.concatenate(rows)
    ).astype(bf16)


def down_weights(act, cotangent, earlier):
    half, hidden = act[0].shape
    length, width = cotangent.shape
    return pl.pallas_call(
        in_order(down_weights_kernel, 3, len(earlier)),
        grid=(hidden // TILE,),
        in_specs=[pl.BlockSpec((half, TILE), lambda i: (0, i))] * 2
        + [whole((length, width))]
        + unread(earlier),
        out_specs=pl.BlockSpec((TILE, width), lambda i: (i + width // TILE, 0)),
        out_shape=jax.ShapeDtypeStruct((width + hidden, width), bf16),
        compiler_params=params(LIMIT),
        cost_estimate=pl.CostEstimate(
            flops=8 * half * width * hidden, bytes_accessed=12 * MIB, transcendentals=0
        ),
        name="down_weights",
    )(*act, cotangent, *earlier)


def middle_kernel(
    info, here, there, x2, cot, gain, w_all, dx2, g, d_0, d_1, d_2, d_3, small, *, me_at
):
    grad = here[...].astype(f32) + there[...].astype(f32)
    hat, inverse = normalized(x2[...])
    dy = cot[...].astype(f32)
    full = dy + norm_back(hat, inverse, gain[...], grad)
    dx2[...] = full
    low = full.astype(bf16)
    g[...] = low
    small[...] = jnp.zeros_like(small)
    small[0:1, :] = jnp.sum(grad * hat, axis=0, keepdims=True)
    small[1:2, :] = jnp.sum(grad, axis=0, keepdims=True)
    small[2:3, :] = jnp.sum(low.astype(f32), axis=0, keepdims=True)
    small[3:4, :] = jnp.sum(dy, axis=0, keepdims=True)
    for j, d_j in enumerate((d_0, d_1, d_2, d_3)):
        d_j[...] = dot_nt(low, w_all[jnp.bitwise_xor(info[me_at], j)]).astype(bf16)


def middle(part, info, me_at, here, there, x2, cotangent, gain, w_all, earlier):
    width = x2.shape[1]
    out = jax.ShapeDtypeStruct
    own = whole((TILE, width))
    return pl.pallas_call(
        in_order(functools.partial(middle_kernel, me_at=me_at), 7, len(earlier)),
        grid_spec=pltpu.PrefetchScalarGridSpec(
            num_scalar_prefetch=1,
            grid=(1,),
            in_specs=[
                own, own, own,
                pl.BlockSpec((TILE, width), lambda i, info: (2 * info[me_at] + part, 0)),
                whole((1, width)), whole(w_all.shape),
            ]
            + unread(earlier),
            out_specs=[own, own] + [whole((TILE, WIDTH))] * 4 + [whole((8, width))],
        ),
        out_shape=[out((TILE, width), f32), out((TILE, width), bf16)]
        + [out((TILE, WIDTH), bf16)] * 4
        + [out((8, width), f32)],
        compiler_params=params(40),
        cost_estimate=pl.CostEstimate(
            flops=2 * TILE * width * width, bytes_accessed=8 * MIB, transcendentals=0
        ),
        name="middle",
    )(info, here, there, x2, cotangent, gain, w_all, *earlier)


def out_weights_kernel(info, oa_a, oa_b, ob_a, ob_b, g_a, g_b, sent, kept):
    for n in range(2):
        kept[n] = (dot_tn(oa_a[n], g_a[...]) + dot_tn(ob_a[n], g_b[...])).astype(bf16)
        sent[n] = (dot_tn(oa_b[n], g_a[...]) + dot_tn(ob_b[n], g_b[...])).astype(bf16)


def out_weights(info, me_at, pairs_a, pairs_b, g_a, g_b):
    width = g_a.shape[1]
    own = pl.BlockSpec((2, TILE, WIDTH), lambda i, info: (0, info[me_at], 0))
    return pl.pallas_call(
        out_weights_kernel,
        grid_spec=pltpu.PrefetchScalarGridSpec(
            num_scalar_prefetch=1,
            grid=(1,),
            in_specs=[own] * 4 + [whole((TILE, width))] * 2,
            out_specs=[whole((2, WIDTH, width))] * 2,
        ),
        out_shape=[jax.ShapeDtypeStruct((2, WIDTH, width), bf16)] * 2,
        compiler_params=params(LIMIT),
        cost_estimate=pl.CostEstimate(
            flops=4 * TILE * width * width, bytes_accessed=6 * MIB, transcendentals=0
        ),
        name="out_weights",
    )(info, *pairs_a, *pairs_b, g_a, g_b)


def attend_back_kernel(
    info, k_aug, v_aug, k_t, q_aug_t, q, v_t, o_t, lse, pad, do_0, do_1, do_2, do_3, pos, table,
    *refs, part, me_at, first,
):
    if first:
        dk_in = dv_in = None
    else:
        dk_in, dv_in, *refs = refs
    dq_out, dk, dv, q_side, do_side, q_lanes, do_lanes, dq_t = refs
    i = pl.program_id(0)
    tile = 2 * jnp.bitwise_xor(info[me_at], i) + part

    @pl.when(i == 0)
    def _():
        if first:
            dk[...] = jnp.zeros_like(dk)
            dv[...] = jnp.zeros_like(dv)
        else:
            dk[...] = dk_in[...]
            dv[...] = dv_in[...]

    here = pl.ds(pl.multiple_of(tile * TILE, TILE), TILE)
    do_here = jnp.where(
        i == 0, do_0[...], jnp.where(i == 1, do_1[...], jnp.where(i == 2, do_2[...], do_3[...]))
    )
    q_here = q[...]
    do_t = do_here.astype(f32).T
    k_here = k_t[:, here].astype(f32)
    padded = jnp.where(pad[...] != 0, 1.0, 0.0)
    row = lax.broadcasted_iota(jnp.int32, (AUG - HEAD_DIM, TILE), 0)
    lane = lax.broadcasted_iota(jnp.int32, (TILE, WIDTH), 1) // HEAD_DIM
    dk_parts, dv_parts = [], []
    for h in range(HEADS):
        feat = slice(h * HEAD_DIM, (h + 1) * HEAD_DIM)
        at = h * AUG
        q_h = q_aug_t[at : at + HEAD_DIM, :]
        do_h = do_t[feat, :]
        delta = jnp.sum(do_h * o_t[feat, :].astype(f32), axis=0, keepdims=True)
        lse_h = lse[h : h + 1, :]
        one, two, three = three_parts(-lse_h)
        extra = q_aug_t[at + HEAD_DIM : at + AUG, :].astype(f32)
        extra = jnp.where(row == 4, one, jnp.where(row == 5, two, jnp.where(row == 6, three, extra)))
        q_side[at : at + HEAD_DIM, :] = q_h
        q_side[at + HEAD_DIM : at + AUG, :] = extra.astype(bf16)
        one, two, three = three_parts(-delta)
        extra = jnp.where(row == 0, one, jnp.where(row == 1, two, jnp.where(row == 2, three, 0.0)))
        do_side[at : at + HEAD_DIM, :] = do_h.astype(bf16)
        do_side[at + HEAD_DIM : at + AUG, :] = extra.astype(bf16)
        q_lanes[h] = jnp.where(lane == h, q_here, jnp.zeros_like(q_here))
        do_lanes[h] = jnp.where(lane == h, do_here, jnp.zeros_like(do_here))
        q_h = q_h.astype(f32)
        k_h = k_here[feat, :]
        p_own = padded * jnp.exp(jnp.sum(q_h * k_h, axis=0, keepdims=True) - lse_h)
        dp_own = jnp.sum(do_h * v_t[feat, :].astype(f32), axis=0, keepdims=True)
        ds_own = p_own * (dp_own - delta)
        dq_t[feat, :] = ds_own * k_h
        dk_parts.append(ds_own * q_h)
        dv_parts.append(p_own * do_h)
    dk[here, :] += jnp.concatenate(dk_parts, axis=0).T
    dv[here, :] += jnp.concatenate(dv_parts, axis=0).T

    def step(j, _):
        keys = pl.ds(pl.multiple_of(j * TILE, TILE), TILE)
        probs, grads = [], []
        for h in range(HEADS):
            wide = slice(h * AUG, (h + 1) * AUG)
            prob = jnp.exp(dot_nn(k_aug[keys, wide], q_side[wide, :]))
            grad = prob * dot_nn(v_aug[keys, wide], do_side[wide, :])
            probs.append(prob.astype(bf16))
            grads.append(grad.astype(bf16))
        deep = (HEADS * TILE, WIDTH)
        dv[keys, :] += dot_nn(jnp.concatenate(probs, axis=1), do_lanes[...].reshape(deep))
        dk[keys, :] += dot_nn(jnp.concatenate(grads, axis=1), q_lanes[...].reshape(deep))
        for h in range(HEADS):
            feat = slice(h * HEAD_DIM, (h + 1) * HEAD_DIM)
            dq_t[feat, :] += dot_nn(k_t[feat, keys], grads[h])
        return 0

    begin, end = clip_range(info, tile, k_aug.shape[0])
    lax.fori_loop(begin, end, step, 0)
    dq = dq_t[...].T * (1.0 / math.sqrt(HEAD_DIM))
    cos, low, high = rope_factors(pos, table)
    dq_out[...] = (dq * cos - turned(dq, low, high)).astype(bf16)


def attend_back(
    part, info, me_at, k_aug, v_aug, k_t, q_aug_t, q, v_t, o_t, lse, padding, do, positions, table,
    dk, dv, earlier,
):
    length = k_aug.shape[0]
    half = length // 2

    def owner(i, info):
        return jnp.bitwise_xor(info[me_at], i)

    def rows(columns):
        return pl.BlockSpec((TILE, columns), lambda i, info: (2 * owner(i, info) + part, 0))

    def columns(count):
        return pl.BlockSpec((count, TILE), lambda i, info: (0, 2 * owner(i, info) + part))

    def packed(count):
        return pl.BlockSpec((count, TILE), lambda i, info: (0, owner(i, info)))

    out = jax.ShapeDtypeStruct
    before = () if dk is None else (dk, dv)
    return pl.pallas_call(
        in_order(
            functools.partial(attend_back_kernel, part=part, me_at=me_at, first=dk is None),
            16 + len(before), len(earlier),
        ),
        grid_spec=pltpu.PrefetchScalarGridSpec(
            num_scalar_prefetch=1,
            grid=(half // TILE,),
            in_specs=[
                whole(k_aug.shape), whole(v_aug.shape), whole(k_t.shape), columns(HEADS * AUG),
                rows(WIDTH), columns(WIDTH), packed(WIDTH), packed(8), columns(1),
            ]
            + [whole((TILE, WIDTH))] * 4
            + [
                pl.BlockSpec(
                    (3, 1, TILE), lambda i, info: (0, 0, 2 * owner(i, info) + part)
                ),
                whole(table.shape),
            ]
            + [whole((length, WIDTH))] * len(before)
            + unread(earlier),
            out_specs=[
                pl.BlockSpec((TILE, WIDTH), lambda i, info: (owner(i, info), 0)),
                whole((length, WIDTH)), whole((length, WIDTH)),
            ],
            scratch_shapes=[
                pltpu.VMEM((HEADS * AUG, TILE), bf16), pltpu.VMEM((HEADS * AUG, TILE), bf16),
                pltpu.VMEM((HEADS, TILE, WIDTH), bf16), pltpu.VMEM((HEADS, TILE, WIDTH), bf16),
                pltpu.VMEM((WIDTH, TILE), f32),
            ],
        ),
        out_shape=[out((half, WIDTH), bf16), out((length, WIDTH), f32), out((length, WIDTH), f32)],
        compiler_params=params(LIMIT),
        cost_estimate=pl.CostEstimate(
            flops=72 * half * length * WIDTH, bytes_accessed=16 * MIB, transcendentals=0
        ),
        name="attend_back",
    )(
        info, k_aug, v_aug, k_t, q_aug_t, q, v_t, o_t, lse, padding, *do, positions, table, *before,
        *earlier,
    )


def pieces(begin, count, period):
    at, end, cuts = begin, begin + count, []
    while at < end:
        length = min(end - at, period - at % period)
        cuts.append((at, length))
        at += length
    return cuts


def stacked_pairs(rows, first, count):
    row = lax.broadcasted_iota(jnp.int32, (count, WIDTH), 0)
    out = jnp.zeros((count, WIDTH), f32)
    for m, value in enumerate(rows, first):
        one, two, _ = three_parts(value)
        out = jnp.where(row == 2 * m, one, jnp.where(row == 2 * m + 1, two, out))
    return out.astype(bf16)


def extra_pairs(width, blocks):
    many = -(-(3 + 5 * width // WIDTH) // blocks)
    few = -(-(2 * width // WIDTH) // blocks)
    return many, few, -(-(many + few) // 8) * 16


def project_weights_kernel(
    info, tok, gain, shift, dq_a, dq_b, dk, dv, pos, table, w, out_kept, out_there, early,
    grads, sums, acc, grad_b, w_wide,
):
    i = pl.program_id(0)

    @pl.when(i == 0)
    def _():
        acc[...] = jnp.zeros_like(acc)
        grad_b[...] = jnp.zeros_like(grad_b)
        for c in range(3):
            w_wide[:, c * WIDTH : (c + 1) * WIDTH] = w[c]

    hat, _ = normalized(tok[...].astype(f32))
    normed = (hat * gain[...] + shift[...]).astype(bf16)
    dq = jnp.where(i % 2 == 0, dq_a[...], dq_b[...])
    dk_here = dk[...]
    cos, low, high = rope_factors(pos, table)
    dk_low = (dk_here * cos - turned(dk_here, low, high)).astype(bf16)
    parts = jnp.concatenate([dq, dk_low, dv[...].astype(bf16)], axis=1)
    grads[...] = parts
    acc[...] += dot_tn(normed, parts)
    grad_b[0:1, :] += jnp.sum(parts.astype(f32), axis=0, keepdims=True)

    @pl.when(i == pl.num_programs(0) - 1)
    def _():
        width = normed.shape[1]
        blocks = sums.shape[0]
        deep = 3 * width // blocks
        extra_at = deep + width // blocks
        extra_rows = sums.shape[1] - extra_at

        def cut(value, count):
            return [value[:, r * WIDTH : (r + 1) * WIDTH] for r in range(count)]

        rows = cut(grad_b[0:1, :], 3)
        for v in range(5):
            rows += cut(early[v : v + 1, :], width // WIDTH)
        for n in range(blocks):
            for at, length in pieces(n * deep, deep, width):
                c, begin = at // width, at % width
                sums[n, at - n * deep : at - n * deep + length, :] = acc[
                    begin : begin + length, c * WIDTH : (c + 1) * WIDTH
                ].astype(bf16)
            share = width // blocks
            for at, length in pieces(n * share, share, WIDTH):
                c, begin = at // WIDTH, at % WIDTH
                to = deep + at - n * share
                here = (slice(begin, begin + length), slice(c * WIDTH, (c + 1) * WIDTH))
                sums[n, to : to + length, :] = (
                    out_kept[here].astype(f32) + out_there[here].astype(f32)
                ).astype(bf16)
            sums[n, extra_at : extra_at + extra_rows, :] = stacked_pairs(
                rows[n::blocks], 0, extra_rows
            )


def project_weights(
    info, me_at, tokens, gain, shift, dq_a, dq_b, dk, dv, positions, table, w, kept, there, early,
    blocks,
):
    length, width = tokens.shape
    tiles = length // TILE

    def rows(columns):
        return pl.BlockSpec((TILE, columns), lambda i, info: (i, 0))

    packed = pl.BlockSpec((TILE, WIDTH), lambda i, info: (i // 2, 0))
    last = pl.BlockSpec((TILE, width), lambda i, info: (2, 0))
    out = jax.ShapeDtypeStruct
    sums = (blocks, 4 * width // blocks + extra_pairs(width, blocks)[2], WIDTH)
    return pl.pallas_call(
        project_weights_kernel,
        grid_spec=pltpu.PrefetchScalarGridSpec(
            num_scalar_prefetch=1,
            grid=(tiles,),
            in_specs=[
                rows(width), whole((1, width)), whole((1, width)), packed, packed,
                rows(WIDTH), rows(WIDTH), pl.BlockSpec((3, 1, TILE), lambda i, info: (0, 0, i)),
                whole(table.shape), whole(w.shape), last, last, whole(early.shape),
            ],
            out_specs=[rows(3 * WIDTH), whole(sums)],
            scratch_shapes=[
                pltpu.VMEM((width, 3 * WIDTH), f32), pltpu.VMEM((8, 3 * WIDTH), f32),
                pltpu.VMEM((width, 3 * WIDTH), bf16),
            ],
        ),
        out_shape=[out((length, 3 * WIDTH), bf16), out(sums, bf16)],
        compiler_params=params(LIMIT),
        cost_estimate=pl.CostEstimate(
            flops=16 * length * width * WIDTH, bytes_accessed=20 * MIB, transcendentals=0
        ),
        name="project_weights",
    )(info, tokens, gain, shift, dq_a, dq_b, dk, dv, positions, table, w, kept, there, early)


def project_rows_kernel(info, tok, grads, w, sent, kept, sums, small, w_wide):
    i = pl.program_id(0)

    @pl.when(i == 0)
    def _():
        small[...] = jnp.zeros_like(small)
        for c in range(3):
            w_wide[:, c * WIDTH : (c + 1) * WIDTH] = w[c]

    grad = dot_nt(grads[...], w_wide[...])
    hat, _ = normalized(tok[...].astype(f32))
    small[0:1, :] += jnp.sum(grad * hat, axis=0, keepdims=True)
    small[1:2, :] += jnp.sum(grad, axis=0, keepdims=True)
    low = grad.astype(bf16)

    @pl.when(i < 2)
    def _():
        sent[0] = low

    @pl.when(i >= 2)
    def _():
        kept[0] = low

    @pl.when(i == pl.num_programs(0) - 1)
    def _():
        blocks, count, _ = sums.shape
        width = small.shape[1]
        rows = [
            small[v : v + 1, r * WIDTH : (r + 1) * WIDTH]
            for v in range(2)
            for r in range(width // WIDTH)
        ]
        for n in range(blocks):
            sums[n] = stacked_pairs(rows[n::blocks], extra_pairs(width, blocks)[0], count)


def project_rows(info, me_at, tokens, grads, w, blocks, earlier):
    length, width = tokens.shape
    rows = 2 * TILE

    def own(columns):
        return pl.BlockSpec(
            (rows, columns), lambda i, info: (jnp.bitwise_xor(info[me_at], (2 * i + 1) % 5), 0)
        )

    out = jax.ShapeDtypeStruct((2, rows, width), bf16)
    sums = (blocks, extra_pairs(width, blocks)[2], WIDTH)
    return pl.pallas_call(
        in_order(project_rows_kernel, 4, len(earlier)),
        grid_spec=pltpu.PrefetchScalarGridSpec(
            num_scalar_prefetch=1,
            grid=(length // rows,),
            in_specs=[own(width), own(3 * WIDTH), whole(w.shape)] + unread(earlier),
            out_specs=[
                pl.BlockSpec((1, rows, width), lambda i, info: (jnp.minimum(i, 1), 0, 0)),
                pl.BlockSpec((1, rows, width), lambda i, info: (jnp.maximum(i - 2, 0), 0, 0)),
                whole(sums),
            ],
            scratch_shapes=[pltpu.VMEM((8, width), f32), pltpu.VMEM((width, 3 * WIDTH), bf16)],
        ),
        out_shape=[out, out, jax.ShapeDtypeStruct(sums, bf16)],
        compiler_params=params(LIMIT),
        cost_estimate=pl.CostEstimate(
            flops=12 * length * width * WIDTH, bytes_accessed=10 * MIB, transcendentals=0
        ),
        name="project_rows",
    )(info, tokens, grads, w, *earlier)


def finish_kernel(info, here, there, tok, gain, dx2_a, dx2_b, out):
    grad = here[...].astype(f32) + there[...].astype(f32)
    hat, inverse = normalized(tok[...].astype(f32))
    dx2 = jnp.where(pl.program_id(0) == 0, dx2_a[...], dx2_b[...])
    out[...] = dx2 + norm_back(hat, inverse, gain[...], grad)


def finish(info, me_at, here, there, tokens, gain, dx2_a, dx2_b):
    width = tokens.shape[1]
    share = here.shape[0]
    rows = pl.BlockSpec((TILE, width), lambda i, info: (i, 0))
    return pl.pallas_call(
        finish_kernel,
        grid_spec=pltpu.PrefetchScalarGridSpec(
            num_scalar_prefetch=1,
            grid=(share // TILE,),
            in_specs=[
                rows, rows,
                pl.BlockSpec((TILE, width), lambda i, info: (2 * info[me_at] + i, 0)),
                whole((1, width)), whole((TILE, width)), whole((TILE, width)),
            ],
            out_specs=rows,
        ),
        out_shape=jax.ShapeDtypeStruct((share, width), f32),
        compiler_params=params(32),
        name="finish",
    )(info, here, there, tokens, gain, dx2_a, dx2_b)


def swap(array, axis, bit=1):
    size = lax.axis_size(axis)
    if size == 1:
        return jnp.zeros_like(array)
    return lax.ppermute(array, axis, [(i, i ^ bit) for i in range(size)])


def swap_both(array):
    return lax.ppermute(array, MP, [(i, i ^ 3) for i in range(4)])


def scattered_sum(rows, axes):
    group = lax.axis_size(axes)
    length, width = rows.shape
    blocks = rows.reshape(group, length // group, width)
    blocks = lax.all_to_all(blocks, axes, 0, 0, tiled=True)
    return jnp.sum(blocks.astype(f32), axis=0)


def spread(block, axes):
    group = lax.axis_size(axes)
    return lax.all_to_all(
        jnp.broadcast_to(block[None], (group,) + block.shape), axes, 0, 0, tiled=True
    )


def both_sums(total):
    if lax.axis_size("zl") == 1:
        return total
    return (total.astype(f32) + swap(total, "zl").astype(f32)).astype(bf16)


def local(
    tokens, cotangent, segments, padding, positions, ln1_gain, ln1_bias, w_qkv, b_qkv, w_out, b_out,
    ln2_gain, ln2_bias, w_up, b_up, w_down, b_down,
):
    width, hidden = w_up.shape
    w_all = lax.all_gather(w_out, MP)
    gain_one, shift_one = ln1_gain[None], ln1_bias[None]
    gain_two, shift_two = ln2_gain[None], ln2_bias[None]
    ends = jnp.sum((segments <= jnp.arange(2)[:, None]).astype(jnp.int32), axis=1)
    info = jnp.concatenate([ends, lax.axis_index(MP)[None].astype(jnp.int32)])
    me_at = 2
    table = jnp.asarray(rope_constants())
    k_aug, v_aug, q_aug_t, q, k_t, v_t = project(
        tokens, w_qkv, b_qkv, gain_one, shift_one, positions, segments, padding, table
    )

    o_0, o_t_0, lse_0 = attend(0, info, k_aug, v_t, q_aug_t, k_t, padding, ())
    o_zh_0 = swap(o_0, "zh")
    o_1, o_t_1, lse_1 = attend(1, info, k_aug, v_t, q_aug_t, k_t, padding, (o_0, w_all))
    o_zh_1 = swap(o_1, "zh")
    pair_0 = paired(o_0, o_zh_0, (o_1,))
    pairs_0 = (pair_0, swap(pair_0, "c"))

    def mlp_half(part, pairs, earlier):
        return mlp(
            part, info, me_at, tokens, cotangent, *pairs, w_all, b_out[None], gain_two, shift_two,
            w_up, b_up[None], w_down, earlier,
        )

    def met(sent, kept):
        other = swap(sent, "c")
        here = (kept[0].astype(f32) + other[0].astype(f32)).astype(bf16)
        return here, (kept[1].astype(f32) + other[1].astype(f32)).astype(bf16)

    x2_0, h2_0, act_0, du_0, mlp_sent_0, mlp_kept_0, dh2_sent, dh2_kept, db_0 = mlp_half(
        0, pairs_0, (o_1,)
    )
    pair_1 = paired(o_1, o_zh_1, (x2_0,))
    pairs_1 = (pair_1, swap(pair_1, "c"))
    here_0, give_0 = met(dh2_sent, dh2_kept)
    there_0 = swap(give_0, "zh")
    x2_1, h2_1, act_1, du_1, mlp_sent_1, mlp_kept_1, dh2_sent, dh2_kept, db_1 = mlp_half(
        1, pairs_1, (give_0,)
    )
    here_1, give_1 = met(dh2_sent, dh2_kept)
    there_1 = swap(give_1, "zh")
    grad_mlp = down_weights((act_0, act_1), cotangent, ())

    def exchanged(d_own, d_c, d_zh, d_both):
        return d_own, swap(d_c, "c"), swap(d_zh, "zh"), swap_both(d_both)

    dx2_0, g_0, *d_0, small_0 = middle(
        0, info, me_at, here_0, there_0, x2_0, cotangent, gain_two, w_all, (grad_mlp, give_1)
    )
    do_0 = exchanged(*d_0)
    grad_mlp = up_weights((h2_0, h2_1), (du_0, du_1), grad_mlp, (g_0,))
    dx2_1, g_1, *d_1, small_1 = middle(
        1, info, me_at, here_1, there_1, x2_1, cotangent, gain_two, w_all, (grad_mlp,)
    )
    do_1 = exchanged(*d_1)
    out_sent, out_kept = out_weights(info, me_at, pairs_0, pairs_1, g_0, g_1)

    others = [swap(sent, "c") for sent in (mlp_sent_0, mlp_sent_1, out_sent)]
    part_sum = scattered_sum(grad_mlp, ("y", "x")).astype(bf16)
    dq_0, dk, dv = attend_back(
        0, info, me_at, k_aug, v_aug, k_t, q_aug_t, q, v_t, o_t_0, lse_0, padding, do_0, positions,
        table, None, None, (out_sent, g_1),
    )

    keep, give = (
        jnp.concatenate(
            [
                (kept[n].astype(f32) + other[n].astype(f32)).astype(bf16)
                for kept, other in zip((mlp_kept_0, mlp_kept_1, out_kept), others)
            ]
        )
        for n in range(2)
    )
    there = swap(give, "zh")
    part_sum = both_sums(part_sum)
    dq_1, dk, dv = attend_back(
        1, info, me_at, k_aug, v_aug, k_t, q_aug_t, q, v_t, o_t_1, lse_1, padding, do_1, positions,
        table, dk, dv, (give, part_sum, dq_0),
    )
    grad_mlp = spread(part_sum, ("y", "x"))
    early = jnp.concatenate([(small_0 + small_1)[0:4], (db_0 + db_1)[0:4]])
    grads, sums = project_weights(
        info, me_at, tokens, gain_one, shift_one, dq_0, dq_1, dk, dv, positions, table, w_qkv, keep,
        there, early, lax.axis_size(DP),
    )
    blocks, deep, _ = sums.shape
    dh1_sent, dh1_kept, more = project_rows(
        info, me_at, tokens, grads, w_qkv, blocks, (grad_mlp, sums)
    )
    total = scattered_sum(sums.reshape(blocks * deep, WIDTH), DP)
    more = scattered_sum(more.reshape(-1, WIDTH), DP)
    total = total + jnp.pad(more, ((deep - more.shape[0], 0), (0, 0)))
    sums = spread(total.astype(bf16), DP)
    here, give = met(dh1_sent, dh1_kept)
    grad_inputs = finish(info, me_at, here, swap(give, "zh"), tokens, gain_one, dx2_0, dx2_1)
    received = keep[: 2 * TILE].astype(f32) + there[: 2 * TILE].astype(f32)
    mixed = (jnp.concatenate([x2_0, x2_1]) + received + b_down[None]).astype(bf16)

    grad_mlp = grad_mlp.reshape(2, width, hidden)
    kept, shared = 3 * width // blocks, width // blocks
    grad_qkv = sums[:, :kept].astype(f32).reshape(w_qkv.shape)
    grad_w_out = sums[:, kept : kept + shared].astype(f32).reshape(width // WIDTH, WIDTH, WIDTH)
    grad_w_out = grad_w_out.transpose(1, 0, 2).reshape(WIDTH, width)
    count = width // WIDTH
    many, few, _ = extra_pairs(width, blocks)
    extra = sums[:, kept + shared :].astype(f32)
    pairs = [extra[:, at] + extra[:, at + 1] for at in range(0, 2 * (many + few), 2)]
    main = jnp.concatenate(pairs[:many])
    group = jnp.concatenate([main[3 : 3 + 4 * count], jnp.concatenate(pairs[many:])[: 2 * count]])
    group = group + swap(group, "c")
    group = (group + swap(group, "zh")).reshape(6, width)
    return (
        mixed, grad_inputs, group[4], group[5], grad_qkv, main[0:3], grad_w_out, group[2], group[0],
        group[1], grad_mlp[0].astype(f32), main[3 + 4 * count : 3 + 5 * count].reshape(hidden),
        grad_mlp[1].astype(f32), group[3],
    )


def solution(mesh):
    packs = mesh.shape["dp"]
    if packs == 32:
        shape = (2, 4, 4, 2, 2)
    else:
        shape = (1, packs, 1, 2, 2)
    split = Mesh(mesh.devices.reshape(shape), EVERY)
    in_specs = (
        P(DP, None), P(DP, None), P(DP, None), P(DP, None), P(None, DP, None), P(), P(),
        P(None, None, MP), P(None, MP), P(MP, None), P(), P(), P(), P(None, MP), P(MP),
        P(MP, None), P(),
    )
    out_specs = (
        P(EVERY, None), P(EVERY, None), P(), P(), P(None, None, MP), P(None, MP), P(MP, None), P(),
        P(), P(), P(None, MP), P(MP), P(MP, None), P(),
    )
    return jax.shard_map(local, mesh=split, in_specs=in_specs, out_specs=out_specs, check_vma=False)
```

```python
import functools
import math

import jax
import jax.numpy as jnp
import ml_dtypes
import numpy as np
from jax import lax
from jax.experimental import pallas as pl
from jax.experimental.pallas import tpu as pltpu
from jax.sharding import Mesh
from jax.sharding import PartitionSpec as P

HEAD_DIM = 64
HEADS = 4
WIDTH = HEADS * HEAD_DIM
AUG = 128
TILE = 256
PLACES = 64
LIMIT = 60
MIB = 1 << 20
DP = ("zl", "y", "x")
MP = ("zh", "c")
EVERY = ("zl", "y", "x", "zh", "c")

epsilon = 1e-06
NEG = -1e30
bf16 = jnp.bfloat16
f32 = jnp.float32


def dot_nn(a, b):
    return lax.dot_general(a, b, (((1,), (0,)), ((), ())), preferred_element_type=f32)


def dot_nt(a, b):
    return lax.dot_general(a, b, (((1,), (1,)), ((), ())), preferred_element_type=f32)


def dot_tn(a, b):
    return lax.dot_general(a, b, (((0,), (0,)), ((), ())), preferred_element_type=f32)


def normalized(values):
    center = jnp.mean(values, axis=-1, keepdims=True)
    shifted = values - center
    spread = jnp.mean(shifted * shifted, axis=-1, keepdims=True)
    inverse = lax.rsqrt(spread + epsilon)
    return shifted * inverse, inverse


def norm_back(hat, inverse, gain, grad):
    scaled = grad * gain
    return inverse * (
        scaled
        - jnp.mean(scaled, axis=-1, keepdims=True)
        - hat * jnp.mean(scaled * hat, axis=-1, keepdims=True)
    )


def turned(x, low, high):
    width = x.shape[1]
    pair = HEAD_DIM // 6
    return pltpu.roll(x, width - pair, 1) * low + pltpu.roll(x, pair, 1) * high


def three_parts(x):
    first = x.astype(bf16).astype(f32)
    rest = x - first
    second = rest.astype(bf16).astype(f32)
    return first, second, rest - second


def params(limit, axes=1):
    return pltpu.CompilerParams(
        dimension_semantics=("arbitrary",) * axes, vmem_limit_bytes=limit * MIB
    )


def in_order(kernel, inputs, earlier):
    def run(*refs):
        kernel(*refs[:inputs], *refs[inputs + earlier :])

    return run


def unread(arrays):
    return [pl.BlockSpec(memory_space=pl.ANY)] * len(arrays)


def whole(shape):
    return pl.BlockSpec(shape, lambda *_: (0,) * len(shape))


def clip_range(info, tile, length):
    first, second = info[0], info[1]
    at = tile * TILE
    begin = jnp.where(second <= at, second, jnp.where(first <= at, first, 0))
    end = jnp.where(
        first >= at + TILE, first, jnp.where(second >= at + TILE, second, length)
    )
    return begin // TILE, (end + TILE - 1) // TILE


def rope_constants():
    pair = HEAD_DIM // 6
    feature = np.arange(WIDTH) % HEAD_DIM
    section, place = feature // (2 * pair), feature % (2 * pair)
    frequency = np.exp(-math.log(10000.0) * (place % pair) / pair)
    table = np.zeros((PLACES, 3, WIDTH))
    for s in range(3):
        for value in range(16):
            angle = value * frequency
            turns = section == s
            table[s * 16 + value, 0] = np.where(turns, np.cos(angle), 0.0)
            table[s * 16 + value, 1] = np.where(turns & (place < pair), -np.sin(angle), 0.0)
            table[s * 16 + value, 2] = np.where(turns & (place >= pair), np.sin(angle), 0.0)
    table[48, 0] = section == 3
    rest = table.reshape(PLACES, 3 * WIDTH).astype(np.float32)
    parts = []
    for _ in range(3):
        part = rest.astype(ml_dtypes.bfloat16)
        parts.append(part)
        rest = rest - part.astype(np.float32)
    return np.concatenate(parts)


def rope_factors(positions, table):
    row = lax.broadcasted_iota(jnp.int32, (PLACES, positions.shape[-1]), 0)
    where = jnp.where(
        row < 16, positions[0], jnp.where(row < 32, positions[1], positions[2])
    )
    hit = ((where == row % 16) & (row < 48)) | (row == 48)
    hit = jnp.where(hit, 1.0, 0.0)
    hits = jnp.concatenate([hit, hit, hit]).astype(bf16)
    factors = dot_tn(hits, table[...])
    return factors[:, :WIDTH], factors[:, WIDTH : 2 * WIDTH], factors[:, 2 * WIDTH :]


def qkv_kernel(
    tok, w, b, gain, shift, pos, seg, pad, table, k_aug, v_aug, q_aug_t, q_out, k_t, v_t, w_wide
):
    @pl.when(pl.program_id(0) == 0)
    def _():
        for c in range(3):
            w_wide[:, c * WIDTH : (c + 1) * WIDTH] = w[c]

    hat, _ = normalized(tok[...].astype(f32))
    normed = (hat * gain[...] + shift[...]).astype(bf16)
    cos, low, high = rope_factors(pos, table)
    all_three = dot_nn(normed, w_wide[...])
    q = all_three[:, :WIDTH] + b[0:1, :]
    k = all_three[:, WIDTH : 2 * WIDTH] + b[1:2, :]
    v = all_three[:, 2 * WIDTH :] + b[2:3, :]
    q = (q * cos + turned(q, low, high)) * (1.0 / math.sqrt(HEAD_DIM))
    k = k * cos + turned(k, low, high)
    q_out[...] = q.astype(bf16)
    q_t = q.T.astype(bf16)
    k_t[...] = k.T.astype(bf16)
    v_t[...] = v.T.astype(bf16)
    row = lax.broadcasted_iota(jnp.int32, (HEAD_DIM, TILE), 0)
    clip = seg[...]
    same = (row >= 1) & (row < 4) & (clip == row - 1)
    mask = jnp.where((row >= 1) & (row < 4) & (clip != row - 1), NEG, 0.0)
    mask = jnp.where(row == 0, jnp.where(pad[...] != 0, NEG, 0.0), mask)
    k_extra = jnp.where((row >= 4) & (row < 7), 1.0, mask)
    q_extra = jnp.where(same | (row == 0), 1.0, 0.0).astype(bf16)
    k_side = jnp.concatenate([jnp.zeros((HEAD_DIM, TILE), f32), k_extra]).T
    lane = lax.broadcasted_iota(jnp.int32, (TILE, AUG), 1)
    ones = jnp.where((lane >= HEAD_DIM) & (lane < HEAD_DIM + 3), 1.0, 0.0)
    for h in range(HEADS):
        pair = slice(h // 2 * AUG, h // 2 * AUG + AUG)
        wide = slice(h * AUG, (h + 1) * AUG)
        k_pair, v_pair = k[:, pair], v[:, pair]
        if h % 2:
            k_pair, v_pair = pltpu.roll(k_pair, HEAD_DIM, 1), pltpu.roll(v_pair, HEAD_DIM, 1)
        k_aug[:, wide] = jnp.where(lane < HEAD_DIM, k_pair, k_side).astype(bf16)
        v_aug[:, wide] = jnp.where(lane < HEAD_DIM, v_pair, ones).astype(bf16)
        q_aug_t[h * AUG : h * AUG + HEAD_DIM, :] = q_t[h * HEAD_DIM : (h + 1) * HEAD_DIM, :]
        q_aug_t[h * AUG + HEAD_DIM : (h + 1) * AUG, :] = q_extra


def project(tokens, w, b, gain, shift, positions, segments, padding, table):
    length, width = tokens.shape
    tiles = length // TILE

    def rows(columns):
        return pl.BlockSpec((TILE, columns), lambda i: (i, 0))

    def columns(count):
        return pl.BlockSpec((count, TILE), lambda i: (0, i))

    out = jax.ShapeDtypeStruct
    wide = out((length, HEADS * AUG), bf16)
    flat = out((WIDTH, length), bf16)
    return pl.pallas_call(
        qkv_kernel,
        grid=(tiles,),
        in_specs=[
            rows(width), whole(w.shape), whole(b.shape), whole((1, width)), whole((1, width)),
            pl.BlockSpec((3, 1, TILE), lambda i: (0, 0, i)), columns(1), columns(1), whole(table.shape),
        ],
        out_specs=[
            rows(HEADS * AUG), rows(HEADS * AUG), columns(HEADS * AUG), rows(WIDTH), columns(WIDTH),
            columns(WIDTH),
        ],
        out_shape=[
            wide, wide, out((HEADS * AUG, length), bf16), out((length, WIDTH), bf16), flat, flat,
        ],
        scratch_shapes=[pltpu.VMEM((width, 3 * WIDTH), bf16)],
        compiler_params=params(LIMIT),
        cost_estimate=pl.CostEstimate(
            flops=6 * length * width * WIDTH, bytes_accessed=20 * MIB, transcendentals=0
        ),
        name="project",
    )(tokens, w, b, gain, shift, positions, segments, padding, table)


def attend_kernel(info, k_aug, v_t, q_aug_t, k_t, pad, o, o_t, lse, top, total, acc, *, part):
    tile = 2 * pl.program_id(0) + part
    padded = pad[...] != 0
    for h in range(HEADS):
        q_h = q_aug_t[h * AUG : h * AUG + HEAD_DIM, :].astype(f32)
        k_h = k_t[h * HEAD_DIM : (h + 1) * HEAD_DIM, :].astype(f32)
        own = jnp.sum(q_h * k_h, axis=0, keepdims=True)
        top[h : h + 1, :] = jnp.where(padded, own, -3e38)
        total[h : h + 1, :] = jnp.where(padded, 1.0, 0.0)
    here = pl.ds(pl.multiple_of(tile * TILE, TILE), TILE)
    acc[...] = jnp.where(padded, v_t[:, here].astype(f32), 0.0)
    feats = [slice(h * HEAD_DIM, (h + 1) * HEAD_DIM) for h in range(HEADS)]
    wides = [slice(h * AUG, (h + 1) * AUG) for h in range(HEADS)]

    def step(j, count):
        keys = pl.ds(pl.multiple_of(j * TILE, TILE), count * TILE)
        scores = [dot_nn(k_aug[keys, wide], q_aug_t[wide, :]) for wide in wides]
        probs, fades = [], []
        for h in range(HEADS):
            old = top[h : h + 1, :]
            new = jnp.maximum(old, jnp.max(scores[h], axis=0, keepdims=True))
            prob = jnp.exp(scores[h] - new)
            fade = jnp.exp(old - new)
            top[h : h + 1, :] = new
            total[h : h + 1, :] = total[h : h + 1, :] * fade + jnp.sum(prob, axis=0, keepdims=True)
            probs.append(prob.astype(bf16))
            fades.append(fade)
        for h, feat in enumerate(feats):
            acc[feat, :] = acc[feat, :] * fades[h] + dot_nn(v_t[feat, keys], probs[h])

    begin, end = clip_range(info, tile, k_aug.shape[0])
    pairs = (end - begin) // 2

    def two(n, _):
        step(begin + 2 * n, 2)
        return 0

    lax.fori_loop(0, pairs, two, 0)

    @pl.when(begin + 2 * pairs < end)
    def _():
        step(end - 1, 1)

    for h, feat in enumerate(feats):
        acc[feat, :] = acc[feat, :] / total[h : h + 1, :]
    lse[...] = jnp.zeros_like(lse)
    lse[0:HEADS, :] = top[0:HEADS, :] + jnp.log(total[0:HEADS, :])
    turned_o = acc[...]
    o_t[...] = turned_o.astype(bf16)
    o[...] = turned_o.T.astype(bf16)


def attend(part, info, k_aug, v_t, q_aug_t, k_t, padding, earlier):
    length = k_aug.shape[0]
    half = length // 2

    def columns(count):
        return pl.BlockSpec((count, TILE), lambda i, *_: (0, 2 * i + part))

    def packed(count):
        return pl.BlockSpec((count, TILE), lambda i, *_: (0, i))

    out = jax.ShapeDtypeStruct
    return pl.pallas_call(
        in_order(functools.partial(attend_kernel, part=part), 6, len(earlier)),
        grid_spec=pltpu.PrefetchScalarGridSpec(
            num_scalar_prefetch=1,
            grid=(half // TILE,),
            in_specs=[
                whole(k_aug.shape), whole(v_t.shape), columns(HEADS * AUG), columns(WIDTH),
                columns(1),
            ]
            + unread(earlier),
            out_specs=[
                pl.BlockSpec((TILE, WIDTH), lambda i, *_: (i, 0)), packed(WIDTH), packed(8),
            ],
            scratch_shapes=[
                pltpu.VMEM((8, TILE), f32), pltpu.VMEM((8, TILE), f32), pltpu.VMEM((WIDTH, TILE), f32),
            ],
        ),
        out_shape=[out((half, WIDTH), bf16), out((WIDTH, half), bf16), out((8, half), f32)],
        compiler_params=params(LIMIT),
        cost_estimate=pl.CostEstimate(
            flops=24 * half * length * WIDTH, bytes_accessed=6 * MIB, transcendentals=0
        ),
        name="attend",
    )(info, k_aug, v_t, q_aug_t, k_t, padding, *earlier)


def pair_kernel(first, second, out):
    out[0] = first[...]
    out[1] = second[...]


def paired(first, second, earlier):
    shape = (2,) + first.shape
    return pl.pallas_call(
        in_order(pair_kernel, 2, len(earlier)),
        in_specs=[pl.BlockSpec(memory_space=pltpu.VMEM)] * 2 + unread(earlier),
        out_specs=pl.BlockSpec(memory_space=pltpu.VMEM),
        out_shape=jax.ShapeDtypeStruct(shape, first.dtype),
        name="paired",
    )(first, second, *earlier)


def gelu_parts(u):
    size = jnp.abs(u)
    t = 1.0 / (1.0 + (0.3275911 / math.sqrt(2.0)) * size)
    bell = jnp.exp(-0.5 * (u * u))
    poly = 0.5 * 1.061405429
    for c in (-1.453152027, 1.421413741, -0.284496736, 0.254829592):
        poly = poly * t + 0.5 * c
    tail = poly * t * bell
    below = jnp.where(u >= 0, 1.0 - tail, tail)
    return u * below, below + u * bell * (1.0 / math.sqrt(2.0 * math.pi))


def mlp_kernel(
    info, tok, cot, o_a, o_b, w_all, b_out, gain, shift, w_up, b_up, w_down,
    x2, dy, h2, act, du, mlp_sent, mlp_kept, dh2_sent, dh2_kept, db_up, w_out, *, me_at,
):
    i = pl.program_id(0)

    @pl.when(i == 0)
    def _():
        for n, j in enumerate((0, 2, 1, 3)):
            w_out[n * WIDTH : (n + 1) * WIDTH, :] = w_all[jnp.bitwise_xor(info[me_at], j)]
        db_up[...] = jnp.zeros_like(db_up)

    heads = jnp.concatenate([o_a[0], o_a[1], o_b[0], o_b[1]], axis=1)
    mid = tok[...].astype(f32) + b_out[...] + dot_nn(heads, w_out[...])

    @pl.when(i == 2)
    def _():
        x2[...] = mid
        dy[...] = cot[...]

    grad_act = dot_nt(cot[...], w_down[...])
    hat, _ = normalized(mid)
    normed = (hat * gain[...] + shift[...]).astype(bf16)
    h2[...] = normed
    u = dot_nn(normed, w_up[...]) + b_up[...]
    value, slope = gelu_parts(u)
    value = value.astype(bf16)
    grad = (grad_act * slope).astype(bf16)
    act[...] = value
    du[...] = grad
    db_up[0:1, :] += jnp.sum(grad.astype(f32), axis=0, keepdims=True)
    mlp_part = dot_nn(value, w_down[...]).astype(bf16)
    dh2_part = dot_nt(grad, w_up[...]).astype(bf16)

    @pl.when(i < 2)
    def _():
        mlp_sent[0] = mlp_part
        dh2_sent[0] = dh2_part

    @pl.when(i >= 2)
    def _():
        mlp_kept[0] = mlp_part
        dh2_kept[0] = dh2_part


def mlp(
    part, info, me_at, tokens, cotangent, o_a, o_b, w_all, b_out, gain, shift, w_up, b_up, w_down,
    earlier,
):
    length, width = tokens.shape
    half = length // 2
    hidden = w_up.shape[1]
    owners = half // TILE

    def owner(i, info):
        return jnp.bitwise_xor(info[me_at], (2 * i + 1) % 5)

    def rows(columns):
        return pl.BlockSpec((TILE, columns), lambda i, info: (2 * owner(i, info) + part, 0))

    def packed(columns):
        return pl.BlockSpec((TILE, columns), lambda i, info: (owner(i, info), 0))

    sent = pl.BlockSpec((1, TILE, width), lambda i, info: (jnp.minimum(i, 1), 0, 0))
    kept = pl.BlockSpec((1, TILE, width), lambda i, info: (jnp.maximum(i - 2, 0), 0, 0))

    out = jax.ShapeDtypeStruct
    return pl.pallas_call(
        in_order(functools.partial(mlp_kernel, me_at=me_at), 12, len(earlier)),
        grid_spec=pltpu.PrefetchScalarGridSpec(
            num_scalar_prefetch=1,
            grid=(owners,),
            in_specs=[rows(width), rows(width)]
            + [pl.BlockSpec((2, TILE, WIDTH), lambda i, info: (0, owner(i, info), 0))] * 2
            + [whole(w_all.shape)]
            + [whole((1, width))] * 3
            + [whole(w_up.shape), whole((1, hidden)), whole(w_down.shape)]
            + unread(earlier),
            out_specs=[
                whole((TILE, width)), whole((TILE, width)), packed(width), packed(hidden),
                packed(hidden), sent, kept, sent, kept, whole((8, hidden)),
            ],
            scratch_shapes=[pltpu.VMEM((4 * WIDTH, width), bf16)],
        ),
        out_shape=[
            out((TILE, width), f32), out((TILE, width), bf16), out((half, width), bf16),
            out((half, hidden), bf16), out((half, hidden), bf16),
        ]
        + [out((owners // 2, TILE, width), bf16)] * 4
        + [out((8, hidden), f32)],
        compiler_params=params(LIMIT),
        cost_estimate=pl.CostEstimate(
            flops=20 * half * width * hidden, bytes_accessed=20 * MIB, transcendentals=0
        ),
        name="mlp",
    )(
        info, tokens, cotangent, o_a, o_b, w_all, b_out, gain, shift, w_up, b_up, w_down, *earlier
    )


def up_weights_kernel(left_a, left_b, right_a, right_b, out):
    left = jnp.concatenate([left_a[...], left_b[...]])
    right = jnp.concatenate([right_a[...], right_b[...]])
    out[...] = dot_tn(left, right).astype(bf16)


def up_weights(h2, du, filled, earlier):
    half, width = h2[0].shape
    hidden = du[0].shape[1]
    return pl.pallas_call(
        in_order(up_weights_kernel, 4, 1 + len(earlier)),
        grid=(width // TILE,),
        in_specs=[pl.BlockSpec((half, TILE), lambda i: (0, i))] * 2
        + [whole((half, hidden))] * 2
        + unread((filled,) + earlier),
        out_specs=pl.BlockSpec((TILE, hidden), lambda i: (i, 0)),
        out_shape=jax.ShapeDtypeStruct(filled.shape, bf16),
        input_output_aliases={4: 0},
        compiler_params=params(LIMIT),
        cost_estimate=pl.CostEstimate(
            flops=8 * half * width * hidden, bytes_accessed=12 * MIB, transcendentals=0
        ),
        name="up_weights",
    )(*h2, *du, filled, *earlier)


def down_weights_kernel(act_a, act_b, cot, out):
    owners = cot.shape[0] // (2 * TILE)
    rows = [cot[n * TILE : (n + 1) * TILE, :] for p in range(2) for n in range(p, 2 * owners, 2)]
    out[...] = dot_tn(
        jnp.concatenate([act_a[...], act_b[...]]), jnp.concatenate(rows)
    ).astype(bf16)


def down_weights(act, cotangent, earlier):
    half, hidden = act[0].shape
    length, width = cotangent.shape
    return pl.pallas_call(
        in_order(down_weights_kernel, 3, len(earlier)),
        grid=(hidden // TILE,),
        in_specs=[pl.BlockSpec((half, TILE), lambda i: (0, i))] * 2
        + [whole((length, width))]
        + unread(earlier),
        out_specs=pl.BlockSpec((TILE, width), lambda i: (i + width // TILE, 0)),
        out_shape=jax.ShapeDtypeStruct((width + hidden, width), bf16),
        compiler_params=params(LIMIT),
        cost_estimate=pl.CostEstimate(
            flops=8 * half * width * hidden, bytes_accessed=12 * MIB, transcendentals=0
        ),
        name="down_weights",
    )(*act, cotangent, *earlier)


def middle_kernel(
    info, kept, other, there, x2, cot, gain, w_all, dx2, g, d_0, d_1, d_2, d_3, small, *, me_at
):
    grad = kept[0].astype(f32) + other[0].astype(f32) + there[...].astype(f32)
    hat, inverse = normalized(x2[...])
    dy = cot[...].astype(f32)
    full = dy + norm_back(hat, inverse, gain[...], grad)
    dx2[...] = full
    low = full.astype(bf16)
    g[...] = low
    small[...] = jnp.zeros_like(small)
    small[0:1, :] = jnp.sum(grad * hat, axis=0, keepdims=True)
    small[1:2, :] = jnp.sum(grad, axis=0, keepdims=True)
    small[2:3, :] = jnp.sum(low.astype(f32), axis=0, keepdims=True)
    small[3:4, :] = jnp.sum(dy, axis=0, keepdims=True)
    for j, d_j in enumerate((d_0, d_1, d_2, d_3)):
        d_j[...] = dot_nt(low, w_all[jnp.bitwise_xor(info[me_at], j)]).astype(bf16)


def middle(info, me_at, kept, other, there, x2, dy, gain, w_all, earlier):
    width = x2.shape[1]
    out = jax.ShapeDtypeStruct
    own = whole((TILE, width))
    return pl.pallas_call(
        in_order(functools.partial(middle_kernel, me_at=me_at), 8, len(earlier)),
        grid_spec=pltpu.PrefetchScalarGridSpec(
            num_scalar_prefetch=1,
            grid=(1,),
            in_specs=[
                whole((1, TILE, width)), whole((1, TILE, width)), own, own, own,
                whole((1, width)), whole(w_all.shape),
            ]
            + unread(earlier),
            out_specs=[own, own] + [whole((TILE, WIDTH))] * 4 + [whole((8, width))],
        ),
        out_shape=[pltpu.HBM((TILE, width), f32), pltpu.HBM((TILE, width), bf16)]
        + [pltpu.HBM((TILE, WIDTH), bf16)] * 4
        + [out((8, width), f32)],
        compiler_params=params(40),
        cost_estimate=pl.CostEstimate(
            flops=2 * TILE * width * width, bytes_accessed=8 * MIB, transcendentals=0
        ),
        name="middle",
    )(info, kept, other, there, x2, dy, gain, w_all, *earlier)


def out_weights_kernel(info, oa_a, oa_b, ob_a, ob_b, g_a, g_b, sent, kept):
    for n in range(2):
        kept[n] = (dot_tn(oa_a[n], g_a[...]) + dot_tn(ob_a[n], g_b[...])).astype(bf16)
        sent[n] = (dot_tn(oa_b[n], g_a[...]) + dot_tn(ob_b[n], g_b[...])).astype(bf16)


def out_weights(info, me_at, pairs_a, pairs_b, g_a, g_b):
    width = g_a.shape[1]
    own = pl.BlockSpec((2, TILE, WIDTH), lambda i, info: (0, info[me_at], 0))
    return pl.pallas_call(
        out_weights_kernel,
        grid_spec=pltpu.PrefetchScalarGridSpec(
            num_scalar_prefetch=1,
            grid=(1,),
            in_specs=[own] * 4 + [whole((TILE, width))] * 2,
            out_specs=[whole((2, WIDTH, width))] * 2,
        ),
        out_shape=[jax.ShapeDtypeStruct((2, WIDTH, width), bf16)] * 2,
        compiler_params=params(LIMIT),
        cost_estimate=pl.CostEstimate(
            flops=4 * TILE * width * width, bytes_accessed=6 * MIB, transcendentals=0
        ),
        name="out_weights",
    )(info, *pairs_a, *pairs_b, g_a, g_b)


def attend_back_kernel(
    info, k_aug, v_aug, k_t, q_aug_t, q, v_t, o_t, lse, pad, do_0, do_1, do_2, do_3, pos, table,
    *refs, part, me_at, first,
):
    if first:
        dk_in = dv_in = None
    else:
        dk_in, dv_in, *refs = refs
    dq_out, dk, dv, q_side, do_side, q_lanes, do_lanes, dq_t = refs
    i = pl.program_id(0)
    tile = 2 * jnp.bitwise_xor(info[me_at], i) + part

    @pl.when(i == 0)
    def _():
        if first:
            dk[...] = jnp.zeros_like(dk)
            dv[...] = jnp.zeros_like(dv)
        else:
            dk[...] = dk_in[...]
            dv[...] = dv_in[...]

    here = pl.ds(pl.multiple_of(tile * TILE, TILE), TILE)
    do_here = jnp.where(
        i == 0, do_0[...], jnp.where(i == 1, do_1[...], jnp.where(i == 2, do_2[...], do_3[...]))
    )
    q_here = q[...]
    do_t = do_here.astype(f32).T
    k_here = k_t[:, here].astype(f32)
    padded = jnp.where(pad[...] != 0, 1.0, 0.0)
    row = lax.broadcasted_iota(jnp.int32, (AUG - HEAD_DIM, TILE), 0)
    lane = lax.broadcasted_iota(jnp.int32, (TILE, WIDTH), 1) // HEAD_DIM
    dk_parts, dv_parts = [], []
    for h in range(HEADS):
        feat = slice(h * HEAD_DIM, (h + 1) * HEAD_DIM)
        at = h * AUG
        q_h = q_aug_t[at : at + HEAD_DIM, :]
        do_h = do_t[feat, :]
        delta = jnp.sum(do_h * o_t[feat, :].astype(f32), axis=0, keepdims=True)
        lse_h = lse[h : h + 1, :]
        one, two, three = three_parts(-lse_h)
        extra = q_aug_t[at + HEAD_DIM : at + AUG, :].astype(f32)
        extra = jnp.where(row == 4, one, jnp.where(row == 5, two, jnp.where(row == 6, three, extra)))
        q_side[at : at + HEAD_DIM, :] = q_h
        q_side[at + HEAD_DIM : at + AUG, :] = extra.astype(bf16)
        one, two, three = three_parts(-delta)
        extra = jnp.where(row == 0, one, jnp.where(row == 1, two, jnp.where(row == 2, three, 0.0)))
        do_side[at : at + HEAD_DIM, :] = do_h.astype(bf16)
        do_side[at + HEAD_DIM : at + AUG, :] = extra.astype(bf16)
        q_lanes[h] = jnp.where(lane == h, q_here, jnp.zeros_like(q_here))
        do_lanes[h] = jnp.where(lane == h, do_here, jnp.zeros_like(do_here))
        q_h = q_h.astype(f32)
        k_h = k_here[feat, :]
        p_own = padded * jnp.exp(jnp.sum(q_h * k_h, axis=0, keepdims=True) - lse_h)
        dp_own = jnp.sum(do_h * v_t[feat, :].astype(f32), axis=0, keepdims=True)
        ds_own = p_own * (dp_own - delta)
        dq_t[feat, :] = ds_own * k_h
        dk_parts.append(ds_own * q_h)
        dv_parts.append(p_own * do_h)
    dk[here, :] += jnp.concatenate(dk_parts, axis=0).T
    dv[here, :] += jnp.concatenate(dv_parts, axis=0).T

    def step(j, _):
        keys = pl.ds(pl.multiple_of(j * TILE, TILE), TILE)
        probs, grads = [], []
        for h in range(HEADS):
            wide = slice(h * AUG, (h + 1) * AUG)
            prob = jnp.exp(dot_nn(k_aug[keys, wide], q_side[wide, :]))
            grad = prob * dot_nn(v_aug[keys, wide], do_side[wide, :])
            probs.append(prob.astype(bf16))
            grads.append(grad.astype(bf16))
        deep = (HEADS * TILE, WIDTH)
        dv[keys, :] += dot_nn(jnp.concatenate(probs, axis=1), do_lanes[...].reshape(deep))
        dk[keys, :] += dot_nn(jnp.concatenate(grads, axis=1), q_lanes[...].reshape(deep))
        for h in range(HEADS):
            feat = slice(h * HEAD_DIM, (h + 1) * HEAD_DIM)
            dq_t[feat, :] += dot_nn(k_t[feat, keys], grads[h])
        return 0

    begin, end = clip_range(info, tile, k_aug.shape[0])
    lax.fori_loop(begin, end, step, 0)
    dq = dq_t[...].T * (1.0 / math.sqrt(HEAD_DIM))
    cos, low, high = rope_factors(pos, table)
    dq_out[...] = (dq * cos - turned(dq, low, high)).astype(bf16)


def attend_back(
    part, info, me_at, k_aug, v_aug, k_t, q_aug_t, q, v_t, o_t, lse, padding, do, positions, table,
    dk, dv, earlier,
):
    length = k_aug.shape[0]
    half = length // 2

    def owner(i, info):
        return jnp.bitwise_xor(info[me_at], i)

    def rows(columns):
        return pl.BlockSpec((TILE, columns), lambda i, info: (2 * owner(i, info) + part, 0))

    def columns(count):
        return pl.BlockSpec((count, TILE), lambda i, info: (0, 2 * owner(i, info) + part))

    def packed(count):
        return pl.BlockSpec((count, TILE), lambda i, info: (0, owner(i, info)))

    out = jax.ShapeDtypeStruct
    before = () if dk is None else (dk, dv)
    return pl.pallas_call(
        in_order(
            functools.partial(attend_back_kernel, part=part, me_at=me_at, first=dk is None),
            16 + len(before), len(earlier),
        ),
        grid_spec=pltpu.PrefetchScalarGridSpec(
            num_scalar_prefetch=1,
            grid=(half // TILE,),
            in_specs=[
                whole(k_aug.shape), whole(v_aug.shape), whole(k_t.shape), columns(HEADS * AUG),
                rows(WIDTH), columns(WIDTH), packed(WIDTH), packed(8), columns(1),
            ]
            + [whole((TILE, WIDTH))] * 4
            + [
                pl.BlockSpec(
                    (3, 1, TILE), lambda i, info: (0, 0, 2 * owner(i, info) + part)
                ),
                whole(table.shape),
            ]
            + [whole((length, WIDTH))] * len(before)
            + unread(earlier),
            out_specs=[
                pl.BlockSpec((TILE, WIDTH), lambda i, info: (owner(i, info), 0)),
                whole((length, WIDTH)), whole((length, WIDTH)),
            ],
            scratch_shapes=[
                pltpu.VMEM((HEADS * AUG, TILE), bf16), pltpu.VMEM((HEADS * AUG, TILE), bf16),
                pltpu.VMEM((HEADS, TILE, WIDTH), bf16), pltpu.VMEM((HEADS, TILE, WIDTH), bf16),
                pltpu.VMEM((WIDTH, TILE), f32),
            ],
        ),
        out_shape=[out((half, WIDTH), bf16), out((length, WIDTH), f32), out((length, WIDTH), f32)],
        compiler_params=params(LIMIT),
        cost_estimate=pl.CostEstimate(
            flops=72 * half * length * WIDTH, bytes_accessed=16 * MIB, transcendentals=0
        ),
        name="attend_back",
    )(
        info, k_aug, v_aug, k_t, q_aug_t, q, v_t, o_t, lse, padding, *do, positions, table, *before,
        *earlier,
    )


def pieces(begin, count, period):
    at, end, cuts = begin, begin + count, []
    while at < end:
        length = min(end - at, period - at % period)
        cuts.append((at, length))
        at += length
    return cuts


def stacked_pairs(rows, count):
    row = lax.broadcasted_iota(jnp.int32, (count, WIDTH), 0)
    out = jnp.zeros((count, WIDTH), f32)
    for m, value in enumerate(rows):
        one, two, _ = three_parts(value)
        out = jnp.where(row == 2 * m, one, jnp.where(row == 2 * m + 1, two, out))
    return out.astype(bf16)


def late_extra(width, blocks):
    vectors = -(-(3 + 7 * width // WIDTH) // blocks)
    return vectors, -(-vectors // 8) * 16


def project_back_kernel(
    info, tok, gain, shift, dq_a, dq_b, dk, dv, pos, table, w, out_kept, out_there, early,
    sent, kept, sums, acc, grad_b, small, w_wide,
):
    i = pl.program_id(0)

    @pl.when(i == 0)
    def _():
        acc[...] = jnp.zeros_like(acc)
        grad_b[...] = jnp.zeros_like(grad_b)
        small[...] = jnp.zeros_like(small)
        for c in range(3):
            w_wide[:, c * WIDTH : (c + 1) * WIDTH] = w[c]

    dk_here = dk[...]
    cos, low, high = rope_factors(pos, table)
    dk_low = (dk_here * cos - turned(dk_here, low, high)).astype(bf16)
    dq = jnp.concatenate([dq_a[...], dq_b[...]])
    parts = jnp.concatenate([dq, dk_low, dv[...].astype(bf16)], axis=1)
    grad = dot_nt(parts, w_wide[...])
    hat, _ = normalized(tok[...].astype(f32))
    normed = (hat * gain[...] + shift[...]).astype(bf16)
    acc[...] += dot_tn(normed, parts)
    grad_b[0:1, :] += jnp.sum(parts.astype(f32), axis=0, keepdims=True)
    small[0:1, :] += jnp.sum(grad * hat, axis=0, keepdims=True)
    small[1:2, :] += jnp.sum(grad, axis=0, keepdims=True)
    grad = grad.astype(bf16)

    @pl.when(i < 2)
    def _():
        sent[0] = grad

    @pl.when(i >= 2)
    def _():
        kept[0] = grad

    @pl.when(i == pl.num_programs(0) - 1)
    def _():
        width = normed.shape[1]
        blocks = sums.shape[0]

        def cut(value, count):
            return [value[:, r * WIDTH : (r + 1) * WIDTH] for r in range(count)]

        rows = cut(grad_b[0:1, :], 3) + cut(early[4:5, :], width // WIDTH)
        for ref, count in ((small, 2), (early, 4)):
            for v in range(count):
                rows += cut(ref[v : v + 1, :], width // WIDTH)
        for n in range(blocks):
            for to, rows_here, c, begin in late_places(n, blocks, width):
                here = (slice(begin, begin + rows_here), slice(c * WIDTH, (c + 1) * WIDTH))
                sums[n, to : to + rows_here, :] = acc[here].astype(bf16)
            for to, rows_here, c, begin in late_places(n, blocks, width, True):
                here = (slice(begin, begin + rows_here), slice(c * WIDTH, (c + 1) * WIDTH))
                sums[n, to : to + rows_here, :] = (
                    out_kept[here].astype(f32) + out_there[here].astype(f32)
                ).astype(bf16)
            extra_at = 4 * width // blocks
            sums[n, extra_at:, :] = stacked_pairs(rows[n::blocks], sums.shape[1] - extra_at)


def late_places(n, blocks, width, out=False):
    deep, period = (width // blocks, WIDTH) if out else (3 * width // blocks, width)
    first = 3 * width // blocks if out else 0
    return [
        (first + at - n * deep, length, at // period, at % period)
        for at, length in pieces(n * deep, deep, period)
    ]


def project_back(
    info, me_at, tokens, gain, shift, dq_a, dq_b, dk, dv, positions, table, w, kept, there, early,
    blocks,
):
    length, width = tokens.shape
    share = 2 * TILE

    def owner(i, info):
        return jnp.bitwise_xor(info[me_at], (2 * i + 1) % 5)

    def rows(count, columns):
        return pl.BlockSpec((count, columns), lambda i, info: (owner(i, info), 0))

    last = pl.BlockSpec((TILE, width), lambda i, info: (2, 0))
    out = jax.ShapeDtypeStruct
    sums = (blocks, 4 * width // blocks + late_extra(width, blocks)[1], WIDTH)
    return pl.pallas_call(
        project_back_kernel,
        grid_spec=pltpu.PrefetchScalarGridSpec(
            num_scalar_prefetch=1,
            grid=(length // share,),
            in_specs=[
                rows(share, width), whole((1, width)), whole((1, width)), rows(TILE, WIDTH),
                rows(TILE, WIDTH), rows(share, WIDTH), rows(share, WIDTH),
                pl.BlockSpec((3, 1, share), lambda i, info: (0, 0, owner(i, info))),
                whole(table.shape), whole(w.shape), last, last, whole(early.shape),
            ],
            out_specs=[
                pl.BlockSpec((1, share, width), lambda i, info: (jnp.minimum(i, 1), 0, 0)),
                pl.BlockSpec((1, share, width), lambda i, info: (jnp.maximum(i - 2, 0), 0, 0)),
                whole(sums),
            ],
            scratch_shapes=[
                pltpu.VMEM((width, 3 * WIDTH), f32), pltpu.VMEM((8, 3 * WIDTH), f32),
                pltpu.VMEM((8, width), f32),
                pltpu.VMEM((width, 3 * WIDTH), bf16),
            ],
        ),
        out_shape=[out((2, share, width), bf16)] * 2 + [out(sums, bf16)],
        compiler_params=params(LIMIT),
        cost_estimate=pl.CostEstimate(
            flops=24 * length * width * WIDTH, bytes_accessed=20 * MIB, transcendentals=0
        ),
        name="project_back",
    )(info, tokens, gain, shift, dq_a, dq_b, dk, dv, positions, table, w, kept, there, early)


def unpack_kernel(sums, grad_qkv, grad_out, grad_b, vectors):
    blocks = sums.shape[0]
    width = grad_out.shape[1]
    grad_b[...] = jnp.zeros_like(grad_b)
    extra_at = 4 * width // blocks
    for n in range(blocks):
        for to, rows, c, begin in late_places(n, blocks, width):
            grad_qkv[c, begin : begin + rows, :] = sums[n, to : to + rows, :].astype(f32)
        for to, rows, c, begin in late_places(n, blocks, width, True):
            grad_out[begin : begin + rows, c * WIDTH : (c + 1) * WIDTH] = sums[
                n, to : to + rows, :
            ].astype(f32)
    vectors[...] = jnp.zeros_like(vectors)
    for v in range(3 + 7 * width // WIDTH):
        n, m = v % blocks, v // blocks
        pair = sums[n, extra_at:, :].astype(f32)
        row = pair[2 * m : 2 * m + 1, :] + pair[2 * m + 1 : 2 * m + 2, :]
        if v < 3:
            grad_b[v : v + 1, :] = row
        else:
            to, at = divmod((v - 3) * WIDTH, width)
            vectors[to : to + 1, at : at + WIDTH] = row


def unpack(sums, width):
    out = jax.ShapeDtypeStruct
    return pl.pallas_call(
        unpack_kernel,
        in_specs=[pl.BlockSpec(memory_space=pltpu.VMEM)],
        out_specs=[pl.BlockSpec(memory_space=pltpu.VMEM)] * 4,
        out_shape=[
            out((3, width, WIDTH), f32), out((WIDTH, width), f32), out((8, WIDTH), f32),
            out((8, width), f32),
        ],
        compiler_params=pltpu.CompilerParams(vmem_limit_bytes=LIMIT * MIB),
        name="unpack",
    )(sums)


def finish_kernel(info, kept, other, there, tok, gain, dx2_a, dx2_b, out):
    grad = kept[0].astype(f32) + other[0].astype(f32) + there[...].astype(f32)
    hat, inverse = normalized(tok[...].astype(f32))
    dx2 = jnp.where(pl.program_id(0) == 0, dx2_a[...], dx2_b[...])
    out[...] = dx2 + norm_back(hat, inverse, gain[...], grad)


def finish(info, me_at, kept, other, there, tokens, gain, dx2_a, dx2_b):
    width = tokens.shape[1]
    share = there.shape[0]
    rows = pl.BlockSpec((TILE, width), lambda i, info: (i, 0))
    first = pl.BlockSpec((1, TILE, width), lambda i, info: (0, i, 0))
    return pl.pallas_call(
        finish_kernel,
        grid_spec=pltpu.PrefetchScalarGridSpec(
            num_scalar_prefetch=1,
            grid=(share // TILE,),
            in_specs=[
                first, first, rows,
                pl.BlockSpec((TILE, width), lambda i, info: (2 * info[me_at] + i, 0)),
                whole((1, width)), whole((TILE, width)), whole((TILE, width)),
            ],
            out_specs=rows,
        ),
        out_shape=jax.ShapeDtypeStruct((share, width), f32),
        compiler_params=params(LIMIT),
        cost_estimate=pl.CostEstimate(
            flops=30 * share * width, bytes_accessed=10 * MIB, transcendentals=0
        ),
        name="finish",
    )(info, kept, other, there, tokens, gain, dx2_a, dx2_b)


def sum_kernel(blocks, out):
    total = blocks[0].astype(f32)
    for n in range(1, blocks.shape[0]):
        total += blocks[n].astype(f32)
    total = total.astype(bf16)
    if len(out.shape) == 2:
        out[...] = total
    else:
        for n in range(blocks.shape[0]):
            out[n] = total


def summed(blocks, copies, steps, earlier):
    count, rows, width = blocks.shape
    tile = rows // steps
    every = pl.BlockSpec((count, tile, width), lambda i: (0, i, 0))
    out = jax.ShapeDtypeStruct
    return pl.pallas_call(
        in_order(sum_kernel, 1, len(earlier)),
        grid=(steps,),
        in_specs=[every] + unread(earlier),
        out_specs=every if copies else pl.BlockSpec((tile, width), lambda i: (i, 0)),
        out_shape=out(blocks.shape if copies else (rows, width), bf16),
        compiler_params=params(LIMIT),
        cost_estimate=pl.CostEstimate(
            flops=count * rows * width, bytes_accessed=4 * count * rows * width, transcendentals=0
        ),
        name="summed",
    )(blocks, *earlier)


def swap(array, axis, bit=1):
    size = lax.axis_size(axis)
    if size == 1:
        return jnp.zeros_like(array)
    return lax.ppermute(array, axis, [(i, i ^ bit) for i in range(size)])


def swap_both(array):
    return lax.ppermute(array, MP, [(i, i ^ 3) for i in range(4)])


def scattered(rows, axes):
    group = lax.axis_size(axes)
    length, width = rows.shape
    return lax.all_to_all(
        rows.reshape(group, length // group, width), axes, 0, 0, tiled=True
    )


def both_sums(total):
    if lax.axis_size("zl") == 1:
        return total
    return (total.astype(f32) + swap(total, "zl").astype(f32)).astype(bf16)


def local(
    tokens, cotangent, segments, padding, positions, ln1_gain, ln1_bias, w_qkv, b_qkv, w_out, b_out,
    ln2_gain, ln2_bias, w_up, b_up, w_down, b_down,
):
    width, hidden = w_up.shape
    w_all = lax.all_gather(w_out, MP)
    gain_one, shift_one = ln1_gain[None], ln1_bias[None]
    gain_two, shift_two = ln2_gain[None], ln2_bias[None]
    ends = jnp.sum((segments <= jnp.arange(2)[:, None]).astype(jnp.int32), axis=1)
    info = jnp.concatenate([ends, lax.axis_index(MP)[None].astype(jnp.int32)])
    me_at = 2
    table = jnp.asarray(rope_constants())
    k_aug, v_aug, q_aug_t, q, k_t, v_t = project(
        tokens, w_qkv, b_qkv, gain_one, shift_one, positions, segments, padding, table
    )

    def exchanged(own, to_c, to_zh, to_both):
        return own, swap(to_c, "c"), swap(to_zh, "zh"), swap_both(to_both)

    o_0, o_t_0, lse_0 = attend(0, info, k_aug, v_t, q_aug_t, k_t, padding, ())
    o_zh_0 = swap(o_0, "zh")
    o_1, o_t_1, lse_1 = attend(1, info, k_aug, v_t, q_aug_t, k_t, padding, (o_0, w_all))
    o_zh_1 = swap(o_1, "zh")
    pair_0 = paired(o_0, o_zh_0, (o_1,))
    pairs_0 = (pair_0, swap(pair_0, "c"))

    def mlp_half(part, pairs, earlier):
        return mlp(
            part, info, me_at, tokens, cotangent, *pairs, w_all, b_out[None], gain_two, shift_two,
            w_up, b_up[None], w_down, earlier,
        )

    def met(sent, kept):
        other = swap(sent, "c")
        return other, (kept[1].astype(f32) + other[1].astype(f32)).astype(bf16)

    x2_0, dy_0, h2_0, act_0, du_0, mlp_sent_0, mlp_kept_0, sent_0, kept_0, db_0 = mlp_half(
        0, pairs_0, (o_1,)
    )
    pair_1 = paired(o_1, o_zh_1, (x2_0,))
    pairs_1 = (pair_1, swap(pair_1, "c"))
    other_0, give_0 = met(sent_0, kept_0)
    there_0 = swap(give_0, "zh")
    x2_1, dy_1, h2_1, act_1, du_1, mlp_sent_1, mlp_kept_1, sent_1, kept_1, db_1 = mlp_half(
        1, pairs_1, (give_0,)
    )
    other_1, give_1 = met(sent_1, kept_1)
    there_1 = swap(give_1, "zh")
    grad_mlp = down_weights((act_0, act_1), cotangent, ())
    dx2_0, g_0, *d_0, small_0 = middle(
        info, me_at, kept_0, other_0, there_0, x2_0, dy_0, gain_two, w_all, (grad_mlp, give_1)
    )
    do_0 = exchanged(*d_0)
    grad_mlp = up_weights((h2_0, h2_1), (du_0, du_1), grad_mlp, (g_0,))
    dx2_1, g_1, *d_1, small_1 = middle(
        info, me_at, kept_1, other_1, there_1, x2_1, dy_1, gain_two, w_all, (grad_mlp,)
    )
    do_1 = exchanged(*d_1)
    out_sent, out_kept = out_weights(info, me_at, pairs_0, pairs_1, g_0, g_1)

    others = [swap(sent, "c") for sent in (mlp_sent_0, mlp_sent_1, out_sent)]
    arrived = scattered(grad_mlp, ("y", "x"))
    dq_0, dk, dv = attend_back(
        0, info, me_at, k_aug, v_aug, k_t, q_aug_t, q, v_t, o_t_0, lse_0, padding, do_0, positions,
        table, None, None, (out_sent, g_1),
    )

    keep, give = (
        jnp.concatenate(
            [
                (kept[n].astype(f32) + other[n].astype(f32)).astype(bf16)
                for kept, other in zip((mlp_kept_0, mlp_kept_1, out_kept), others)
            ]
        )
        for n in range(2)
    )
    there = swap(give, "zh")
    part_sum = both_sums(summed(arrived, False, 2, (give, dq_0)))
    dq_1, dk, dv = attend_back(
        1, info, me_at, k_aug, v_aug, k_t, q_aug_t, q, v_t, o_t_1, lse_1, padding, do_1, positions,
        table, dk, dv, (give, part_sum, dq_0),
    )
    grad_mlp = lax.all_gather(part_sum, ("y", "x"), axis=0, tiled=True)
    early = jnp.concatenate([(small_0 + small_1)[0:4], (db_0 + db_1)[0:4]])
    dh1_sent, dh1_kept, sums = project_back(
        info, me_at, tokens, gain_one, shift_one, dq_0, dq_1, dk, dv, positions, table, w_qkv, keep,
        there, early, lax.axis_size(DP),
    )
    other, give = met(dh1_sent, dh1_kept)
    arrived = scattered(sums.reshape(-1, WIDTH), DP)
    late = lax.all_to_all(summed(arrived, True, 1, (give,)), DP, 0, 0, tiled=True)
    grad_qkv, grad_w_out, grad_b, vectors = unpack(late, width)
    grad_inputs = finish(
        info, me_at, dh1_kept, other, swap(give, "zh"), tokens, gain_one, dx2_0, dx2_1
    )
    by_c, by_zh, by_both = swap(vectors, "c"), swap(vectors, "zh"), swap_both(vectors)
    group = (vectors + by_c) + (by_zh + by_both)
    received = keep[: 2 * TILE].astype(f32) + there[: 2 * TILE].astype(f32)
    mixed = (jnp.concatenate([x2_0, x2_1]) + received + b_down[None]).astype(bf16)
    grad_mlp = grad_mlp.reshape(2, width, hidden).astype(f32)
    return (
        mixed, grad_inputs, group[1], group[2], grad_qkv, grad_b[0:3], grad_w_out, group[5],
        group[3], group[4], grad_mlp[0], vectors[0], grad_mlp[1], group[6],
    )


def solution(mesh):
    packs = mesh.shape["dp"]
    if packs == 32:
        shape = (2, 4, 4, 2, 2)
    else:
        shape = (1, packs, 1, 2, 2)
    split = Mesh(mesh.devices.reshape(shape), EVERY)
    in_specs = (
        P(DP, None), P(DP, None), P(DP, None), P(DP, None), P(None, DP, None), P(), P(),
        P(None, None, MP), P(None, MP), P(MP, None), P(), P(), P(), P(None, MP), P(MP),
        P(MP, None), P(),
    )
    out_specs = (
        P(EVERY, None), P(EVERY, None), P(), P(), P(None, None, MP), P(None, MP), P(MP, None), P(),
        P(), P(), P(None, MP), P(MP), P(MP, None), P(),
    )
    return jax.shard_map(local, mesh=split, in_specs=in_specs, out_specs=out_specs, check_vma=False)
```

```python
import functools
import math

import jax
import jax.numpy as jnp
import ml_dtypes
import numpy as np
from jax import lax
from jax.experimental import pallas as pl
from jax.experimental.pallas import tpu as pltpu
from jax.sharding import Mesh
from jax.sharding import PartitionSpec as P

HEAD_DIM = 64
HEADS = 4
WIDTH = HEADS * HEAD_DIM
AUG = 128
TILE = 256
PLACES = 64
LIMIT = 60
MIB = 1 << 20
DP = ("zl", "y", "x")
MP = ("zh", "c")
EVERY = ("zl", "y", "x", "zh", "c")

epsilon = 1e-06
NEG = -1e30
bf16 = jnp.bfloat16
f32 = jnp.float32


def dot_nn(a, b):
    return lax.dot_general(a, b, (((1,), (0,)), ((), ())), preferred_element_type=f32)


def dot_nt(a, b):
    return lax.dot_general(a, b, (((1,), (1,)), ((), ())), preferred_element_type=f32)


def dot_tn(a, b):
    return lax.dot_general(a, b, (((0,), (0,)), ((), ())), preferred_element_type=f32)


def normalized(values):
    center = jnp.mean(values, axis=-1, keepdims=True)
    shifted = values - center
    spread = jnp.mean(shifted * shifted, axis=-1, keepdims=True)
    inverse = lax.rsqrt(spread + epsilon)
    return shifted * inverse, inverse


def norm_back(hat, inverse, gain, grad):
    scaled = grad * gain
    return inverse * (
        scaled
        - jnp.mean(scaled, axis=-1, keepdims=True)
        - hat * jnp.mean(scaled * hat, axis=-1, keepdims=True)
    )


def turned(x, low, high):
    width = x.shape[1]
    pair = HEAD_DIM // 6
    return pltpu.roll(x, width - pair, 1) * low + pltpu.roll(x, pair, 1) * high


def three_parts(x):
    first = x.astype(bf16).astype(f32)
    rest = x - first
    second = rest.astype(bf16).astype(f32)
    return first, second, rest - second


def params(limit, axes=1):
    return pltpu.CompilerParams(
        dimension_semantics=("arbitrary",) * axes, vmem_limit_bytes=limit * MIB
    )


def in_order(kernel, inputs, earlier):
    def run(*refs):
        kernel(*refs[:inputs], *refs[inputs + earlier :])

    return run


def unread(arrays):
    return [pl.BlockSpec(memory_space=pl.ANY)] * len(arrays)


def whole(shape):
    return pl.BlockSpec(shape, lambda *_: (0,) * len(shape))


def clip_range(info, tile, length):
    first, second = info[0], info[1]
    at = tile * TILE
    begin = jnp.where(second <= at, second, jnp.where(first <= at, first, 0))
    end = jnp.where(
        first >= at + TILE, first, jnp.where(second >= at + TILE, second, length)
    )
    return begin // TILE, (end + TILE - 1) // TILE


def rope_constants():
    pair = HEAD_DIM // 6
    feature = np.arange(WIDTH) % HEAD_DIM
    section, place = feature // (2 * pair), feature % (2 * pair)
    frequency = np.exp(-math.log(10000.0) * (place % pair) / pair)
    table = np.zeros((PLACES, 3, WIDTH))
    for s in range(3):
        for value in range(16):
            angle = value * frequency
            turns = section == s
            table[s * 16 + value, 0] = np.where(turns, np.cos(angle), 0.0)
            table[s * 16 + value, 1] = np.where(turns & (place < pair), -np.sin(angle), 0.0)
            table[s * 16 + value, 2] = np.where(turns & (place >= pair), np.sin(angle), 0.0)
    table[48, 0] = section == 3
    rest = table.reshape(PLACES, 3 * WIDTH).astype(np.float32)
    parts = []
    for _ in range(3):
        part = rest.astype(ml_dtypes.bfloat16)
        parts.append(part)
        rest = rest - part.astype(np.float32)
    return np.concatenate(parts)


def rope_factors(positions, table):
    row = lax.broadcasted_iota(jnp.int32, (PLACES, positions.shape[-1]), 0)
    where = jnp.where(
        row < 16, positions[0], jnp.where(row < 32, positions[1], positions[2])
    )
    hit = ((where == row % 16) & (row < 48)) | (row == 48)
    hit = jnp.where(hit, 1.0, 0.0)
    hits = jnp.concatenate([hit, hit, hit]).astype(bf16)
    factors = dot_tn(hits, table[...])
    return factors[:, :WIDTH], factors[:, WIDTH : 2 * WIDTH], factors[:, 2 * WIDTH :]


def qkv_kernel(
    tok, w, b, gain, shift, pos, seg, pad, table, k_aug, v_aug, q_aug_t, q_out, k_t, v_t, w_wide
):
    @pl.when(pl.program_id(0) == 0)
    def _():
        for c in range(3):
            w_wide[:, c * WIDTH : (c + 1) * WIDTH] = w[c]

    hat, _ = normalized(tok[...].astype(f32))
    normed = (hat * gain[...] + shift[...]).astype(bf16)
    cos, low, high = rope_factors(pos, table)
    all_three = dot_nn(normed, w_wide[...])
    q = all_three[:, :WIDTH] + b[0:1, :]
    k = all_three[:, WIDTH : 2 * WIDTH] + b[1:2, :]
    v = all_three[:, 2 * WIDTH :] + b[2:3, :]
    q = (q * cos + turned(q, low, high)) * (1.0 / math.sqrt(HEAD_DIM))
    k = k * cos + turned(k, low, high)
    q_out[...] = q.astype(bf16)
    q_t = q.T.astype(bf16)
    k_t[...] = k.T.astype(bf16)
    v_t[...] = v.T.astype(bf16)
    row = lax.broadcasted_iota(jnp.int32, (HEAD_DIM, TILE), 0)
    clip = seg[...]
    same = (row >= 1) & (row < 4) & (clip == row - 1)
    mask = jnp.where((row >= 1) & (row < 4) & (clip != row - 1), NEG, 0.0)
    mask = jnp.where(row == 0, jnp.where(pad[...] != 0, NEG, 0.0), mask)
    k_extra = jnp.where((row >= 4) & (row < 7), 1.0, mask)
    q_extra = jnp.where(same | (row == 0), 1.0, 0.0).astype(bf16)
    k_side = jnp.concatenate([jnp.zeros((HEAD_DIM, TILE), f32), k_extra]).T
    lane = lax.broadcasted_iota(jnp.int32, (TILE, AUG), 1)
    ones = jnp.where((lane >= HEAD_DIM) & (lane < HEAD_DIM + 3), 1.0, 0.0)
    for h in range(HEADS):
        pair = slice(h // 2 * AUG, h // 2 * AUG + AUG)
        wide = slice(h * AUG, (h + 1) * AUG)
        k_pair, v_pair = k[:, pair], v[:, pair]
        if h % 2:
            k_pair, v_pair = pltpu.roll(k_pair, HEAD_DIM, 1), pltpu.roll(v_pair, HEAD_DIM, 1)
        k_aug[:, wide] = jnp.where(lane < HEAD_DIM, k_pair, k_side).astype(bf16)
        v_aug[:, wide] = jnp.where(lane < HEAD_DIM, v_pair, ones).astype(bf16)
        q_aug_t[h * AUG : h * AUG + HEAD_DIM, :] = q_t[h * HEAD_DIM : (h + 1) * HEAD_DIM, :]
        q_aug_t[h * AUG + HEAD_DIM : (h + 1) * AUG, :] = q_extra


def project(tokens, w, b, gain, shift, positions, segments, padding, table):
    length, width = tokens.shape
    tiles = length // TILE

    def rows(columns):
        return pl.BlockSpec((TILE, columns), lambda i: (i, 0))

    def columns(count):
        return pl.BlockSpec((count, TILE), lambda i: (0, i))

    out = jax.ShapeDtypeStruct
    wide = out((length, HEADS * AUG), bf16)
    flat = out((WIDTH, length), bf16)
    return pl.pallas_call(
        qkv_kernel,
        grid=(tiles,),
        in_specs=[
            rows(width), whole(w.shape), whole(b.shape), whole((1, width)), whole((1, width)),
            pl.BlockSpec((3, 1, TILE), lambda i: (0, 0, i)), columns(1), columns(1), whole(table.shape),
        ],
        out_specs=[
            rows(HEADS * AUG), rows(HEADS * AUG), columns(HEADS * AUG), rows(WIDTH), columns(WIDTH),
            columns(WIDTH),
        ],
        out_shape=[
            wide, wide, out((HEADS * AUG, length), bf16), out((length, WIDTH), bf16), flat, flat,
        ],
        scratch_shapes=[pltpu.VMEM((width, 3 * WIDTH), bf16)],
        compiler_params=params(LIMIT),
        cost_estimate=pl.CostEstimate(
            flops=6 * length * width * WIDTH, bytes_accessed=20 * MIB, transcendentals=0
        ),
        name="project",
    )(tokens, w, b, gain, shift, positions, segments, padding, table)


def attend_kernel(info, k_aug, v_t, q_aug_t, k_t, pad, o, o_t, lse, top, total, acc, *, part):
    tile = 2 * pl.program_id(0) + part
    padded = pad[...] != 0
    for h in range(HEADS):
        q_h = q_aug_t[h * AUG : h * AUG + HEAD_DIM, :].astype(f32)
        k_h = k_t[h * HEAD_DIM : (h + 1) * HEAD_DIM, :].astype(f32)
        own = jnp.sum(q_h * k_h, axis=0, keepdims=True)
        top[h : h + 1, :] = jnp.where(padded, own, -3e38)
        total[h : h + 1, :] = jnp.where(padded, 1.0, 0.0)
    here = pl.ds(pl.multiple_of(tile * TILE, TILE), TILE)
    acc[...] = jnp.where(padded, v_t[:, here].astype(f32), 0.0)
    feats = [slice(h * HEAD_DIM, (h + 1) * HEAD_DIM) for h in range(HEADS)]
    wides = [slice(h * AUG, (h + 1) * AUG) for h in range(HEADS)]

    def step(j, count):
        keys = pl.ds(pl.multiple_of(j * TILE, TILE), count * TILE)
        scores = [dot_nn(k_aug[keys, wide], q_aug_t[wide, :]) for wide in wides]
        probs, fades = [], []
        for h in range(HEADS):
            old = top[h : h + 1, :]
            new = jnp.maximum(old, jnp.max(scores[h], axis=0, keepdims=True))
            prob = jnp.exp(scores[h] - new)
            fade = jnp.exp(old - new)
            top[h : h + 1, :] = new
            total[h : h + 1, :] = total[h : h + 1, :] * fade + jnp.sum(prob, axis=0, keepdims=True)
            probs.append(prob.astype(bf16))
            fades.append(fade)
        for h, feat in enumerate(feats):
            acc[feat, :] = acc[feat, :] * fades[h] + dot_nn(v_t[feat, keys], probs[h])

    begin, end = clip_range(info, tile, k_aug.shape[0])
    pairs = (end - begin) // 2

    def two(n, _):
        step(begin + 2 * n, 2)
        return 0

    lax.fori_loop(0, pairs, two, 0)

    @pl.when(begin + 2 * pairs < end)
    def _():
        step(end - 1, 1)

    for h, feat in enumerate(feats):
        acc[feat, :] = acc[feat, :] / total[h : h + 1, :]
    lse[...] = jnp.zeros_like(lse)
    lse[0:HEADS, :] = top[0:HEADS, :] + jnp.log(total[0:HEADS, :])
    turned_o = acc[...]
    o_t[...] = turned_o.astype(bf16)
    o[...] = turned_o.T.astype(bf16)


def attend(part, info, k_aug, v_t, q_aug_t, k_t, padding, earlier):
    length = k_aug.shape[0]
    half = length // 2

    def columns(count):
        return pl.BlockSpec((count, TILE), lambda i, *_: (0, 2 * i + part))

    def packed(count):
        return pl.BlockSpec((count, TILE), lambda i, *_: (0, i))

    out = jax.ShapeDtypeStruct
    return pl.pallas_call(
        in_order(functools.partial(attend_kernel, part=part), 6, len(earlier)),
        grid_spec=pltpu.PrefetchScalarGridSpec(
            num_scalar_prefetch=1,
            grid=(half // TILE,),
            in_specs=[
                whole(k_aug.shape), whole(v_t.shape), columns(HEADS * AUG), columns(WIDTH),
                columns(1),
            ]
            + unread(earlier),
            out_specs=[
                pl.BlockSpec((TILE, WIDTH), lambda i, *_: (i, 0)), packed(WIDTH), packed(8),
            ],
            scratch_shapes=[
                pltpu.VMEM((8, TILE), f32), pltpu.VMEM((8, TILE), f32), pltpu.VMEM((WIDTH, TILE), f32),
            ],
        ),
        out_shape=[out((half, WIDTH), bf16), out((WIDTH, half), bf16), out((8, half), f32)],
        compiler_params=params(LIMIT),
        cost_estimate=pl.CostEstimate(
            flops=24 * half * length * WIDTH, bytes_accessed=6 * MIB, transcendentals=0
        ),
        name="attend",
    )(info, k_aug, v_t, q_aug_t, k_t, padding, *earlier)


def nothing(*refs):
    del refs


def after(value, earlier):
    return pl.pallas_call(
        nothing,
        in_specs=unread((value,) + earlier),
        out_specs=pl.BlockSpec(memory_space=pl.ANY),
        out_shape=jax.ShapeDtypeStruct(value.shape, value.dtype),
        input_output_aliases={0: 0},
        name="after",
    )(value, *earlier)


def pair_kernel(first, second, out):
    out[0] = first[...]
    out[1] = second[...]


def paired(first, second, earlier):
    shape = (2,) + first.shape
    return pl.pallas_call(
        in_order(pair_kernel, 2, len(earlier)),
        in_specs=[pl.BlockSpec(memory_space=pltpu.VMEM)] * 2 + unread(earlier),
        out_specs=pl.BlockSpec(memory_space=pltpu.VMEM),
        out_shape=jax.ShapeDtypeStruct(shape, first.dtype),
        name="paired",
    )(first, second, *earlier)


def head_block(at, owner):
    if at is None:
        return pl.BlockSpec((TILE, WIDTH), lambda i, info: (owner(i, info), 0))
    return pl.BlockSpec((None, TILE, WIDTH), lambda i, info: (at, owner(i, info), 0))


def relative(i):
    return i % 2 * 2 + i // 2


def gelu_parts(u):
    size = jnp.abs(u)
    t = 1.0 / (1.0 + (0.3275911 / math.sqrt(2.0)) * size)
    bell = jnp.exp(-0.5 * (u * u))
    poly = 0.5 * 1.061405429
    for c in (-1.453152027, 1.421413741, -0.284496736, 0.254829592):
        poly = poly * t + 0.5 * c
    tail = poly * t * bell
    below = jnp.where(u >= 0, 1.0 - tail, tail)
    return u * below, below + u * bell * (1.0 / math.sqrt(2.0 * math.pi))


def mlp_kernel(
    info, tok, cot, o_0, o_1, o_2, o_3, w_all, b_out, gain, shift, w_up, b_up, w_down,
    x2, dy, h2, act, du, mlp, mlp_sent, dh2, dh2_sent, db_up, w_out, *, me_at,
):
    i = pl.program_id(0)

    @pl.when(i == 0)
    def _():
        for j in range(4):
            w_out[j * WIDTH : (j + 1) * WIDTH, :] = w_all[jnp.bitwise_xor(info[me_at], j)]
        db_up[...] = jnp.zeros_like(db_up)

    heads = jnp.concatenate([o_0[...], o_1[...], o_2[...], o_3[...]], axis=1)
    mid = tok[...].astype(f32) + b_out[...] + dot_nn(heads, w_out[...])

    @pl.when(i == 0)
    def _():
        x2[...] = mid
        dy[...] = cot[...]

    hat, _ = normalized(mid)
    normed = (hat * gain[...] + shift[...]).astype(bf16)
    h2[...] = normed
    u = dot_nn(normed, w_up[...]) + b_up[...]
    grad_act = dot_nt(cot[...], w_down[...])
    value, slope = gelu_parts(u)
    value = value.astype(bf16)
    grad = (grad_act * slope).astype(bf16)
    act[...] = value
    du[...] = grad
    db_up[0:1, :] += jnp.sum(grad.astype(f32), axis=0, keepdims=True)
    mlp_part = dot_nn(value, w_down[...]).astype(bf16)
    dh2_part = dot_nt(grad, w_up[...]).astype(bf16)
    mlp[0] = mlp_part
    mlp_sent[0] = mlp_part
    dh2[0] = dh2_part
    dh2_sent[0] = dh2_part


def mlp(
    part, info, me_at, tokens, cotangent, o_parts, w_all, b_out, gain, shift, w_up, b_up, w_down,
    earlier,
):
    length, width = tokens.shape
    half = length // 2
    hidden = w_up.shape[1]
    owners = half // TILE

    def owner(i, info):
        return jnp.bitwise_xor(info[me_at], relative(i))

    def rows(columns):
        return pl.BlockSpec((TILE, columns), lambda i, info: (2 * owner(i, info) + part, 0))

    def packed(columns):
        return pl.BlockSpec((TILE, columns), lambda i, info: (owner(i, info), 0))

    ordered = pl.BlockSpec((1, TILE, width), lambda i, info: (i, 0, 0))
    sent = pl.BlockSpec((1, TILE, width), lambda i, info: (jnp.maximum(i - 2, 0), 0, 0))

    out = jax.ShapeDtypeStruct
    return pl.pallas_call(
        in_order(functools.partial(mlp_kernel, me_at=me_at), 14, len(earlier)),
        grid_spec=pltpu.PrefetchScalarGridSpec(
            num_scalar_prefetch=1,
            grid=(owners,),
            in_specs=[rows(width), rows(width)]
            + [head_block(at, owner) for _, at in o_parts]
            + [whole(w_all.shape)]
            + [whole((1, width))] * 3
            + [whole(w_up.shape), whole((1, hidden)), whole(w_down.shape)]
            + unread(earlier),
            out_specs=[
                whole((TILE, width)), whole((TILE, width)), packed(width), packed(hidden),
                packed(hidden), ordered, sent, ordered, sent, whole((8, hidden)),
            ],
            scratch_shapes=[pltpu.VMEM((4 * WIDTH, width), bf16)],
        ),
        out_shape=[
            out((TILE, width), f32), out((TILE, width), bf16), out((half, width), bf16),
            out((half, hidden), bf16), out((half, hidden), bf16),
        ]
        + [out((owners, TILE, width), bf16), out((2, TILE, width), bf16)] * 2
        + [out((8, hidden), f32)],
        compiler_params=params(LIMIT),
        cost_estimate=pl.CostEstimate(
            flops=20 * half * width * hidden, bytes_accessed=20 * MIB, transcendentals=0
        ),
        name="mlp",
    )(
        info, tokens, cotangent, *(part for part, _ in o_parts), w_all, b_out, gain, shift, w_up,
        b_up, w_down, *earlier
    )


def up_weights_kernel(left_a, left_b, right_a, right_b, out):
    left = jnp.concatenate([left_a[...], left_b[...]])
    right = jnp.concatenate([right_a[...], right_b[...]])
    out[...] = dot_tn(left, right).astype(bf16)


def up_weights(h2, du, earlier):
    half, width = h2[0].shape
    hidden = du[0].shape[1]
    return pl.pallas_call(
        in_order(up_weights_kernel, 4, len(earlier)),
        grid=(width // TILE,),
        in_specs=[pl.BlockSpec((half, TILE), lambda i: (0, i))] * 2
        + [whole((half, hidden))] * 2
        + unread(earlier),
        out_specs=pl.BlockSpec((TILE, hidden), lambda i: (i, 0)),
        out_shape=pltpu.HBM((width, hidden), bf16),
        compiler_params=params(LIMIT),
        cost_estimate=pl.CostEstimate(
            flops=8 * half * width * hidden, bytes_accessed=12 * MIB, transcendentals=0
        ),
        name="up_weights",
    )(*h2, *du, *earlier)


def down_weights_kernel(act_a, act_b, cot, out):
    owners = cot.shape[0] // (2 * TILE)
    rows = [cot[n * TILE : (n + 1) * TILE, :] for p in range(2) for n in range(p, 2 * owners, 2)]
    out[...] = dot_tn(
        jnp.concatenate([act_a[...], act_b[...]]), jnp.concatenate(rows)
    ).astype(bf16)


def down_weights(act, cotangent, earlier):
    half, hidden = act[0].shape
    length, width = cotangent.shape
    return pl.pallas_call(
        in_order(down_weights_kernel, 3, len(earlier)),
        grid=(hidden // TILE,),
        in_specs=[pl.BlockSpec((half, TILE), lambda i: (0, i))] * 2
        + [whole((length, width))]
        + unread(earlier),
        out_specs=pl.BlockSpec((TILE, width), lambda i: (i, 0)),
        out_shape=pltpu.HBM((hidden, width), bf16),
        compiler_params=params(LIMIT),
        cost_estimate=pl.CostEstimate(
            flops=8 * half * width * hidden, bytes_accessed=12 * MIB, transcendentals=0
        ),
        name="down_weights",
    )(*act, cotangent, *earlier)


def add_kernel(parts, other, out):
    out[...] = (parts[0].astype(f32) + other[0].astype(f32)).astype(bf16)


def to_give(parts, other, earlier):
    _, rows, width = parts.shape
    tile = min(rows, TILE)
    return pl.pallas_call(
        in_order(add_kernel, 2, len(earlier)),
        grid=(rows // tile,),
        in_specs=[
            pl.BlockSpec((1, tile, width), lambda i: (1, i, 0)),
            pl.BlockSpec((1, tile, width), lambda i: (1, i, 0)),
        ]
        + unread(earlier),
        out_specs=pl.BlockSpec((tile, width), lambda i: (i, 0)),
        out_shape=pltpu.HBM((rows, width), bf16),
        compiler_params=params(LIMIT),
        name="to_give",
    )(parts, other, *earlier)


def merge_kernel(parts_0, parts_1, parts_2, other_0, other_1, other_2, keep, give):
    for n, (parts, other) in enumerate(
        ((parts_0, other_0), (parts_1, other_1), (parts_2, other_2))
    ):
        rows = slice(n * TILE, (n + 1) * TILE)
        keep[rows, :] = (parts[0].astype(f32) + other[0].astype(f32)).astype(bf16)
        give[rows, :] = (parts[1].astype(f32) + other[1].astype(f32)).astype(bf16)


def merged(parts, others, earlier):
    _, rows, width = parts[0].shape
    block = (2, rows, width)
    out = pltpu.HBM((3 * rows, width), bf16)
    return pl.pallas_call(
        in_order(merge_kernel, 6, len(earlier)),
        grid=(1,),
        in_specs=[pl.BlockSpec(block, lambda i: (0, 0, 0))] * 6
        + unread(earlier),
        out_specs=[whole((3 * rows, width))] * 2,
        out_shape=[out, out],
        compiler_params=params(LIMIT),
        name="merged",
    )(*parts, *others, *earlier)


def middle_kernel(
    info, kept, other, there, x2, cot, gain, w_all, dx2, g, d_0, d_1, d_2, d_3, small, *, me_at
):
    grad = kept[0].astype(f32) + other[0].astype(f32) + there[...].astype(f32)
    hat, inverse = normalized(x2[...])
    dy = cot[...].astype(f32)
    full = dy + norm_back(hat, inverse, gain[...], grad)
    dx2[...] = full
    low = full.astype(bf16)
    g[...] = low
    small[...] = jnp.zeros_like(small)
    small[0:1, :] = jnp.sum(grad * hat, axis=0, keepdims=True)
    small[1:2, :] = jnp.sum(grad, axis=0, keepdims=True)
    small[2:3, :] = jnp.sum(low.astype(f32), axis=0, keepdims=True)
    small[3:4, :] = jnp.sum(dy, axis=0, keepdims=True)
    for j, d_j in enumerate((d_0, d_1, d_2, d_3)):
        d_j[...] = dot_nt(low, w_all[jnp.bitwise_xor(info[me_at], j)]).astype(bf16)


def middle(info, me_at, kept, other, there, x2, dy, gain, w_all, earlier):
    width = x2.shape[1]
    out = jax.ShapeDtypeStruct
    own = whole((TILE, width))
    return pl.pallas_call(
        in_order(functools.partial(middle_kernel, me_at=me_at), 8, len(earlier)),
        grid_spec=pltpu.PrefetchScalarGridSpec(
            num_scalar_prefetch=1,
            grid=(1,),
            in_specs=[
                pl.BlockSpec((1, TILE, width), lambda i, info: (0, 0, 0)),
                pl.BlockSpec((1, TILE, width), lambda i, info: (0, 0, 0)), own, own, own,
                whole((1, width)), whole(w_all.shape),
            ]
            + unread(earlier),
            out_specs=[own, own] + [whole((TILE, WIDTH))] * 4 + [whole((8, width))],
        ),
        out_shape=[pltpu.HBM((TILE, width), f32), pltpu.HBM((TILE, width), bf16)]
        + [pltpu.HBM((TILE, WIDTH), bf16)] * 4
        + [out((8, width), f32)],
        compiler_params=params(40),
        cost_estimate=pl.CostEstimate(
            flops=2 * TILE * width * width, bytes_accessed=8 * MIB, transcendentals=0
        ),
        name="middle",
    )(info, kept, other, there, x2, dy, gain, w_all, *earlier)


def out_weights_kernel(info, *refs):
    parts_a, parts_b, (g_a, g_b, kept, sent) = refs[0:4], refs[4:8], refs[8:]
    for n in range(2):
        for out, j in ((kept, 2 * n), (sent, 2 * n + 1)):
            grad = dot_tn(parts_a[j][...], g_a[...]) + dot_tn(parts_b[j][...], g_b[...])
            out[n] = grad.astype(bf16)


def out_weights(info, me_at, parts_a, parts_b, g_a, g_b):
    width = g_a.shape[1]

    def owner(i, info):
        return info[me_at]

    return pl.pallas_call(
        out_weights_kernel,
        grid_spec=pltpu.PrefetchScalarGridSpec(
            num_scalar_prefetch=1,
            grid=(1,),
            in_specs=[head_block(at, owner) for _, at in parts_a + parts_b]
            + [whole((TILE, width))] * 2,
            out_specs=[whole((2, WIDTH, width))] * 2,
        ),
        out_shape=[pltpu.HBM((2, WIDTH, width), bf16)] * 2,
        compiler_params=params(LIMIT),
        cost_estimate=pl.CostEstimate(
            flops=4 * TILE * width * width, bytes_accessed=6 * MIB, transcendentals=0
        ),
        name="out_weights",
    )(info, *(part for part, _ in parts_a + parts_b), g_a, g_b)


def attend_back_kernel(
    info, k_aug, v_aug, k_t, q_aug_t, q, v_t, o_t, lse, pad, do_0, do_1, do_2, do_3, pos, table,
    *refs, part, me_at, first,
):
    if first:
        dk_in = dv_in = None
    else:
        dk_in, dv_in, *refs = refs
    dq_out, dk, dv, q_side, do_side, q_lanes, do_lanes, dq_t = refs
    i = pl.program_id(0)
    tile = 2 * jnp.bitwise_xor(info[me_at], i) + part

    @pl.when(i == 0)
    def _():
        if first:
            dk[...] = jnp.zeros_like(dk)
            dv[...] = jnp.zeros_like(dv)
        else:
            dk[...] = dk_in[...]
            dv[...] = dv_in[...]

    here = pl.ds(pl.multiple_of(tile * TILE, TILE), TILE)
    do_here = jnp.where(
        i == 0, do_0[...], jnp.where(i == 1, do_1[...], jnp.where(i == 2, do_2[...], do_3[...]))
    )
    q_here = q[...]
    do_t = do_here.astype(f32).T
    k_here = k_t[:, here].astype(f32)
    padded = jnp.where(pad[...] != 0, 1.0, 0.0)
    row = lax.broadcasted_iota(jnp.int32, (AUG - HEAD_DIM, TILE), 0)
    lane = lax.broadcasted_iota(jnp.int32, (TILE, WIDTH), 1) // HEAD_DIM
    dk_parts, dv_parts = [], []
    for h in range(HEADS):
        feat = slice(h * HEAD_DIM, (h + 1) * HEAD_DIM)
        at = h * AUG
        q_h = q_aug_t[at : at + HEAD_DIM, :]
        do_h = do_t[feat, :]
        delta = jnp.sum(do_h * o_t[feat, :].astype(f32), axis=0, keepdims=True)
        lse_h = lse[h : h + 1, :]
        one, two, three = three_parts(-lse_h)
        extra = q_aug_t[at + HEAD_DIM : at + AUG, :].astype(f32)
        extra = jnp.where(row == 4, one, jnp.where(row == 5, two, jnp.where(row == 6, three, extra)))
        q_side[at : at + HEAD_DIM, :] = q_h
        q_side[at + HEAD_DIM : at + AUG, :] = extra.astype(bf16)
        one, two, three = three_parts(-delta)
        extra = jnp.where(row == 0, one, jnp.where(row == 1, two, jnp.where(row == 2, three, 0.0)))
        do_side[at : at + HEAD_DIM, :] = do_h.astype(bf16)
        do_side[at + HEAD_DIM : at + AUG, :] = extra.astype(bf16)
        q_lanes[h] = jnp.where(lane == h, q_here, jnp.zeros_like(q_here))
        do_lanes[h] = jnp.where(lane == h, do_here, jnp.zeros_like(do_here))
        q_h = q_h.astype(f32)
        k_h = k_here[feat, :]
        p_own = padded * jnp.exp(jnp.sum(q_h * k_h, axis=0, keepdims=True) - lse_h)
        dp_own = jnp.sum(do_h * v_t[feat, :].astype(f32), axis=0, keepdims=True)
        ds_own = p_own * (dp_own - delta)
        dq_t[feat, :] = ds_own * k_h
        dk_parts.append(ds_own * q_h)
        dv_parts.append(p_own * do_h)
    dk[here, :] += jnp.concatenate(dk_parts, axis=0).T
    dv[here, :] += jnp.concatenate(dv_parts, axis=0).T

    def step(j, _):
        keys = pl.ds(pl.multiple_of(j * TILE, TILE), TILE)
        probs, grads = [], []
        for h in range(HEADS):
            wide = slice(h * AUG, (h + 1) * AUG)
            prob = jnp.exp(dot_nn(k_aug[keys, wide], q_side[wide, :]))
            grad = prob * dot_nn(v_aug[keys, wide], do_side[wide, :])
            probs.append(prob.astype(bf16))
            grads.append(grad.astype(bf16))
        deep = (HEADS * TILE, WIDTH)
        dv[keys, :] += dot_nn(jnp.concatenate(probs, axis=1), do_lanes[...].reshape(deep))
        dk[keys, :] += dot_nn(jnp.concatenate(grads, axis=1), q_lanes[...].reshape(deep))
        for h in range(HEADS):
            feat = slice(h * HEAD_DIM, (h + 1) * HEAD_DIM)
            dq_t[feat, :] += dot_nn(k_t[feat, keys], grads[h])
        return 0

    begin, end = clip_range(info, tile, k_aug.shape[0])
    lax.fori_loop(begin, end, step, 0)
    dq = dq_t[...].T * (1.0 / math.sqrt(HEAD_DIM))
    cos, low, high = rope_factors(pos, table)
    dq_out[...] = (dq * cos - turned(dq, low, high)).astype(bf16)


def attend_back(
    part, info, me_at, k_aug, v_aug, k_t, q_aug_t, q, v_t, o_t, lse, padding, do, positions, table,
    dk, dv, earlier,
):
    length = k_aug.shape[0]
    half = length // 2

    def owner(i, info):
        return jnp.bitwise_xor(info[me_at], i)

    def rows(columns):
        return pl.BlockSpec((TILE, columns), lambda i, info: (2 * owner(i, info) + part, 0))

    def columns(count):
        return pl.BlockSpec((count, TILE), lambda i, info: (0, 2 * owner(i, info) + part))

    def packed(count):
        return pl.BlockSpec((count, TILE), lambda i, info: (0, owner(i, info)))

    out = jax.ShapeDtypeStruct
    before = () if dk is None else (dk, dv)
    return pl.pallas_call(
        in_order(
            functools.partial(attend_back_kernel, part=part, me_at=me_at, first=dk is None),
            16 + len(before), len(earlier),
        ),
        grid_spec=pltpu.PrefetchScalarGridSpec(
            num_scalar_prefetch=1,
            grid=(half // TILE,),
            in_specs=[
                whole(k_aug.shape), whole(v_aug.shape), whole(k_t.shape), columns(HEADS * AUG),
                rows(WIDTH), columns(WIDTH), packed(WIDTH), packed(8), columns(1),
            ]
            + [whole((TILE, WIDTH))] * 4
            + [
                pl.BlockSpec(
                    (3, 1, TILE), lambda i, info: (0, 0, 2 * owner(i, info) + part)
                ),
                whole(table.shape),
            ]
            + [whole((length, WIDTH))] * len(before)
            + unread(earlier),
            out_specs=[
                pl.BlockSpec((TILE, WIDTH), lambda i, info: (owner(i, info), 0)),
                whole((length, WIDTH)), whole((length, WIDTH)),
            ],
            scratch_shapes=[
                pltpu.VMEM((HEADS * AUG, TILE), bf16), pltpu.VMEM((HEADS * AUG, TILE), bf16),
                pltpu.VMEM((HEADS, TILE, WIDTH), bf16), pltpu.VMEM((HEADS, TILE, WIDTH), bf16),
                pltpu.VMEM((WIDTH, TILE), f32),
            ],
        ),
        out_shape=[out((half, WIDTH), bf16), out((length, WIDTH), f32), out((length, WIDTH), f32)],
        compiler_params=params(LIMIT),
        cost_estimate=pl.CostEstimate(
            flops=72 * half * length * WIDTH, bytes_accessed=16 * MIB, transcendentals=0
        ),
        name="attend_back",
    )(
        info, k_aug, v_aug, k_t, q_aug_t, q, v_t, o_t, lse, padding, *do, positions, table, *before,
        *earlier,
    )


def pieces(begin, count, period):
    at, end, cuts = begin, begin + count, []
    while at < end:
        length = min(end - at, period - at % period)
        cuts.append((at, length))
        at += length
    return cuts


def stacked_pairs(rows, count):
    row = lax.broadcasted_iota(jnp.int32, (count, WIDTH), 0)
    out = jnp.zeros((count, WIDTH), f32)
    for m, value in enumerate(rows):
        one, two, _ = three_parts(value)
        out = jnp.where(row == 2 * m, one, jnp.where(row == 2 * m + 1, two, out))
    return out.astype(bf16)


def late_extra(width, blocks):
    vectors = -(-(3 + 7 * width // WIDTH) // blocks)
    return vectors, -(-vectors // 8) * 16


def project_back_kernel(
    info, tok, gain, shift, dq_a, dq_b, dk, dv, pos, table, w, out_kept, out_there, early,
    dh1, dh1_sent, sums, acc, grad_b, small, w_wide,
):
    i = pl.program_id(0)

    @pl.when(i == 0)
    def _():
        acc[...] = jnp.zeros_like(acc)
        grad_b[...] = jnp.zeros_like(grad_b)
        small[...] = jnp.zeros_like(small)
        for c in range(3):
            w_wide[:, c * WIDTH : (c + 1) * WIDTH] = w[c]

    dk_here = dk[...]
    cos, low, high = rope_factors(pos, table)
    dk_low = (dk_here * cos - turned(dk_here, low, high)).astype(bf16)
    dq = jnp.concatenate([dq_a[...], dq_b[...]])
    parts = jnp.concatenate([dq, dk_low, dv[...].astype(bf16)], axis=1)
    grad = dot_nt(parts, w_wide[...])
    hat, _ = normalized(tok[...].astype(f32))
    normed = (hat * gain[...] + shift[...]).astype(bf16)
    acc[...] += dot_tn(normed, parts)
    grad_b[0:1, :] += jnp.sum(parts.astype(f32), axis=0, keepdims=True)
    small[0:1, :] += jnp.sum(grad * hat, axis=0, keepdims=True)
    small[1:2, :] += jnp.sum(grad, axis=0, keepdims=True)
    low_grad = grad.astype(bf16)
    dh1[0] = low_grad
    dh1_sent[0] = low_grad

    @pl.when(i == pl.num_programs(0) - 1)
    def _():
        width = normed.shape[1]
        blocks = sums.shape[0]

        def cut(value, count):
            return [value[:, r * WIDTH : (r + 1) * WIDTH] for r in range(count)]

        rows = cut(grad_b[0:1, :], 3) + cut(early[4:5, :], width // WIDTH)
        for ref, count in ((small, 2), (early, 4)):
            for v in range(count):
                rows += cut(ref[v : v + 1, :], width // WIDTH)
        for n in range(blocks):
            for to, rows_here, c, begin in late_places(n, blocks, width):
                here = (slice(begin, begin + rows_here), slice(c * WIDTH, (c + 1) * WIDTH))
                sums[n, to : to + rows_here, :] = acc[here].astype(bf16)
            for to, rows_here, c, begin in late_places(n, blocks, width, True):
                here = (slice(begin, begin + rows_here), slice(c * WIDTH, (c + 1) * WIDTH))
                sums[n, to : to + rows_here, :] = (
                    out_kept[here].astype(f32) + out_there[here].astype(f32)
                ).astype(bf16)
            extra_at = 4 * width // blocks
            sums[n, extra_at:, :] = stacked_pairs(rows[n::blocks], sums.shape[1] - extra_at)


def late_places(n, blocks, width, out=False):
    deep, period = (width // blocks, WIDTH) if out else (3 * width // blocks, width)
    first = 3 * width // blocks if out else 0
    return [
        (first + at - n * deep, length, at // period, at % period)
        for at, length in pieces(n * deep, deep, period)
    ]


def project_back(
    info, me_at, tokens, gain, shift, dq_a, dq_b, dk, dv, positions, table, w, kept, there, early,
    blocks,
):
    length, width = tokens.shape
    share = 2 * TILE

    def owner(i, info):
        return jnp.bitwise_xor(info[me_at], relative(i))

    def rows(count, columns):
        return pl.BlockSpec((count, columns), lambda i, info: (owner(i, info), 0))

    last = pl.BlockSpec((TILE, width), lambda i, info: (2, 0))
    out = jax.ShapeDtypeStruct
    sums = (blocks, 4 * width // blocks + late_extra(width, blocks)[1], WIDTH)
    return pl.pallas_call(
        project_back_kernel,
        grid_spec=pltpu.PrefetchScalarGridSpec(
            num_scalar_prefetch=1,
            grid=(length // share,),
            in_specs=[
                rows(share, width), whole((1, width)), whole((1, width)), rows(TILE, WIDTH),
                rows(TILE, WIDTH), rows(share, WIDTH), rows(share, WIDTH),
                pl.BlockSpec((3, 1, share), lambda i, info: (0, 0, owner(i, info))),
                whole(table.shape), whole(w.shape), last, last, whole(early.shape),
            ],
            out_specs=[
                pl.BlockSpec((1, share, width), lambda i, info: (i, 0, 0)),
                pl.BlockSpec((1, share, width), lambda i, info: (jnp.maximum(i - 2, 0), 0, 0)),
                whole(sums),
            ],
            scratch_shapes=[
                pltpu.VMEM((width, 3 * WIDTH), f32), pltpu.VMEM((8, 3 * WIDTH), f32),
                pltpu.VMEM((8, width), f32),
                pltpu.VMEM((width, 3 * WIDTH), bf16),
            ],
        ),
        out_shape=[
            pltpu.HBM((4, share, width), bf16), pltpu.HBM((2, share, width), bf16),
            pltpu.HBM(sums, bf16),
        ],
        compiler_params=params(LIMIT),
        cost_estimate=pl.CostEstimate(
            flops=24 * length * width * WIDTH, bytes_accessed=20 * MIB, transcendentals=0
        ),
        name="project_back",
    )(info, tokens, gain, shift, dq_a, dq_b, dk, dv, positions, table, w, kept, there, early)


def unpack_kernel(sums, grad_qkv, grad_out, grad_b, vectors):
    blocks = sums.shape[0]
    width = grad_out.shape[1]
    grad_b[...] = jnp.zeros_like(grad_b)
    extra_at = 4 * width // blocks
    for n in range(blocks):
        for to, rows, c, begin in late_places(n, blocks, width):
            grad_qkv[c, begin : begin + rows, :] = sums[n, to : to + rows, :].astype(f32)
        for to, rows, c, begin in late_places(n, blocks, width, True):
            grad_out[begin : begin + rows, c * WIDTH : (c + 1) * WIDTH] = sums[
                n, to : to + rows, :
            ].astype(f32)
    vectors[...] = jnp.zeros_like(vectors)
    for v in range(3 + 7 * width // WIDTH):
        n, m = v % blocks, v // blocks
        pair = sums[n, extra_at:, :].astype(f32)
        row = pair[2 * m : 2 * m + 1, :] + pair[2 * m + 1 : 2 * m + 2, :]
        if v < 3:
            grad_b[v : v + 1, :] = row
        else:
            to, at = divmod((v - 3) * WIDTH, width)
            vectors[to : to + 1, at : at + WIDTH] = row


def unpack(sums, width, earlier):
    out = jax.ShapeDtypeStruct
    return pl.pallas_call(
        in_order(unpack_kernel, 1, len(earlier)),
        in_specs=[pl.BlockSpec(memory_space=pltpu.VMEM)] + unread(earlier),
        out_specs=[pl.BlockSpec(memory_space=pltpu.VMEM)] * 4,
        out_shape=[
            out((3, width, WIDTH), f32), out((WIDTH, width), f32), out((8, WIDTH), f32),
            out((8, width), f32),
        ],
        compiler_params=pltpu.CompilerParams(vmem_limit_bytes=LIMIT * MIB),
        name="unpack",
    )(sums, *earlier)


def finish_kernel(info, parts, other, there, tok, gain, dx2_a, dx2_b, out):
    grad = parts[0].astype(f32) + other[0].astype(f32) + there[...].astype(f32)
    hat, inverse = normalized(tok[...].astype(f32))
    dx2 = jnp.where(pl.program_id(0) == 0, dx2_a[...], dx2_b[...])
    out[...] = dx2 + norm_back(hat, inverse, gain[...], grad)


def finish(info, me_at, parts, other, there, tokens, gain, dx2_a, dx2_b):
    width = tokens.shape[1]
    share = there.shape[0]
    rows = pl.BlockSpec((TILE, width), lambda i, info: (i, 0))
    return pl.pallas_call(
        finish_kernel,
        grid_spec=pltpu.PrefetchScalarGridSpec(
            num_scalar_prefetch=1,
            grid=(share // TILE,),
            in_specs=[
                pl.BlockSpec((1, TILE, width), lambda i, info: (0, i, 0)),
                pl.BlockSpec((1, TILE, width), lambda i, info: (0, i, 0)), rows,
                pl.BlockSpec((TILE, width), lambda i, info: (2 * info[me_at] + i, 0)),
                whole((1, width)), whole((TILE, width)), whole((TILE, width)),
            ],
            out_specs=rows,
        ),
        out_shape=jax.ShapeDtypeStruct((share, width), f32),
        compiler_params=params(LIMIT),
        cost_estimate=pl.CostEstimate(
            flops=30 * share * width, bytes_accessed=10 * MIB, transcendentals=0
        ),
        name="finish",
    )(info, parts, other, there, tokens, gain, dx2_a, dx2_b)


def total_of(blocks):
    total = blocks[0].astype(f32)
    for n in range(1, blocks.shape[0]):
        total += blocks[n].astype(f32)
    return total.astype(bf16)


def sums_kernel(blocks_a, blocks_b, out):
    rows = blocks_a.shape[1]
    out[:rows, :] = total_of(blocks_a)
    out[rows:, :] = total_of(blocks_b)


def two_sums(blocks_a, blocks_b, earlier):
    _, rows, width = blocks_a.shape
    return pl.pallas_call(
        in_order(sums_kernel, 2, len(earlier)),
        grid=(1,),
        in_specs=[whole(blocks_a.shape), whole(blocks_b.shape)] + unread(earlier),
        out_specs=whole((2 * rows, width)),
        out_shape=jax.ShapeDtypeStruct((2 * rows, width), bf16),
        compiler_params=params(LIMIT),
        name="two_sums",
    )(blocks_a, blocks_b, *earlier)


def copies_kernel(blocks, out):
    total = total_of(blocks)
    for n in range(blocks.shape[0]):
        out[n] = total


def sum_copies(blocks, earlier):
    return pl.pallas_call(
        in_order(copies_kernel, 1, len(earlier)),
        grid=(1,),
        in_specs=[whole(blocks.shape)] + unread(earlier),
        out_specs=whole(blocks.shape),
        out_shape=pltpu.HBM(blocks.shape, bf16),
        compiler_params=params(LIMIT),
        name="sum_copies",
    )(blocks, *earlier)


def swap(array, axis, bit=1):
    size = lax.axis_size(axis)
    if size == 1:
        return jnp.zeros_like(array)
    return lax.ppermute(array, axis, [(i, i ^ bit) for i in range(size)])


def swap_both(array):
    return lax.ppermute(array, MP, [(i, i ^ 3) for i in range(4)])


def scattered(rows, axes):
    group = lax.axis_size(axes)
    length, width = rows.shape
    return lax.all_to_all(
        rows.reshape(group, length // group, width), axes, 0, 0, tiled=True
    )


def both_sums(total):
    if lax.axis_size("zl") == 1:
        return total
    return (total.astype(f32) + swap(total, "zl").astype(f32)).astype(bf16)


def local(
    tokens, cotangent, segments, padding, positions, ln1_gain, ln1_bias, w_qkv, b_qkv, w_out, b_out,
    ln2_gain, ln2_bias, w_up, b_up, w_down, b_down,
):
    width, hidden = w_up.shape
    w_all = lax.all_gather(w_out, MP)
    gain_one, shift_one = ln1_gain[None], ln1_bias[None]
    gain_two, shift_two = ln2_gain[None], ln2_bias[None]
    ends = jnp.sum((segments <= jnp.arange(2)[:, None]).astype(jnp.int32), axis=1)
    info = jnp.concatenate([ends, lax.axis_index(MP)[None].astype(jnp.int32)])
    me_at = 2
    table = jnp.asarray(rope_constants())
    k_aug, v_aug, q_aug_t, q, k_t, v_t = project(
        tokens, w_qkv, b_qkv, gain_one, shift_one, positions, segments, padding, table
    )

    def exchanged(own, to_c, to_zh, to_both):
        return own, swap(to_c, "c"), swap(to_zh, "zh"), swap_both(to_both)

    o_0, o_t_0, lse_0 = attend(0, info, k_aug, v_t, q_aug_t, k_t, padding, ())
    o_zh_0, o_c_0 = swap(o_0, "zh"), swap(o_0, "c")
    o_1, o_t_1, lse_1 = attend(1, info, k_aug, v_t, q_aug_t, k_t, padding, (o_0, w_all))
    o_zh_1 = swap(o_1, "zh")
    o_zh_0 = after(o_zh_0, (o_1,))
    o_parts_0 = tuple((part, None) for part in (o_0, o_c_0, o_zh_0, swap(o_zh_0, "c")))

    def mlp_half(part, o_parts, earlier):
        return mlp(
            part, info, me_at, tokens, cotangent, o_parts, w_all, b_out[None], gain_two, shift_two,
            w_up, b_up[None], w_down, earlier,
        )

    x2_0, dy_0, h2_0, act_0, du_0, mlp_0, mlp_sent_0, dh2_0, sent, db_0 = mlp_half(
        0, o_parts_0, (o_1,)
    )
    pair = paired(o_1, o_zh_1, (x2_0,))
    pair_c = swap(pair, "c")
    o_parts_1 = ((pair, 0), (pair_c, 0), (pair, 1), (pair_c, 1))
    other_0 = swap(sent, "c")
    give_0 = to_give(dh2_0, other_0, ())
    there_0 = swap(give_0, "zh")
    x2_1, dy_1, h2_1, act_1, du_1, mlp_1, mlp_sent_1, dh2_1, sent, db_1 = mlp_half(
        1, o_parts_1, (give_0,)
    )
    other_1 = swap(sent, "c")
    grad_down = down_weights((act_0, act_1), cotangent, ())
    arrived_down = scattered(grad_down, ("y", "x"))
    give_1 = to_give(dh2_1, other_1, (grad_down,))
    there_1 = swap(give_1, "zh")
    dx2_0, g_0, *d_0, small_0 = middle(
        info, me_at, dh2_0, other_0, there_0, x2_0, dy_0, gain_two, w_all, (grad_down, give_1)
    )
    do_0 = exchanged(*d_0)
    grad_up = up_weights((h2_0, h2_1), (du_0, du_1), (g_0,))
    dx2_1, g_1, *d_1, small_1 = middle(
        info, me_at, dh2_1, other_1, there_1, x2_1, dy_1, gain_two, w_all, (grad_up,)
    )
    do_1 = exchanged(*d_1)
    grad_out, out_sent = out_weights(info, me_at, o_parts_0, o_parts_1, g_0, g_1)
    arrived_up = scattered(grad_up, ("y", "x"))

    mixed_parts = (mlp_0, mlp_1, grad_out)
    others = [swap(parts, "c") for parts in (mlp_sent_0, mlp_sent_1, out_sent)]
    dq_0, dk, dv = attend_back(
        0, info, me_at, k_aug, v_aug, k_t, q_aug_t, q, v_t, o_t_0, lse_0, padding, do_0, positions,
        table, None, None, (grad_out, g_1),
    )
    keep, give = merged(mixed_parts, others, (dq_0,))
    there = swap(give, "zh")
    part_sum = both_sums(two_sums(arrived_up, arrived_down, (give, dq_0)))
    dq_1, dk, dv = attend_back(
        1, info, me_at, k_aug, v_aug, k_t, q_aug_t, q, v_t, o_t_1, lse_1, padding, do_1, positions,
        table, dk, dv, (give, part_sum, dq_0),
    )
    grad_mlp = lax.all_gather(part_sum, ("y", "x"), axis=0, tiled=True)
    early = jnp.concatenate([(small_0 + small_1)[0:4], (db_0 + db_1)[0:4]])
    dh1, sent, sums = project_back(
        info, me_at, tokens, gain_one, shift_one, dq_0, dq_1, dk, dv, positions, table, w_qkv, keep,
        there, early, lax.axis_size(DP),
    )
    other = swap(sent, "c")
    back = swap(to_give(dh1, other, (sums,)), "zh")
    arrived = scattered(sums.reshape(-1, WIDTH), DP)
    late = lax.all_to_all(sum_copies(arrived, (back,)), DP, 0, 0, tiled=True)
    grad_inputs = finish(info, me_at, dh1, other, back, tokens, gain_one, dx2_0, dx2_1)
    received = keep[: 2 * TILE].astype(f32) + there[: 2 * TILE].astype(f32)
    mixed = (jnp.concatenate([x2_0, x2_1]) + received + b_down[None]).astype(bf16)
    group_size = lax.axis_size(("y", "x"))
    grad_mlp = grad_mlp.reshape(group_size, 2, width // group_size, hidden)
    grad_up = grad_mlp[:, 0].astype(f32).reshape(width, hidden)
    grad_down = grad_mlp[:, 1].astype(f32).reshape(hidden, width)
    grad_qkv, grad_w_out, grad_b, vectors = unpack(
        late, width, (grad_inputs, mixed, grad_up, grad_down)
    )
    by_c, by_zh, by_both = swap(vectors, "c"), swap(vectors, "zh"), swap_both(vectors)
    group = (vectors + by_c) + (by_zh + by_both)
    return (
        mixed, grad_inputs, group[1], group[2], grad_qkv, grad_b[0:3], grad_w_out, group[5],
        group[3], group[4], grad_up, vectors[0], grad_down, group[6],
    )


def solution(mesh):
    packs = mesh.shape["dp"]
    if packs == 32:
        shape = (2, 4, 4, 2, 2)
    else:
        shape = (1, packs, 1, 2, 2)
    split = Mesh(mesh.devices.reshape(shape), EVERY)
    in_specs = (
        P(DP, None), P(DP, None), P(DP, None), P(DP, None), P(None, DP, None), P(), P(),
        P(None, None, MP), P(None, MP), P(MP, None), P(), P(), P(), P(None, MP), P(MP),
        P(MP, None), P(),
    )
    out_specs = (
        P(EVERY, None), P(EVERY, None), P(), P(), P(None, None, MP), P(None, MP), P(MP, None), P(),
        P(), P(), P(None, MP), P(MP), P(MP, None), P(),
    )
    return jax.shard_map(local, mesh=split, in_specs=in_specs, out_specs=out_specs, check_vma=False)
```

```python
import functools
import math

import jax
import jax.numpy as jnp
import ml_dtypes
import numpy as np
from jax import lax
from jax.experimental import pallas as pl
from jax.experimental.pallas import tpu as pltpu
from jax.sharding import Mesh
from jax.sharding import PartitionSpec as P

HEAD_DIM = 64
HEADS = 4
WIDTH = HEADS * HEAD_DIM
AUG = 128
TILE = 256
PLACES = 64
LIMIT = 64
MIB = 1 << 20
DP = ("zl", "y", "x")
MP = ("zh", "c")
EVERY = ("zl", "y", "x", "zh", "c")

epsilon = 1e-06
NEG = -1e30
bf16 = jnp.bfloat16
f32 = jnp.float32


def dot_nn(a, b):
    return lax.dot_general(a, b, (((1,), (0,)), ((), ())), preferred_element_type=f32)


def dot_nt(a, b):
    return lax.dot_general(a, b, (((1,), (1,)), ((), ())), preferred_element_type=f32)


def dot_tn(a, b):
    return lax.dot_general(a, b, (((0,), (0,)), ((), ())), preferred_element_type=f32)


def normalized(values):
    center = jnp.mean(values, axis=-1, keepdims=True)
    shifted = values - center
    spread = jnp.mean(shifted * shifted, axis=-1, keepdims=True)
    inverse = lax.rsqrt(spread + epsilon)
    return shifted * inverse, inverse


def norm_back(hat, inverse, gain, grad):
    scaled = grad * gain
    return inverse * (
        scaled
        - jnp.mean(scaled, axis=-1, keepdims=True)
        - hat * jnp.mean(scaled * hat, axis=-1, keepdims=True)
    )


def turned(x, low, high):
    width = x.shape[1]
    pair = HEAD_DIM // 6
    return pltpu.roll(x, width - pair, 1) * low + pltpu.roll(x, pair, 1) * high


def three_parts(x):
    first = x.astype(bf16).astype(f32)
    rest = x - first
    second = rest.astype(bf16).astype(f32)
    return first, second, rest - second


def params(limit, axes=1):
    return pltpu.CompilerParams(
        dimension_semantics=("arbitrary",) * axes, vmem_limit_bytes=limit * MIB
    )


def in_order(kernel, inputs, earlier):
    def run(*refs):
        kernel(*refs[:inputs], *refs[inputs + earlier :])

    return run


def unread(arrays):
    return [pl.BlockSpec(memory_space=pl.ANY)] * len(arrays)


def whole(shape):
    return pl.BlockSpec(shape, lambda *_: (0,) * len(shape))


def clip_range(info, tile, length):
    first, second = info[0], info[1]
    at = tile * TILE
    begin = jnp.where(second <= at, second, jnp.where(first <= at, first, 0))
    end = jnp.where(
        first >= at + TILE, first, jnp.where(second >= at + TILE, second, length)
    )
    return begin // TILE, (end + TILE - 1) // TILE


def rope_constants():
    pair = HEAD_DIM // 6
    feature = np.arange(WIDTH) % HEAD_DIM
    section, place = feature // (2 * pair), feature % (2 * pair)
    frequency = np.exp(-math.log(10000.0) * (place % pair) / pair)
    table = np.zeros((PLACES, 3, WIDTH))
    for s in range(3):
        for value in range(16):
            angle = value * frequency
            turns = section == s
            table[s * 16 + value, 0] = np.where(turns, np.cos(angle), 0.0)
            table[s * 16 + value, 1] = np.where(turns & (place < pair), -np.sin(angle), 0.0)
            table[s * 16 + value, 2] = np.where(turns & (place >= pair), np.sin(angle), 0.0)
    table[48, 0] = section == 3
    rest = table.reshape(PLACES, 3 * WIDTH).astype(np.float32)
    parts = []
    for _ in range(3):
        part = rest.astype(ml_dtypes.bfloat16)
        parts.append(part)
        rest = rest - part.astype(np.float32)
    return np.concatenate(parts)


def rope_factors(positions, table):
    row = lax.broadcasted_iota(jnp.int32, (PLACES, positions.shape[-1]), 0)
    where = jnp.where(
        row < 16, positions[0], jnp.where(row < 32, positions[1], positions[2])
    )
    hit = ((where == row % 16) & (row < 48)) | (row == 48)
    hit = jnp.where(hit, 1.0, 0.0)
    hits = jnp.concatenate([hit, hit, hit]).astype(bf16)
    factors = dot_tn(hits, table[...])
    return factors[:, :WIDTH], factors[:, WIDTH : 2 * WIDTH], factors[:, 2 * WIDTH :]


def qkv_kernel(
    tok, w, b, gain, shift, pos, seg, pad, table, k_aug, v_aug, q_aug_t, q_out, k_t, v_t, w_wide
):
    @pl.when(pl.program_id(0) == 0)
    def _():
        for c in range(3):
            w_wide[:, c * WIDTH : (c + 1) * WIDTH] = w[c]

    hat, _ = normalized(tok[...].astype(f32))
    normed = (hat * gain[...] + shift[...]).astype(bf16)
    cos, low, high = rope_factors(pos, table)
    all_three = dot_nn(normed, w_wide[...])
    q = all_three[:, :WIDTH] + b[0:1, :]
    k = all_three[:, WIDTH : 2 * WIDTH] + b[1:2, :]
    v = all_three[:, 2 * WIDTH :] + b[2:3, :]
    q = (q * cos + turned(q, low, high)) * (1.0 / math.sqrt(HEAD_DIM))
    k = k * cos + turned(k, low, high)
    q_out[...] = q.astype(bf16)
    q_t = q.T.astype(bf16)
    k_t[...] = k.T.astype(bf16)
    v_t[...] = v.T.astype(bf16)
    row = lax.broadcasted_iota(jnp.int32, (HEAD_DIM, TILE), 0)
    clip = seg[...]
    same = (row >= 1) & (row < 4) & (clip == row - 1)
    mask = jnp.where((row >= 1) & (row < 4) & (clip != row - 1), NEG, 0.0)
    mask = jnp.where(row == 0, jnp.where(pad[...] != 0, NEG, 0.0), mask)
    k_extra = jnp.where((row >= 4) & (row < 7), 1.0, mask)
    q_extra = jnp.where(same | (row == 0), 1.0, 0.0).astype(bf16)
    k_side = jnp.concatenate([jnp.zeros((HEAD_DIM, TILE), f32), k_extra]).T
    lane = lax.broadcasted_iota(jnp.int32, (TILE, AUG), 1)
    ones = jnp.where((lane >= HEAD_DIM) & (lane < HEAD_DIM + 3), 1.0, 0.0)
    for h in range(HEADS):
        pair = slice(h // 2 * AUG, h // 2 * AUG + AUG)
        wide = slice(h * AUG, (h + 1) * AUG)
        k_pair, v_pair = k[:, pair], v[:, pair]
        if h % 2:
            k_pair, v_pair = pltpu.roll(k_pair, HEAD_DIM, 1), pltpu.roll(v_pair, HEAD_DIM, 1)
        k_aug[:, wide] = jnp.where(lane < HEAD_DIM, k_pair, k_side).astype(bf16)
        v_aug[:, wide] = jnp.where(lane < HEAD_DIM, v_pair, ones).astype(bf16)
        q_aug_t[h * AUG : h * AUG + HEAD_DIM, :] = q_t[h * HEAD_DIM : (h + 1) * HEAD_DIM, :]
        q_aug_t[h * AUG + HEAD_DIM : (h + 1) * AUG, :] = q_extra


def project(tokens, w, b, gain, shift, positions, segments, padding, table):
    length, width = tokens.shape
    tiles = length // TILE

    def rows(columns):
        return pl.BlockSpec((TILE, columns), lambda i: (i, 0))

    def columns(count):
        return pl.BlockSpec((count, TILE), lambda i: (0, i))

    out = jax.ShapeDtypeStruct
    wide = out((length, HEADS * AUG), bf16)
    flat = out((WIDTH, length), bf16)
    return pl.pallas_call(
        qkv_kernel,
        grid=(tiles,),
        in_specs=[
            rows(width), whole(w.shape), whole(b.shape), whole((1, width)), whole((1, width)),
            pl.BlockSpec((3, 1, TILE), lambda i: (0, 0, i)), columns(1), columns(1), whole(table.shape),
        ],
        out_specs=[
            rows(HEADS * AUG), rows(HEADS * AUG), columns(HEADS * AUG), rows(WIDTH), columns(WIDTH),
            columns(WIDTH),
        ],
        out_shape=[
            wide, wide, out((HEADS * AUG, length), bf16), out((length, WIDTH), bf16), flat, flat,
        ],
        scratch_shapes=[pltpu.VMEM((width, 3 * WIDTH), bf16)],
        compiler_params=params(LIMIT),
        cost_estimate=pl.CostEstimate(
            flops=6 * length * width * WIDTH, bytes_accessed=20 * MIB, transcendentals=0
        ),
        name="project",
    )(tokens, w, b, gain, shift, positions, segments, padding, table)


def attend_kernel(info, k_aug, v_t, q_aug_t, k_t, pad, o, o_t, lse, top, total, acc, *, part):
    tile = 2 * pl.program_id(0) + part
    padded = pad[...] != 0
    for h in range(HEADS):
        q_h = q_aug_t[h * AUG : h * AUG + HEAD_DIM, :].astype(f32)
        k_h = k_t[h * HEAD_DIM : (h + 1) * HEAD_DIM, :].astype(f32)
        own = jnp.sum(q_h * k_h, axis=0, keepdims=True)
        top[h : h + 1, :] = jnp.where(padded, own, -3e38)
        total[h : h + 1, :] = jnp.where(padded, 1.0, 0.0)
    here = pl.ds(pl.multiple_of(tile * TILE, TILE), TILE)
    acc[...] = jnp.where(padded, v_t[:, here].astype(f32), 0.0)
    feats = [slice(h * HEAD_DIM, (h + 1) * HEAD_DIM) for h in range(HEADS)]
    wides = [slice(h * AUG, (h + 1) * AUG) for h in range(HEADS)]

    def step(j, count):
        keys = pl.ds(pl.multiple_of(j * TILE, TILE), count * TILE)
        scores = [dot_nn(k_aug[keys, wide], q_aug_t[wide, :]) for wide in wides]
        probs, fades = [], []
        for h in range(HEADS):
            old = top[h : h + 1, :]
            new = jnp.maximum(old, jnp.max(scores[h], axis=0, keepdims=True))
            prob = jnp.exp(scores[h] - new)
            fade = jnp.exp(old - new)
            top[h : h + 1, :] = new
            total[h : h + 1, :] = total[h : h + 1, :] * fade + jnp.sum(prob, axis=0, keepdims=True)
            probs.append(prob.astype(bf16))
            fades.append(fade)
        for h, feat in enumerate(feats):
            acc[feat, :] = acc[feat, :] * fades[h] + dot_nn(v_t[feat, keys], probs[h])

    begin, end = clip_range(info, tile, k_aug.shape[0])
    pairs = (end - begin) // 2

    def two(n, _):
        step(begin + 2 * n, 2)
        return 0

    lax.fori_loop(0, pairs, two, 0)

    @pl.when(begin + 2 * pairs < end)
    def _():
        step(end - 1, 1)

    for h, feat in enumerate(feats):
        acc[feat, :] = acc[feat, :] / total[h : h + 1, :]
    lse[...] = jnp.zeros_like(lse)
    lse[0:HEADS, :] = top[0:HEADS, :] + jnp.log(total[0:HEADS, :])
    turned_o = acc[...]
    o_t[...] = turned_o.astype(bf16)
    o[...] = turned_o.T.astype(bf16)


def attend(part, info, k_aug, v_t, q_aug_t, k_t, padding, earlier):
    length = k_aug.shape[0]
    half = length // 2

    def columns(count):
        return pl.BlockSpec((count, TILE), lambda i, *_: (0, 2 * i + part))

    def packed(count):
        return pl.BlockSpec((count, TILE), lambda i, *_: (0, i))

    out = jax.ShapeDtypeStruct
    return pl.pallas_call(
        in_order(functools.partial(attend_kernel, part=part), 6, len(earlier)),
        grid_spec=pltpu.PrefetchScalarGridSpec(
            num_scalar_prefetch=1,
            grid=(half // TILE,),
            in_specs=[
                whole(k_aug.shape), whole(v_t.shape), columns(HEADS * AUG), columns(WIDTH),
                columns(1),
            ]
            + unread(earlier),
            out_specs=[
                pl.BlockSpec((TILE, WIDTH), lambda i, *_: (i, 0)), packed(WIDTH), packed(8),
            ],
            scratch_shapes=[
                pltpu.VMEM((8, TILE), f32), pltpu.VMEM((8, TILE), f32), pltpu.VMEM((WIDTH, TILE), f32),
            ],
        ),
        out_shape=[out((half, WIDTH), bf16), out((WIDTH, half), bf16), out((8, half), f32)],
        compiler_params=params(LIMIT),
        cost_estimate=pl.CostEstimate(
            flops=24 * half * length * WIDTH, bytes_accessed=6 * MIB, transcendentals=0
        ),
        name="attend",
    )(info, k_aug, v_t, q_aug_t, k_t, padding, *earlier)


def nothing(*refs):
    del refs


def after(value, earlier):
    return pl.pallas_call(
        nothing,
        in_specs=unread((value,) + earlier),
        out_specs=pl.BlockSpec(memory_space=pl.ANY),
        out_shape=jax.ShapeDtypeStruct(value.shape, value.dtype),
        input_output_aliases={0: 0},
        name="after",
    )(value, *earlier)


def pair_kernel(first, second, out):
    out[0] = first[...]
    out[1] = second[...]


def paired(first, second, earlier):
    shape = (2,) + first.shape
    return pl.pallas_call(
        in_order(pair_kernel, 2, len(earlier)),
        in_specs=[pl.BlockSpec(memory_space=pltpu.VMEM)] * 2 + unread(earlier),
        out_specs=pl.BlockSpec(memory_space=pltpu.VMEM),
        out_shape=jax.ShapeDtypeStruct(shape, first.dtype),
        name="paired",
    )(first, second, *earlier)


def head_block(at, owner):
    if at is None:
        return pl.BlockSpec((TILE, WIDTH), lambda i, info: (owner(i, info), 0))
    return pl.BlockSpec((None, TILE, WIDTH), lambda i, info: (at, owner(i, info), 0))


def relative(i):
    return i % 2 * 2 + i // 2


def gelu_parts(u):
    size = jnp.abs(u)
    t = 1.0 / (1.0 + (0.3275911 / math.sqrt(2.0)) * size)
    bell = jnp.exp(-0.5 * (u * u))
    poly = 0.5 * 1.061405429
    for c in (-1.453152027, 1.421413741, -0.284496736, 0.254829592):
        poly = poly * t + 0.5 * c
    tail = poly * t * bell
    below = jnp.where(u >= 0, 1.0 - tail, tail)
    return u * below, below + u * bell * (1.0 / math.sqrt(2.0 * math.pi))


def mlp_kernel(
    info, tok, cot, o_0, o_1, o_2, o_3, w_all, b_out, gain, shift, w_up, b_up, w_down,
    x2, dy, h2, act, du, mlp, mlp_sent, dh2, dh2_sent, db_up, w_out, *, me_at,
):
    i = pl.program_id(0)

    @pl.when(i == 0)
    def _():
        for j in range(4):
            w_out[j * WIDTH : (j + 1) * WIDTH, :] = w_all[jnp.bitwise_xor(info[me_at], j)]
        db_up[...] = jnp.zeros_like(db_up)

    heads = jnp.concatenate([o_0[...], o_1[...], o_2[...], o_3[...]], axis=1)
    mid = tok[...].astype(f32) + b_out[...] + dot_nn(heads, w_out[...])

    @pl.when(i == 0)
    def _():
        x2[...] = mid
        dy[...] = cot[...]

    hat, _ = normalized(mid)
    normed = (hat * gain[...] + shift[...]).astype(bf16)
    h2[...] = normed
    u = dot_nn(normed, w_up[...]) + b_up[...]
    grad_act = dot_nt(cot[...], w_down[...])
    value, slope = gelu_parts(u)
    value = value.astype(bf16)
    grad = (grad_act * slope).astype(bf16)
    act[...] = value
    du[...] = grad
    db_up[0:1, :] += jnp.sum(grad.astype(f32), axis=0, keepdims=True)
    mlp_part = dot_nn(value, w_down[...]).astype(bf16)
    dh2_part = dot_nt(grad, w_up[...]).astype(bf16)
    mlp[0] = mlp_part
    mlp_sent[0] = mlp_part
    dh2[0] = dh2_part
    dh2_sent[0] = dh2_part


def mlp(
    part, info, me_at, tokens, cotangent, o_parts, w_all, b_out, gain, shift, w_up, b_up, w_down,
    earlier,
):
    length, width = tokens.shape
    half = length // 2
    hidden = w_up.shape[1]
    owners = half // TILE

    def owner(i, info):
        return jnp.bitwise_xor(info[me_at], relative(i))

    def rows(columns):
        return pl.BlockSpec((TILE, columns), lambda i, info: (2 * owner(i, info) + part, 0))

    def packed(columns):
        return pl.BlockSpec((TILE, columns), lambda i, info: (owner(i, info), 0))

    ordered = pl.BlockSpec((1, TILE, width), lambda i, info: (i, 0, 0))
    sent = pl.BlockSpec((1, TILE, width), lambda i, info: (jnp.maximum(i - 2, 0), 0, 0))

    out = jax.ShapeDtypeStruct
    return pl.pallas_call(
        in_order(functools.partial(mlp_kernel, me_at=me_at), 14, len(earlier)),
        grid_spec=pltpu.PrefetchScalarGridSpec(
            num_scalar_prefetch=1,
            grid=(owners,),
            in_specs=[rows(width), rows(width)]
            + [head_block(at, owner) for _, at in o_parts]
            + [whole(w_all.shape)]
            + [whole((1, width))] * 3
            + [whole(w_up.shape), whole((1, hidden)), whole(w_down.shape)]
            + unread(earlier),
            out_specs=[
                whole((TILE, width)), whole((TILE, width)), packed(width), packed(hidden),
                packed(hidden), ordered, sent, ordered, sent, whole((8, hidden)),
            ],
            scratch_shapes=[pltpu.VMEM((4 * WIDTH, width), bf16)],
        ),
        out_shape=[
            out((TILE, width), f32), out((TILE, width), bf16), out((half, width), bf16),
            out((half, hidden), bf16), out((half, hidden), bf16),
        ]
        + [out((owners, TILE, width), bf16), out((2, TILE, width), bf16)] * 2
        + [out((8, hidden), f32)],
        compiler_params=params(LIMIT),
        cost_estimate=pl.CostEstimate(
            flops=20 * half * width * hidden, bytes_accessed=20 * MIB, transcendentals=0
        ),
        name="mlp",
    )(
        info, tokens, cotangent, *(part for part, _ in o_parts), w_all, b_out, gain, shift, w_up,
        b_up, w_down, *earlier
    )


def up_weights_kernel(left_a, left_b, right_a, right_b, out):
    left = jnp.concatenate([left_a[...], left_b[...]])
    right = jnp.concatenate([right_a[...], right_b[...]])
    out[...] = dot_tn(left, right).astype(bf16)


def up_weights(h2, du, filled, earlier):
    half, width = h2[0].shape
    hidden = du[0].shape[1]
    return pl.pallas_call(
        in_order(up_weights_kernel, 4, 1 + len(earlier)),
        grid=(width // TILE,),
        in_specs=[pl.BlockSpec((half, TILE), lambda i: (0, i))] * 2
        + [whole((half, hidden))] * 2
        + unread((filled,) + earlier),
        out_specs=pl.BlockSpec((TILE, hidden), lambda i: (i, 0)),
        out_shape=jax.ShapeDtypeStruct(filled.shape, bf16),
        input_output_aliases={4: 0},
        compiler_params=params(LIMIT),
        cost_estimate=pl.CostEstimate(
            flops=8 * half * width * hidden, bytes_accessed=12 * MIB, transcendentals=0
        ),
        name="up_weights",
    )(*h2, *du, filled, *earlier)


def down_weights_kernel(act_a, act_b, cot, out):
    owners = cot.shape[0] // (2 * TILE)
    rows = [cot[n * TILE : (n + 1) * TILE, :] for p in range(2) for n in range(p, 2 * owners, 2)]
    out[...] = dot_tn(
        jnp.concatenate([act_a[...], act_b[...]]), jnp.concatenate(rows)
    ).astype(bf16)


def down_weights(act, cotangent, earlier):
    half, hidden = act[0].shape
    length, width = cotangent.shape
    return pl.pallas_call(
        in_order(down_weights_kernel, 3, len(earlier)),
        grid=(hidden // TILE,),
        in_specs=[pl.BlockSpec((half, TILE), lambda i: (0, i))] * 2
        + [whole((length, width))]
        + unread(earlier),
        out_specs=pl.BlockSpec((TILE, width), lambda i: (i + width // TILE, 0)),
        out_shape=jax.ShapeDtypeStruct((width + hidden, width), bf16),
        compiler_params=params(LIMIT),
        cost_estimate=pl.CostEstimate(
            flops=8 * half * width * hidden, bytes_accessed=12 * MIB, transcendentals=0
        ),
        name="down_weights",
    )(*act, cotangent, *earlier)


def add_kernel(parts, other, out):
    out[...] = (parts[0].astype(f32) + other[0].astype(f32)).astype(bf16)


def to_give(parts, other, earlier):
    _, rows, width = parts.shape
    tile = min(rows, TILE)
    return pl.pallas_call(
        in_order(add_kernel, 2, len(earlier)),
        grid=(rows // tile,),
        in_specs=[
            pl.BlockSpec((1, tile, width), lambda i: (1, i, 0)),
            pl.BlockSpec((1, tile, width), lambda i: (1, i, 0)),
        ]
        + unread(earlier),
        out_specs=pl.BlockSpec((tile, width), lambda i: (i, 0)),
        out_shape=pltpu.HBM((rows, width), bf16),
        compiler_params=params(LIMIT),
        name="to_give",
    )(parts, other, *earlier)


def merge_kernel(parts_0, parts_1, parts_2, other_0, other_1, other_2, keep, give):
    for n, (parts, other) in enumerate(
        ((parts_0, other_0), (parts_1, other_1), (parts_2, other_2))
    ):
        keep[n] = (parts[0].astype(f32) + other[0].astype(f32)).astype(bf16)
        give[n] = (parts[1].astype(f32) + other[1].astype(f32)).astype(bf16)


def merged(parts, others, earlier):
    _, rows, width = parts[0].shape
    tile = rows // 4
    out = pltpu.HBM((3, rows, width), bf16)
    return pl.pallas_call(
        in_order(merge_kernel, 6, len(earlier)),
        grid=(rows // tile,),
        in_specs=[pl.BlockSpec((2, tile, width), lambda i: (0, i, 0))] * 6 + unread(earlier),
        out_specs=[pl.BlockSpec((3, tile, width), lambda i: (0, i, 0))] * 2,
        out_shape=[out, out],
        compiler_params=params(LIMIT),
        name="merged",
    )(*parts, *others, *earlier)


def middle_kernel(
    info, kept, other, there, x2, cot, gain, w_all, dx2, g, d_0, d_1, d_2, d_3, small, *, me_at
):
    grad = kept[0].astype(f32) + other[0].astype(f32) + there[...].astype(f32)
    hat, inverse = normalized(x2[...])
    dy = cot[...].astype(f32)
    full = dy + norm_back(hat, inverse, gain[...], grad)
    dx2[...] = full
    low = full.astype(bf16)
    g[...] = low
    small[...] = jnp.zeros_like(small)
    small[0:1, :] = jnp.sum(grad * hat, axis=0, keepdims=True)
    small[1:2, :] = jnp.sum(grad, axis=0, keepdims=True)
    small[2:3, :] = jnp.sum(low.astype(f32), axis=0, keepdims=True)
    small[3:4, :] = jnp.sum(dy, axis=0, keepdims=True)
    for j, d_j in enumerate((d_0, d_1, d_2, d_3)):
        d_j[...] = dot_nt(low, w_all[jnp.bitwise_xor(info[me_at], j)]).astype(bf16)


def middle(info, me_at, kept, other, there, x2, dy, gain, w_all, earlier):
    width = x2.shape[1]
    out = jax.ShapeDtypeStruct
    own = whole((TILE, width))
    return pl.pallas_call(
        in_order(functools.partial(middle_kernel, me_at=me_at), 8, len(earlier)),
        grid_spec=pltpu.PrefetchScalarGridSpec(
            num_scalar_prefetch=1,
            grid=(1,),
            in_specs=[
                pl.BlockSpec((1, TILE, width), lambda i, info: (0, 0, 0)),
                pl.BlockSpec((1, TILE, width), lambda i, info: (0, 0, 0)), own, own, own,
                whole((1, width)), whole(w_all.shape),
            ]
            + unread(earlier),
            out_specs=[own, own] + [whole((TILE, WIDTH))] * 4 + [whole((8, width))],
        ),
        out_shape=[pltpu.HBM((TILE, width), f32), pltpu.HBM((TILE, width), bf16)]
        + [pltpu.HBM((TILE, WIDTH), bf16)] * 4
        + [out((8, width), f32)],
        compiler_params=params(LIMIT),
        cost_estimate=pl.CostEstimate(
            flops=2 * TILE * width * width, bytes_accessed=8 * MIB, transcendentals=0
        ),
        name="middle",
    )(info, kept, other, there, x2, dy, gain, w_all, *earlier)


def out_weights_kernel(info, *refs):
    parts_a, parts_b, (g_a, g_b, kept, sent) = refs[0:4], refs[4:8], refs[8:]
    for n in range(2):
        for out, j in ((kept, 2 * n), (sent, 2 * n + 1)):
            grad = dot_tn(parts_a[j][...], g_a[...]) + dot_tn(parts_b[j][...], g_b[...])
            out[n] = grad.astype(bf16)


def out_weights(info, me_at, parts_a, parts_b, g_a, g_b):
    width = g_a.shape[1]

    def owner(i, info):
        return info[me_at]

    return pl.pallas_call(
        out_weights_kernel,
        grid_spec=pltpu.PrefetchScalarGridSpec(
            num_scalar_prefetch=1,
            grid=(1,),
            in_specs=[head_block(at, owner) for _, at in parts_a + parts_b]
            + [whole((TILE, width))] * 2,
            out_specs=[whole((2, WIDTH, width))] * 2,
        ),
        out_shape=[pltpu.HBM((2, WIDTH, width), bf16)] * 2,
        compiler_params=params(LIMIT),
        cost_estimate=pl.CostEstimate(
            flops=4 * TILE * width * width, bytes_accessed=6 * MIB, transcendentals=0
        ),
        name="out_weights",
    )(info, *(part for part, _ in parts_a + parts_b), g_a, g_b)


def attend_back_kernel(
    info, k_aug, v_aug, k_t, q_aug_t, q, v_t, o_t, lse, pad, do_0, do_1, do_2, do_3, pos, table,
    *refs, part, me_at, first,
):
    if first:
        dk_in = dv_in = None
    else:
        dk_in, dv_in, *refs = refs
    dq_out, dk, dv, q_side, do_side, q_lanes, do_lanes, dq_t = refs
    i = pl.program_id(0)
    tile = 2 * jnp.bitwise_xor(info[me_at], i) + part

    @pl.when(i == 0)
    def _():
        if first:
            dk[...] = jnp.zeros_like(dk)
            dv[...] = jnp.zeros_like(dv)
        else:
            dk[...] = dk_in[...]
            dv[...] = dv_in[...]

    here = pl.ds(pl.multiple_of(tile * TILE, TILE), TILE)
    do_here = jnp.where(
        i == 0, do_0[...], jnp.where(i == 1, do_1[...], jnp.where(i == 2, do_2[...], do_3[...]))
    )
    q_here = q[...]
    do_t = do_here.astype(f32).T
    k_here = k_t[:, here].astype(f32)
    padded = jnp.where(pad[...] != 0, 1.0, 0.0)
    row = lax.broadcasted_iota(jnp.int32, (AUG - HEAD_DIM, TILE), 0)
    lane = lax.broadcasted_iota(jnp.int32, (TILE, WIDTH), 1) // HEAD_DIM
    dk_parts, dv_parts = [], []
    for h in range(HEADS):
        feat = slice(h * HEAD_DIM, (h + 1) * HEAD_DIM)
        at = h * AUG
        q_h = q_aug_t[at : at + HEAD_DIM, :]
        do_h = do_t[feat, :]
        delta = jnp.sum(do_h * o_t[feat, :].astype(f32), axis=0, keepdims=True)
        lse_h = lse[h : h + 1, :]
        one, two, three = three_parts(-lse_h)
        extra = q_aug_t[at + HEAD_DIM : at + AUG, :].astype(f32)
        extra = jnp.where(row == 4, one, jnp.where(row == 5, two, jnp.where(row == 6, three, extra)))
        q_side[at : at + HEAD_DIM, :] = q_h
        q_side[at + HEAD_DIM : at + AUG, :] = extra.astype(bf16)
        one, two, three = three_parts(-delta)
        extra = jnp.where(row == 0, one, jnp.where(row == 1, two, jnp.where(row == 2, three, 0.0)))
        do_side[at : at + HEAD_DIM, :] = do_h.astype(bf16)
        do_side[at + HEAD_DIM : at + AUG, :] = extra.astype(bf16)
        q_lanes[h] = jnp.where(lane == h, q_here, jnp.zeros_like(q_here))
        do_lanes[h] = jnp.where(lane == h, do_here, jnp.zeros_like(do_here))
        q_h = q_h.astype(f32)
        k_h = k_here[feat, :]
        p_own = padded * jnp.exp(jnp.sum(q_h * k_h, axis=0, keepdims=True) - lse_h)
        dp_own = jnp.sum(do_h * v_t[feat, :].astype(f32), axis=0, keepdims=True)
        ds_own = p_own * (dp_own - delta)
        dq_t[feat, :] = ds_own * k_h
        dk_parts.append(ds_own * q_h)
        dv_parts.append(p_own * do_h)
    dk[here, :] += jnp.concatenate(dk_parts, axis=0).T
    dv[here, :] += jnp.concatenate(dv_parts, axis=0).T

    def step(j, _):
        keys = pl.ds(pl.multiple_of(j * TILE, TILE), TILE)
        probs, grads = [], []
        for h in range(HEADS):
            wide = slice(h * AUG, (h + 1) * AUG)
            prob = jnp.exp(dot_nn(k_aug[keys, wide], q_side[wide, :]))
            grad = prob * dot_nn(v_aug[keys, wide], do_side[wide, :])
            probs.append(prob.astype(bf16))
            grads.append(grad.astype(bf16))
        deep = (HEADS * TILE, WIDTH)
        dv[keys, :] += dot_nn(jnp.concatenate(probs, axis=1), do_lanes[...].reshape(deep))
        dk[keys, :] += dot_nn(jnp.concatenate(grads, axis=1), q_lanes[...].reshape(deep))
        for h in range(HEADS):
            feat = slice(h * HEAD_DIM, (h + 1) * HEAD_DIM)
            dq_t[feat, :] += dot_nn(k_t[feat, keys], grads[h])
        return 0

    begin, end = clip_range(info, tile, k_aug.shape[0])
    lax.fori_loop(begin, end, step, 0)
    dq = dq_t[...].T * (1.0 / math.sqrt(HEAD_DIM))
    cos, low, high = rope_factors(pos, table)
    dq_out[...] = (dq * cos - turned(dq, low, high)).astype(bf16)


def attend_back(
    part, info, me_at, k_aug, v_aug, k_t, q_aug_t, q, v_t, o_t, lse, padding, do, positions, table,
    dk, dv, earlier,
):
    length = k_aug.shape[0]
    half = length // 2

    def owner(i, info):
        return jnp.bitwise_xor(info[me_at], i)

    def rows(columns):
        return pl.BlockSpec((TILE, columns), lambda i, info: (2 * owner(i, info) + part, 0))

    def columns(count):
        return pl.BlockSpec((count, TILE), lambda i, info: (0, 2 * owner(i, info) + part))

    def packed(count):
        return pl.BlockSpec((count, TILE), lambda i, info: (0, owner(i, info)))

    out = jax.ShapeDtypeStruct
    before = () if dk is None else (dk, dv)
    return pl.pallas_call(
        in_order(
            functools.partial(attend_back_kernel, part=part, me_at=me_at, first=dk is None),
            16 + len(before), len(earlier),
        ),
        grid_spec=pltpu.PrefetchScalarGridSpec(
            num_scalar_prefetch=1,
            grid=(half // TILE,),
            in_specs=[
                whole(k_aug.shape), whole(v_aug.shape), whole(k_t.shape), columns(HEADS * AUG),
                rows(WIDTH), columns(WIDTH), packed(WIDTH), packed(8), columns(1),
            ]
            + [whole((TILE, WIDTH))] * 4
            + [
                pl.BlockSpec(
                    (3, 1, TILE), lambda i, info: (0, 0, 2 * owner(i, info) + part)
                ),
                whole(table.shape),
            ]
            + [whole((length, WIDTH))] * len(before)
            + unread(earlier),
            out_specs=[
                pl.BlockSpec((TILE, WIDTH), lambda i, info: (owner(i, info), 0)),
                whole((length, WIDTH)), whole((length, WIDTH)),
            ],
            scratch_shapes=[
                pltpu.VMEM((HEADS * AUG, TILE), bf16), pltpu.VMEM((HEADS * AUG, TILE), bf16),
                pltpu.VMEM((HEADS, TILE, WIDTH), bf16), pltpu.VMEM((HEADS, TILE, WIDTH), bf16),
                pltpu.VMEM((WIDTH, TILE), f32),
            ],
        ),
        out_shape=[out((half, WIDTH), bf16), out((length, WIDTH), f32), out((length, WIDTH), f32)],
        compiler_params=params(LIMIT),
        cost_estimate=pl.CostEstimate(
            flops=72 * half * length * WIDTH, bytes_accessed=16 * MIB, transcendentals=0
        ),
        name="attend_back",
    )(
        info, k_aug, v_aug, k_t, q_aug_t, q, v_t, o_t, lse, padding, *do, positions, table, *before,
        *earlier,
    )


def pieces(begin, count, period):
    at, end, cuts = begin, begin + count, []
    while at < end:
        length = min(end - at, period - at % period)
        cuts.append((at, length))
        at += length
    return cuts


def stacked_pairs(rows, count):
    row = lax.broadcasted_iota(jnp.int32, (count, WIDTH), 0)
    out = jnp.zeros((count, WIDTH), f32)
    for m, value in enumerate(rows):
        one, two, _ = three_parts(value)
        out = jnp.where(row == 2 * m, one, jnp.where(row == 2 * m + 1, two, out))
    return out.astype(bf16)


def late_extra(width, blocks):
    vectors = -(-(3 + 7 * width // WIDTH) // blocks)
    return vectors, -(-vectors // 8) * 16


def project_back_kernel(
    info, tok, gain, shift, dq_a, dq_b, dk, dv, pos, table, w, out_kept, out_there, early,
    dh1, dh1_sent, sums, acc, grad_b, small, w_wide,
):
    i = pl.program_id(0)

    @pl.when(i == 0)
    def _():
        acc[...] = jnp.zeros_like(acc)
        grad_b[...] = jnp.zeros_like(grad_b)
        small[...] = jnp.zeros_like(small)
        for c in range(3):
            w_wide[:, c * WIDTH : (c + 1) * WIDTH] = w[c]

    dk_here = dk[...]
    cos, low, high = rope_factors(pos, table)
    dk_low = (dk_here * cos - turned(dk_here, low, high)).astype(bf16)
    dq = jnp.concatenate([dq_a[...], dq_b[...]])
    parts = jnp.concatenate([dq, dk_low, dv[...].astype(bf16)], axis=1)
    grad = dot_nt(parts, w_wide[...])
    hat, _ = normalized(tok[...].astype(f32))
    normed = (hat * gain[...] + shift[...]).astype(bf16)
    acc[...] += dot_tn(normed, parts)
    grad_b[0:1, :] += jnp.sum(parts.astype(f32), axis=0, keepdims=True)
    small[0:1, :] += jnp.sum(grad * hat, axis=0, keepdims=True)
    small[1:2, :] += jnp.sum(grad, axis=0, keepdims=True)
    low_grad = grad.astype(bf16)
    dh1[0] = low_grad
    dh1_sent[0] = low_grad

    @pl.when(i == pl.num_programs(0) - 1)
    def _():
        width = normed.shape[1]
        blocks = sums.shape[0]

        def cut(value, count):
            return [value[:, r * WIDTH : (r + 1) * WIDTH] for r in range(count)]

        rows = cut(grad_b[0:1, :], 3) + cut(early[4:5, :], width // WIDTH)
        for ref, count in ((small, 2), (early, 4)):
            for v in range(count):
                rows += cut(ref[v : v + 1, :], width // WIDTH)
        for n in range(blocks):
            for to, rows_here, c, begin in late_places(n, blocks, width):
                here = (slice(begin, begin + rows_here), slice(c * WIDTH, (c + 1) * WIDTH))
                sums[n, to : to + rows_here, :] = acc[here].astype(bf16)
            for to, rows_here, c, begin in late_places(n, blocks, width, True):
                here = (slice(begin, begin + rows_here), slice(c * WIDTH, (c + 1) * WIDTH))
                sums[n, to : to + rows_here, :] = (
                    out_kept[here].astype(f32) + out_there[here].astype(f32)
                ).astype(bf16)
            extra_at = 4 * width // blocks
            sums[n, extra_at:, :] = stacked_pairs(rows[n::blocks], sums.shape[1] - extra_at)


def late_places(n, blocks, width, out=False):
    deep, period = (width // blocks, WIDTH) if out else (3 * width // blocks, width)
    first = 3 * width // blocks if out else 0
    return [
        (first + at - n * deep, length, at // period, at % period)
        for at, length in pieces(n * deep, deep, period)
    ]


def project_back(
    info, me_at, tokens, gain, shift, dq_a, dq_b, dk, dv, positions, table, w, kept, there, early,
    blocks, earlier,
):
    length, width = tokens.shape
    share = 2 * TILE

    def owner(i, info):
        return jnp.bitwise_xor(info[me_at], relative(i))

    def rows(count, columns):
        return pl.BlockSpec((count, columns), lambda i, info: (owner(i, info), 0))

    last = pl.BlockSpec((None, TILE, width), lambda i, info: (2, 0, 0))
    out = jax.ShapeDtypeStruct
    sums = (blocks, 4 * width // blocks + late_extra(width, blocks)[1], WIDTH)
    return pl.pallas_call(
        in_order(project_back_kernel, 14, len(earlier)),
        grid_spec=pltpu.PrefetchScalarGridSpec(
            num_scalar_prefetch=1,
            grid=(length // share,),
            in_specs=[
                rows(share, width), whole((1, width)), whole((1, width)), rows(TILE, WIDTH),
                rows(TILE, WIDTH), rows(share, WIDTH), rows(share, WIDTH),
                pl.BlockSpec((3, 1, share), lambda i, info: (0, 0, owner(i, info))),
                whole(table.shape), whole(w.shape), last, last, whole(early.shape),
            ]
            + unread(earlier),
            out_specs=[
                pl.BlockSpec((1, share, width), lambda i, info: (i, 0, 0)),
                pl.BlockSpec((1, share, width), lambda i, info: (jnp.maximum(i - 2, 0), 0, 0)),
                whole(sums),
            ],
            scratch_shapes=[
                pltpu.VMEM((width, 3 * WIDTH), f32), pltpu.VMEM((8, 3 * WIDTH), f32),
                pltpu.VMEM((8, width), f32),
                pltpu.VMEM((width, 3 * WIDTH), bf16),
            ],
        ),
        out_shape=[
            pltpu.HBM((4, share, width), bf16), pltpu.HBM((2, share, width), bf16),
            pltpu.HBM(sums, bf16),
        ],
        compiler_params=params(LIMIT),
        cost_estimate=pl.CostEstimate(
            flops=24 * length * width * WIDTH, bytes_accessed=20 * MIB, transcendentals=0
        ),
        name="project_back",
    )(info, tokens, gain, shift, dq_a, dq_b, dk, dv, positions, table, w, kept, there, early, *earlier)


def vectors_kernel(extra, grad_b, vectors):
    blocks = extra.shape[0]
    width = vectors.shape[1]
    grad_b[...] = jnp.zeros_like(grad_b)
    vectors[...] = jnp.zeros_like(vectors)
    for v in range(3 + 7 * width // WIDTH):
        n, m = v % blocks, v // blocks
        pair = extra[n].astype(f32)
        row = pair[2 * m : 2 * m + 1, :] + pair[2 * m + 1 : 2 * m + 2, :]
        if v < 3:
            grad_b[v : v + 1, :] = row
        else:
            to, at = divmod((v - 3) * WIDTH, width)
            vectors[to : to + 1, at : at + WIDTH] = row


def unpack_vectors(sums, width):
    blocks = sums.shape[0]
    at, rows = 4 * width // blocks, late_extra(width, blocks)[1]
    return pl.pallas_call(
        vectors_kernel,
        grid=(1,),
        in_specs=[pl.BlockSpec((blocks, rows, WIDTH), lambda i: (0, at // rows, 0))],
        out_specs=[whole((8, WIDTH)), whole((8, width))],
        out_shape=[pltpu.HBM((8, WIDTH), f32), pltpu.HBM((8, width), f32)],
        compiler_params=params(LIMIT),
        name="unpack_vectors",
    )(sums)


def unpack_kernel(sums, grad_qkv, grad_out):
    blocks = sums.shape[0]
    width = grad_out.shape[1]
    for n in range(blocks):
        for to, rows, c, begin in late_places(n, blocks, width):
            grad_qkv[c, begin : begin + rows, :] = sums[n, to : to + rows, :].astype(f32)
        for to, rows, c, begin in late_places(n, blocks, width, True):
            grad_out[begin : begin + rows, c * WIDTH : (c + 1) * WIDTH] = sums[
                n, to : to + rows, :
            ].astype(f32)


def unpack(sums, width, earlier):
    out = jax.ShapeDtypeStruct
    return pl.pallas_call(
        in_order(unpack_kernel, 1, len(earlier)),
        in_specs=[pl.BlockSpec(memory_space=pltpu.VMEM)] + unread(earlier),
        out_specs=[pl.BlockSpec(memory_space=pltpu.VMEM)] * 2,
        out_shape=[out((3, width, WIDTH), f32), out((WIDTH, width), f32)],
        compiler_params=pltpu.CompilerParams(vmem_limit_bytes=LIMIT * MIB),
        name="unpack",
    )(sums, *earlier)


def finish_kernel(info, parts, other, there, tok, gain, dx2_a, dx2_b, out):
    grad = parts[0].astype(f32) + other[0].astype(f32) + there[...].astype(f32)
    hat, inverse = normalized(tok[...].astype(f32))
    dx2 = jnp.where(pl.program_id(0) == 0, dx2_a[...], dx2_b[...])
    out[...] = dx2 + norm_back(hat, inverse, gain[...], grad)


def finish(info, me_at, parts, other, there, tokens, gain, dx2_a, dx2_b):
    width = tokens.shape[1]
    share = there.shape[0]
    rows = pl.BlockSpec((TILE, width), lambda i, info: (i, 0))
    return pl.pallas_call(
        finish_kernel,
        grid_spec=pltpu.PrefetchScalarGridSpec(
            num_scalar_prefetch=1,
            grid=(share // TILE,),
            in_specs=[
                pl.BlockSpec((1, TILE, width), lambda i, info: (0, i, 0)),
                pl.BlockSpec((1, TILE, width), lambda i, info: (0, i, 0)), rows,
                pl.BlockSpec((TILE, width), lambda i, info: (2 * info[me_at] + i, 0)),
                whole((1, width)), whole((TILE, width)), whole((TILE, width)),
            ],
            out_specs=rows,
        ),
        out_shape=jax.ShapeDtypeStruct((share, width), f32),
        compiler_params=params(LIMIT),
        cost_estimate=pl.CostEstimate(
            flops=30 * share * width, bytes_accessed=10 * MIB, transcendentals=0
        ),
        name="finish",
    )(info, parts, other, there, tokens, gain, dx2_a, dx2_b)


def total_of(blocks):
    total = blocks[0].astype(f32)
    for n in range(1, blocks.shape[0]):
        total += blocks[n].astype(f32)
    return total.astype(bf16)


def sum_kernel(blocks, out):
    out[...] = total_of(blocks)


def summed(blocks, steps, earlier):
    count, rows, width = blocks.shape
    tile = rows // steps
    return pl.pallas_call(
        in_order(sum_kernel, 1, len(earlier)),
        grid=(steps,),
        in_specs=[pl.BlockSpec((count, tile, width), lambda i: (0, i, 0))] + unread(earlier),
        out_specs=pl.BlockSpec((tile, width), lambda i: (i, 0)),
        out_shape=pltpu.HBM((rows, width), bf16),
        compiler_params=params(LIMIT),
        name="summed",
    )(blocks, *earlier)


def copies_kernel(first, second, out):
    total = (first[...].astype(f32) + second[...].astype(f32)).astype(bf16)
    for n in range(out.shape[0]):
        out[n] = total


def sum_copies(first, second, count, earlier):
    rows, width = first.shape
    return pl.pallas_call(
        in_order(copies_kernel, 2, len(earlier)),
        grid=(1,),
        in_specs=[whole((rows, width))] * 2 + unread(earlier),
        out_specs=whole((count, rows, width)),
        out_shape=pltpu.HBM((count, rows, width), bf16),
        compiler_params=params(LIMIT),
        name="sum_copies",
    )(first, second, *earlier)


def swap(array, axis, bit=1):
    size = lax.axis_size(axis)
    if size == 1:
        return jnp.zeros_like(array)
    return lax.ppermute(array, axis, [(i, i ^ bit) for i in range(size)])


def swap_both(array):
    return lax.ppermute(array, MP, [(i, i ^ 3) for i in range(4)])


def scattered(rows, axes):
    group = lax.axis_size(axes)
    length, width = rows.shape
    return lax.all_to_all(
        rows.reshape(group, length // group, width), axes, 0, 0, tiled=True
    )


def both_sums(total):
    if lax.axis_size("zl") == 1:
        return total
    return (total.astype(f32) + swap(total, "zl").astype(f32)).astype(bf16)


def local(
    tokens, cotangent, segments, padding, positions, ln1_gain, ln1_bias, w_qkv, b_qkv, w_out, b_out,
    ln2_gain, ln2_bias, w_up, b_up, w_down, b_down,
):
    width, hidden = w_up.shape
    w_all = lax.all_gather(w_out, MP)
    gain_one, shift_one = ln1_gain[None], ln1_bias[None]
    gain_two, shift_two = ln2_gain[None], ln2_bias[None]
    ends = jnp.sum((segments <= jnp.arange(2)[:, None]).astype(jnp.int32), axis=1)
    info = jnp.concatenate([ends, lax.axis_index(MP)[None].astype(jnp.int32)])
    me_at = 2
    table = jnp.asarray(rope_constants())
    k_aug, v_aug, q_aug_t, q, k_t, v_t = project(
        tokens, w_qkv, b_qkv, gain_one, shift_one, positions, segments, padding, table
    )

    def exchanged(own, to_c, to_zh, to_both):
        return own, swap(to_c, "c"), swap(to_zh, "zh"), swap_both(to_both)

    o_0, o_t_0, lse_0 = attend(0, info, k_aug, v_t, q_aug_t, k_t, padding, ())
    o_zh_0, o_c_0 = swap(o_0, "zh"), swap(o_0, "c")
    o_1, o_t_1, lse_1 = attend(1, info, k_aug, v_t, q_aug_t, k_t, padding, (o_0, w_all))
    o_zh_1 = swap(o_1, "zh")
    o_zh_0 = after(o_zh_0, (o_1,))
    o_parts_0 = tuple((part, None) for part in (o_0, o_c_0, o_zh_0, swap(o_zh_0, "c")))

    def mlp_half(part, o_parts, earlier):
        return mlp(
            part, info, me_at, tokens, cotangent, o_parts, w_all, b_out[None], gain_two, shift_two,
            w_up, b_up[None], w_down, earlier,
        )

    x2_0, dy_0, h2_0, act_0, du_0, mlp_0, mlp_sent_0, dh2_0, sent, db_0 = mlp_half(
        0, o_parts_0, (o_1,)
    )
    pair = paired(o_1, o_zh_1, (x2_0,))
    pair_c = swap(pair, "c")
    o_parts_1 = ((pair, 0), (pair_c, 0), (pair, 1), (pair_c, 1))
    other_0 = swap(sent, "c")
    give_0 = to_give(dh2_0, other_0, ())
    there_0 = swap(give_0, "zh")
    x2_1, dy_1, h2_1, act_1, du_1, mlp_1, mlp_sent_1, dh2_1, sent, db_1 = mlp_half(
        1, o_parts_1, (give_0,)
    )
    other_1 = swap(sent, "c")
    grad_mlp = down_weights((act_0, act_1), cotangent, ())
    give_1 = to_give(dh2_1, other_1, (grad_mlp,))
    there_1 = swap(give_1, "zh")
    grad_mlp = up_weights((h2_0, h2_1), (du_0, du_1), grad_mlp, (give_1,))
    arrived = scattered(grad_mlp, ("y", "x"))
    dx2_0, g_0, *d_0, small_0 = middle(
        info, me_at, dh2_0, other_0, there_0, x2_0, dy_0, gain_two, w_all, (grad_mlp,)
    )
    do_0 = exchanged(*d_0)
    dx2_1, g_1, *d_1, small_1 = middle(
        info, me_at, dh2_1, other_1, there_1, x2_1, dy_1, gain_two, w_all, (g_0,)
    )
    do_1 = exchanged(*d_1)
    grad_out, out_sent = out_weights(info, me_at, o_parts_0, o_parts_1, g_0, g_1)

    mixed_parts = (mlp_0, mlp_1, grad_out)
    others = [swap(parts, "c") for parts in (mlp_sent_0, mlp_sent_1, out_sent)]
    dq_0, dk, dv = attend_back(
        0, info, me_at, k_aug, v_aug, k_t, q_aug_t, q, v_t, o_t_0, lse_0, padding, do_0, positions,
        table, None, None, (grad_out, g_1),
    )
    keep, give = merged(mixed_parts, others, (dq_0,))
    there = swap(give, "zh")
    dq_1, dk, dv = attend_back(
        1, info, me_at, k_aug, v_aug, k_t, q_aug_t, q, v_t, o_t_1, lse_1, padding, do_1, positions,
        table, dk, dv, (give, dq_0),
    )
    part_sum = summed(arrived, 2, (dq_1,))
    early = jnp.concatenate([(small_0 + small_1)[0:4], (db_0 + db_1)[0:4]])
    dh1, sent, sums = project_back(
        info, me_at, tokens, gain_one, shift_one, dq_0, dq_1, dk, dv, positions, table, w_qkv, keep,
        there, early, lax.axis_size(("y", "x")), (part_sum,),
    )
    grad_mlp = lax.all_gather(both_sums(part_sum), ("y", "x"), axis=0, tiled=True)
    other = swap(sent, "c")
    back = swap(to_give(dh1, other, (sums,)), "zh")
    arrived = scattered(sums.reshape(-1, WIDTH), ("y", "x"))
    total = summed(arrived, 1, (back,))
    late = lax.all_to_all(
        sum_copies(total, swap(total, "zl"), sums.shape[0], ()), ("y", "x"), 0, 0, tiled=True
    )
    grad_inputs = finish(info, me_at, dh1, other, back, tokens, gain_one, dx2_0, dx2_1)
    received = (keep[:2].astype(f32) + there[:2].astype(f32)).reshape(2 * TILE, width)
    mixed = (jnp.concatenate([x2_0, x2_1]) + received + b_down[None]).astype(bf16)
    grad_mlp = grad_mlp.reshape(2, width, hidden).astype(f32)
    grad_up, grad_down = grad_mlp[0], grad_mlp[1]
    grad_b, vectors = unpack_vectors(late, width)
    by_c, by_zh, by_both = swap(vectors, "c"), swap(vectors, "zh"), swap_both(vectors)
    grad_qkv, grad_w_out = unpack(
        late, width, (grad_inputs, mixed, grad_up, grad_down, vectors)
    )
    group = (vectors + by_c) + (by_zh + by_both)
    return (
        mixed, grad_inputs, group[1], group[2], grad_qkv, grad_b[0:3], grad_w_out, group[5],
        group[3], group[4], grad_up, vectors[0], grad_down, group[6],
    )


def solution(mesh):
    packs = mesh.shape["dp"]
    if packs == 32:
        shape = (2, 4, 4, 2, 2)
    else:
        shape = (1, packs, 1, 2, 2)
    split = Mesh(mesh.devices.reshape(shape), EVERY)
    in_specs = (
        P(DP, None), P(DP, None), P(DP, None), P(DP, None), P(None, DP, None), P(), P(),
        P(None, None, MP), P(None, MP), P(MP, None), P(), P(), P(), P(None, MP), P(MP),
        P(MP, None), P(),
    )
    out_specs = (
        P(EVERY, None), P(EVERY, None), P(), P(), P(None, None, MP), P(None, MP), P(MP, None), P(),
        P(), P(), P(None, MP), P(MP), P(MP, None), P(),
    )
    return jax.shard_map(local, mesh=split, in_specs=in_specs, out_specs=out_specs, check_vma=False)
```

```python
import functools
import math

import jax
import jax.numpy as jnp
import ml_dtypes
import numpy as np
from jax import lax
from jax.experimental import pallas as pl
from jax.experimental.pallas import tpu as pltpu
from jax.sharding import Mesh
from jax.sharding import PartitionSpec as P

HEAD_DIM = 64
HEADS = 4
WIDTH = HEADS * HEAD_DIM
AUG = 128
TILE = 256
PLACES = 64
LIMIT = 64
MIB = 1 << 20
DP = ("zl", "y", "x")
MP = ("zh", "c")
EVERY = ("zl", "y", "x", "zh", "c")

epsilon = 1e-06
NEG = -1e30
bf16 = jnp.bfloat16
f32 = jnp.float32


def dot_nn(a, b):
    return lax.dot_general(a, b, (((1,), (0,)), ((), ())), preferred_element_type=f32)


def dot_nt(a, b):
    return lax.dot_general(a, b, (((1,), (1,)), ((), ())), preferred_element_type=f32)


def dot_tn(a, b):
    return lax.dot_general(a, b, (((0,), (0,)), ((), ())), preferred_element_type=f32)


def normalized(values):
    center = jnp.mean(values, axis=-1, keepdims=True)
    shifted = values - center
    spread = jnp.mean(shifted * shifted, axis=-1, keepdims=True)
    inverse = lax.rsqrt(spread + epsilon)
    return shifted * inverse, inverse


def norm_back(hat, inverse, gain, grad):
    scaled = grad * gain
    return inverse * (
        scaled
        - jnp.mean(scaled, axis=-1, keepdims=True)
        - hat * jnp.mean(scaled * hat, axis=-1, keepdims=True)
    )


def turned(x, low, high):
    width = x.shape[1]
    pair = HEAD_DIM // 6
    return pltpu.roll(x, width - pair, 1) * low + pltpu.roll(x, pair, 1) * high


def three_parts(x):
    first = x.astype(bf16).astype(f32)
    rest = x - first
    second = rest.astype(bf16).astype(f32)
    return first, second, rest - second


def params(limit, axes=1):
    return pltpu.CompilerParams(
        dimension_semantics=("arbitrary",) * axes, vmem_limit_bytes=limit * MIB
    )


def in_order(kernel, inputs, earlier):
    def run(*refs):
        kernel(*refs[:inputs], *refs[inputs + earlier :])

    return run


def unread(arrays):
    return [pl.BlockSpec(memory_space=pl.ANY)] * len(arrays)


def whole(shape):
    return pl.BlockSpec(shape, lambda *_: (0,) * len(shape))


def clip_range(info, tile, length):
    first, second = info[0], info[1]
    at = tile * TILE
    begin = jnp.where(second <= at, second, jnp.where(first <= at, first, 0))
    end = jnp.where(
        first >= at + TILE, first, jnp.where(second >= at + TILE, second, length)
    )
    return begin // TILE, (end + TILE - 1) // TILE


def rope_constants():
    pair = HEAD_DIM // 6
    feature = np.arange(WIDTH) % HEAD_DIM
    section, place = feature // (2 * pair), feature % (2 * pair)
    frequency = np.exp(-math.log(10000.0) * (place % pair) / pair)
    table = np.zeros((PLACES, 3, WIDTH))
    for s in range(3):
        for value in range(16):
            angle = value * frequency
            turns = section == s
            table[s * 16 + value, 0] = np.where(turns, np.cos(angle), 0.0)
            table[s * 16 + value, 1] = np.where(turns & (place < pair), -np.sin(angle), 0.0)
            table[s * 16 + value, 2] = np.where(turns & (place >= pair), np.sin(angle), 0.0)
    table[48, 0] = section == 3
    rest = table.reshape(PLACES, 3 * WIDTH).astype(np.float32)
    parts = []
    for _ in range(3):
        part = rest.astype(ml_dtypes.bfloat16)
        parts.append(part)
        rest = rest - part.astype(np.float32)
    return np.concatenate(parts)


def rope_factors(positions, table):
    row = lax.broadcasted_iota(jnp.int32, (PLACES, positions.shape[-1]), 0)
    where = jnp.where(
        row < 16, positions[0], jnp.where(row < 32, positions[1], positions[2])
    )
    hit = ((where == row % 16) & (row < 48)) | (row == 48)
    hit = jnp.where(hit, 1.0, 0.0)
    hits = jnp.concatenate([hit, hit, hit]).astype(bf16)
    factors = dot_tn(hits, table[...])
    return factors[:, :WIDTH], factors[:, WIDTH : 2 * WIDTH], factors[:, 2 * WIDTH :]


def qkv_kernel(
    tok, w, b, gain, shift, pos, seg, pad, table, k_aug, v_aug, q_aug_t, q_out, k_t, v_t, w_wide
):
    @pl.when(pl.program_id(0) == 0)
    def _():
        for c in range(3):
            w_wide[:, c * WIDTH : (c + 1) * WIDTH] = w[c]

    hat, _ = normalized(tok[...].astype(f32))
    normed = (hat * gain[...] + shift[...]).astype(bf16)
    cos, low, high = rope_factors(pos, table)
    all_three = dot_nn(normed, w_wide[...])
    q = all_three[:, :WIDTH] + b[0:1, :]
    k = all_three[:, WIDTH : 2 * WIDTH] + b[1:2, :]
    v = all_three[:, 2 * WIDTH :] + b[2:3, :]
    q = (q * cos + turned(q, low, high)) * (1.0 / math.sqrt(HEAD_DIM))
    k = k * cos + turned(k, low, high)
    q_out[...] = q.astype(bf16)
    q_t = q.T.astype(bf16)
    k_t[...] = k.T.astype(bf16)
    v_t[...] = v.T.astype(bf16)
    row = lax.broadcasted_iota(jnp.int32, (HEAD_DIM, TILE), 0)
    clip = seg[...]
    same = (row >= 1) & (row < 4) & (clip == row - 1)
    mask = jnp.where((row >= 1) & (row < 4) & (clip != row - 1), NEG, 0.0)
    mask = jnp.where(row == 0, jnp.where(pad[...] != 0, NEG, 0.0), mask)
    k_extra = jnp.where((row >= 4) & (row < 7), 1.0, mask)
    q_extra = jnp.where(same | (row == 0), 1.0, 0.0).astype(bf16)
    k_side = jnp.concatenate([jnp.zeros((HEAD_DIM, TILE), f32), k_extra]).T
    lane = lax.broadcasted_iota(jnp.int32, (TILE, AUG), 1)
    ones = jnp.where((lane >= HEAD_DIM) & (lane < HEAD_DIM + 3), 1.0, 0.0)
    for h in range(HEADS):
        pair = slice(h // 2 * AUG, h // 2 * AUG + AUG)
        wide = slice(h * AUG, (h + 1) * AUG)
        k_pair, v_pair = k[:, pair], v[:, pair]
        if h % 2:
            k_pair, v_pair = pltpu.roll(k_pair, HEAD_DIM, 1), pltpu.roll(v_pair, HEAD_DIM, 1)
        k_aug[:, wide] = jnp.where(lane < HEAD_DIM, k_pair, k_side).astype(bf16)
        v_aug[:, wide] = jnp.where(lane < HEAD_DIM, v_pair, ones).astype(bf16)
        q_aug_t[h * AUG : h * AUG + HEAD_DIM, :] = q_t[h * HEAD_DIM : (h + 1) * HEAD_DIM, :]
        q_aug_t[h * AUG + HEAD_DIM : (h + 1) * AUG, :] = q_extra


def project(tokens, w, b, gain, shift, positions, segments, padding, table):
    length, width = tokens.shape
    tiles = length // TILE

    def rows(columns):
        return pl.BlockSpec((TILE, columns), lambda i: (i, 0))

    def columns(count):
        return pl.BlockSpec((count, TILE), lambda i: (0, i))

    out = jax.ShapeDtypeStruct
    wide = out((length, HEADS * AUG), bf16)
    flat = out((WIDTH, length), bf16)
    return pl.pallas_call(
        qkv_kernel,
        grid=(tiles,),
        in_specs=[
            rows(width), whole(w.shape), whole(b.shape), whole((1, width)), whole((1, width)),
            pl.BlockSpec((3, 1, TILE), lambda i: (0, 0, i)), columns(1), columns(1), whole(table.shape),
        ],
        out_specs=[
            rows(HEADS * AUG), rows(HEADS * AUG), columns(HEADS * AUG), rows(WIDTH), columns(WIDTH),
            columns(WIDTH),
        ],
        out_shape=[
            wide, wide, out((HEADS * AUG, length), bf16), out((length, WIDTH), bf16), flat, flat,
        ],
        scratch_shapes=[pltpu.VMEM((width, 3 * WIDTH), bf16)],
        compiler_params=params(LIMIT),
        cost_estimate=pl.CostEstimate(
            flops=6 * length * width * WIDTH, bytes_accessed=20 * MIB, transcendentals=0
        ),
        name="project",
    )(tokens, w, b, gain, shift, positions, segments, padding, table)


def attend_kernel(info, k_aug, v_t, q_aug_t, k_t, pad, o, o_t, lse, top, total, acc, *, part):
    tile = 2 * pl.program_id(0) + part
    padded = pad[...] != 0
    for h in range(HEADS):
        q_h = q_aug_t[h * AUG : h * AUG + HEAD_DIM, :].astype(f32)
        k_h = k_t[h * HEAD_DIM : (h + 1) * HEAD_DIM, :].astype(f32)
        own = jnp.sum(q_h * k_h, axis=0, keepdims=True)
        top[h : h + 1, :] = jnp.where(padded, own, -3e38)
        total[h : h + 1, :] = jnp.where(padded, 1.0, 0.0)
    here = pl.ds(pl.multiple_of(tile * TILE, TILE), TILE)
    acc[...] = jnp.where(padded, v_t[:, here].astype(f32), 0.0)
    feats = [slice(h * HEAD_DIM, (h + 1) * HEAD_DIM) for h in range(HEADS)]
    wides = [slice(h * AUG, (h + 1) * AUG) for h in range(HEADS)]

    def step(j, count):
        keys = pl.ds(pl.multiple_of(j * TILE, TILE), count * TILE)
        scores = [dot_nn(k_aug[keys, wide], q_aug_t[wide, :]) for wide in wides]
        probs, fades = [], []
        for h in range(HEADS):
            old = top[h : h + 1, :]
            new = jnp.maximum(old, jnp.max(scores[h], axis=0, keepdims=True))
            prob = jnp.exp(scores[h] - new)
            fade = jnp.exp(old - new)
            top[h : h + 1, :] = new
            total[h : h + 1, :] = total[h : h + 1, :] * fade + jnp.sum(prob, axis=0, keepdims=True)
            probs.append(prob.astype(bf16))
            fades.append(fade)
        for h, feat in enumerate(feats):
            acc[feat, :] = acc[feat, :] * fades[h] + dot_nn(v_t[feat, keys], probs[h])

    begin, end = clip_range(info, tile, k_aug.shape[0])
    pairs = (end - begin) // 2

    def two(n, _):
        step(begin + 2 * n, 2)
        return 0

    lax.fori_loop(0, pairs, two, 0)

    @pl.when(begin + 2 * pairs < end)
    def _():
        step(end - 1, 1)

    for h, feat in enumerate(feats):
        acc[feat, :] = acc[feat, :] / total[h : h + 1, :]
    lse[...] = jnp.zeros_like(lse)
    lse[0:HEADS, :] = top[0:HEADS, :] + jnp.log(total[0:HEADS, :])
    turned_o = acc[...]
    o_t[...] = turned_o.astype(bf16)
    o[...] = turned_o.T.astype(bf16)


def attend(part, info, k_aug, v_t, q_aug_t, k_t, padding, earlier):
    length = k_aug.shape[0]
    half = length // 2

    def columns(count):
        return pl.BlockSpec((count, TILE), lambda i, *_: (0, 2 * i + part))

    def packed(count):
        return pl.BlockSpec((count, TILE), lambda i, *_: (0, i))

    out = jax.ShapeDtypeStruct
    return pl.pallas_call(
        in_order(functools.partial(attend_kernel, part=part), 6, len(earlier)),
        grid_spec=pltpu.PrefetchScalarGridSpec(
            num_scalar_prefetch=1,
            grid=(half // TILE,),
            in_specs=[
                whole(k_aug.shape), whole(v_t.shape), columns(HEADS * AUG), columns(WIDTH),
                columns(1),
            ]
            + unread(earlier),
            out_specs=[
                pl.BlockSpec((TILE, WIDTH), lambda i, *_: (i, 0)), packed(WIDTH), packed(8),
            ],
            scratch_shapes=[
                pltpu.VMEM((8, TILE), f32), pltpu.VMEM((8, TILE), f32), pltpu.VMEM((WIDTH, TILE), f32),
            ],
        ),
        out_shape=[out((half, WIDTH), bf16), out((WIDTH, half), bf16), out((8, half), f32)],
        compiler_params=params(LIMIT),
        cost_estimate=pl.CostEstimate(
            flops=24 * half * length * WIDTH, bytes_accessed=6 * MIB, transcendentals=0
        ),
        name="attend",
    )(info, k_aug, v_t, q_aug_t, k_t, padding, *earlier)


def nothing(*refs):
    del refs


def after(value, earlier):
    return pl.pallas_call(
        nothing,
        in_specs=unread((value,) + earlier),
        out_specs=pl.BlockSpec(memory_space=pl.ANY),
        out_shape=jax.ShapeDtypeStruct(value.shape, value.dtype),
        input_output_aliases={0: 0},
        name="after",
    )(value, *earlier)


def pair_kernel(first, second, out):
    out[0] = first[...]
    out[1] = second[...]


def paired(first, second, earlier):
    shape = (2,) + first.shape
    return pl.pallas_call(
        in_order(pair_kernel, 2, len(earlier)),
        in_specs=[pl.BlockSpec(memory_space=pltpu.VMEM)] * 2 + unread(earlier),
        out_specs=pl.BlockSpec(memory_space=pltpu.VMEM),
        out_shape=jax.ShapeDtypeStruct(shape, first.dtype),
        name="paired",
    )(first, second, *earlier)


def head_block(at, owner):
    if at is None:
        return pl.BlockSpec((TILE, WIDTH), lambda i, info: (owner(i, info), 0))
    return pl.BlockSpec((None, TILE, WIDTH), lambda i, info: (at, owner(i, info), 0))


def relative(i):
    return i % 2 * 2 + i // 2


def gelu_parts(u):
    size = jnp.abs(u)
    t = 1.0 / (1.0 + (0.3275911 / math.sqrt(2.0)) * size)
    bell = jnp.exp(-0.5 * (u * u))
    poly = 0.5 * 1.061405429
    for c in (-1.453152027, 1.421413741, -0.284496736, 0.254829592):
        poly = poly * t + 0.5 * c
    tail = poly * t * bell
    below = jnp.where(u >= 0, 1.0 - tail, tail)
    return u * below, below + u * bell * (1.0 / math.sqrt(2.0 * math.pi))


def mlp_kernel(
    info, tok, cot, o_0, o_1, o_2, o_3, w_all, b_out, gain, shift, w_up, b_up, w_down,
    x2, dy, h2, act, du, mlp, mlp_sent, dh2, dh2_sent, db_up, w_out, *, me_at,
):
    i = pl.program_id(0)

    @pl.when(i == 0)
    def _():
        for j in range(4):
            w_out[j * WIDTH : (j + 1) * WIDTH, :] = w_all[jnp.bitwise_xor(info[me_at], j)]
        db_up[...] = jnp.zeros_like(db_up)

    heads = jnp.concatenate([o_0[...], o_1[...], o_2[...], o_3[...]], axis=1)
    mid = tok[...].astype(f32) + b_out[...] + dot_nn(heads, w_out[...])

    @pl.when(i == 0)
    def _():
        x2[...] = mid
        dy[...] = cot[...]

    hat, _ = normalized(mid)
    normed = (hat * gain[...] + shift[...]).astype(bf16)
    h2[...] = normed
    u = dot_nn(normed, w_up[...]) + b_up[...]
    grad_act = dot_nt(cot[...], w_down[...])
    value, slope = gelu_parts(u)
    value = value.astype(bf16)
    grad = (grad_act * slope).astype(bf16)
    act[...] = value
    du[...] = grad
    db_up[0:1, :] += jnp.sum(grad.astype(f32), axis=0, keepdims=True)
    mlp_part = dot_nn(value, w_down[...]).astype(bf16)
    dh2_part = dot_nt(grad, w_up[...]).astype(bf16)
    mlp[0] = mlp_part
    mlp_sent[0] = mlp_part
    dh2[0] = dh2_part
    dh2_sent[0] = dh2_part


def mlp(
    part, info, me_at, tokens, cotangent, o_parts, w_all, b_out, gain, shift, w_up, b_up, w_down,
    earlier,
):
    length, width = tokens.shape
    half = length // 2
    hidden = w_up.shape[1]
    owners = half // TILE

    def owner(i, info):
        return jnp.bitwise_xor(info[me_at], relative(i))

    def rows(columns):
        return pl.BlockSpec((TILE, columns), lambda i, info: (2 * owner(i, info) + part, 0))

    def packed(columns):
        return pl.BlockSpec((TILE, columns), lambda i, info: (owner(i, info), 0))

    ordered = pl.BlockSpec((1, TILE, width), lambda i, info: (i, 0, 0))
    sent = pl.BlockSpec((1, TILE, width), lambda i, info: (jnp.maximum(i - 2, 0), 0, 0))

    out = jax.ShapeDtypeStruct
    return pl.pallas_call(
        in_order(functools.partial(mlp_kernel, me_at=me_at), 14, len(earlier)),
        grid_spec=pltpu.PrefetchScalarGridSpec(
            num_scalar_prefetch=1,
            grid=(owners,),
            in_specs=[rows(width), rows(width)]
            + [head_block(at, owner) for _, at in o_parts]
            + [whole(w_all.shape)]
            + [whole((1, width))] * 3
            + [whole(w_up.shape), whole((1, hidden)), whole(w_down.shape)]
            + unread(earlier),
            out_specs=[
                whole((TILE, width)), whole((TILE, width)), packed(width), packed(hidden),
                packed(hidden), ordered, sent, ordered, sent, whole((8, hidden)),
            ],
            scratch_shapes=[pltpu.VMEM((4 * WIDTH, width), bf16)],
        ),
        out_shape=[
            out((TILE, width), f32), out((TILE, width), bf16), out((half, width), bf16),
            out((half, hidden), bf16), out((half, hidden), bf16),
        ]
        + [out((owners, TILE, width), bf16), out((2, TILE, width), bf16)] * 2
        + [out((8, hidden), f32)],
        compiler_params=params(LIMIT),
        cost_estimate=pl.CostEstimate(
            flops=20 * half * width * hidden, bytes_accessed=20 * MIB, transcendentals=0
        ),
        name="mlp",
    )(
        info, tokens, cotangent, *(part for part, _ in o_parts), w_all, b_out, gain, shift, w_up,
        b_up, w_down, *earlier
    )


def up_weights_kernel(left_a, left_b, right_a, right_b, out):
    left = jnp.concatenate([left_a[...], left_b[...]])
    right = jnp.concatenate([right_a[...], right_b[...]])
    out[...] = dot_tn(left, right).astype(bf16)


def up_weights(h2, du, filled, earlier):
    half, width = h2[0].shape
    hidden = du[0].shape[1]
    return pl.pallas_call(
        in_order(up_weights_kernel, 4, 1 + len(earlier)),
        grid=(width // TILE,),
        in_specs=[pl.BlockSpec((half, TILE), lambda i: (0, i))] * 2
        + [whole((half, hidden))] * 2
        + unread((filled,) + earlier),
        out_specs=pl.BlockSpec((TILE, hidden), lambda i: (i, 0)),
        out_shape=jax.ShapeDtypeStruct(filled.shape, bf16),
        input_output_aliases={4: 0},
        compiler_params=params(LIMIT),
        cost_estimate=pl.CostEstimate(
            flops=8 * half * width * hidden, bytes_accessed=12 * MIB, transcendentals=0
        ),
        name="up_weights",
    )(*h2, *du, filled, *earlier)


def down_weights_kernel(act_a, act_b, cot, out):
    owners = cot.shape[0] // (2 * TILE)
    rows = [cot[n * TILE : (n + 1) * TILE, :] for p in range(2) for n in range(p, 2 * owners, 2)]
    out[...] = dot_tn(
        jnp.concatenate([act_a[...], act_b[...]]), jnp.concatenate(rows)
    ).astype(bf16)


def down_weights(act, cotangent, earlier):
    half, hidden = act[0].shape
    length, width = cotangent.shape
    return pl.pallas_call(
        in_order(down_weights_kernel, 3, len(earlier)),
        grid=(hidden // TILE,),
        in_specs=[pl.BlockSpec((half, TILE), lambda i: (0, i))] * 2
        + [whole((length, width))]
        + unread(earlier),
        out_specs=pl.BlockSpec((TILE, width), lambda i: (i + width // TILE, 0)),
        out_shape=jax.ShapeDtypeStruct((width + hidden, width), bf16),
        compiler_params=params(LIMIT),
        cost_estimate=pl.CostEstimate(
            flops=8 * half * width * hidden, bytes_accessed=12 * MIB, transcendentals=0
        ),
        name="down_weights",
    )(*act, cotangent, *earlier)


def add_kernel(parts, other, out):
    out[...] = (parts[0].astype(f32) + other[0].astype(f32)).astype(bf16)


def to_give(parts, other, earlier):
    _, rows, width = parts.shape
    tile = min(rows, TILE)
    return pl.pallas_call(
        in_order(add_kernel, 2, len(earlier)),
        grid=(rows // tile,),
        in_specs=[
            pl.BlockSpec((1, tile, width), lambda i: (1, i, 0)),
            pl.BlockSpec((1, tile, width), lambda i: (1, i, 0)),
        ]
        + unread(earlier),
        out_specs=pl.BlockSpec((tile, width), lambda i: (i, 0)),
        out_shape=pltpu.HBM((rows, width), bf16),
        compiler_params=params(LIMIT),
        name="to_give",
    )(parts, other, *earlier)


def two_kernel(parts_a, parts_b, other_a, other_b, out):
    for n, (parts, other) in enumerate(((parts_a, other_a), (parts_b, other_b))):
        out[n] = (parts[0].astype(f32) + other[0].astype(f32)).astype(bf16)


def two_to_give(parts, others, earlier):
    _, rows, width = parts[0].shape
    tile = rows // 2
    return pl.pallas_call(
        in_order(two_kernel, 4, len(earlier)),
        grid=(rows // tile,),
        in_specs=[pl.BlockSpec((1, tile, width), lambda i: (1, i, 0))] * 4 + unread(earlier),
        out_specs=pl.BlockSpec((2, tile, width), lambda i: (0, i, 0)),
        out_shape=pltpu.HBM((2, rows, width), bf16),
        compiler_params=params(LIMIT),
        name="two_to_give",
    )(*parts, *others, *earlier)


def mixed_kernel(x2_a, x2_b, parts_a, parts_b, other_a, other_b, there, shift, out):
    for n, (x2, parts, other) in enumerate(
        ((x2_a, parts_a, other_a), (x2_b, parts_b, other_b))
    ):
        total = parts[0].astype(f32) + other[0].astype(f32) + there[n].astype(f32)
        out[n * TILE : (n + 1) * TILE, :] = (x2[...] + total + shift[...]).astype(bf16)


def mixed_rows(x2, parts, others, there, shift, earlier):
    rows, width = x2[0].shape
    first = pl.BlockSpec((1, rows, width), lambda i: (0, 0, 0))
    return pl.pallas_call(
        in_order(mixed_kernel, 8, len(earlier)),
        grid=(1,),
        in_specs=[whole((rows, width))] * 2
        + [first] * 4
        + [whole((2, rows, width)), whole((1, width))]
        + unread(earlier),
        out_specs=whole((2 * rows, width)),
        out_shape=jax.ShapeDtypeStruct((2 * rows, width), bf16),
        compiler_params=params(LIMIT),
        name="mixed_rows",
    )(*x2, *parts, *others, there, shift, *earlier)


def middle_kernel(info, *refs, me_at):
    halves, (gain, w_all, dx2, g, d_0, d_1, d_2, d_3, small) = (refs[0:5], refs[5:10]), refs[10:]
    small[...] = jnp.zeros_like(small)
    for part, (kept, other, there, x2, dy) in enumerate(halves):
        rows = slice(part * TILE, (part + 1) * TILE)
        grad = kept[0].astype(f32) + other[0].astype(f32) + there[...].astype(f32)
        hat, inverse = normalized(x2[...])
        dy = dy[...].astype(f32)
        full = dy + norm_back(hat, inverse, gain[...], grad)
        dx2[rows, :] = full
        low = full.astype(bf16)
        g[rows, :] = low
        small[0:1, :] += jnp.sum(grad * hat, axis=0, keepdims=True)
        small[1:2, :] += jnp.sum(grad, axis=0, keepdims=True)
        small[2:3, :] += jnp.sum(low.astype(f32), axis=0, keepdims=True)
        small[3:4, :] += jnp.sum(dy, axis=0, keepdims=True)
    low = g[...]
    for j, d_j in enumerate((d_0, d_1, d_2, d_3)):
        d_j[...] = dot_nt(low, w_all[jnp.bitwise_xor(info[me_at], j)]).astype(bf16)


def middle(info, me_at, half_a, half_b, gain, w_all, earlier):
    width = gain.shape[1]
    rows = 2 * TILE
    own = whole((TILE, width))
    first = pl.BlockSpec((1, TILE, width), lambda i, info: (0, 0, 0))
    return pl.pallas_call(
        in_order(functools.partial(middle_kernel, me_at=me_at), 13, len(earlier)),
        grid_spec=pltpu.PrefetchScalarGridSpec(
            num_scalar_prefetch=1,
            grid=(1,),
            in_specs=[first, first, own, own, own] * 2
            + [whole((1, width)), whole(w_all.shape)]
            + unread(earlier),
            out_specs=[whole((rows, width))] * 2
            + [whole((rows, WIDTH))] * 4
            + [whole((8, width))],
        ),
        out_shape=[pltpu.HBM((rows, width), f32), pltpu.HBM((rows, width), bf16)]
        + [pltpu.HBM((rows, WIDTH), bf16)] * 4
        + [pltpu.HBM((8, width), f32)],
        compiler_params=params(LIMIT),
        cost_estimate=pl.CostEstimate(
            flops=4 * TILE * width * width, bytes_accessed=12 * MIB, transcendentals=0
        ),
        name="middle",
    )(info, *half_a, *half_b, gain, w_all, *earlier)


def out_weights_kernel(info, *refs):
    parts_a, parts_b, (g, kept, sent) = refs[0:4], refs[4:8], refs[8:]
    for n in range(2):
        for out, j in ((kept, 2 * n), (sent, 2 * n + 1)):
            heads = jnp.concatenate([parts_a[j][...], parts_b[j][...]])
            out[n] = dot_tn(heads, g[...]).astype(bf16)


def out_weights(info, me_at, parts_a, parts_b, g):
    width = g.shape[1]

    def owner(i, info):
        return info[me_at]

    return pl.pallas_call(
        out_weights_kernel,
        grid_spec=pltpu.PrefetchScalarGridSpec(
            num_scalar_prefetch=1,
            grid=(1,),
            in_specs=[head_block(at, owner) for _, at in parts_a + parts_b]
            + [whole(g.shape)],
            out_specs=[whole((2, WIDTH, width))] * 2,
        ),
        out_shape=[pltpu.HBM((2, WIDTH, width), bf16)] * 2,
        compiler_params=params(LIMIT),
        cost_estimate=pl.CostEstimate(
            flops=4 * TILE * width * width, bytes_accessed=6 * MIB, transcendentals=0
        ),
        name="out_weights",
    )(info, *(part for part, _ in parts_a + parts_b), g)


def attend_back_kernel(
    info, k_aug, v_aug, k_t, q_aug_t, q, v_t, o_t, lse, pad, do_0, do_1, do_2, do_3, pos, table,
    *refs, part, me_at, first,
):
    if first:
        dk_in = dv_in = None
    else:
        dk_in, dv_in, *refs = refs
    dq_out, dk, dv, q_side, do_side, q_lanes, do_lanes, dq_t = refs
    i = pl.program_id(0)
    tile = 2 * jnp.bitwise_xor(info[me_at], i) + part

    @pl.when(i == 0)
    def _():
        if first:
            dk[...] = jnp.zeros_like(dk)
            dv[...] = jnp.zeros_like(dv)
        else:
            dk[...] = dk_in[...]
            dv[...] = dv_in[...]

    here = pl.ds(pl.multiple_of(tile * TILE, TILE), TILE)
    do_here = jnp.where(
        i == 0, do_0[...], jnp.where(i == 1, do_1[...], jnp.where(i == 2, do_2[...], do_3[...]))
    )
    q_here = q[...]
    do_t = do_here.astype(f32).T
    k_here = k_t[:, here].astype(f32)
    padded = jnp.where(pad[...] != 0, 1.0, 0.0)
    row = lax.broadcasted_iota(jnp.int32, (AUG - HEAD_DIM, TILE), 0)
    lane = lax.broadcasted_iota(jnp.int32, (TILE, WIDTH), 1) // HEAD_DIM
    dk_parts, dv_parts = [], []
    for h in range(HEADS):
        feat = slice(h * HEAD_DIM, (h + 1) * HEAD_DIM)
        at = h * AUG
        q_h = q_aug_t[at : at + HEAD_DIM, :]
        do_h = do_t[feat, :]
        delta = jnp.sum(do_h * o_t[feat, :].astype(f32), axis=0, keepdims=True)
        lse_h = lse[h : h + 1, :]
        one, two, three = three_parts(-lse_h)
        extra = q_aug_t[at + HEAD_DIM : at + AUG, :].astype(f32)
        extra = jnp.where(row == 4, one, jnp.where(row == 5, two, jnp.where(row == 6, three, extra)))
        q_side[at : at + HEAD_DIM, :] = q_h
        q_side[at + HEAD_DIM : at + AUG, :] = extra.astype(bf16)
        one, two, three = three_parts(-delta)
        extra = jnp.where(row == 0, one, jnp.where(row == 1, two, jnp.where(row == 2, three, 0.0)))
        do_side[at : at + HEAD_DIM, :] = do_h.astype(bf16)
        do_side[at + HEAD_DIM : at + AUG, :] = extra.astype(bf16)
        q_lanes[h] = jnp.where(lane == h, q_here, jnp.zeros_like(q_here))
        do_lanes[h] = jnp.where(lane == h, do_here, jnp.zeros_like(do_here))
        q_h = q_h.astype(f32)
        k_h = k_here[feat, :]
        p_own = padded * jnp.exp(jnp.sum(q_h * k_h, axis=0, keepdims=True) - lse_h)
        dp_own = jnp.sum(do_h * v_t[feat, :].astype(f32), axis=0, keepdims=True)
        ds_own = p_own * (dp_own - delta)
        dq_t[feat, :] = ds_own * k_h
        dk_parts.append(ds_own * q_h)
        dv_parts.append(p_own * do_h)
    dk[here, :] += jnp.concatenate(dk_parts, axis=0).T
    dv[here, :] += jnp.concatenate(dv_parts, axis=0).T

    def step(j, _):
        keys = pl.ds(pl.multiple_of(j * TILE, TILE), TILE)
        probs, grads = [], []
        for h in range(HEADS):
            wide = slice(h * AUG, (h + 1) * AUG)
            prob = jnp.exp(dot_nn(k_aug[keys, wide], q_side[wide, :]))
            grad = prob * dot_nn(v_aug[keys, wide], do_side[wide, :])
            probs.append(prob.astype(bf16))
            grads.append(grad.astype(bf16))
        deep = (HEADS * TILE, WIDTH)
        dv[keys, :] += dot_nn(jnp.concatenate(probs, axis=1), do_lanes[...].reshape(deep))
        dk[keys, :] += dot_nn(jnp.concatenate(grads, axis=1), q_lanes[...].reshape(deep))
        for h in range(HEADS):
            feat = slice(h * HEAD_DIM, (h + 1) * HEAD_DIM)
            dq_t[feat, :] += dot_nn(k_t[feat, keys], grads[h])
        return 0

    begin, end = clip_range(info, tile, k_aug.shape[0])
    lax.fori_loop(begin, end, step, 0)
    dq = dq_t[...].T * (1.0 / math.sqrt(HEAD_DIM))
    cos, low, high = rope_factors(pos, table)
    dq_out[...] = (dq * cos - turned(dq, low, high)).astype(bf16)


def attend_back(
    part, info, me_at, k_aug, v_aug, k_t, q_aug_t, q, v_t, o_t, lse, padding, do, positions, table,
    dk, dv, earlier,
):
    length = k_aug.shape[0]
    half = length // 2

    def owner(i, info):
        return jnp.bitwise_xor(info[me_at], i)

    def rows(columns):
        return pl.BlockSpec((TILE, columns), lambda i, info: (2 * owner(i, info) + part, 0))

    def columns(count):
        return pl.BlockSpec((count, TILE), lambda i, info: (0, 2 * owner(i, info) + part))

    def packed(count):
        return pl.BlockSpec((count, TILE), lambda i, info: (0, owner(i, info)))

    out = jax.ShapeDtypeStruct
    before = () if dk is None else (dk, dv)
    return pl.pallas_call(
        in_order(
            functools.partial(attend_back_kernel, part=part, me_at=me_at, first=dk is None),
            16 + len(before), len(earlier),
        ),
        grid_spec=pltpu.PrefetchScalarGridSpec(
            num_scalar_prefetch=1,
            grid=(half // TILE,),
            in_specs=[
                whole(k_aug.shape), whole(v_aug.shape), whole(k_t.shape), columns(HEADS * AUG),
                rows(WIDTH), columns(WIDTH), packed(WIDTH), packed(8), columns(1),
            ]
            + [pl.BlockSpec((TILE, WIDTH), lambda i, info: (part, 0))] * 4
            + [
                pl.BlockSpec(
                    (3, 1, TILE), lambda i, info: (0, 0, 2 * owner(i, info) + part)
                ),
                whole(table.shape),
            ]
            + [whole((length, WIDTH))] * len(before)
            + unread(earlier),
            out_specs=[
                pl.BlockSpec((TILE, WIDTH), lambda i, info: (owner(i, info), 0)),
                whole((length, WIDTH)), whole((length, WIDTH)),
            ],
            scratch_shapes=[
                pltpu.VMEM((HEADS * AUG, TILE), bf16), pltpu.VMEM((HEADS * AUG, TILE), bf16),
                pltpu.VMEM((HEADS, TILE, WIDTH), bf16), pltpu.VMEM((HEADS, TILE, WIDTH), bf16),
                pltpu.VMEM((WIDTH, TILE), f32),
            ],
        ),
        out_shape=[out((half, WIDTH), bf16), out((length, WIDTH), f32), out((length, WIDTH), f32)],
        compiler_params=params(LIMIT),
        cost_estimate=pl.CostEstimate(
            flops=72 * half * length * WIDTH, bytes_accessed=16 * MIB, transcendentals=0
        ),
        name="attend_back",
    )(
        info, k_aug, v_aug, k_t, q_aug_t, q, v_t, o_t, lse, padding, *do, positions, table, *before,
        *earlier,
    )


def pieces(begin, count, period):
    at, end, cuts = begin, begin + count, []
    while at < end:
        length = min(end - at, period - at % period)
        cuts.append((at, length))
        at += length
    return cuts


def stacked_pairs(rows, count):
    row = lax.broadcasted_iota(jnp.int32, (count, WIDTH), 0)
    out = jnp.zeros((count, WIDTH), f32)
    for m, value in enumerate(rows):
        one, two, _ = three_parts(value)
        out = jnp.where(row == 2 * m, one, jnp.where(row == 2 * m + 1, two, out))
    return out.astype(bf16)


def late_extra(width, blocks):
    vectors = -(-(3 + 7 * width // WIDTH) // blocks)
    return vectors, -(-vectors // 8) * 16


def project_back_kernel(
    info, tok, gain, shift, dq_a, dq_b, dk, dv, pos, table, w, out_kept, out_other, out_there, early,
    dh1, dh1_sent, sums, acc, grad_b, small, w_wide,
):
    i = pl.program_id(0)

    @pl.when(i == 0)
    def _():
        acc[...] = jnp.zeros_like(acc)
        grad_b[...] = jnp.zeros_like(grad_b)
        small[...] = jnp.zeros_like(small)
        for c in range(3):
            w_wide[:, c * WIDTH : (c + 1) * WIDTH] = w[c]

    dk_here = dk[...]
    cos, low, high = rope_factors(pos, table)
    dk_low = (dk_here * cos - turned(dk_here, low, high)).astype(bf16)
    dq = jnp.concatenate([dq_a[...], dq_b[...]])
    parts = jnp.concatenate([dq, dk_low, dv[...].astype(bf16)], axis=1)
    grad = dot_nt(parts, w_wide[...])
    hat, _ = normalized(tok[...].astype(f32))
    normed = (hat * gain[...] + shift[...]).astype(bf16)
    acc[...] += dot_tn(normed, parts)
    grad_b[0:1, :] += jnp.sum(parts.astype(f32), axis=0, keepdims=True)
    small[0:1, :] += jnp.sum(grad * hat, axis=0, keepdims=True)
    small[1:2, :] += jnp.sum(grad, axis=0, keepdims=True)
    low_grad = grad.astype(bf16)
    dh1[0] = low_grad
    dh1_sent[0] = low_grad

    @pl.when(i == pl.num_programs(0) - 1)
    def _():
        width = normed.shape[1]
        blocks = sums.shape[0]

        def cut(value, count):
            return [value[:, r * WIDTH : (r + 1) * WIDTH] for r in range(count)]

        rows = cut(grad_b[0:1, :], 3) + cut(early[4:5, :], width // WIDTH)
        for ref, count in ((small, 2), (early, 4)):
            for v in range(count):
                rows += cut(ref[v : v + 1, :], width // WIDTH)
        for n in range(blocks):
            for to, rows_here, c, begin in late_places(n, blocks, width):
                here = (slice(begin, begin + rows_here), slice(c * WIDTH, (c + 1) * WIDTH))
                sums[n, to : to + rows_here, :] = acc[here].astype(bf16)
            for to, rows_here, c, begin in late_places(n, blocks, width, True):
                here = (slice(begin, begin + rows_here), slice(c * WIDTH, (c + 1) * WIDTH))
                sums[n, to : to + rows_here, :] = (
                    out_kept[here].astype(f32)
                    + out_other[here].astype(f32)
                    + out_there[here].astype(f32)
                ).astype(bf16)
            extra_at = 4 * width // blocks
            sums[n, extra_at:, :] = stacked_pairs(rows[n::blocks], sums.shape[1] - extra_at)


def late_places(n, blocks, width, out=False):
    deep, period = (width // blocks, WIDTH) if out else (3 * width // blocks, width)
    first = 3 * width // blocks if out else 0
    return [
        (first + at - n * deep, length, at // period, at % period)
        for at, length in pieces(n * deep, deep, period)
    ]


def project_back(
    info, me_at, tokens, gain, shift, dq_a, dq_b, dk, dv, positions, table, w, kept, other, there,
    early, blocks, earlier,
):
    length, width = tokens.shape
    share = 2 * TILE

    def owner(i, info):
        return jnp.bitwise_xor(info[me_at], relative(i))

    def rows(count, columns):
        return pl.BlockSpec((count, columns), lambda i, info: (owner(i, info), 0))

    first = pl.BlockSpec((None, TILE, width), lambda i, info: (0, 0, 0))
    out = jax.ShapeDtypeStruct
    sums = (blocks, 4 * width // blocks + late_extra(width, blocks)[1], WIDTH)
    return pl.pallas_call(
        in_order(project_back_kernel, 15, len(earlier)),
        grid_spec=pltpu.PrefetchScalarGridSpec(
            num_scalar_prefetch=1,
            grid=(length // share,),
            in_specs=[
                rows(share, width), whole((1, width)), whole((1, width)), rows(TILE, WIDTH),
                rows(TILE, WIDTH), rows(share, WIDTH), rows(share, WIDTH),
                pl.BlockSpec((3, 1, share), lambda i, info: (0, 0, owner(i, info))),
                whole(table.shape), whole(w.shape), first, first, whole((TILE, width)),
                whole(early.shape),
            ]
            + unread(earlier),
            out_specs=[
                pl.BlockSpec((1, share, width), lambda i, info: (i, 0, 0)),
                pl.BlockSpec((1, share, width), lambda i, info: (jnp.maximum(i - 2, 0), 0, 0)),
                whole(sums),
            ],
            scratch_shapes=[
                pltpu.VMEM((width, 3 * WIDTH), f32), pltpu.VMEM((8, 3 * WIDTH), f32),
                pltpu.VMEM((8, width), f32),
                pltpu.VMEM((width, 3 * WIDTH), bf16),
            ],
        ),
        out_shape=[
            pltpu.HBM((4, share, width), bf16), pltpu.HBM((2, share, width), bf16),
            pltpu.HBM(sums, bf16),
        ],
        compiler_params=params(LIMIT),
        cost_estimate=pl.CostEstimate(
            flops=24 * length * width * WIDTH, bytes_accessed=20 * MIB, transcendentals=0
        ),
        name="project_back",
    )(
        info, tokens, gain, shift, dq_a, dq_b, dk, dv, positions, table, w, kept, other, there, early,
        *earlier,
    )


def vectors_kernel(extra, grad_b, vectors):
    blocks = extra.shape[0]
    width = vectors.shape[1]
    grad_b[...] = jnp.zeros_like(grad_b)
    vectors[...] = jnp.zeros_like(vectors)
    for v in range(3 + 7 * width // WIDTH):
        n, m = v % blocks, v // blocks
        pair = extra[n].astype(f32)
        row = pair[2 * m : 2 * m + 1, :] + pair[2 * m + 1 : 2 * m + 2, :]
        if v < 3:
            grad_b[v : v + 1, :] = row
        else:
            to, at = divmod((v - 3) * WIDTH, width)
            vectors[to : to + 1, at : at + WIDTH] = row


def unpack_vectors(sums, width, earlier):
    blocks = sums.shape[0]
    at, rows = 4 * width // blocks, late_extra(width, blocks)[1]
    return pl.pallas_call(
        in_order(vectors_kernel, 1, len(earlier)),
        grid=(1,),
        in_specs=[pl.BlockSpec((blocks, rows, WIDTH), lambda i: (0, at // rows, 0))]
        + unread(earlier),
        out_specs=[whole((8, WIDTH)), whole((8, width))],
        out_shape=[pltpu.HBM((8, WIDTH), f32), pltpu.HBM((8, width), f32)],
        compiler_params=params(LIMIT),
        name="unpack_vectors",
    )(sums, *earlier)


def unpack_kernel(sums, grad_qkv, grad_out):
    blocks = sums.shape[0]
    width = grad_out.shape[1]
    for n in range(blocks):
        for to, rows, c, begin in late_places(n, blocks, width):
            grad_qkv[c, begin : begin + rows, :] = sums[n, to : to + rows, :].astype(f32)
        for to, rows, c, begin in late_places(n, blocks, width, True):
            grad_out[begin : begin + rows, c * WIDTH : (c + 1) * WIDTH] = sums[
                n, to : to + rows, :
            ].astype(f32)


def unpack(sums, width, earlier):
    out = jax.ShapeDtypeStruct
    return pl.pallas_call(
        in_order(unpack_kernel, 1, len(earlier)),
        in_specs=[pl.BlockSpec(memory_space=pltpu.VMEM)] + unread(earlier),
        out_specs=[pl.BlockSpec(memory_space=pltpu.VMEM)] * 2,
        out_shape=[out((3, width, WIDTH), f32), out((WIDTH, width), f32)],
        compiler_params=pltpu.CompilerParams(vmem_limit_bytes=LIMIT * MIB),
        name="unpack",
    )(sums, *earlier)


def finish_kernel(info, parts, other, there, tok, gain, dx2, out):
    grad = parts[0].astype(f32) + other[0].astype(f32) + there[...].astype(f32)
    hat, inverse = normalized(tok[...].astype(f32))
    out[...] = dx2[...] + norm_back(hat, inverse, gain[...], grad)


def finish(info, me_at, parts, other, there, tokens, gain, dx2, earlier):
    width = tokens.shape[1]
    share = there.shape[0]
    rows = pl.BlockSpec((TILE, width), lambda i, info: (i, 0))
    return pl.pallas_call(
        in_order(finish_kernel, 7, len(earlier)),
        grid_spec=pltpu.PrefetchScalarGridSpec(
            num_scalar_prefetch=1,
            grid=(share // TILE,),
            in_specs=[
                pl.BlockSpec((1, TILE, width), lambda i, info: (0, i, 0)),
                pl.BlockSpec((1, TILE, width), lambda i, info: (0, i, 0)), rows,
                pl.BlockSpec((TILE, width), lambda i, info: (2 * info[me_at] + i, 0)),
                whole((1, width)), rows,
            ]
            + unread(earlier),
            out_specs=rows,
        ),
        out_shape=jax.ShapeDtypeStruct((share, width), f32),
        compiler_params=params(LIMIT),
        cost_estimate=pl.CostEstimate(
            flops=30 * share * width, bytes_accessed=10 * MIB, transcendentals=0
        ),
        name="finish",
    )(info, parts, other, there, tokens, gain, dx2, *earlier)


def total_of(blocks):
    total = blocks[0].astype(f32)
    for n in range(1, blocks.shape[0]):
        total += blocks[n].astype(f32)
    return total.astype(bf16)


def sum_kernel(blocks, out):
    out[...] = total_of(blocks)


def summed(blocks, steps, earlier):
    count, rows, width = blocks.shape
    tile = rows // steps
    return pl.pallas_call(
        in_order(sum_kernel, 1, len(earlier)),
        grid=(steps,),
        in_specs=[pl.BlockSpec((count, tile, width), lambda i: (0, i, 0))] + unread(earlier),
        out_specs=pl.BlockSpec((tile, width), lambda i: (i, 0)),
        out_shape=pltpu.HBM((rows, width), bf16),
        compiler_params=params(LIMIT),
        name="summed",
    )(blocks, *earlier)


def copies_kernel(first, second, out):
    total = (first[...].astype(f32) + second[...].astype(f32)).astype(bf16)
    for n in range(out.shape[0]):
        out[n] = total


def sum_copies(first, second, count, earlier):
    rows, width = first.shape
    return pl.pallas_call(
        in_order(copies_kernel, 2, len(earlier)),
        grid=(1,),
        in_specs=[whole((rows, width))] * 2 + unread(earlier),
        out_specs=whole((count, rows, width)),
        out_shape=pltpu.HBM((count, rows, width), bf16),
        compiler_params=params(LIMIT),
        name="sum_copies",
    )(first, second, *earlier)


def swap(array, axis, bit=1):
    size = lax.axis_size(axis)
    if size == 1:
        return jnp.zeros_like(array)
    return lax.ppermute(array, axis, [(i, i ^ bit) for i in range(size)])


def swap_both(array):
    return lax.ppermute(array, MP, [(i, i ^ 3) for i in range(4)])


def scattered(rows, axes):
    group = lax.axis_size(axes)
    length, width = rows.shape
    return lax.all_to_all(
        rows.reshape(group, length // group, width), axes, 0, 0, tiled=True
    )


def both_sums(total):
    if lax.axis_size("zl") == 1:
        return total
    return (total.astype(f32) + swap(total, "zl").astype(f32)).astype(bf16)


def local(
    tokens, cotangent, segments, padding, positions, ln1_gain, ln1_bias, w_qkv, b_qkv, w_out, b_out,
    ln2_gain, ln2_bias, w_up, b_up, w_down, b_down,
):
    width, hidden = w_up.shape
    w_all = lax.all_gather(w_out, MP)
    gain_one, shift_one = ln1_gain[None], ln1_bias[None]
    gain_two, shift_two = ln2_gain[None], ln2_bias[None]
    ends = jnp.sum((segments <= jnp.arange(2)[:, None]).astype(jnp.int32), axis=1)
    info = jnp.concatenate([ends, lax.axis_index(MP)[None].astype(jnp.int32)])
    me_at = 2
    table = jnp.asarray(rope_constants())
    k_aug, v_aug, q_aug_t, q, k_t, v_t = project(
        tokens, w_qkv, b_qkv, gain_one, shift_one, positions, segments, padding, table
    )

    def exchanged(own, to_c, to_zh, to_both):
        return own, swap(to_c, "c"), swap(to_zh, "zh"), swap_both(to_both)

    o_0, o_t_0, lse_0 = attend(0, info, k_aug, v_t, q_aug_t, k_t, padding, ())
    o_zh_0, o_c_0 = swap(o_0, "zh"), swap(o_0, "c")
    o_1, o_t_1, lse_1 = attend(1, info, k_aug, v_t, q_aug_t, k_t, padding, (o_0, w_all))
    o_zh_1 = swap(o_1, "zh")
    o_zh_0 = after(o_zh_0, (o_1,))
    o_parts_0 = tuple((part, None) for part in (o_0, o_c_0, o_zh_0, swap(o_zh_0, "c")))

    def mlp_half(part, o_parts, earlier):
        return mlp(
            part, info, me_at, tokens, cotangent, o_parts, w_all, b_out[None], gain_two, shift_two,
            w_up, b_up[None], w_down, earlier,
        )

    x2_0, dy_0, h2_0, act_0, du_0, mlp_0, mlp_sent_0, dh2_0, sent, db_0 = mlp_half(
        0, o_parts_0, (o_1,)
    )
    pair = paired(o_1, o_zh_1, (x2_0,))
    pair_c = swap(pair, "c")
    o_parts_1 = ((pair, 0), (pair_c, 0), (pair, 1), (pair_c, 1))
    other_0 = swap(sent, "c")
    give_0 = to_give(dh2_0, other_0, ())
    there_0 = swap(give_0, "zh")
    x2_1, dy_1, h2_1, act_1, du_1, mlp_1, mlp_sent_1, dh2_1, sent, db_1 = mlp_half(
        1, o_parts_1, (give_0,)
    )
    other_1 = swap(sent, "c")
    grad_mlp = down_weights((act_0, act_1), cotangent, ())
    give_1 = to_give(dh2_1, other_1, (grad_mlp,))
    there_1 = swap(give_1, "zh")
    grad_mlp = up_weights((h2_0, h2_1), (du_0, du_1), grad_mlp, (give_1,))
    arrived = scattered(grad_mlp, ("y", "x"))
    dx2, g, *d_parts, small = middle(
        info, me_at, (dh2_0, other_0, there_0, x2_0, dy_0), (dh2_1, other_1, there_1, x2_1, dy_1),
        gain_two, w_all, (grad_mlp,),
    )
    do = exchanged(*d_parts)
    grad_out, out_sent = out_weights(info, me_at, o_parts_0, o_parts_1, g)
    out_other = swap(out_sent, "c")
    mlp_parts = (mlp_0, mlp_1)
    mlp_others = (swap(mlp_sent_0, "c"), swap(mlp_sent_1, "c"))
    dq_0, dk, dv = attend_back(
        0, info, me_at, k_aug, v_aug, k_t, q_aug_t, q, v_t, o_t_0, lse_0, padding, do, positions,
        table, None, None, (grad_out, g),
    )
    give = to_give(grad_out, out_other, (dq_0,))
    out_there = swap(give, "zh")
    part_sum = both_sums(summed(arrived, 2, (give,)))
    dq_1, dk, dv = attend_back(
        1, info, me_at, k_aug, v_aug, k_t, q_aug_t, q, v_t, o_t_1, lse_1, padding, do, positions,
        table, dk, dv, (give, part_sum),
    )
    grad_mlp = lax.all_gather(part_sum, ("y", "x"), axis=0, tiled=True)
    early = jnp.concatenate([small[0:4], (db_0 + db_1)[0:4]])
    dh1, sent, sums = project_back(
        info, me_at, tokens, gain_one, shift_one, dq_0, dq_1, dk, dv, positions, table, w_qkv,
        grad_out, out_other, out_there, early, lax.axis_size(("y", "x")), (),
    )
    other = swap(sent, "c")
    back = swap(to_give(dh1, other, (sums,)), "zh")
    arrived = scattered(sums.reshape(-1, WIDTH), ("y", "x"))
    mlp_there = swap(two_to_give(mlp_parts, mlp_others, (sums,)), "zh")
    total = summed(arrived, 1, (back,))
    copies = sum_copies(total, swap(total, "zl"), sums.shape[0], ())
    late = lax.all_to_all(copies, ("y", "x"), 0, 0, tiled=True)
    grad_inputs = finish(info, me_at, dh1, other, back, tokens, gain_one, dx2, (copies,))
    mixed = mixed_rows(
        (x2_0, x2_1), mlp_parts, mlp_others, mlp_there, b_down[None], (copies,)
    )
    grad_mlp = grad_mlp.reshape(2, width, hidden).astype(f32)
    grad_up, grad_down = grad_mlp[0], grad_mlp[1]
    grad_b, vectors = unpack_vectors(late, width, (grad_inputs, mixed, grad_up, grad_down))
    by_c, by_zh, by_both = swap(vectors, "c"), swap(vectors, "zh"), swap_both(vectors)
    grad_qkv, grad_w_out = unpack(late, width, (vectors,))
    group = (vectors + by_c) + (by_zh + by_both)
    return (
        mixed, grad_inputs, group[1], group[2], grad_qkv, grad_b[0:3], grad_w_out, group[5],
        group[3], group[4], grad_up, vectors[0], grad_down, group[6],
    )


def solution(mesh):
    packs = mesh.shape["dp"]
    if packs == 32:
        shape = (2, 4, 4, 2, 2)
    else:
        shape = (1, packs, 1, 2, 2)
    split = Mesh(mesh.devices.reshape(shape), EVERY)
    in_specs = (
        P(DP, None), P(DP, None), P(DP, None), P(DP, None), P(None, DP, None), P(), P(),
        P(None, None, MP), P(None, MP), P(MP, None), P(), P(), P(), P(None, MP), P(MP),
        P(MP, None), P(),
    )
    out_specs = (
        P(EVERY, None), P(EVERY, None), P(), P(), P(None, None, MP), P(None, MP), P(MP, None), P(),
        P(), P(), P(None, MP), P(MP), P(MP, None), P(),
    )
    return jax.shard_map(local, mesh=split, in_specs=in_specs, out_specs=out_specs, check_vma=False)
```

```python
import functools
import math

import jax
import jax.numpy as jnp
import ml_dtypes
import numpy as np
from jax import lax
from jax.experimental import pallas as pl
from jax.experimental.pallas import tpu as pltpu
from jax.sharding import Mesh
from jax.sharding import PartitionSpec as P

HEAD_DIM = 64
HEADS = 4
WIDTH = HEADS * HEAD_DIM
AUG = 128
TILE = 256
PLACES = 64
LIMIT = 64
MIB = 1 << 20
DP = ("zl", "y", "x")
MP = ("zh", "c")
EVERY = ("zl", "y", "x", "zh", "c")

epsilon = 1e-06
NEG = -1e30
bf16 = jnp.bfloat16
f32 = jnp.float32


def dot_nn(a, b):
    return lax.dot_general(a, b, (((1,), (0,)), ((), ())), preferred_element_type=f32)


def dot_nt(a, b):
    return lax.dot_general(a, b, (((1,), (1,)), ((), ())), preferred_element_type=f32)


def dot_tn(a, b):
    return lax.dot_general(a, b, (((0,), (0,)), ((), ())), preferred_element_type=f32)


def normalized(values):
    center = jnp.mean(values, axis=-1, keepdims=True)
    shifted = values - center
    spread = jnp.mean(shifted * shifted, axis=-1, keepdims=True)
    inverse = lax.rsqrt(spread + epsilon)
    return shifted * inverse, inverse


def norm_back(hat, inverse, gain, grad):
    scaled = grad * gain
    return inverse * (
        scaled
        - jnp.mean(scaled, axis=-1, keepdims=True)
        - hat * jnp.mean(scaled * hat, axis=-1, keepdims=True)
    )


def turned(x, low, high):
    width = x.shape[1]
    pair = HEAD_DIM // 6
    return pltpu.roll(x, width - pair, 1) * low + pltpu.roll(x, pair, 1) * high


def three_parts(x):
    first = x.astype(bf16).astype(f32)
    rest = x - first
    second = rest.astype(bf16).astype(f32)
    return first, second, rest - second


def params(limit, axes=1):
    return pltpu.CompilerParams(
        dimension_semantics=("arbitrary",) * axes, vmem_limit_bytes=limit * MIB
    )


def in_order(kernel, inputs, earlier):
    def run(*refs):
        kernel(*refs[:inputs], *refs[inputs + earlier :])

    return run


def unread(arrays):
    return [pl.BlockSpec(memory_space=pl.ANY)] * len(arrays)


def whole(shape):
    return pl.BlockSpec(shape, lambda *_: (0,) * len(shape))


def clip_range(info, tile, length):
    first, second = info[0], info[1]
    at = tile * TILE
    begin = jnp.where(second <= at, second, jnp.where(first <= at, first, 0))
    end = jnp.where(
        first >= at + TILE, first, jnp.where(second >= at + TILE, second, length)
    )
    return begin // TILE, (end + TILE - 1) // TILE


def rope_constants():
    pair = HEAD_DIM // 6
    feature = np.arange(WIDTH) % HEAD_DIM
    section, place = feature // (2 * pair), feature % (2 * pair)
    frequency = np.exp(-math.log(10000.0) * (place % pair) / pair)
    table = np.zeros((PLACES, 3, WIDTH))
    for s in range(3):
        for value in range(16):
            angle = value * frequency
            turns = section == s
            table[s * 16 + value, 0] = np.where(turns, np.cos(angle), 0.0)
            table[s * 16 + value, 1] = np.where(turns & (place < pair), -np.sin(angle), 0.0)
            table[s * 16 + value, 2] = np.where(turns & (place >= pair), np.sin(angle), 0.0)
    table[48, 0] = section == 3
    rest = table.reshape(PLACES, 3 * WIDTH).astype(np.float32)
    parts = []
    for _ in range(3):
        part = rest.astype(ml_dtypes.bfloat16)
        parts.append(part)
        rest = rest - part.astype(np.float32)
    return np.concatenate(parts)


def rope_factors(positions, table):
    row = lax.broadcasted_iota(jnp.int32, (PLACES, positions.shape[-1]), 0)
    where = jnp.where(
        row < 16, positions[0], jnp.where(row < 32, positions[1], positions[2])
    )
    hit = ((where == row % 16) & (row < 48)) | (row == 48)
    hit = jnp.where(hit, 1.0, 0.0)
    hits = jnp.concatenate([hit, hit, hit]).astype(bf16)
    factors = dot_tn(hits, table[...])
    return factors[:, :WIDTH], factors[:, WIDTH : 2 * WIDTH], factors[:, 2 * WIDTH :]


def qkv_kernel(
    tok, w, b, gain, shift, pos, seg, pad, table, k_aug, v_aug, q_aug_t, q_out, k_t, v_t, w_wide
):
    @pl.when(pl.program_id(0) == 0)
    def _():
        for c in range(3):
            w_wide[:, c * WIDTH : (c + 1) * WIDTH] = w[c]

    hat, _ = normalized(tok[...].astype(f32))
    normed = (hat * gain[...] + shift[...]).astype(bf16)
    cos, low, high = rope_factors(pos, table)
    all_three = dot_nn(normed, w_wide[...])
    q = all_three[:, :WIDTH] + b[0:1, :]
    k = all_three[:, WIDTH : 2 * WIDTH] + b[1:2, :]
    v = all_three[:, 2 * WIDTH :] + b[2:3, :]
    q = (q * cos + turned(q, low, high)) * (1.0 / math.sqrt(HEAD_DIM))
    k = k * cos + turned(k, low, high)
    q_out[...] = q.astype(bf16)
    q_t = q.T.astype(bf16)
    k_t[...] = k.T.astype(bf16)
    v_t[...] = v.T.astype(bf16)
    row = lax.broadcasted_iota(jnp.int32, (HEAD_DIM, TILE), 0)
    clip = seg[...]
    same = (row >= 1) & (row < 4) & (clip == row - 1)
    mask = jnp.where((row >= 1) & (row < 4) & (clip != row - 1), NEG, 0.0)
    mask = jnp.where(row == 0, jnp.where(pad[...] != 0, NEG, 0.0), mask)
    k_extra = jnp.where((row >= 4) & (row < 7), 1.0, mask)
    q_extra = jnp.where(same | (row == 0), 1.0, 0.0).astype(bf16)
    k_side = jnp.concatenate([jnp.zeros((HEAD_DIM, TILE), f32), k_extra]).T
    lane = lax.broadcasted_iota(jnp.int32, (TILE, AUG), 1)
    ones = jnp.where((lane >= HEAD_DIM) & (lane < HEAD_DIM + 3), 1.0, 0.0)
    for h in range(HEADS):
        pair = slice(h // 2 * AUG, h // 2 * AUG + AUG)
        wide = slice(h * AUG, (h + 1) * AUG)
        k_pair, v_pair = k[:, pair], v[:, pair]
        if h % 2:
            k_pair, v_pair = pltpu.roll(k_pair, HEAD_DIM, 1), pltpu.roll(v_pair, HEAD_DIM, 1)
        k_aug[:, wide] = jnp.where(lane < HEAD_DIM, k_pair, k_side).astype(bf16)
        v_aug[:, wide] = jnp.where(lane < HEAD_DIM, v_pair, ones).astype(bf16)
        q_aug_t[h * AUG : h * AUG + HEAD_DIM, :] = q_t[h * HEAD_DIM : (h + 1) * HEAD_DIM, :]
        q_aug_t[h * AUG + HEAD_DIM : (h + 1) * AUG, :] = q_extra


def project(tokens, w, b, gain, shift, positions, segments, padding, table):
    length, width = tokens.shape
    tiles = length // TILE

    def rows(columns):
        return pl.BlockSpec((TILE, columns), lambda i: (i, 0))

    def columns(count):
        return pl.BlockSpec((count, TILE), lambda i: (0, i))

    out = jax.ShapeDtypeStruct
    wide = out((length, HEADS * AUG), bf16)
    flat = out((WIDTH, length), bf16)
    return pl.pallas_call(
        qkv_kernel,
        grid=(tiles,),
        in_specs=[
            rows(width), whole(w.shape), whole(b.shape), whole((1, width)), whole((1, width)),
            pl.BlockSpec((3, 1, TILE), lambda i: (0, 0, i)), columns(1), columns(1), whole(table.shape),
        ],
        out_specs=[
            rows(HEADS * AUG), rows(HEADS * AUG), columns(HEADS * AUG), rows(WIDTH), columns(WIDTH),
            columns(WIDTH),
        ],
        out_shape=[
            wide, wide, out((HEADS * AUG, length), bf16), out((length, WIDTH), bf16), flat, flat,
        ],
        scratch_shapes=[pltpu.VMEM((width, 3 * WIDTH), bf16)],
        compiler_params=params(LIMIT),
        cost_estimate=pl.CostEstimate(
            flops=6 * length * width * WIDTH, bytes_accessed=20 * MIB, transcendentals=0
        ),
        name="project",
    )(tokens, w, b, gain, shift, positions, segments, padding, table)


def attend_kernel(info, k_aug, v_t, q_aug_t, k_t, pad, o, o_t, lse, top, total, acc, *, part):
    tile = 2 * pl.program_id(0) + part
    padded = pad[...] != 0
    for h in range(HEADS):
        q_h = q_aug_t[h * AUG : h * AUG + HEAD_DIM, :].astype(f32)
        k_h = k_t[h * HEAD_DIM : (h + 1) * HEAD_DIM, :].astype(f32)
        own = jnp.sum(q_h * k_h, axis=0, keepdims=True)
        top[h : h + 1, :] = jnp.where(padded, own, -3e38)
        total[h : h + 1, :] = jnp.where(padded, 1.0, 0.0)
    here = pl.ds(pl.multiple_of(tile * TILE, TILE), TILE)
    acc[...] = jnp.where(padded, v_t[:, here].astype(f32), 0.0)
    feats = [slice(h * HEAD_DIM, (h + 1) * HEAD_DIM) for h in range(HEADS)]
    wides = [slice(h * AUG, (h + 1) * AUG) for h in range(HEADS)]

    def step(j, count):
        keys = pl.ds(pl.multiple_of(j * TILE, TILE), count * TILE)
        scores = [dot_nn(k_aug[keys, wide], q_aug_t[wide, :]) for wide in wides]
        probs, fades = [], []
        for h in range(HEADS):
            old = top[h : h + 1, :]
            new = jnp.maximum(old, jnp.max(scores[h], axis=0, keepdims=True))
            prob = jnp.exp(scores[h] - new)
            fade = jnp.exp(old - new)
            top[h : h + 1, :] = new
            total[h : h + 1, :] = total[h : h + 1, :] * fade + jnp.sum(prob, axis=0, keepdims=True)
            probs.append(prob.astype(bf16))
            fades.append(fade)
        for h, feat in enumerate(feats):
            acc[feat, :] = acc[feat, :] * fades[h] + dot_nn(v_t[feat, keys], probs[h])

    begin, end = clip_range(info, tile, k_aug.shape[0])
    pairs = (end - begin) // 2

    def two(n, _):
        step(begin + 2 * n, 2)
        return 0

    lax.fori_loop(0, pairs, two, 0)

    @pl.when(begin + 2 * pairs < end)
    def _():
        step(end - 1, 1)

    for h, feat in enumerate(feats):
        acc[feat, :] = acc[feat, :] / total[h : h + 1, :]
    lse[...] = jnp.zeros_like(lse)
    lse[0:HEADS, :] = top[0:HEADS, :] + jnp.log(total[0:HEADS, :])
    turned_o = acc[...]
    o_t[...] = turned_o.astype(bf16)
    o[...] = turned_o.T.astype(bf16)


def attend(part, info, k_aug, v_t, q_aug_t, k_t, padding, earlier):
    length = k_aug.shape[0]
    half = length // 2

    def columns(count):
        return pl.BlockSpec((count, TILE), lambda i, *_: (0, 2 * i + part))

    def packed(count):
        return pl.BlockSpec((count, TILE), lambda i, *_: (0, i))

    out = jax.ShapeDtypeStruct
    return pl.pallas_call(
        in_order(functools.partial(attend_kernel, part=part), 6, len(earlier)),
        grid_spec=pltpu.PrefetchScalarGridSpec(
            num_scalar_prefetch=1,
            grid=(half // TILE,),
            in_specs=[
                whole(k_aug.shape), whole(v_t.shape), columns(HEADS * AUG), columns(WIDTH),
                columns(1),
            ]
            + unread(earlier),
            out_specs=[
                pl.BlockSpec((TILE, WIDTH), lambda i, *_: (i, 0)), packed(WIDTH), packed(8),
            ],
            scratch_shapes=[
                pltpu.VMEM((8, TILE), f32), pltpu.VMEM((8, TILE), f32), pltpu.VMEM((WIDTH, TILE), f32),
            ],
        ),
        out_shape=[out((half, WIDTH), bf16), out((WIDTH, half), bf16), out((8, half), f32)],
        compiler_params=params(LIMIT),
        cost_estimate=pl.CostEstimate(
            flops=24 * half * length * WIDTH, bytes_accessed=6 * MIB, transcendentals=0
        ),
        name="attend",
    )(info, k_aug, v_t, q_aug_t, k_t, padding, *earlier)


def nothing(*refs):
    del refs


def after(value, earlier):
    return pl.pallas_call(
        nothing,
        in_specs=unread((value,) + earlier),
        out_specs=pl.BlockSpec(memory_space=pl.ANY),
        out_shape=jax.ShapeDtypeStruct(value.shape, value.dtype),
        input_output_aliases={0: 0},
        name="after",
    )(value, *earlier)


def pair_kernel(first, second, out):
    out[0] = first[...]
    out[1] = second[...]


def paired(first, second, earlier):
    shape = (2,) + first.shape
    return pl.pallas_call(
        in_order(pair_kernel, 2, len(earlier)),
        in_specs=[pl.BlockSpec(memory_space=pltpu.VMEM)] * 2 + unread(earlier),
        out_specs=pl.BlockSpec(memory_space=pltpu.VMEM),
        out_shape=jax.ShapeDtypeStruct(shape, first.dtype),
        name="paired",
    )(first, second, *earlier)


def head_block(at, owner):
    if at is None:
        return pl.BlockSpec((TILE, WIDTH), lambda i, info: (owner(i, info), 0))
    return pl.BlockSpec((None, TILE, WIDTH), lambda i, info: (at, owner(i, info), 0))


def relative(i):
    return i % 2 * 2 + i // 2


def gelu_parts(u):
    size = jnp.abs(u)
    t = 1.0 / (1.0 + (0.3275911 / math.sqrt(2.0)) * size)
    bell = jnp.exp(-0.5 * (u * u))
    poly = 0.5 * 1.061405429
    for c in (-1.453152027, 1.421413741, -0.284496736, 0.254829592):
        poly = poly * t + 0.5 * c
    tail = poly * t * bell
    below = jnp.where(u >= 0, 1.0 - tail, tail)
    return u * below, below + u * bell * (1.0 / math.sqrt(2.0 * math.pi))


def mlp_kernel(
    info, tok, cot, o_0, o_1, o_2, o_3, w_all, b_out, gain, shift, w_up, b_up, w_down,
    x2, dy, h2, act, du, mlp, mlp_sent, dh2, dh2_sent, db_up, w_out, *, me_at,
):
    i = pl.program_id(0)

    @pl.when(i == 0)
    def _():
        for j in range(4):
            w_out[j * WIDTH : (j + 1) * WIDTH, :] = w_all[jnp.bitwise_xor(info[me_at], j)]
        db_up[...] = jnp.zeros_like(db_up)

    heads = jnp.concatenate([o_0[...], o_1[...], o_2[...], o_3[...]], axis=1)
    mid = tok[...].astype(f32) + b_out[...] + dot_nn(heads, w_out[...])

    @pl.when(i == 0)
    def _():
        x2[...] = mid
        dy[...] = cot[...]

    hat, _ = normalized(mid)
    normed = (hat * gain[...] + shift[...]).astype(bf16)
    h2[...] = normed
    u = dot_nn(normed, w_up[...]) + b_up[...]
    grad_act = dot_nt(cot[...], w_down[...])
    value, slope = gelu_parts(u)
    value = value.astype(bf16)
    grad = (grad_act * slope).astype(bf16)
    act[...] = value
    du[...] = grad
    db_up[0:1, :] += jnp.sum(grad.astype(f32), axis=0, keepdims=True)
    mlp_part = dot_nn(value, w_down[...]).astype(bf16)
    dh2_part = dot_nt(grad, w_up[...]).astype(bf16)
    mlp[0] = mlp_part
    mlp_sent[0] = mlp_part
    dh2[0] = dh2_part
    dh2_sent[0] = dh2_part


def mlp(
    part, info, me_at, tokens, cotangent, o_parts, w_all, b_out, gain, shift, w_up, b_up, w_down,
    earlier,
):
    length, width = tokens.shape
    half = length // 2
    hidden = w_up.shape[1]
    owners = half // TILE

    def owner(i, info):
        return jnp.bitwise_xor(info[me_at], relative(i))

    def rows(columns):
        return pl.BlockSpec((TILE, columns), lambda i, info: (2 * owner(i, info) + part, 0))

    def packed(columns):
        return pl.BlockSpec((TILE, columns), lambda i, info: (owner(i, info), 0))

    ordered = pl.BlockSpec((1, TILE, width), lambda i, info: (i, 0, 0))
    sent = pl.BlockSpec((1, TILE, width), lambda i, info: (jnp.maximum(i - 2, 0), 0, 0))

    out = jax.ShapeDtypeStruct
    return pl.pallas_call(
        in_order(functools.partial(mlp_kernel, me_at=me_at), 14, len(earlier)),
        grid_spec=pltpu.PrefetchScalarGridSpec(
            num_scalar_prefetch=1,
            grid=(owners,),
            in_specs=[rows(width), rows(width)]
            + [head_block(at, owner) for _, at in o_parts]
            + [whole(w_all.shape)]
            + [whole((1, width))] * 3
            + [whole(w_up.shape), whole((1, hidden)), whole(w_down.shape)]
            + unread(earlier),
            out_specs=[
                whole((TILE, width)), whole((TILE, width)), packed(width), packed(hidden),
                packed(hidden), ordered, sent, ordered, sent, whole((8, hidden)),
            ],
            scratch_shapes=[pltpu.VMEM((4 * WIDTH, width), bf16)],
        ),
        out_shape=[
            out((TILE, width), f32), out((TILE, width), bf16), out((half, width), bf16),
            out((half, hidden), bf16), out((half, hidden), bf16),
        ]
        + [out((owners, TILE, width), bf16), out((2, TILE, width), bf16)] * 2
        + [out((8, hidden), f32)],
        compiler_params=params(LIMIT),
        cost_estimate=pl.CostEstimate(
            flops=20 * half * width * hidden, bytes_accessed=20 * MIB, transcendentals=0
        ),
        name="mlp",
    )(
        info, tokens, cotangent, *(part for part, _ in o_parts), w_all, b_out, gain, shift, w_up,
        b_up, w_down, *earlier
    )


def up_weights_kernel(left_a, left_b, right_a, right_b, out):
    left = jnp.concatenate([left_a[...], left_b[...]])
    right = jnp.concatenate([right_a[...], right_b[...]])
    out[...] = dot_tn(left, right).astype(bf16)


def up_weights(h2, du, earlier):
    half, width = h2[0].shape
    hidden = du[0].shape[1]
    return pl.pallas_call(
        in_order(up_weights_kernel, 4, len(earlier)),
        grid=(width // TILE,),
        in_specs=[pl.BlockSpec((half, TILE), lambda i: (0, i))] * 2
        + [whole((half, hidden))] * 2
        + unread(earlier),
        out_specs=pl.BlockSpec((TILE, hidden), lambda i: (i, 0)),
        out_shape=pltpu.HBM((width, hidden), bf16),
        compiler_params=params(LIMIT),
        cost_estimate=pl.CostEstimate(
            flops=8 * half * width * hidden, bytes_accessed=12 * MIB, transcendentals=0
        ),
        name="up_weights",
    )(*h2, *du, *earlier)


def down_weights_kernel(act_a, act_b, cot, out):
    owners = cot.shape[0] // (2 * TILE)
    rows = [cot[n * TILE : (n + 1) * TILE, :] for p in range(2) for n in range(p, 2 * owners, 2)]
    out[...] = dot_tn(
        jnp.concatenate([act_a[...], act_b[...]]), jnp.concatenate(rows)
    ).astype(bf16)


def down_weights(act, cotangent, earlier):
    half, hidden = act[0].shape
    length, width = cotangent.shape
    return pl.pallas_call(
        in_order(down_weights_kernel, 3, len(earlier)),
        grid=(hidden // TILE,),
        in_specs=[pl.BlockSpec((half, TILE), lambda i: (0, i))] * 2
        + [whole((length, width))]
        + unread(earlier),
        out_specs=pl.BlockSpec((TILE, width), lambda i: (i, 0)),
        out_shape=pltpu.HBM((hidden, width), bf16),
        compiler_params=params(LIMIT),
        cost_estimate=pl.CostEstimate(
            flops=8 * half * width * hidden, bytes_accessed=12 * MIB, transcendentals=0
        ),
        name="down_weights",
    )(*act, cotangent, *earlier)


def add_kernel(parts, other, out):
    out[...] = (parts[0].astype(f32) + other[0].astype(f32)).astype(bf16)


def to_give(parts, other, earlier):
    _, rows, width = parts.shape
    tile = min(rows, TILE)
    return pl.pallas_call(
        in_order(add_kernel, 2, len(earlier)),
        grid=(rows // tile,),
        in_specs=[
            pl.BlockSpec((1, tile, width), lambda i: (1, i, 0)),
            pl.BlockSpec((1, tile, width), lambda i: (1, i, 0)),
        ]
        + unread(earlier),
        out_specs=pl.BlockSpec((tile, width), lambda i: (i, 0)),
        out_shape=pltpu.HBM((rows, width), bf16),
        compiler_params=params(LIMIT),
        name="to_give",
    )(parts, other, *earlier)


def two_kernel(parts_a, parts_b, other_a, other_b, out):
    for n, (parts, other) in enumerate(((parts_a, other_a), (parts_b, other_b))):
        out[n] = (parts[0].astype(f32) + other[0].astype(f32)).astype(bf16)


def two_to_give(parts, others, earlier):
    _, rows, width = parts[0].shape
    tile = rows // 2
    return pl.pallas_call(
        in_order(two_kernel, 4, len(earlier)),
        grid=(rows // tile,),
        in_specs=[pl.BlockSpec((1, tile, width), lambda i: (1, i, 0))] * 4 + unread(earlier),
        out_specs=pl.BlockSpec((2, tile, width), lambda i: (0, i, 0)),
        out_shape=pltpu.HBM((2, rows, width), bf16),
        compiler_params=params(LIMIT),
        name="two_to_give",
    )(*parts, *others, *earlier)


def mixed_kernel(x2_a, x2_b, parts_a, parts_b, other_a, other_b, there, shift, out):
    for n, (x2, parts, other) in enumerate(
        ((x2_a, parts_a, other_a), (x2_b, parts_b, other_b))
    ):
        total = parts[0].astype(f32) + other[0].astype(f32) + there[n].astype(f32)
        out[n * TILE : (n + 1) * TILE, :] = (x2[...] + total + shift[...]).astype(bf16)


def mixed_rows(x2, parts, others, there, shift, earlier):
    rows, width = x2[0].shape
    first = pl.BlockSpec((1, rows, width), lambda i: (0, 0, 0))
    return pl.pallas_call(
        in_order(mixed_kernel, 8, len(earlier)),
        grid=(1,),
        in_specs=[whole((rows, width))] * 2
        + [first] * 4
        + [whole((2, rows, width)), whole((1, width))]
        + unread(earlier),
        out_specs=whole((2 * rows, width)),
        out_shape=jax.ShapeDtypeStruct((2 * rows, width), bf16),
        compiler_params=params(LIMIT),
        name="mixed_rows",
    )(*x2, *parts, *others, there, shift, *earlier)


def middle_kernel(info, *refs, me_at):
    halves, (gain, w_all, dx2, g, d_0, d_1, d_2, d_3, small) = (refs[0:5], refs[5:10]), refs[10:]
    small[...] = jnp.zeros_like(small)
    for part, (kept, other, there, x2, dy) in enumerate(halves):
        rows = slice(part * TILE, (part + 1) * TILE)
        grad = kept[0].astype(f32) + other[0].astype(f32) + there[...].astype(f32)
        hat, inverse = normalized(x2[...])
        dy = dy[...].astype(f32)
        full = dy + norm_back(hat, inverse, gain[...], grad)
        dx2[rows, :] = full
        low = full.astype(bf16)
        g[rows, :] = low
        small[0:1, :] += jnp.sum(grad * hat, axis=0, keepdims=True)
        small[1:2, :] += jnp.sum(grad, axis=0, keepdims=True)
        small[2:3, :] += jnp.sum(low.astype(f32), axis=0, keepdims=True)
        small[3:4, :] += jnp.sum(dy, axis=0, keepdims=True)
    low = g[...]
    for j, d_j in enumerate((d_0, d_1, d_2, d_3)):
        d_j[...] = dot_nt(low, w_all[jnp.bitwise_xor(info[me_at], j)]).astype(bf16)


def middle(info, me_at, half_a, half_b, gain, w_all, earlier):
    width = gain.shape[1]
    rows = 2 * TILE
    own = whole((TILE, width))
    first = pl.BlockSpec((1, TILE, width), lambda i, info: (0, 0, 0))
    return pl.pallas_call(
        in_order(functools.partial(middle_kernel, me_at=me_at), 13, len(earlier)),
        grid_spec=pltpu.PrefetchScalarGridSpec(
            num_scalar_prefetch=1,
            grid=(1,),
            in_specs=[first, first, own, own, own] * 2
            + [whole((1, width)), whole(w_all.shape)]
            + unread(earlier),
            out_specs=[whole((rows, width))] * 2
            + [whole((rows, WIDTH))] * 4
            + [whole((8, width))],
        ),
        out_shape=[pltpu.HBM((rows, width), f32), pltpu.HBM((rows, width), bf16)]
        + [pltpu.HBM((rows, WIDTH), bf16)] * 4
        + [pltpu.HBM((8, width), f32)],
        compiler_params=params(LIMIT),
        cost_estimate=pl.CostEstimate(
            flops=4 * TILE * width * width, bytes_accessed=12 * MIB, transcendentals=0
        ),
        name="middle",
    )(info, *half_a, *half_b, gain, w_all, *earlier)


def out_weights_kernel(info, *refs):
    parts_a, parts_b, (g, kept, sent) = refs[0:4], refs[4:8], refs[8:]
    for n in range(2):
        for out, j in ((kept, 2 * n), (sent, 2 * n + 1)):
            heads = jnp.concatenate([parts_a[j][...], parts_b[j][...]])
            out[n] = dot_tn(heads, g[...]).astype(bf16)


def out_weights(info, me_at, parts_a, parts_b, g):
    width = g.shape[1]

    def owner(i, info):
        return info[me_at]

    return pl.pallas_call(
        out_weights_kernel,
        grid_spec=pltpu.PrefetchScalarGridSpec(
            num_scalar_prefetch=1,
            grid=(1,),
            in_specs=[head_block(at, owner) for _, at in parts_a + parts_b]
            + [whole(g.shape)],
            out_specs=[whole((2, WIDTH, width))] * 2,
        ),
        out_shape=[pltpu.HBM((2, WIDTH, width), bf16)] * 2,
        compiler_params=params(LIMIT),
        cost_estimate=pl.CostEstimate(
            flops=4 * TILE * width * width, bytes_accessed=6 * MIB, transcendentals=0
        ),
        name="out_weights",
    )(info, *(part for part, _ in parts_a + parts_b), g)


def attend_back_kernel(
    info, k_aug, v_aug, k_t, q_aug_t, q, v_t, o_t, lse, pad, do_0, do_1, do_2, do_3, pos, table,
    *refs, part, me_at, first,
):
    if first:
        dk_in = dv_in = None
    else:
        dk_in, dv_in, *refs = refs
    dq_out, dk, dv, q_side, do_side, q_lanes, do_lanes, dq_t = refs
    i = pl.program_id(0)
    tile = 2 * jnp.bitwise_xor(info[me_at], i) + part

    @pl.when(i == 0)
    def _():
        if first:
            dk[...] = jnp.zeros_like(dk)
            dv[...] = jnp.zeros_like(dv)
        else:
            dk[...] = dk_in[...]
            dv[...] = dv_in[...]

    here = pl.ds(pl.multiple_of(tile * TILE, TILE), TILE)
    do_here = jnp.where(
        i == 0, do_0[...], jnp.where(i == 1, do_1[...], jnp.where(i == 2, do_2[...], do_3[...]))
    )
    q_here = q[...]
    do_t = do_here.astype(f32).T
    k_here = k_t[:, here].astype(f32)
    padded = jnp.where(pad[...] != 0, 1.0, 0.0)
    row = lax.broadcasted_iota(jnp.int32, (AUG - HEAD_DIM, TILE), 0)
    lane = lax.broadcasted_iota(jnp.int32, (TILE, WIDTH), 1) // HEAD_DIM
    dk_parts, dv_parts = [], []
    for h in range(HEADS):
        feat = slice(h * HEAD_DIM, (h + 1) * HEAD_DIM)
        at = h * AUG
        q_h = q_aug_t[at : at + HEAD_DIM, :]
        do_h = do_t[feat, :]
        delta = jnp.sum(do_h * o_t[feat, :].astype(f32), axis=0, keepdims=True)
        lse_h = lse[h : h + 1, :]
        one, two, three = three_parts(-lse_h)
        extra = q_aug_t[at + HEAD_DIM : at + AUG, :].astype(f32)
        extra = jnp.where(row == 4, one, jnp.where(row == 5, two, jnp.where(row == 6, three, extra)))
        q_side[at : at + HEAD_DIM, :] = q_h
        q_side[at + HEAD_DIM : at + AUG, :] = extra.astype(bf16)
        one, two, three = three_parts(-delta)
        extra = jnp.where(row == 0, one, jnp.where(row == 1, two, jnp.where(row == 2, three, 0.0)))
        do_side[at : at + HEAD_DIM, :] = do_h.astype(bf16)
        do_side[at + HEAD_DIM : at + AUG, :] = extra.astype(bf16)
        q_lanes[h] = jnp.where(lane == h, q_here, jnp.zeros_like(q_here))
        do_lanes[h] = jnp.where(lane == h, do_here, jnp.zeros_like(do_here))
        q_h = q_h.astype(f32)
        k_h = k_here[feat, :]
        p_own = padded * jnp.exp(jnp.sum(q_h * k_h, axis=0, keepdims=True) - lse_h)
        dp_own = jnp.sum(do_h * v_t[feat, :].astype(f32), axis=0, keepdims=True)
        ds_own = p_own * (dp_own - delta)
        dq_t[feat, :] = ds_own * k_h
        dk_parts.append(ds_own * q_h)
        dv_parts.append(p_own * do_h)
    dk[here, :] += jnp.concatenate(dk_parts, axis=0).T
    dv[here, :] += jnp.concatenate(dv_parts, axis=0).T

    def step(j, _):
        keys = pl.ds(pl.multiple_of(j * TILE, TILE), TILE)
        probs, grads = [], []
        for h in range(HEADS):
            wide = slice(h * AUG, (h + 1) * AUG)
            prob = jnp.exp(dot_nn(k_aug[keys, wide], q_side[wide, :]))
            grad = prob * dot_nn(v_aug[keys, wide], do_side[wide, :])
            probs.append(prob.astype(bf16))
            grads.append(grad.astype(bf16))
        deep = (HEADS * TILE, WIDTH)
        dv[keys, :] += dot_nn(jnp.concatenate(probs, axis=1), do_lanes[...].reshape(deep))
        dk[keys, :] += dot_nn(jnp.concatenate(grads, axis=1), q_lanes[...].reshape(deep))
        for h in range(HEADS):
            feat = slice(h * HEAD_DIM, (h + 1) * HEAD_DIM)
            dq_t[feat, :] += dot_nn(k_t[feat, keys], grads[h])
        return 0

    begin, end = clip_range(info, tile, k_aug.shape[0])
    lax.fori_loop(begin, end, step, 0)
    dq = dq_t[...].T * (1.0 / math.sqrt(HEAD_DIM))
    cos, low, high = rope_factors(pos, table)
    dq_out[...] = (dq * cos - turned(dq, low, high)).astype(bf16)


def attend_back(
    part, info, me_at, k_aug, v_aug, k_t, q_aug_t, q, v_t, o_t, lse, padding, do, positions, table,
    dk, dv, earlier,
):
    length = k_aug.shape[0]
    half = length // 2

    def owner(i, info):
        return jnp.bitwise_xor(info[me_at], i)

    def rows(columns):
        return pl.BlockSpec((TILE, columns), lambda i, info: (2 * owner(i, info) + part, 0))

    def columns(count):
        return pl.BlockSpec((count, TILE), lambda i, info: (0, 2 * owner(i, info) + part))

    def packed(count):
        return pl.BlockSpec((count, TILE), lambda i, info: (0, owner(i, info)))

    out = jax.ShapeDtypeStruct
    before = () if dk is None else (dk, dv)
    return pl.pallas_call(
        in_order(
            functools.partial(attend_back_kernel, part=part, me_at=me_at, first=dk is None),
            16 + len(before), len(earlier),
        ),
        grid_spec=pltpu.PrefetchScalarGridSpec(
            num_scalar_prefetch=1,
            grid=(half // TILE,),
            in_specs=[
                whole(k_aug.shape), whole(v_aug.shape), whole(k_t.shape), columns(HEADS * AUG),
                rows(WIDTH), columns(WIDTH), packed(WIDTH), packed(8), columns(1),
            ]
            + [pl.BlockSpec((TILE, WIDTH), lambda i, info: (part, 0))] * 4
            + [
                pl.BlockSpec(
                    (3, 1, TILE), lambda i, info: (0, 0, 2 * owner(i, info) + part)
                ),
                whole(table.shape),
            ]
            + [whole((length, WIDTH))] * len(before)
            + unread(earlier),
            out_specs=[
                pl.BlockSpec((TILE, WIDTH), lambda i, info: (owner(i, info), 0)),
                whole((length, WIDTH)), whole((length, WIDTH)),
            ],
            scratch_shapes=[
                pltpu.VMEM((HEADS * AUG, TILE), bf16), pltpu.VMEM((HEADS * AUG, TILE), bf16),
                pltpu.VMEM((HEADS, TILE, WIDTH), bf16), pltpu.VMEM((HEADS, TILE, WIDTH), bf16),
                pltpu.VMEM((WIDTH, TILE), f32),
            ],
        ),
        out_shape=[out((half, WIDTH), bf16), out((length, WIDTH), f32), out((length, WIDTH), f32)],
        compiler_params=params(LIMIT),
        cost_estimate=pl.CostEstimate(
            flops=72 * half * length * WIDTH, bytes_accessed=16 * MIB, transcendentals=0
        ),
        name="attend_back",
    )(
        info, k_aug, v_aug, k_t, q_aug_t, q, v_t, o_t, lse, padding, *do, positions, table, *before,
        *earlier,
    )


def pieces(begin, count, period):
    at, end, cuts = begin, begin + count, []
    while at < end:
        length = min(end - at, period - at % period)
        cuts.append((at, length))
        at += length
    return cuts


def stacked_pairs(rows, count):
    row = lax.broadcasted_iota(jnp.int32, (count, WIDTH), 0)
    out = jnp.zeros((count, WIDTH), f32)
    for m, value in enumerate(rows):
        one, two, _ = three_parts(value)
        out = jnp.where(row == 2 * m, one, jnp.where(row == 2 * m + 1, two, out))
    return out.astype(bf16)


def late_extra(width, blocks):
    vectors = -(-(3 + 7 * width // WIDTH) // blocks)
    return vectors, -(-vectors // 8) * 16


def project_back_kernel(
    info, tok, gain, shift, dq_a, dq_b, dk, dv, pos, table, w, out_kept, out_other, out_there, early,
    dh1, dh1_sent, sums, acc, grad_b, small, w_wide,
):
    i = pl.program_id(0)

    @pl.when(i == 0)
    def _():
        acc[...] = jnp.zeros_like(acc)
        grad_b[...] = jnp.zeros_like(grad_b)
        small[...] = jnp.zeros_like(small)
        for c in range(3):
            w_wide[:, c * WIDTH : (c + 1) * WIDTH] = w[c]

    dk_here = dk[...]
    cos, low, high = rope_factors(pos, table)
    dk_low = (dk_here * cos - turned(dk_here, low, high)).astype(bf16)
    dq = jnp.concatenate([dq_a[...], dq_b[...]])
    parts = jnp.concatenate([dq, dk_low, dv[...].astype(bf16)], axis=1)
    grad = dot_nt(parts, w_wide[...])
    hat, _ = normalized(tok[...].astype(f32))
    normed = (hat * gain[...] + shift[...]).astype(bf16)
    acc[...] += dot_tn(normed, parts)
    grad_b[0:1, :] += jnp.sum(parts.astype(f32), axis=0, keepdims=True)
    small[0:1, :] += jnp.sum(grad * hat, axis=0, keepdims=True)
    small[1:2, :] += jnp.sum(grad, axis=0, keepdims=True)
    low_grad = grad.astype(bf16)
    dh1[0] = low_grad
    dh1_sent[0] = low_grad

    @pl.when(i == pl.num_programs(0) - 1)
    def _():
        width = normed.shape[1]
        blocks = sums.shape[0]

        def cut(value, count):
            return [value[:, r * WIDTH : (r + 1) * WIDTH] for r in range(count)]

        rows = cut(grad_b[0:1, :], 3) + cut(early[4:5, :], width // WIDTH)
        for ref, count in ((small, 2), (early, 4)):
            for v in range(count):
                rows += cut(ref[v : v + 1, :], width // WIDTH)
        for n in range(blocks):
            for to, rows_here, c, begin in late_places(n, blocks, width):
                here = (slice(begin, begin + rows_here), slice(c * WIDTH, (c + 1) * WIDTH))
                sums[n, to : to + rows_here, :] = acc[here].astype(bf16)
            for to, rows_here, c, begin in late_places(n, blocks, width, True):
                here = (slice(begin, begin + rows_here), slice(c * WIDTH, (c + 1) * WIDTH))
                sums[n, to : to + rows_here, :] = (
                    out_kept[here].astype(f32)
                    + out_other[here].astype(f32)
                    + out_there[here].astype(f32)
                ).astype(bf16)
            extra_at = 4 * width // blocks
            sums[n, extra_at:, :] = stacked_pairs(rows[n::blocks], sums.shape[1] - extra_at)


def late_places(n, blocks, width, out=False):
    deep, period = (width // blocks, WIDTH) if out else (3 * width // blocks, width)
    first = 3 * width // blocks if out else 0
    return [
        (first + at - n * deep, length, at // period, at % period)
        for at, length in pieces(n * deep, deep, period)
    ]


def project_back(
    info, me_at, tokens, gain, shift, dq_a, dq_b, dk, dv, positions, table, w, kept, other, there,
    early, blocks, earlier,
):
    length, width = tokens.shape
    share = 2 * TILE

    def owner(i, info):
        return jnp.bitwise_xor(info[me_at], relative(i))

    def rows(count, columns):
        return pl.BlockSpec((count, columns), lambda i, info: (owner(i, info), 0))

    first = pl.BlockSpec((None, TILE, width), lambda i, info: (0, 0, 0))
    out = jax.ShapeDtypeStruct
    sums = (blocks, 4 * width // blocks + late_extra(width, blocks)[1], WIDTH)
    return pl.pallas_call(
        in_order(project_back_kernel, 15, len(earlier)),
        grid_spec=pltpu.PrefetchScalarGridSpec(
            num_scalar_prefetch=1,
            grid=(length // share,),
            in_specs=[
                rows(share, width), whole((1, width)), whole((1, width)), rows(TILE, WIDTH),
                rows(TILE, WIDTH), rows(share, WIDTH), rows(share, WIDTH),
                pl.BlockSpec((3, 1, share), lambda i, info: (0, 0, owner(i, info))),
                whole(table.shape), whole(w.shape), first, first, whole((TILE, width)),
                whole(early.shape),
            ]
            + unread(earlier),
            out_specs=[
                pl.BlockSpec((1, share, width), lambda i, info: (i, 0, 0)),
                pl.BlockSpec((1, share, width), lambda i, info: (jnp.maximum(i - 2, 0), 0, 0)),
                whole(sums),
            ],
            scratch_shapes=[
                pltpu.VMEM((width, 3 * WIDTH), f32), pltpu.VMEM((8, 3 * WIDTH), f32),
                pltpu.VMEM((8, width), f32),
                pltpu.VMEM((width, 3 * WIDTH), bf16),
            ],
        ),
        out_shape=[
            pltpu.HBM((4, share, width), bf16), pltpu.HBM((2, share, width), bf16),
            pltpu.HBM(sums, bf16),
        ],
        compiler_params=params(LIMIT),
        cost_estimate=pl.CostEstimate(
            flops=24 * length * width * WIDTH, bytes_accessed=20 * MIB, transcendentals=0
        ),
        name="project_back",
    )(
        info, tokens, gain, shift, dq_a, dq_b, dk, dv, positions, table, w, kept, other, there, early,
        *earlier,
    )


def vectors_kernel(extra, grad_b, vectors):
    blocks = extra.shape[0]
    width = vectors.shape[1]
    grad_b[...] = jnp.zeros_like(grad_b)
    vectors[...] = jnp.zeros_like(vectors)
    for v in range(3 + 7 * width // WIDTH):
        n, m = v % blocks, v // blocks
        pair = extra[n].astype(f32)
        row = pair[2 * m : 2 * m + 1, :] + pair[2 * m + 1 : 2 * m + 2, :]
        if v < 3:
            grad_b[v : v + 1, :] = row
        else:
            to, at = divmod((v - 3) * WIDTH, width)
            vectors[to : to + 1, at : at + WIDTH] = row


def unpack_vectors(sums, width, earlier):
    blocks = sums.shape[0]
    at, rows = 4 * width // blocks, late_extra(width, blocks)[1]
    return pl.pallas_call(
        in_order(vectors_kernel, 1, len(earlier)),
        grid=(1,),
        in_specs=[pl.BlockSpec((blocks, rows, WIDTH), lambda i: (0, at // rows, 0))]
        + unread(earlier),
        out_specs=[whole((8, WIDTH)), whole((8, width))],
        out_shape=[pltpu.HBM((8, WIDTH), f32), pltpu.HBM((8, width), f32)],
        compiler_params=params(LIMIT),
        name="unpack_vectors",
    )(sums, *earlier)


def unpack_kernel(sums, grad_qkv, grad_out):
    blocks = sums.shape[0]
    width = grad_out.shape[1]
    for n in range(blocks):
        for to, rows, c, begin in late_places(n, blocks, width):
            grad_qkv[c, begin : begin + rows, :] = sums[n, to : to + rows, :].astype(f32)
        for to, rows, c, begin in late_places(n, blocks, width, True):
            grad_out[begin : begin + rows, c * WIDTH : (c + 1) * WIDTH] = sums[
                n, to : to + rows, :
            ].astype(f32)


def unpack(sums, width, earlier):
    out = jax.ShapeDtypeStruct
    return pl.pallas_call(
        in_order(unpack_kernel, 1, len(earlier)),
        in_specs=[pl.BlockSpec(memory_space=pltpu.VMEM)] + unread(earlier),
        out_specs=[pl.BlockSpec(memory_space=pltpu.VMEM)] * 2,
        out_shape=[out((3, width, WIDTH), f32), out((WIDTH, width), f32)],
        compiler_params=pltpu.CompilerParams(vmem_limit_bytes=LIMIT * MIB),
        name="unpack",
    )(sums, *earlier)


def finish_kernel(info, parts, other, there, tok, gain, dx2, out):
    grad = parts[0].astype(f32) + other[0].astype(f32) + there[...].astype(f32)
    hat, inverse = normalized(tok[...].astype(f32))
    out[...] = dx2[...] + norm_back(hat, inverse, gain[...], grad)


def finish(info, me_at, parts, other, there, tokens, gain, dx2, earlier):
    width = tokens.shape[1]
    share = there.shape[0]
    rows = pl.BlockSpec((TILE, width), lambda i, info: (i, 0))
    return pl.pallas_call(
        in_order(finish_kernel, 7, len(earlier)),
        grid_spec=pltpu.PrefetchScalarGridSpec(
            num_scalar_prefetch=1,
            grid=(share // TILE,),
            in_specs=[
                pl.BlockSpec((1, TILE, width), lambda i, info: (0, i, 0)),
                pl.BlockSpec((1, TILE, width), lambda i, info: (0, i, 0)), rows,
                pl.BlockSpec((TILE, width), lambda i, info: (2 * info[me_at] + i, 0)),
                whole((1, width)), rows,
            ]
            + unread(earlier),
            out_specs=rows,
        ),
        out_shape=jax.ShapeDtypeStruct((share, width), f32),
        compiler_params=params(LIMIT),
        cost_estimate=pl.CostEstimate(
            flops=30 * share * width, bytes_accessed=10 * MIB, transcendentals=0
        ),
        name="finish",
    )(info, parts, other, there, tokens, gain, dx2, *earlier)


def total_of(blocks):
    total = blocks[0].astype(f32)
    for n in range(1, blocks.shape[0]):
        total += blocks[n].astype(f32)
    return total.astype(bf16)


def sums_kernel(blocks_a, blocks_b, out):
    rows = blocks_a.shape[1]
    out[:rows, :] = total_of(blocks_a)
    out[rows:, :] = total_of(blocks_b)


def two_sums(blocks_a, blocks_b, earlier):
    _, rows, width = blocks_a.shape
    return pl.pallas_call(
        in_order(sums_kernel, 2, len(earlier)),
        grid=(1,),
        in_specs=[whole(blocks_a.shape), whole(blocks_b.shape)] + unread(earlier),
        out_specs=whole((2 * rows, width)),
        out_shape=pltpu.HBM((2 * rows, width), bf16),
        compiler_params=params(LIMIT),
        name="two_sums",
    )(blocks_a, blocks_b, *earlier)


def sum_kernel(blocks, out):
    out[...] = total_of(blocks)


def summed(blocks, steps, earlier):
    count, rows, width = blocks.shape
    tile = rows // steps
    return pl.pallas_call(
        in_order(sum_kernel, 1, len(earlier)),
        grid=(steps,),
        in_specs=[pl.BlockSpec((count, tile, width), lambda i: (0, i, 0))] + unread(earlier),
        out_specs=pl.BlockSpec((tile, width), lambda i: (i, 0)),
        out_shape=pltpu.HBM((rows, width), bf16),
        compiler_params=params(LIMIT),
        name="summed",
    )(blocks, *earlier)


def copies_kernel(first, second, out):
    total = (first[...].astype(f32) + second[...].astype(f32)).astype(bf16)
    for n in range(out.shape[0]):
        out[n] = total


def sum_copies(first, second, count, earlier):
    rows, width = first.shape
    return pl.pallas_call(
        in_order(copies_kernel, 2, len(earlier)),
        grid=(1,),
        in_specs=[whole((rows, width))] * 2 + unread(earlier),
        out_specs=whole((count, rows, width)),
        out_shape=pltpu.HBM((count, rows, width), bf16),
        compiler_params=params(LIMIT),
        name="sum_copies",
    )(first, second, *earlier)


def swap(array, axis, bit=1):
    size = lax.axis_size(axis)
    if size == 1:
        return jnp.zeros_like(array)
    return lax.ppermute(array, axis, [(i, i ^ bit) for i in range(size)])


def swap_both(array):
    return lax.ppermute(array, MP, [(i, i ^ 3) for i in range(4)])


def scattered(rows, axes):
    group = lax.axis_size(axes)
    length, width = rows.shape
    return lax.all_to_all(
        rows.reshape(group, length // group, width), axes, 0, 0, tiled=True
    )


def both_sums(total):
    if lax.axis_size("zl") == 1:
        return total
    return (total.astype(f32) + swap(total, "zl").astype(f32)).astype(bf16)


def local(
    tokens, cotangent, segments, padding, positions, ln1_gain, ln1_bias, w_qkv, b_qkv, w_out, b_out,
    ln2_gain, ln2_bias, w_up, b_up, w_down, b_down,
):
    width, hidden = w_up.shape
    w_all = lax.all_gather(w_out, MP)
    gain_one, shift_one = ln1_gain[None], ln1_bias[None]
    gain_two, shift_two = ln2_gain[None], ln2_bias[None]
    ends = jnp.sum((segments <= jnp.arange(2)[:, None]).astype(jnp.int32), axis=1)
    info = jnp.concatenate([ends, lax.axis_index(MP)[None].astype(jnp.int32)])
    me_at = 2
    table = jnp.asarray(rope_constants())
    k_aug, v_aug, q_aug_t, q, k_t, v_t = project(
        tokens, w_qkv, b_qkv, gain_one, shift_one, positions, segments, padding, table
    )

    def exchanged(own, to_c, to_zh, to_both):
        return own, swap(to_c, "c"), swap(to_zh, "zh"), swap_both(to_both)

    o_0, o_t_0, lse_0 = attend(0, info, k_aug, v_t, q_aug_t, k_t, padding, ())
    o_zh_0, o_c_0 = swap(o_0, "zh"), swap(o_0, "c")
    o_1, o_t_1, lse_1 = attend(1, info, k_aug, v_t, q_aug_t, k_t, padding, (o_0, w_all))
    o_zh_1 = swap(o_1, "zh")
    o_zh_0 = after(o_zh_0, (o_1,))
    o_parts_0 = tuple((part, None) for part in (o_0, o_c_0, o_zh_0, swap(o_zh_0, "c")))

    def mlp_half(part, o_parts, earlier):
        return mlp(
            part, info, me_at, tokens, cotangent, o_parts, w_all, b_out[None], gain_two, shift_two,
            w_up, b_up[None], w_down, earlier,
        )

    x2_0, dy_0, h2_0, act_0, du_0, mlp_0, mlp_sent_0, dh2_0, sent, db_0 = mlp_half(
        0, o_parts_0, (o_1,)
    )
    pair = paired(o_1, o_zh_1, (x2_0,))
    pair_c = swap(pair, "c")
    o_parts_1 = ((pair, 0), (pair_c, 0), (pair, 1), (pair_c, 1))
    other_0 = swap(sent, "c")
    give_0 = to_give(dh2_0, other_0, ())
    there_0 = swap(give_0, "zh")
    x2_1, dy_1, h2_1, act_1, du_1, mlp_1, mlp_sent_1, dh2_1, sent, db_1 = mlp_half(
        1, o_parts_1, (give_0,)
    )
    other_1 = swap(sent, "c")
    grad_down = down_weights((act_0, act_1), cotangent, ())
    arrived_down = scattered(grad_down, ("y", "x"))
    give_1 = to_give(dh2_1, other_1, (grad_down,))
    there_1 = swap(give_1, "zh")
    grad_up = up_weights((h2_0, h2_1), (du_0, du_1), (give_1,))
    dx2, g, *d_parts, small = middle(
        info, me_at, (dh2_0, other_0, there_0, x2_0, dy_0), (dh2_1, other_1, there_1, x2_1, dy_1),
        gain_two, w_all, (grad_up,),
    )
    do = exchanged(*d_parts)
    arrived_up = scattered(after(grad_up, (g,)), ("y", "x"))
    grad_out, out_sent = out_weights(info, me_at, o_parts_0, o_parts_1, g)
    out_other = swap(out_sent, "c")
    mlp_parts = (mlp_0, mlp_1)
    mlp_others = (swap(mlp_sent_0, "c"), swap(mlp_sent_1, "c"))
    dq_0, dk, dv = attend_back(
        0, info, me_at, k_aug, v_aug, k_t, q_aug_t, q, v_t, o_t_0, lse_0, padding, do, positions,
        table, None, None, (grad_out, g),
    )
    give = to_give(grad_out, out_other, (dq_0,))
    out_there = swap(give, "zh")
    mlp_give = two_to_give(mlp_parts, mlp_others, (give,))
    mlp_there = swap(mlp_give, "zh")
    part_sum = both_sums(two_sums(arrived_up, arrived_down, (mlp_give,)))
    dq_1, dk, dv = attend_back(
        1, info, me_at, k_aug, v_aug, k_t, q_aug_t, q, v_t, o_t_1, lse_1, padding, do, positions,
        table, dk, dv, (give, part_sum),
    )
    grad_mlp = lax.all_gather(part_sum, ("y", "x"), axis=0, tiled=True)
    early = jnp.concatenate([small[0:4], (db_0 + db_1)[0:4]])
    dh1, sent, sums = project_back(
        info, me_at, tokens, gain_one, shift_one, dq_0, dq_1, dk, dv, positions, table, w_qkv,
        grad_out, out_other, out_there, early, lax.axis_size(("y", "x")), (),
    )
    other = swap(sent, "c")
    back = swap(to_give(dh1, other, (sums,)), "zh")
    arrived = scattered(sums.reshape(-1, WIDTH), ("y", "x"))
    total = summed(arrived, 1, (back,))
    copies = sum_copies(total, swap(total, "zl"), sums.shape[0], ())
    late = lax.all_to_all(copies, ("y", "x"), 0, 0, tiled=True)
    grad_inputs = finish(info, me_at, dh1, other, back, tokens, gain_one, dx2, (copies,))
    mixed = mixed_rows(
        (x2_0, x2_1), mlp_parts, mlp_others, mlp_there, b_down[None], (copies,)
    )
    count = lax.axis_size(("y", "x"))
    grad_mlp = grad_mlp.reshape(count, 2, width // count, hidden)
    grad_up = grad_mlp[:, 0].astype(f32).reshape(width, hidden)
    grad_down = grad_mlp[:, 1].astype(f32).reshape(hidden, width)
    grad_b, vectors = unpack_vectors(late, width, (grad_inputs, mixed, grad_up, grad_down))
    by_c, by_zh, by_both = swap(vectors, "c"), swap(vectors, "zh"), swap_both(vectors)
    grad_qkv, grad_w_out = unpack(late, width, (vectors,))
    group = (vectors + by_c) + (by_zh + by_both)
    return (
        mixed, grad_inputs, group[1], group[2], grad_qkv, grad_b[0:3], grad_w_out, group[5],
        group[3], group[4], grad_up, vectors[0], grad_down, group[6],
    )


def solution(mesh):
    packs = mesh.shape["dp"]
    if packs == 32:
        shape = (2, 4, 4, 2, 2)
    else:
        shape = (1, packs, 1, 2, 2)
    split = Mesh(mesh.devices.reshape(shape), EVERY)
    in_specs = (
        P(DP, None), P(DP, None), P(DP, None), P(DP, None), P(None, DP, None), P(), P(),
        P(None, None, MP), P(None, MP), P(MP, None), P(), P(), P(), P(None, MP), P(MP),
        P(MP, None), P(),
    )
    out_specs = (
        P(EVERY, None), P(EVERY, None), P(), P(), P(None, None, MP), P(None, MP), P(MP, None), P(),
        P(), P(), P(None, MP), P(MP), P(MP, None), P(),
    )
    return jax.shard_map(local, mesh=split, in_specs=in_specs, out_specs=out_specs, check_vma=False)
```

```python
import functools
import math

import jax
import jax.numpy as jnp
import ml_dtypes
import numpy as np
from jax import lax
from jax.experimental import pallas as pl
from jax.experimental.pallas import tpu as pltpu
from jax.sharding import Mesh
from jax.sharding import PartitionSpec as P

HEAD_DIM = 64
HEADS = 4
WIDTH = HEADS * HEAD_DIM
AUG = 128
TILE = 256
PLACES = 64
LIMIT = 64
MIB = 1 << 20
DP = ("zl", "y", "x")
MP = ("zh", "c")
EVERY = ("zl", "y", "x", "zh", "c")

epsilon = 1e-06
NEG = -1e30
bf16 = jnp.bfloat16
f32 = jnp.float32


def dot_nn(a, b):
    return lax.dot_general(a, b, (((1,), (0,)), ((), ())), preferred_element_type=f32)


def dot_nt(a, b):
    return lax.dot_general(a, b, (((1,), (1,)), ((), ())), preferred_element_type=f32)


def dot_tn(a, b):
    return lax.dot_general(a, b, (((0,), (0,)), ((), ())), preferred_element_type=f32)


def normalized(values):
    center = jnp.mean(values, axis=-1, keepdims=True)
    shifted = values - center
    spread = jnp.mean(shifted * shifted, axis=-1, keepdims=True)
    inverse = lax.rsqrt(spread + epsilon)
    return shifted * inverse, inverse


def norm_back(hat, inverse, gain, grad):
    scaled = grad * gain
    return inverse * (
        scaled
        - jnp.mean(scaled, axis=-1, keepdims=True)
        - hat * jnp.mean(scaled * hat, axis=-1, keepdims=True)
    )


def turned(x, low, high):
    width = x.shape[1]
    pair = HEAD_DIM // 6
    return pltpu.roll(x, width - pair, 1) * low + pltpu.roll(x, pair, 1) * high


def three_parts(x):
    first = x.astype(bf16).astype(f32)
    rest = x - first
    second = rest.astype(bf16).astype(f32)
    return first, second, rest - second


def params(limit, axes=1):
    return pltpu.CompilerParams(
        dimension_semantics=("arbitrary",) * axes, vmem_limit_bytes=limit * MIB
    )


def in_order(kernel, inputs, earlier):
    def run(*refs):
        kernel(*refs[:inputs], *refs[inputs + earlier :])

    return run


def unread(arrays):
    return [pl.BlockSpec(memory_space=pl.ANY)] * len(arrays)


def whole(shape):
    return pl.BlockSpec(shape, lambda *_: (0,) * len(shape))


def clip_range(info, tile, length):
    first, second = info[0], info[1]
    at = tile * TILE
    begin = jnp.where(second <= at, second, jnp.where(first <= at, first, 0))
    end = jnp.where(
        first >= at + TILE, first, jnp.where(second >= at + TILE, second, length)
    )
    return begin // TILE, (end + TILE - 1) // TILE


def rope_constants():
    pair = HEAD_DIM // 6
    feature = np.arange(WIDTH) % HEAD_DIM
    section, place = feature // (2 * pair), feature % (2 * pair)
    frequency = np.exp(-math.log(10000.0) * (place % pair) / pair)
    table = np.zeros((PLACES, 3, WIDTH))
    for s in range(3):
        for value in range(16):
            angle = value * frequency
            turns = section == s
            table[s * 16 + value, 0] = np.where(turns, np.cos(angle), 0.0)
            table[s * 16 + value, 1] = np.where(turns & (place < pair), -np.sin(angle), 0.0)
            table[s * 16 + value, 2] = np.where(turns & (place >= pair), np.sin(angle), 0.0)
    table[48, 0] = section == 3
    rest = table.reshape(PLACES, 3 * WIDTH).astype(np.float32)
    parts = []
    for _ in range(3):
        part = rest.astype(ml_dtypes.bfloat16)
        parts.append(part)
        rest = rest - part.astype(np.float32)
    return np.concatenate(parts)


def rope_factors(positions, table):
    row = lax.broadcasted_iota(jnp.int32, (PLACES, positions.shape[-1]), 0)
    where = jnp.where(
        row < 16, positions[0], jnp.where(row < 32, positions[1], positions[2])
    )
    hit = ((where == row % 16) & (row < 48)) | (row == 48)
    hit = jnp.where(hit, 1.0, 0.0)
    hits = jnp.concatenate([hit, hit, hit]).astype(bf16)
    factors = dot_tn(hits, table[...])
    return factors[:, :WIDTH], factors[:, WIDTH : 2 * WIDTH], factors[:, 2 * WIDTH :]


def qkv_kernel(
    tok, w, b, gain, shift, pos, seg, pad, table, k_aug, v_aug, q_aug_t, q_out, k_t, v_t, w_wide
):
    @pl.when(pl.program_id(0) == 0)
    def _():
        for c in range(3):
            w_wide[:, c * WIDTH : (c + 1) * WIDTH] = w[c]

    hat, _ = normalized(tok[...].astype(f32))
    normed = (hat * gain[...] + shift[...]).astype(bf16)
    cos, low, high = rope_factors(pos, table)
    all_three = dot_nn(normed, w_wide[...])
    q = all_three[:, :WIDTH] + b[0:1, :]
    k = all_three[:, WIDTH : 2 * WIDTH] + b[1:2, :]
    v = all_three[:, 2 * WIDTH :] + b[2:3, :]
    q = (q * cos + turned(q, low, high)) * (1.0 / math.sqrt(HEAD_DIM))
    k = k * cos + turned(k, low, high)
    q_out[...] = q.astype(bf16)
    q_t = q.T.astype(bf16)
    k_t[...] = k.T.astype(bf16)
    v_t[...] = v.T.astype(bf16)
    row = lax.broadcasted_iota(jnp.int32, (HEAD_DIM, TILE), 0)
    clip = seg[...]
    same = (row >= 1) & (row < 4) & (clip == row - 1)
    mask = jnp.where((row >= 1) & (row < 4) & (clip != row - 1), NEG, 0.0)
    mask = jnp.where(row == 0, jnp.where(pad[...] != 0, NEG, 0.0), mask)
    k_extra = jnp.where((row >= 4) & (row < 7), 1.0, mask)
    q_extra = jnp.where(same | (row == 0), 1.0, 0.0).astype(bf16)
    k_side = jnp.concatenate([jnp.zeros((HEAD_DIM, TILE), f32), k_extra]).T
    lane = lax.broadcasted_iota(jnp.int32, (TILE, AUG), 1)
    ones = jnp.where((lane >= HEAD_DIM) & (lane < HEAD_DIM + 3), 1.0, 0.0)
    for h in range(HEADS):
        pair = slice(h // 2 * AUG, h // 2 * AUG + AUG)
        wide = slice(h * AUG, (h + 1) * AUG)
        k_pair, v_pair = k[:, pair], v[:, pair]
        if h % 2:
            k_pair, v_pair = pltpu.roll(k_pair, HEAD_DIM, 1), pltpu.roll(v_pair, HEAD_DIM, 1)
        k_aug[:, wide] = jnp.where(lane < HEAD_DIM, k_pair, k_side).astype(bf16)
        v_aug[:, wide] = jnp.where(lane < HEAD_DIM, v_pair, ones).astype(bf16)
        q_aug_t[h * AUG : h * AUG + HEAD_DIM, :] = q_t[h * HEAD_DIM : (h + 1) * HEAD_DIM, :]
        q_aug_t[h * AUG + HEAD_DIM : (h + 1) * AUG, :] = q_extra


def project(tokens, w, b, gain, shift, positions, segments, padding, table):
    length, width = tokens.shape
    tiles = length // TILE

    def rows(columns):
        return pl.BlockSpec((TILE, columns), lambda i: (i, 0))

    def columns(count):
        return pl.BlockSpec((count, TILE), lambda i: (0, i))

    out = jax.ShapeDtypeStruct
    wide = out((length, HEADS * AUG), bf16)
    flat = out((WIDTH, length), bf16)
    return pl.pallas_call(
        qkv_kernel,
        grid=(tiles,),
        in_specs=[
            rows(width), whole(w.shape), whole(b.shape), whole((1, width)), whole((1, width)),
            pl.BlockSpec((3, 1, TILE), lambda i: (0, 0, i)), columns(1), columns(1), whole(table.shape),
        ],
        out_specs=[
            rows(HEADS * AUG), rows(HEADS * AUG), columns(HEADS * AUG), rows(WIDTH), columns(WIDTH),
            columns(WIDTH),
        ],
        out_shape=[
            wide, wide, out((HEADS * AUG, length), bf16), out((length, WIDTH), bf16), flat, flat,
        ],
        scratch_shapes=[pltpu.VMEM((width, 3 * WIDTH), bf16)],
        compiler_params=params(LIMIT),
        cost_estimate=pl.CostEstimate(
            flops=6 * length * width * WIDTH, bytes_accessed=20 * MIB, transcendentals=0
        ),
        name="project",
    )(tokens, w, b, gain, shift, positions, segments, padding, table)


def attend_kernel(info, k_aug, v_t, q_aug_t, k_t, pad, o, o_t, lse, top, total, acc, *, part):
    tile = 2 * pl.program_id(0) + part
    padded = pad[...] != 0
    for h in range(HEADS):
        q_h = q_aug_t[h * AUG : h * AUG + HEAD_DIM, :].astype(f32)
        k_h = k_t[h * HEAD_DIM : (h + 1) * HEAD_DIM, :].astype(f32)
        own = jnp.sum(q_h * k_h, axis=0, keepdims=True)
        top[h : h + 1, :] = jnp.where(padded, own, -3e38)
        total[h : h + 1, :] = jnp.where(padded, 1.0, 0.0)
    here = pl.ds(pl.multiple_of(tile * TILE, TILE), TILE)
    acc[...] = jnp.where(padded, v_t[:, here].astype(f32), 0.0)
    feats = [slice(h * HEAD_DIM, (h + 1) * HEAD_DIM) for h in range(HEADS)]
    wides = [slice(h * AUG, (h + 1) * AUG) for h in range(HEADS)]

    def step(j, count):
        keys = pl.ds(pl.multiple_of(j * TILE, TILE), count * TILE)
        scores = [dot_nn(k_aug[keys, wide], q_aug_t[wide, :]) for wide in wides]
        probs, fades = [], []
        for h in range(HEADS):
            old = top[h : h + 1, :]
            new = jnp.maximum(old, jnp.max(scores[h], axis=0, keepdims=True))
            prob = jnp.exp(scores[h] - new)
            fade = jnp.exp(old - new)
            top[h : h + 1, :] = new
            total[h : h + 1, :] = total[h : h + 1, :] * fade + jnp.sum(prob, axis=0, keepdims=True)
            probs.append(prob.astype(bf16))
            fades.append(fade)
        for h, feat in enumerate(feats):
            acc[feat, :] = acc[feat, :] * fades[h] + dot_nn(v_t[feat, keys], probs[h])

    begin, end = clip_range(info, tile, k_aug.shape[0])
    pairs = (end - begin) // 2

    def two(n, _):
        step(begin + 2 * n, 2)
        return 0

    lax.fori_loop(0, pairs, two, 0)

    @pl.when(begin + 2 * pairs < end)
    def _():
        step(end - 1, 1)

    for h, feat in enumerate(feats):
        acc[feat, :] = acc[feat, :] / total[h : h + 1, :]
    lse[...] = jnp.zeros_like(lse)
    lse[0:HEADS, :] = top[0:HEADS, :] + jnp.log(total[0:HEADS, :])
    turned_o = acc[...]
    o_t[...] = turned_o.astype(bf16)
    o[...] = turned_o.T.astype(bf16)


def attend(part, info, k_aug, v_t, q_aug_t, k_t, padding, earlier):
    length = k_aug.shape[0]
    half = length // 2

    def columns(count):
        return pl.BlockSpec((count, TILE), lambda i, *_: (0, 2 * i + part))

    def packed(count):
        return pl.BlockSpec((count, TILE), lambda i, *_: (0, i))

    out = jax.ShapeDtypeStruct
    return pl.pallas_call(
        in_order(functools.partial(attend_kernel, part=part), 6, len(earlier)),
        grid_spec=pltpu.PrefetchScalarGridSpec(
            num_scalar_prefetch=1,
            grid=(half // TILE,),
            in_specs=[
                whole(k_aug.shape), whole(v_t.shape), columns(HEADS * AUG), columns(WIDTH),
                columns(1),
            ]
            + unread(earlier),
            out_specs=[
                pl.BlockSpec((TILE, WIDTH), lambda i, *_: (i, 0)), packed(WIDTH), packed(8),
            ],
            scratch_shapes=[
                pltpu.VMEM((8, TILE), f32), pltpu.VMEM((8, TILE), f32), pltpu.VMEM((WIDTH, TILE), f32),
            ],
        ),
        out_shape=[out((half, WIDTH), bf16), out((WIDTH, half), bf16), out((8, half), f32)],
        compiler_params=params(LIMIT),
        cost_estimate=pl.CostEstimate(
            flops=24 * half * length * WIDTH, bytes_accessed=6 * MIB, transcendentals=0
        ),
        name="attend",
    )(info, k_aug, v_t, q_aug_t, k_t, padding, *earlier)


def nothing(*refs):
    del refs


def after(value, earlier):
    return pl.pallas_call(
        nothing,
        in_specs=unread((value,) + earlier),
        out_specs=pl.BlockSpec(memory_space=pl.ANY),
        out_shape=jax.ShapeDtypeStruct(value.shape, value.dtype),
        input_output_aliases={0: 0},
        name="after",
    )(value, *earlier)


def pair_kernel(first, second, out):
    out[0] = first[...]
    out[1] = second[...]


def paired(first, second, earlier):
    shape = (2,) + first.shape
    return pl.pallas_call(
        in_order(pair_kernel, 2, len(earlier)),
        in_specs=[pl.BlockSpec(memory_space=pltpu.VMEM)] * 2 + unread(earlier),
        out_specs=pl.BlockSpec(memory_space=pltpu.VMEM),
        out_shape=jax.ShapeDtypeStruct(shape, first.dtype),
        name="paired",
    )(first, second, *earlier)


def head_block(at, owner):
    if at is None:
        return pl.BlockSpec((TILE, WIDTH), lambda i, info: (owner(i, info), 0))
    return pl.BlockSpec((None, TILE, WIDTH), lambda i, info: (at, owner(i, info), 0))


def relative(i):
    return i % 2 * 2 + i // 2


def gelu_parts(u):
    size = jnp.abs(u)
    t = 1.0 / (1.0 + (0.3275911 / math.sqrt(2.0)) * size)
    bell = jnp.exp(-0.5 * (u * u))
    poly = 0.5 * 1.061405429
    for c in (-1.453152027, 1.421413741, -0.284496736, 0.254829592):
        poly = poly * t + 0.5 * c
    tail = poly * t * bell
    below = jnp.where(u >= 0, 1.0 - tail, tail)
    return u * below, below + u * bell * (1.0 / math.sqrt(2.0 * math.pi))


def mlp_kernel(
    info, tok, cot, o_0, o_1, o_2, o_3, w_all, b_out, gain, shift, w_up, b_up, w_down,
    x2, dy, h2, act, du, mlp, mlp_sent, dh2, dh2_sent, db_up, w_out, *, me_at,
):
    i = pl.program_id(0)

    @pl.when(i == 0)
    def _():
        for j in range(4):
            w_out[j * WIDTH : (j + 1) * WIDTH, :] = w_all[jnp.bitwise_xor(info[me_at], j)]
        db_up[...] = jnp.zeros_like(db_up)

    heads = jnp.concatenate([o_0[...], o_1[...], o_2[...], o_3[...]], axis=1)
    mid = tok[...].astype(f32) + b_out[...] + dot_nn(heads, w_out[...])

    @pl.when(i == 0)
    def _():
        x2[...] = mid
        dy[...] = cot[...]

    hat, _ = normalized(mid)
    normed = (hat * gain[...] + shift[...]).astype(bf16)
    h2[...] = normed
    u = dot_nn(normed, w_up[...]) + b_up[...]
    grad_act = dot_nt(cot[...], w_down[...])
    value, slope = gelu_parts(u)
    value = value.astype(bf16)
    grad = (grad_act * slope).astype(bf16)
    act[...] = value
    du[...] = grad
    db_up[0:1, :] += jnp.sum(grad.astype(f32), axis=0, keepdims=True)
    mlp_part = dot_nn(value, w_down[...]).astype(bf16)
    dh2_part = dot_nt(grad, w_up[...]).astype(bf16)
    mlp[0] = mlp_part
    mlp_sent[0] = mlp_part
    dh2[0] = dh2_part
    dh2_sent[0] = dh2_part


def mlp(
    part, info, me_at, tokens, cotangent, o_parts, w_all, b_out, gain, shift, w_up, b_up, w_down,
    earlier,
):
    length, width = tokens.shape
    half = length // 2
    hidden = w_up.shape[1]
    owners = half // TILE

    def owner(i, info):
        return jnp.bitwise_xor(info[me_at], relative(i))

    def rows(columns):
        return pl.BlockSpec((TILE, columns), lambda i, info: (2 * owner(i, info) + part, 0))

    def packed(columns):
        return pl.BlockSpec((TILE, columns), lambda i, info: (owner(i, info), 0))

    ordered = pl.BlockSpec((1, TILE, width), lambda i, info: (i, 0, 0))
    sent = pl.BlockSpec((1, TILE, width), lambda i, info: (jnp.maximum(i - 2, 0), 0, 0))

    out = jax.ShapeDtypeStruct
    return pl.pallas_call(
        in_order(functools.partial(mlp_kernel, me_at=me_at), 14, len(earlier)),
        grid_spec=pltpu.PrefetchScalarGridSpec(
            num_scalar_prefetch=1,
            grid=(owners,),
            in_specs=[rows(width), rows(width)]
            + [head_block(at, owner) for _, at in o_parts]
            + [whole(w_all.shape)]
            + [whole((1, width))] * 3
            + [whole(w_up.shape), whole((1, hidden)), whole(w_down.shape)]
            + unread(earlier),
            out_specs=[
                whole((TILE, width)), whole((TILE, width)), packed(width), packed(hidden),
                packed(hidden), ordered, sent, ordered, sent, whole((8, hidden)),
            ],
            scratch_shapes=[pltpu.VMEM((4 * WIDTH, width), bf16)],
        ),
        out_shape=[
            out((TILE, width), f32), out((TILE, width), bf16), out((half, width), bf16),
            out((half, hidden), bf16), out((half, hidden), bf16),
        ]
        + [out((owners, TILE, width), bf16), out((2, TILE, width), bf16)] * 2
        + [out((8, hidden), f32)],
        compiler_params=params(LIMIT),
        cost_estimate=pl.CostEstimate(
            flops=20 * half * width * hidden, bytes_accessed=20 * MIB, transcendentals=0
        ),
        name="mlp",
    )(
        info, tokens, cotangent, *(part for part, _ in o_parts), w_all, b_out, gain, shift, w_up,
        b_up, w_down, *earlier
    )


def up_weights_kernel(left_a, left_b, right_a, right_b, out):
    left = jnp.concatenate([left_a[...], left_b[...]])
    right = jnp.concatenate([right_a[...], right_b[...]])
    out[...] = dot_tn(left, right).astype(bf16)


def up_weights(h2, du, earlier):
    half, width = h2[0].shape
    hidden = du[0].shape[1]
    return pl.pallas_call(
        in_order(up_weights_kernel, 4, len(earlier)),
        grid=(width // TILE,),
        in_specs=[pl.BlockSpec((half, TILE), lambda i: (0, i))] * 2
        + [whole((half, hidden))] * 2
        + unread(earlier),
        out_specs=pl.BlockSpec((TILE, hidden), lambda i: (i, 0)),
        out_shape=pltpu.HBM((width, hidden), bf16),
        compiler_params=params(LIMIT),
        cost_estimate=pl.CostEstimate(
            flops=8 * half * width * hidden, bytes_accessed=12 * MIB, transcendentals=0
        ),
        name="up_weights",
    )(*h2, *du, *earlier)


def down_weights_kernel(act_a, act_b, cot, out):
    owners = cot.shape[0] // (2 * TILE)
    rows = [cot[n * TILE : (n + 1) * TILE, :] for p in range(2) for n in range(p, 2 * owners, 2)]
    out[...] = dot_tn(
        jnp.concatenate([act_a[...], act_b[...]]), jnp.concatenate(rows)
    ).astype(bf16)


def down_weights(act, cotangent, earlier):
    half, hidden = act[0].shape
    length, width = cotangent.shape
    return pl.pallas_call(
        in_order(down_weights_kernel, 3, len(earlier)),
        grid=(hidden // TILE,),
        in_specs=[pl.BlockSpec((half, TILE), lambda i: (0, i))] * 2
        + [whole((length, width))]
        + unread(earlier),
        out_specs=pl.BlockSpec((TILE, width), lambda i: (i, 0)),
        out_shape=pltpu.HBM((hidden, width), bf16),
        compiler_params=params(LIMIT),
        cost_estimate=pl.CostEstimate(
            flops=8 * half * width * hidden, bytes_accessed=12 * MIB, transcendentals=0
        ),
        name="down_weights",
    )(*act, cotangent, *earlier)


def add_kernel(parts, other, out):
    out[...] = (parts[0].astype(f32) + other[0].astype(f32)).astype(bf16)


def to_give(parts, other, earlier):
    _, rows, width = parts.shape
    tile = min(rows, TILE)
    return pl.pallas_call(
        in_order(add_kernel, 2, len(earlier)),
        grid=(rows // tile,),
        in_specs=[
            pl.BlockSpec((1, tile, width), lambda i: (1, i, 0)),
            pl.BlockSpec((1, tile, width), lambda i: (1, i, 0)),
        ]
        + unread(earlier),
        out_specs=pl.BlockSpec((tile, width), lambda i: (i, 0)),
        out_shape=pltpu.HBM((rows, width), bf16),
        compiler_params=params(LIMIT),
        name="to_give",
    )(parts, other, *earlier)


def two_kernel(parts_a, parts_b, other_a, other_b, out):
    for n, (parts, other) in enumerate(((parts_a, other_a), (parts_b, other_b))):
        out[n] = (parts[0].astype(f32) + other[0].astype(f32)).astype(bf16)


def two_to_give(parts, others, earlier):
    _, rows, width = parts[0].shape
    tile = rows // 2
    return pl.pallas_call(
        in_order(two_kernel, 4, len(earlier)),
        grid=(rows // tile,),
        in_specs=[pl.BlockSpec((1, tile, width), lambda i: (1, i, 0))] * 4 + unread(earlier),
        out_specs=pl.BlockSpec((2, tile, width), lambda i: (0, i, 0)),
        out_shape=pltpu.HBM((2, rows, width), bf16),
        compiler_params=params(LIMIT),
        name="two_to_give",
    )(*parts, *others, *earlier)


def mixed_kernel(x2_a, x2_b, parts_a, parts_b, other_a, other_b, there, shift, out):
    for n, (x2, parts, other) in enumerate(
        ((x2_a, parts_a, other_a), (x2_b, parts_b, other_b))
    ):
        total = parts[0].astype(f32) + other[0].astype(f32) + there[n].astype(f32)
        out[n * TILE : (n + 1) * TILE, :] = (x2[...] + total + shift[...]).astype(bf16)


def mixed_rows(x2, parts, others, there, shift, earlier):
    rows, width = x2[0].shape
    first = pl.BlockSpec((1, rows, width), lambda i: (0, 0, 0))
    return pl.pallas_call(
        in_order(mixed_kernel, 8, len(earlier)),
        grid=(1,),
        in_specs=[whole((rows, width))] * 2
        + [first] * 4
        + [whole((2, rows, width)), whole((1, width))]
        + unread(earlier),
        out_specs=whole((2 * rows, width)),
        out_shape=jax.ShapeDtypeStruct((2 * rows, width), bf16),
        compiler_params=params(LIMIT),
        name="mixed_rows",
    )(*x2, *parts, *others, there, shift, *earlier)


def middle_kernel(info, *refs, me_at):
    halves, (gain, w_all, dx2, g, d_0, d_1, d_2, d_3, small) = (refs[0:5], refs[5:10]), refs[10:]
    small[...] = jnp.zeros_like(small)
    for part, (kept, other, there, x2, dy) in enumerate(halves):
        rows = slice(part * TILE, (part + 1) * TILE)
        grad = kept[0].astype(f32) + other[0].astype(f32) + there[...].astype(f32)
        hat, inverse = normalized(x2[...])
        dy = dy[...].astype(f32)
        full = dy + norm_back(hat, inverse, gain[...], grad)
        dx2[rows, :] = full
        low = full.astype(bf16)
        g[rows, :] = low
        small[0:1, :] += jnp.sum(grad * hat, axis=0, keepdims=True)
        small[1:2, :] += jnp.sum(grad, axis=0, keepdims=True)
        small[2:3, :] += jnp.sum(low.astype(f32), axis=0, keepdims=True)
        small[3:4, :] += jnp.sum(dy, axis=0, keepdims=True)
    low = g[...]
    for j, d_j in enumerate((d_0, d_1, d_2, d_3)):
        d_j[...] = dot_nt(low, w_all[jnp.bitwise_xor(info[me_at], j)]).astype(bf16)


def middle(info, me_at, half_a, half_b, gain, w_all, earlier):
    width = gain.shape[1]
    rows = 2 * TILE
    own = whole((TILE, width))
    first = pl.BlockSpec((1, TILE, width), lambda i, info: (0, 0, 0))
    return pl.pallas_call(
        in_order(functools.partial(middle_kernel, me_at=me_at), 13, len(earlier)),
        grid_spec=pltpu.PrefetchScalarGridSpec(
            num_scalar_prefetch=1,
            grid=(1,),
            in_specs=[first, first, own, own, own] * 2
            + [whole((1, width)), whole(w_all.shape)]
            + unread(earlier),
            out_specs=[whole((rows, width))] * 2
            + [whole((rows, WIDTH))] * 4
            + [whole((8, width))],
        ),
        out_shape=[pltpu.HBM((rows, width), f32), pltpu.HBM((rows, width), bf16)]
        + [pltpu.HBM((rows, WIDTH), bf16)] * 4
        + [pltpu.HBM((8, width), f32)],
        compiler_params=params(LIMIT),
        cost_estimate=pl.CostEstimate(
            flops=4 * TILE * width * width, bytes_accessed=12 * MIB, transcendentals=0
        ),
        name="middle",
    )(info, *half_a, *half_b, gain, w_all, *earlier)


def out_weights_kernel(info, *refs):
    parts_a, parts_b, (g, kept, sent) = refs[0:4], refs[4:8], refs[8:]
    for n in range(2):
        for out, j in ((kept, 2 * n), (sent, 2 * n + 1)):
            heads = jnp.concatenate([parts_a[j][...], parts_b[j][...]])
            out[n] = dot_tn(heads, g[...]).astype(bf16)


def out_weights(info, me_at, parts_a, parts_b, g):
    width = g.shape[1]

    def owner(i, info):
        return info[me_at]

    return pl.pallas_call(
        out_weights_kernel,
        grid_spec=pltpu.PrefetchScalarGridSpec(
            num_scalar_prefetch=1,
            grid=(1,),
            in_specs=[head_block(at, owner) for _, at in parts_a + parts_b]
            + [whole(g.shape)],
            out_specs=[whole((2, WIDTH, width))] * 2,
        ),
        out_shape=[pltpu.HBM((2, WIDTH, width), bf16)] * 2,
        compiler_params=params(LIMIT),
        cost_estimate=pl.CostEstimate(
            flops=4 * TILE * width * width, bytes_accessed=6 * MIB, transcendentals=0
        ),
        name="out_weights",
    )(info, *(part for part, _ in parts_a + parts_b), g)


def attend_back_kernel(
    info, k_aug, v_aug, k_t, q_aug_t, q, v_t, o_t, lse, pad, do_0, do_1, do_2, do_3, pos, table,
    *refs, part, me_at, first,
):
    if first:
        dk_in = dv_in = None
    else:
        dk_in, dv_in, *refs = refs
    dq_out, dk, dv, q_side, do_side, q_lanes, do_lanes, dq_t = refs
    i = pl.program_id(0)
    tile = 2 * jnp.bitwise_xor(info[me_at], i) + part

    @pl.when(i == 0)
    def _():
        if first:
            dk[...] = jnp.zeros_like(dk)
            dv[...] = jnp.zeros_like(dv)
        else:
            dk[...] = dk_in[...]
            dv[...] = dv_in[...]

    here = pl.ds(pl.multiple_of(tile * TILE, TILE), TILE)
    do_here = jnp.where(
        i == 0, do_0[...], jnp.where(i == 1, do_1[...], jnp.where(i == 2, do_2[...], do_3[...]))
    )
    q_here = q[...]
    do_t = do_here.astype(f32).T
    k_here = k_t[:, here].astype(f32)
    padded = jnp.where(pad[...] != 0, 1.0, 0.0)
    row = lax.broadcasted_iota(jnp.int32, (AUG - HEAD_DIM, TILE), 0)
    lane = lax.broadcasted_iota(jnp.int32, (TILE, WIDTH), 1) // HEAD_DIM
    dk_parts, dv_parts = [], []
    for h in range(HEADS):
        feat = slice(h * HEAD_DIM, (h + 1) * HEAD_DIM)
        at = h * AUG
        q_h = q_aug_t[at : at + HEAD_DIM, :]
        do_h = do_t[feat, :]
        delta = jnp.sum(do_h * o_t[feat, :].astype(f32), axis=0, keepdims=True)
        lse_h = lse[h : h + 1, :]
        one, two, three = three_parts(-lse_h)
        extra = q_aug_t[at + HEAD_DIM : at + AUG, :].astype(f32)
        extra = jnp.where(row == 4, one, jnp.where(row == 5, two, jnp.where(row == 6, three, extra)))
        q_side[at : at + HEAD_DIM, :] = q_h
        q_side[at + HEAD_DIM : at + AUG, :] = extra.astype(bf16)
        one, two, three = three_parts(-delta)
        extra = jnp.where(row == 0, one, jnp.where(row == 1, two, jnp.where(row == 2, three, 0.0)))
        do_side[at : at + HEAD_DIM, :] = do_h.astype(bf16)
        do_side[at + HEAD_DIM : at + AUG, :] = extra.astype(bf16)
        q_lanes[h] = jnp.where(lane == h, q_here, jnp.zeros_like(q_here))
        do_lanes[h] = jnp.where(lane == h, do_here, jnp.zeros_like(do_here))
        q_h = q_h.astype(f32)
        k_h = k_here[feat, :]
        p_own = padded * jnp.exp(jnp.sum(q_h * k_h, axis=0, keepdims=True) - lse_h)
        dp_own = jnp.sum(do_h * v_t[feat, :].astype(f32), axis=0, keepdims=True)
        ds_own = p_own * (dp_own - delta)
        dq_t[feat, :] = ds_own * k_h
        dk_parts.append(ds_own * q_h)
        dv_parts.append(p_own * do_h)
    dk[here, :] += jnp.concatenate(dk_parts, axis=0).T
    dv[here, :] += jnp.concatenate(dv_parts, axis=0).T

    def step(j, _):
        keys = pl.ds(pl.multiple_of(j * TILE, TILE), TILE)
        probs, grads = [], []
        for h in range(HEADS):
            wide = slice(h * AUG, (h + 1) * AUG)
            prob = jnp.exp(dot_nn(k_aug[keys, wide], q_side[wide, :]))
            grad = prob * dot_nn(v_aug[keys, wide], do_side[wide, :])
            probs.append(prob.astype(bf16))
            grads.append(grad.astype(bf16))
        deep = (HEADS * TILE, WIDTH)
        dv[keys, :] += dot_nn(jnp.concatenate(probs, axis=1), do_lanes[...].reshape(deep))
        dk[keys, :] += dot_nn(jnp.concatenate(grads, axis=1), q_lanes[...].reshape(deep))
        for h in range(HEADS):
            feat = slice(h * HEAD_DIM, (h + 1) * HEAD_DIM)
            dq_t[feat, :] += dot_nn(k_t[feat, keys], grads[h])
        return 0

    begin, end = clip_range(info, tile, k_aug.shape[0])
    lax.fori_loop(begin, end, step, 0)
    dq = dq_t[...].T * (1.0 / math.sqrt(HEAD_DIM))
    cos, low, high = rope_factors(pos, table)
    dq_out[...] = (dq * cos - turned(dq, low, high)).astype(bf16)


def attend_back(
    part, info, me_at, k_aug, v_aug, k_t, q_aug_t, q, v_t, o_t, lse, padding, do, positions, table,
    dk, dv, earlier,
):
    length = k_aug.shape[0]
    half = length // 2

    def owner(i, info):
        return jnp.bitwise_xor(info[me_at], i)

    def rows(columns):
        return pl.BlockSpec((TILE, columns), lambda i, info: (2 * owner(i, info) + part, 0))

    def columns(count):
        return pl.BlockSpec((count, TILE), lambda i, info: (0, 2 * owner(i, info) + part))

    def packed(count):
        return pl.BlockSpec((count, TILE), lambda i, info: (0, owner(i, info)))

    out = jax.ShapeDtypeStruct
    before = () if dk is None else (dk, dv)
    return pl.pallas_call(
        in_order(
            functools.partial(attend_back_kernel, part=part, me_at=me_at, first=dk is None),
            16 + len(before), len(earlier),
        ),
        grid_spec=pltpu.PrefetchScalarGridSpec(
            num_scalar_prefetch=1,
            grid=(half // TILE,),
            in_specs=[
                whole(k_aug.shape), whole(v_aug.shape), whole(k_t.shape), columns(HEADS * AUG),
                rows(WIDTH), columns(WIDTH), packed(WIDTH), packed(8), columns(1),
            ]
            + [pl.BlockSpec((TILE, WIDTH), lambda i, info: (part, 0))] * 4
            + [
                pl.BlockSpec(
                    (3, 1, TILE), lambda i, info: (0, 0, 2 * owner(i, info) + part)
                ),
                whole(table.shape),
            ]
            + [whole((length, WIDTH))] * len(before)
            + unread(earlier),
            out_specs=[
                pl.BlockSpec((TILE, WIDTH), lambda i, info: (owner(i, info), 0)),
                whole((length, WIDTH)), whole((length, WIDTH)),
            ],
            scratch_shapes=[
                pltpu.VMEM((HEADS * AUG, TILE), bf16), pltpu.VMEM((HEADS * AUG, TILE), bf16),
                pltpu.VMEM((HEADS, TILE, WIDTH), bf16), pltpu.VMEM((HEADS, TILE, WIDTH), bf16),
                pltpu.VMEM((WIDTH, TILE), f32),
            ],
        ),
        out_shape=[out((half, WIDTH), bf16), out((length, WIDTH), f32), out((length, WIDTH), f32)],
        compiler_params=params(LIMIT),
        cost_estimate=pl.CostEstimate(
            flops=72 * half * length * WIDTH, bytes_accessed=16 * MIB, transcendentals=0
        ),
        name="attend_back",
    )(
        info, k_aug, v_aug, k_t, q_aug_t, q, v_t, o_t, lse, padding, *do, positions, table, *before,
        *earlier,
    )


def pieces(begin, count, period):
    at, end, cuts = begin, begin + count, []
    while at < end:
        length = min(end - at, period - at % period)
        cuts.append((at, length))
        at += length
    return cuts


def stacked_pairs(rows, count):
    row = lax.broadcasted_iota(jnp.int32, (count, WIDTH), 0)
    out = jnp.zeros((count, WIDTH), f32)
    for m, value in enumerate(rows):
        one, two, _ = three_parts(value)
        out = jnp.where(row == 2 * m, one, jnp.where(row == 2 * m + 1, two, out))
    return out.astype(bf16)


def late_extra(width, blocks):
    vectors = -(-(3 + 7 * width // WIDTH) // blocks)
    return vectors, -(-vectors // 8) * 16


def project_back_kernel(
    info, tok, gain, shift, dq_a, dq_b, dk, dv, pos, table, w, out_kept, out_other, out_there, early,
    dh1, dh1_sent, sums, acc, grad_b, small, w_wide,
):
    i = pl.program_id(0)

    @pl.when(i == 0)
    def _():
        acc[...] = jnp.zeros_like(acc)
        grad_b[...] = jnp.zeros_like(grad_b)
        small[...] = jnp.zeros_like(small)
        for c in range(3):
            w_wide[:, c * WIDTH : (c + 1) * WIDTH] = w[c]

    dk_here = dk[...]
    cos, low, high = rope_factors(pos, table)
    dk_low = (dk_here * cos - turned(dk_here, low, high)).astype(bf16)
    dq = jnp.concatenate([dq_a[...], dq_b[...]])
    parts = jnp.concatenate([dq, dk_low, dv[...].astype(bf16)], axis=1)
    grad = dot_nt(parts, w_wide[...])
    hat, _ = normalized(tok[...].astype(f32))
    normed = (hat * gain[...] + shift[...]).astype(bf16)
    acc[...] += dot_tn(normed, parts)
    grad_b[0:1, :] += jnp.sum(parts.astype(f32), axis=0, keepdims=True)
    small[0:1, :] += jnp.sum(grad * hat, axis=0, keepdims=True)
    small[1:2, :] += jnp.sum(grad, axis=0, keepdims=True)
    low_grad = grad.astype(bf16)
    dh1[0] = low_grad
    dh1_sent[0] = low_grad

    @pl.when(i == pl.num_programs(0) - 1)
    def _():
        width = normed.shape[1]
        blocks = sums.shape[0]

        def cut(value, count):
            return [value[:, r * WIDTH : (r + 1) * WIDTH] for r in range(count)]

        rows = cut(grad_b[0:1, :], 3) + cut(early[4:5, :], width // WIDTH)
        for ref, count in ((small, 2), (early, 4)):
            for v in range(count):
                rows += cut(ref[v : v + 1, :], width // WIDTH)
        for n in range(blocks):
            for to, rows_here, c, begin in late_places(n, blocks, width):
                here = (slice(begin, begin + rows_here), slice(c * WIDTH, (c + 1) * WIDTH))
                sums[n, to : to + rows_here, :] = acc[here].astype(bf16)
            for to, rows_here, c, begin in late_places(n, blocks, width, True):
                here = (slice(begin, begin + rows_here), slice(c * WIDTH, (c + 1) * WIDTH))
                sums[n, to : to + rows_here, :] = (
                    out_kept[here].astype(f32)
                    + out_other[here].astype(f32)
                    + out_there[here].astype(f32)
                ).astype(bf16)
            extra_at = 4 * width // blocks
            sums[n, extra_at:, :] = stacked_pairs(rows[n::blocks], sums.shape[1] - extra_at)


def late_places(n, blocks, width, out=False):
    deep, period = (width // blocks, WIDTH) if out else (3 * width // blocks, width)
    first = 3 * width // blocks if out else 0
    return [
        (first + at - n * deep, length, at // period, at % period)
        for at, length in pieces(n * deep, deep, period)
    ]


def project_back(
    info, me_at, tokens, gain, shift, dq_a, dq_b, dk, dv, positions, table, w, kept, other, there,
    early, blocks, earlier,
):
    length, width = tokens.shape
    share = 2 * TILE

    def owner(i, info):
        return jnp.bitwise_xor(info[me_at], relative(i))

    def rows(count, columns):
        return pl.BlockSpec((count, columns), lambda i, info: (owner(i, info), 0))

    first = pl.BlockSpec((None, TILE, width), lambda i, info: (0, 0, 0))
    out = jax.ShapeDtypeStruct
    sums = (blocks, 4 * width // blocks + late_extra(width, blocks)[1], WIDTH)
    return pl.pallas_call(
        in_order(project_back_kernel, 15, len(earlier)),
        grid_spec=pltpu.PrefetchScalarGridSpec(
            num_scalar_prefetch=1,
            grid=(length // share,),
            in_specs=[
                rows(share, width), whole((1, width)), whole((1, width)), rows(TILE, WIDTH),
                rows(TILE, WIDTH), rows(share, WIDTH), rows(share, WIDTH),
                pl.BlockSpec((3, 1, share), lambda i, info: (0, 0, owner(i, info))),
                whole(table.shape), whole(w.shape), first, first, whole((TILE, width)),
                whole(early.shape),
            ]
            + unread(earlier),
            out_specs=[
                pl.BlockSpec((1, share, width), lambda i, info: (i, 0, 0)),
                pl.BlockSpec((1, share, width), lambda i, info: (jnp.maximum(i - 2, 0), 0, 0)),
                whole(sums),
            ],
            scratch_shapes=[
                pltpu.VMEM((width, 3 * WIDTH), f32), pltpu.VMEM((8, 3 * WIDTH), f32),
                pltpu.VMEM((8, width), f32),
                pltpu.VMEM((width, 3 * WIDTH), bf16),
            ],
        ),
        out_shape=[
            pltpu.HBM((4, share, width), bf16), pltpu.HBM((2, share, width), bf16),
            pltpu.HBM(sums, bf16),
        ],
        compiler_params=params(LIMIT),
        cost_estimate=pl.CostEstimate(
            flops=24 * length * width * WIDTH, bytes_accessed=20 * MIB, transcendentals=0
        ),
        name="project_back",
    )(
        info, tokens, gain, shift, dq_a, dq_b, dk, dv, positions, table, w, kept, other, there, early,
        *earlier,
    )


def vectors_kernel(extra, grad_b, vectors):
    blocks = extra.shape[0]
    width = vectors.shape[1]
    grad_b[...] = jnp.zeros_like(grad_b)
    vectors[...] = jnp.zeros_like(vectors)
    for v in range(3 + 7 * width // WIDTH):
        n, m = v % blocks, v // blocks
        pair = extra[n].astype(f32)
        row = pair[2 * m : 2 * m + 1, :] + pair[2 * m + 1 : 2 * m + 2, :]
        if v < 3:
            grad_b[v : v + 1, :] = row
        else:
            to, at = divmod((v - 3) * WIDTH, width)
            vectors[to : to + 1, at : at + WIDTH] = row


def unpack_vectors(sums, width, earlier):
    blocks = sums.shape[0]
    at, rows = 4 * width // blocks, late_extra(width, blocks)[1]
    return pl.pallas_call(
        in_order(vectors_kernel, 1, len(earlier)),
        grid=(1,),
        in_specs=[pl.BlockSpec((blocks, rows, WIDTH), lambda i: (0, at // rows, 0))]
        + unread(earlier),
        out_specs=[whole((8, WIDTH)), whole((8, width))],
        out_shape=[pltpu.HBM((8, WIDTH), f32), pltpu.HBM((8, width), f32)],
        compiler_params=params(LIMIT),
        name="unpack_vectors",
    )(sums, *earlier)


def unpack_kernel(sums, grad_qkv, grad_out):
    blocks = sums.shape[0]
    width = grad_out.shape[1]
    for n in range(blocks):
        for to, rows, c, begin in late_places(n, blocks, width):
            grad_qkv[c, begin : begin + rows, :] = sums[n, to : to + rows, :].astype(f32)
        for to, rows, c, begin in late_places(n, blocks, width, True):
            grad_out[begin : begin + rows, c * WIDTH : (c + 1) * WIDTH] = sums[
                n, to : to + rows, :
            ].astype(f32)


def unpack(sums, width, earlier):
    out = jax.ShapeDtypeStruct
    return pl.pallas_call(
        in_order(unpack_kernel, 1, len(earlier)),
        in_specs=[pl.BlockSpec(memory_space=pltpu.VMEM)] + unread(earlier),
        out_specs=[pl.BlockSpec(memory_space=pltpu.VMEM)] * 2,
        out_shape=[out((3, width, WIDTH), f32), out((WIDTH, width), f32)],
        compiler_params=pltpu.CompilerParams(vmem_limit_bytes=LIMIT * MIB),
        name="unpack",
    )(sums, *earlier)


def finish_kernel(info, parts, other, there, tok, gain, dx2, out):
    grad = parts[0].astype(f32) + other[0].astype(f32) + there[...].astype(f32)
    hat, inverse = normalized(tok[...].astype(f32))
    out[...] = dx2[...] + norm_back(hat, inverse, gain[...], grad)


def finish(info, me_at, parts, other, there, tokens, gain, dx2, earlier):
    width = tokens.shape[1]
    share = there.shape[0]
    rows = pl.BlockSpec((TILE, width), lambda i, info: (i, 0))
    return pl.pallas_call(
        in_order(finish_kernel, 7, len(earlier)),
        grid_spec=pltpu.PrefetchScalarGridSpec(
            num_scalar_prefetch=1,
            grid=(share // TILE,),
            in_specs=[
                pl.BlockSpec((1, TILE, width), lambda i, info: (0, i, 0)),
                pl.BlockSpec((1, TILE, width), lambda i, info: (0, i, 0)), rows,
                pl.BlockSpec((TILE, width), lambda i, info: (2 * info[me_at] + i, 0)),
                whole((1, width)), rows,
            ]
            + unread(earlier),
            out_specs=rows,
        ),
        out_shape=jax.ShapeDtypeStruct((share, width), f32),
        compiler_params=params(LIMIT),
        cost_estimate=pl.CostEstimate(
            flops=30 * share * width, bytes_accessed=10 * MIB, transcendentals=0
        ),
        name="finish",
    )(info, parts, other, there, tokens, gain, dx2, *earlier)


def total_of(blocks):
    total = blocks[0].astype(f32)
    for n in range(1, blocks.shape[0]):
        total += blocks[n].astype(f32)
    return total.astype(bf16)


def sums_kernel(blocks_a, blocks_b, out):
    rows = blocks_a.shape[1]
    out[:rows, :] = total_of(blocks_a)
    out[rows:, :] = total_of(blocks_b)


def two_sums(blocks_a, blocks_b, earlier):
    _, rows, width = blocks_a.shape
    return pl.pallas_call(
        in_order(sums_kernel, 2, len(earlier)),
        grid=(1,),
        in_specs=[whole(blocks_a.shape), whole(blocks_b.shape)] + unread(earlier),
        out_specs=whole((2 * rows, width)),
        out_shape=pltpu.HBM((2 * rows, width), bf16),
        compiler_params=params(LIMIT),
        name="two_sums",
    )(blocks_a, blocks_b, *earlier)


def sum_kernel(blocks, out):
    out[...] = total_of(blocks)


def summed(blocks, steps, earlier):
    count, rows, width = blocks.shape
    tile = rows // steps
    return pl.pallas_call(
        in_order(sum_kernel, 1, len(earlier)),
        grid=(steps,),
        in_specs=[pl.BlockSpec((count, tile, width), lambda i: (0, i, 0))] + unread(earlier),
        out_specs=pl.BlockSpec((tile, width), lambda i: (i, 0)),
        out_shape=pltpu.HBM((rows, width), bf16),
        compiler_params=params(LIMIT),
        name="summed",
    )(blocks, *earlier)


def copies_kernel(first, second, out):
    total = (first[...].astype(f32) + second[...].astype(f32)).astype(bf16)
    for n in range(out.shape[0]):
        out[n] = total


def sum_copies(first, second, count, earlier):
    rows, width = first.shape
    return pl.pallas_call(
        in_order(copies_kernel, 2, len(earlier)),
        grid=(1,),
        in_specs=[whole((rows, width))] * 2 + unread(earlier),
        out_specs=whole((count, rows, width)),
        out_shape=pltpu.HBM((count, rows, width), bf16),
        compiler_params=params(LIMIT),
        name="sum_copies",
    )(first, second, *earlier)


def swap(array, axis, bit=1):
    size = lax.axis_size(axis)
    if size == 1:
        return jnp.zeros_like(array)
    return lax.ppermute(array, axis, [(i, i ^ bit) for i in range(size)])


def swap_both(array):
    return lax.ppermute(array, MP, [(i, i ^ 3) for i in range(4)])


def scattered(rows, axes):
    group = lax.axis_size(axes)
    length, width = rows.shape
    return lax.all_to_all(
        rows.reshape(group, length // group, width), axes, 0, 0, tiled=True
    )


def both_sums(total):
    if lax.axis_size("zl") == 1:
        return total
    return (total.astype(f32) + swap(total, "zl").astype(f32)).astype(bf16)


def local(
    tokens, cotangent, segments, padding, positions, ln1_gain, ln1_bias, w_qkv, b_qkv, w_out, b_out,
    ln2_gain, ln2_bias, w_up, b_up, w_down, b_down,
):
    width, hidden = w_up.shape
    w_all = lax.all_gather(w_out, MP)
    gain_one, shift_one = ln1_gain[None], ln1_bias[None]
    gain_two, shift_two = ln2_gain[None], ln2_bias[None]
    ends = jnp.sum((segments <= jnp.arange(2)[:, None]).astype(jnp.int32), axis=1)
    info = jnp.concatenate([ends, lax.axis_index(MP)[None].astype(jnp.int32)])
    me_at = 2
    table = jnp.asarray(rope_constants())
    k_aug, v_aug, q_aug_t, q, k_t, v_t = project(
        tokens, w_qkv, b_qkv, gain_one, shift_one, positions, segments, padding, table
    )

    def exchanged(own, to_c, to_zh, to_both):
        return own, swap(to_c, "c"), swap(to_zh, "zh"), swap_both(to_both)

    o_0, o_t_0, lse_0 = attend(0, info, k_aug, v_t, q_aug_t, k_t, padding, ())
    o_zh_0, o_c_0 = swap(o_0, "zh"), swap(o_0, "c")
    o_1, o_t_1, lse_1 = attend(1, info, k_aug, v_t, q_aug_t, k_t, padding, (o_0, w_all))
    o_zh_1 = swap(o_1, "zh")
    o_zh_0 = after(o_zh_0, (o_1,))
    o_parts_0 = tuple((part, None) for part in (o_0, o_c_0, o_zh_0, swap(o_zh_0, "c")))

    def mlp_half(part, o_parts, earlier):
        return mlp(
            part, info, me_at, tokens, cotangent, o_parts, w_all, b_out[None], gain_two, shift_two,
            w_up, b_up[None], w_down, earlier,
        )

    x2_0, dy_0, h2_0, act_0, du_0, mlp_0, mlp_sent_0, dh2_0, sent, db_0 = mlp_half(
        0, o_parts_0, (o_1,)
    )
    pair = paired(o_1, o_zh_1, (x2_0,))
    pair_c = swap(pair, "c")
    o_parts_1 = ((pair, 0), (pair_c, 0), (pair, 1), (pair_c, 1))
    other_0 = swap(sent, "c")
    give_0 = to_give(dh2_0, other_0, ())
    there_0 = swap(give_0, "zh")
    x2_1, dy_1, h2_1, act_1, du_1, mlp_1, mlp_sent_1, dh2_1, sent, db_1 = mlp_half(
        1, o_parts_1, (give_0,)
    )
    other_1 = swap(sent, "c")
    grad_down = down_weights((act_0, act_1), cotangent, (there_0,))
    arrived_down = scattered(grad_down, ("y", "x"))
    give_1 = to_give(dh2_1, other_1, (grad_down,))
    there_1 = swap(give_1, "zh")
    grad_up = up_weights((h2_0, h2_1), (du_0, du_1), (give_1,))
    dx2, g, *d_parts, small = middle(
        info, me_at, (dh2_0, other_0, there_0, x2_0, dy_0), (dh2_1, other_1, there_1, x2_1, dy_1),
        gain_two, w_all, (grad_up,),
    )
    do = exchanged(*d_parts)
    arrived_up = scattered(after(grad_up, (g,)), ("y", "x"))
    grad_out, out_sent = out_weights(info, me_at, o_parts_0, o_parts_1, g)
    out_other = swap(out_sent, "c")
    mlp_parts = (mlp_0, mlp_1)
    mlp_others = (swap(mlp_sent_0, "c"), swap(mlp_sent_1, "c"))
    dq_0, dk, dv = attend_back(
        0, info, me_at, k_aug, v_aug, k_t, q_aug_t, q, v_t, o_t_0, lse_0, padding, do, positions,
        table, None, None, (grad_out, g),
    )
    give = to_give(grad_out, out_other, (dq_0,))
    out_there = swap(give, "zh")
    mlp_give = two_to_give(mlp_parts, mlp_others, (give,))
    mlp_there = swap(mlp_give, "zh")
    part_sum = both_sums(two_sums(arrived_up, arrived_down, (mlp_give,)))
    dq_1, dk, dv = attend_back(
        1, info, me_at, k_aug, v_aug, k_t, q_aug_t, q, v_t, o_t_1, lse_1, padding, do, positions,
        table, dk, dv, (give, part_sum),
    )
    grad_mlp = lax.all_gather(part_sum, ("y", "x"), axis=0, tiled=True)
    early = jnp.concatenate([small[0:4], (db_0 + db_1)[0:4]])
    dh1, sent, sums = project_back(
        info, me_at, tokens, gain_one, shift_one, dq_0, dq_1, dk, dv, positions, table, w_qkv,
        grad_out, out_other, out_there, early, lax.axis_size(("y", "x")), (mlp_there,),
    )
    other = swap(sent, "c")
    back = swap(to_give(dh1, other, (sums,)), "zh")
    arrived = scattered(sums.reshape(-1, WIDTH), ("y", "x"))
    total = summed(arrived, 1, (back,))
    copies = sum_copies(total, swap(total, "zl"), sums.shape[0], ())
    late = lax.all_to_all(copies, ("y", "x"), 0, 0, tiled=True)
    grad_inputs = finish(info, me_at, dh1, other, back, tokens, gain_one, dx2, (copies,))
    mixed = mixed_rows(
        (x2_0, x2_1), mlp_parts, mlp_others, mlp_there, b_down[None], (copies,)
    )
    count = lax.axis_size(("y", "x"))
    grad_mlp = grad_mlp.reshape(count, 2, width // count, hidden)
    grad_up = grad_mlp[:, 0].astype(f32).reshape(width, hidden)
    grad_down = grad_mlp[:, 1].astype(f32).reshape(hidden, width)
    grad_b, vectors = unpack_vectors(late, width, (grad_inputs, mixed, grad_up, grad_down))
    by_c, by_zh, by_both = swap(vectors, "c"), swap(vectors, "zh"), swap_both(vectors)
    grad_qkv, grad_w_out = unpack(late, width, (vectors,))
    group = (vectors + by_c) + (by_zh + by_both)
    return (
        mixed, grad_inputs, group[1], group[2], grad_qkv, grad_b[0:3], grad_w_out, group[5],
        group[3], group[4], grad_up, vectors[0], grad_down, group[6],
    )


def solution(mesh):
    packs = mesh.shape["dp"]
    if packs == 32:
        shape = (2, 4, 4, 2, 2)
    else:
        shape = (1, packs, 1, 2, 2)
    split = Mesh(mesh.devices.reshape(shape), EVERY)
    in_specs = (
        P(DP, None), P(DP, None), P(DP, None), P(DP, None), P(None, DP, None), P(), P(),
        P(None, None, MP), P(None, MP), P(MP, None), P(), P(), P(), P(None, MP), P(MP),
        P(MP, None), P(),
    )
    out_specs = (
        P(EVERY, None), P(EVERY, None), P(), P(), P(None, None, MP), P(None, MP), P(MP, None), P(),
        P(), P(), P(None, MP), P(MP), P(MP, None), P(),
    )
    return jax.shard_map(local, mesh=split, in_specs=in_specs, out_specs=out_specs, check_vma=False)
```

```python
import functools
import math

import jax
import jax.numpy as jnp
import ml_dtypes
import numpy as np
from jax import lax
from jax.experimental import pallas as pl
from jax.experimental.pallas import tpu as pltpu
from jax.sharding import Mesh
from jax.sharding import PartitionSpec as P

HEAD_DIM = 64
HEADS = 4
WIDTH = HEADS * HEAD_DIM
AUG = 128
TILE = 256
ROWS = 2 * TILE
PLACES = 64
LIMIT = 64
MIB = 1 << 20
DP = ("zl", "y", "x")
MP = ("zh", "c")
EVERY = ("zl", "y", "x", "zh", "c")

epsilon = 1e-06
NEG = -1e30
bf16 = jnp.bfloat16
f32 = jnp.float32


def dot_nn(a, b):
    return lax.dot_general(a, b, (((1,), (0,)), ((), ())), preferred_element_type=f32)


def dot_nt(a, b):
    return lax.dot_general(a, b, (((1,), (1,)), ((), ())), preferred_element_type=f32)


def dot_tn(a, b):
    return lax.dot_general(a, b, (((0,), (0,)), ((), ())), preferred_element_type=f32)


def normalized(values):
    center = jnp.mean(values, axis=-1, keepdims=True)
    shifted = values - center
    spread = jnp.mean(shifted * shifted, axis=-1, keepdims=True)
    inverse = lax.rsqrt(spread + epsilon)
    return shifted * inverse, inverse


def norm_back(hat, inverse, gain, grad):
    scaled = grad * gain
    return inverse * (
        scaled
        - jnp.mean(scaled, axis=-1, keepdims=True)
        - hat * jnp.mean(scaled * hat, axis=-1, keepdims=True)
    )


def turned(x, low, high):
    width = x.shape[1]
    pair = HEAD_DIM // 6
    return pltpu.roll(x, width - pair, 1) * low + pltpu.roll(x, pair, 1) * high


def three_parts(x):
    first = x.astype(bf16).astype(f32)
    rest = x - first
    second = rest.astype(bf16).astype(f32)
    return first, second, rest - second


def params(limit, axes=1):
    return pltpu.CompilerParams(
        dimension_semantics=("arbitrary",) * axes, vmem_limit_bytes=limit * MIB
    )


def in_order(kernel, inputs, earlier):
    def run(*refs):
        kernel(*refs[:inputs], *refs[inputs + earlier :])

    return run


def unread(arrays):
    return [pl.BlockSpec(memory_space=pl.ANY)] * len(arrays)


def whole(shape):
    return pl.BlockSpec(shape, lambda *_: (0,) * len(shape))


def clip_range(info, tile, length):
    half = TILE // 2
    first, second = info[0], info[1]
    at = tile * TILE
    begin = jnp.where(second <= at, second, jnp.where(first <= at, first, 0))
    end = jnp.where(
        first >= at + TILE, first, jnp.where(second >= at + TILE, second, length)
    )
    end = (end + half - 1) // half
    count = (end - begin // half + 1) // 2
    return jnp.maximum(end - 2 * count, 0), count


def key_tiles(begin, at, count):
    return pl.ds(pl.multiple_of(begin * (TILE // 2) + at * TILE, TILE // 2), count * TILE)


def rope_constants():
    pair = HEAD_DIM // 6
    feature = np.arange(WIDTH) % HEAD_DIM
    section, place = feature // (2 * pair), feature % (2 * pair)
    frequency = np.exp(-math.log(10000.0) * (place % pair) / pair)
    table = np.zeros((PLACES, 3, WIDTH))
    for s in range(3):
        for value in range(16):
            angle = value * frequency
            turns = section == s
            table[s * 16 + value, 0] = np.where(turns, np.cos(angle), 0.0)
            table[s * 16 + value, 1] = np.where(turns & (place < pair), -np.sin(angle), 0.0)
            table[s * 16 + value, 2] = np.where(turns & (place >= pair), np.sin(angle), 0.0)
    table[48, 0] = section == 3
    rest = table.reshape(PLACES, 3 * WIDTH).astype(np.float32)
    parts = []
    for _ in range(3):
        part = rest.astype(ml_dtypes.bfloat16)
        parts.append(part)
        rest = rest - part.astype(np.float32)
    return np.concatenate(parts)


def rope_factors(positions, table):
    row = lax.broadcasted_iota(jnp.int32, (PLACES, positions.shape[-1]), 0)
    where = jnp.where(
        row < 16, positions[0], jnp.where(row < 32, positions[1], positions[2])
    )
    hit = ((where == row % 16) & (row < 48)) | (row == 48)
    hit = jnp.where(hit, 1.0, 0.0)
    hits = jnp.concatenate([hit, hit, hit]).astype(bf16)
    factors = dot_tn(hits, table[...])
    return factors[:, :WIDTH], factors[:, WIDTH : 2 * WIDTH], factors[:, 2 * WIDTH :]


def qkv_kernel(
    tok, w, b, gain, shift, pos, seg, pad, table, k_aug, v_aug, q_aug_t, q_out, k_t, v_t, w_wide
):
    @pl.when(pl.program_id(0) == 0)
    def _():
        for c in range(3):
            w_wide[:, c * WIDTH : (c + 1) * WIDTH] = w[c]

    hat, _ = normalized(tok[...].astype(f32))
    normed = (hat * gain[...] + shift[...]).astype(bf16)
    cos, low, high = rope_factors(pos, table)
    all_three = dot_nn(normed, w_wide[...])
    q = all_three[:, :WIDTH] + b[0:1, :]
    k = all_three[:, WIDTH : 2 * WIDTH] + b[1:2, :]
    v = all_three[:, 2 * WIDTH :] + b[2:3, :]
    q = (q * cos + turned(q, low, high)) * (1.0 / math.sqrt(HEAD_DIM))
    k = k * cos + turned(k, low, high)
    q_out[...] = q.astype(bf16)
    q_t = q.T.astype(bf16)
    k_t[...] = k.T.astype(bf16)
    v_t[...] = v.T.astype(bf16)
    row = lax.broadcasted_iota(jnp.int32, (HEAD_DIM, ROWS), 0)
    clip = seg[...]
    same = (row >= 1) & (row < 4) & (clip == row - 1)
    mask = jnp.where((row >= 1) & (row < 4) & (clip != row - 1), NEG, 0.0)
    mask = jnp.where(row == 0, jnp.where(pad[...] != 0, NEG, 0.0), mask)
    k_extra = jnp.where((row >= 4) & (row < 7), 1.0, mask)
    q_extra = jnp.where(same | (row == 0), 1.0, 0.0).astype(bf16)
    k_side = jnp.concatenate([jnp.zeros((HEAD_DIM, ROWS), f32), k_extra]).T
    lane = lax.broadcasted_iota(jnp.int32, (ROWS, AUG), 1)
    ones = jnp.where((lane >= HEAD_DIM) & (lane < HEAD_DIM + 3), 1.0, 0.0)
    for h in range(HEADS):
        pair = slice(h // 2 * AUG, h // 2 * AUG + AUG)
        wide = slice(h * AUG, (h + 1) * AUG)
        k_pair, v_pair = k[:, pair], v[:, pair]
        if h % 2:
            k_pair, v_pair = pltpu.roll(k_pair, HEAD_DIM, 1), pltpu.roll(v_pair, HEAD_DIM, 1)
        k_aug[:, wide] = jnp.where(lane < HEAD_DIM, k_pair, k_side).astype(bf16)
        v_aug[:, wide] = jnp.where(lane < HEAD_DIM, v_pair, ones).astype(bf16)
        q_aug_t[h * AUG : h * AUG + HEAD_DIM, :] = q_t[h * HEAD_DIM : (h + 1) * HEAD_DIM, :]
        q_aug_t[h * AUG + HEAD_DIM : (h + 1) * AUG, :] = q_extra


def project(tokens, w, b, gain, shift, positions, segments, padding, table):
    length, width = tokens.shape
    tiles = length // ROWS

    def rows(columns):
        return pl.BlockSpec((ROWS, columns), lambda i: (i, 0))

    def columns(count):
        return pl.BlockSpec((count, ROWS), lambda i: (0, i))

    out = jax.ShapeDtypeStruct
    wide = out((length, HEADS * AUG), bf16)
    flat = out((WIDTH, length), bf16)
    return pl.pallas_call(
        qkv_kernel,
        grid=(tiles,),
        in_specs=[
            rows(width), whole(w.shape), whole(b.shape), whole((1, width)), whole((1, width)),
            pl.BlockSpec((3, 1, ROWS), lambda i: (0, 0, i)), columns(1), columns(1), whole(table.shape),
        ],
        out_specs=[
            rows(HEADS * AUG), rows(HEADS * AUG), columns(HEADS * AUG), rows(WIDTH), columns(WIDTH),
            columns(WIDTH),
        ],
        out_shape=[
            wide, wide, out((HEADS * AUG, length), bf16), out((length, WIDTH), bf16), flat, flat,
        ],
        scratch_shapes=[pltpu.VMEM((width, 3 * WIDTH), bf16)],
        compiler_params=params(LIMIT),
        cost_estimate=pl.CostEstimate(
            flops=6 * length * width * WIDTH, bytes_accessed=20 * MIB, transcendentals=0
        ),
        name="project",
    )(tokens, w, b, gain, shift, positions, segments, padding, table)


def attend_kernel(info, k_aug, v_t, q_aug_t, k_t, pad, o, o_t, lse, top, total, acc, *, part):
    tile = 2 * pl.program_id(0) + part
    padded = pad[...] != 0
    for h in range(HEADS):
        q_h = q_aug_t[h * AUG : h * AUG + HEAD_DIM, :].astype(f32)
        k_h = k_t[h * HEAD_DIM : (h + 1) * HEAD_DIM, :].astype(f32)
        own = jnp.sum(q_h * k_h, axis=0, keepdims=True)
        top[h : h + 1, :] = jnp.where(padded, own, -3e38)
        total[h : h + 1, :] = jnp.where(padded, 1.0, 0.0)
    here = pl.ds(pl.multiple_of(tile * TILE, TILE), TILE)
    acc[...] = jnp.where(padded, v_t[:, here].astype(f32), 0.0)
    feats = [slice(h * HEAD_DIM, (h + 1) * HEAD_DIM) for h in range(HEADS)]
    wides = [slice(h * AUG, (h + 1) * AUG) for h in range(HEADS)]

    begin, tiles = clip_range(info, tile, k_aug.shape[0])

    def step(j, count):
        keys = key_tiles(begin, j, count)
        scores = [dot_nn(k_aug[keys, wide], q_aug_t[wide, :]) for wide in wides]
        probs, fades = [], []
        for h in range(HEADS):
            old = top[h : h + 1, :]
            new = jnp.maximum(old, jnp.max(scores[h], axis=0, keepdims=True))
            prob = jnp.exp(scores[h] - new)
            fade = jnp.exp(old - new)
            top[h : h + 1, :] = new
            total[h : h + 1, :] = total[h : h + 1, :] * fade + jnp.sum(prob, axis=0, keepdims=True)
            probs.append(prob.astype(bf16))
            fades.append(fade)
        for h, feat in enumerate(feats):
            acc[feat, :] = acc[feat, :] * fades[h] + dot_nn(v_t[feat, keys], probs[h])

    pairs = tiles // 2

    def two(n, _):
        step(2 * n, 2)
        return 0

    lax.fori_loop(0, pairs, two, 0)

    @pl.when(2 * pairs < tiles)
    def _():
        step(tiles - 1, 1)

    for h, feat in enumerate(feats):
        acc[feat, :] = acc[feat, :] / total[h : h + 1, :]
    lse[...] = jnp.zeros_like(lse)
    lse[0:HEADS, :] = top[0:HEADS, :] + jnp.log(total[0:HEADS, :])
    turned_o = acc[...]
    o_t[...] = turned_o.astype(bf16)
    o[...] = turned_o.T.astype(bf16)


def attend(part, info, k_aug, v_t, q_aug_t, k_t, padding, earlier):
    length = k_aug.shape[0]
    half = length // 2

    def columns(count):
        return pl.BlockSpec((count, TILE), lambda i, *_: (0, 2 * i + part))

    def packed(count):
        return pl.BlockSpec((count, TILE), lambda i, *_: (0, i))

    out = jax.ShapeDtypeStruct
    return pl.pallas_call(
        in_order(functools.partial(attend_kernel, part=part), 6, len(earlier)),
        grid_spec=pltpu.PrefetchScalarGridSpec(
            num_scalar_prefetch=1,
            grid=(half // TILE,),
            in_specs=[
                whole(k_aug.shape), whole(v_t.shape), columns(HEADS * AUG), columns(WIDTH),
                columns(1),
            ]
            + unread(earlier),
            out_specs=[
                pl.BlockSpec((TILE, WIDTH), lambda i, *_: (i, 0)), packed(WIDTH), packed(8),
            ],
            scratch_shapes=[
                pltpu.VMEM((8, TILE), f32), pltpu.VMEM((8, TILE), f32), pltpu.VMEM((WIDTH, TILE), f32),
            ],
        ),
        out_shape=[out((half, WIDTH), bf16), out((WIDTH, half), bf16), out((8, half), f32)],
        compiler_params=params(LIMIT),
        cost_estimate=pl.CostEstimate(
            flops=24 * half * length * WIDTH, bytes_accessed=6 * MIB, transcendentals=0
        ),
        name="attend",
    )(info, k_aug, v_t, q_aug_t, k_t, padding, *earlier)


def nothing(*refs):
    del refs


def after(value, earlier):
    return pl.pallas_call(
        nothing,
        in_specs=unread((value,) + earlier),
        out_specs=pl.BlockSpec(memory_space=pl.ANY),
        out_shape=jax.ShapeDtypeStruct(value.shape, value.dtype),
        input_output_aliases={0: 0},
        name="after",
    )(value, *earlier)


def pair_kernel(first, second, out):
    out[0] = first[...]
    out[1] = second[...]


def paired(first, second, earlier):
    shape = (2,) + first.shape
    return pl.pallas_call(
        in_order(pair_kernel, 2, len(earlier)),
        in_specs=[pl.BlockSpec(memory_space=pltpu.VMEM)] * 2 + unread(earlier),
        out_specs=pl.BlockSpec(memory_space=pltpu.VMEM),
        out_shape=jax.ShapeDtypeStruct(shape, first.dtype),
        name="paired",
    )(first, second, *earlier)


def head_block(at, owner):
    if at is None:
        return pl.BlockSpec((TILE, WIDTH), lambda i, info: (owner(i, info), 0))
    return pl.BlockSpec((None, TILE, WIDTH), lambda i, info: (at, owner(i, info), 0))


def relative(i):
    return i % 2 * 2 + i // 2


def gelu_parts(u):
    size = jnp.abs(u)
    t = 1.0 / (1.0 + (0.3275911 / math.sqrt(2.0)) * size)
    bell = jnp.exp(-0.5 * (u * u))
    poly = 0.5 * 1.061405429
    for c in (-1.453152027, 1.421413741, -0.284496736, 0.254829592):
        poly = poly * t + 0.5 * c
    tail = poly * t * bell
    below = jnp.where(u >= 0, 1.0 - tail, tail)
    return u * below, below + u * bell * (1.0 / math.sqrt(2.0 * math.pi))


def mlp_kernel(
    info, tok, cot, o_0, o_1, o_2, o_3, w_all, b_out, gain, shift, w_up, b_up, w_down,
    x2, dy, h2, act, du, mlp, mlp_sent, dh2, dh2_sent, db_up, w_out, *, me_at,
):
    i = pl.program_id(0)

    @pl.when(i == 0)
    def _():
        for j in range(4):
            w_out[j * WIDTH : (j + 1) * WIDTH, :] = w_all[jnp.bitwise_xor(info[me_at], j)]
        db_up[...] = jnp.zeros_like(db_up)

    heads = jnp.concatenate([o_0[...], o_1[...], o_2[...], o_3[...]], axis=1)
    mid = tok[...].astype(f32) + b_out[...] + dot_nn(heads, w_out[...])

    @pl.when(i == 0)
    def _():
        x2[...] = mid
        dy[...] = cot[...]

    hat, _ = normalized(mid)
    normed = (hat * gain[...] + shift[...]).astype(bf16)
    h2[...] = normed
    u = dot_nn(normed, w_up[...]) + b_up[...]
    grad_act = dot_nt(cot[...], w_down[...])
    value, slope = gelu_parts(u)
    value = value.astype(bf16)
    grad = (grad_act * slope).astype(bf16)
    act[...] = value
    du[...] = grad
    db_up[0:1, :] += jnp.sum(grad.astype(f32), axis=0, keepdims=True)
    mlp_part = dot_nn(value, w_down[...]).astype(bf16)
    dh2_part = dot_nt(grad, w_up[...]).astype(bf16)
    mlp[0] = mlp_part
    mlp_sent[0] = mlp_part
    dh2[0] = dh2_part
    dh2_sent[0] = dh2_part


def mlp(
    part, info, me_at, tokens, cotangent, o_parts, w_all, b_out, gain, shift, w_up, b_up, w_down,
    earlier,
):
    length, width = tokens.shape
    half = length // 2
    hidden = w_up.shape[1]
    owners = half // TILE

    def owner(i, info):
        return jnp.bitwise_xor(info[me_at], relative(i))

    def rows(columns):
        return pl.BlockSpec((TILE, columns), lambda i, info: (2 * owner(i, info) + part, 0))

    def packed(columns):
        return pl.BlockSpec((TILE, columns), lambda i, info: (owner(i, info), 0))

    ordered = pl.BlockSpec((1, TILE, width), lambda i, info: (i, 0, 0))
    sent = pl.BlockSpec((1, TILE, width), lambda i, info: (jnp.maximum(i - 2, 0), 0, 0))

    out = jax.ShapeDtypeStruct
    return pl.pallas_call(
        in_order(functools.partial(mlp_kernel, me_at=me_at), 14, len(earlier)),
        grid_spec=pltpu.PrefetchScalarGridSpec(
            num_scalar_prefetch=1,
            grid=(owners,),
            in_specs=[rows(width), rows(width)]
            + [head_block(at, owner) for _, at in o_parts]
            + [whole(w_all.shape)]
            + [whole((1, width))] * 3
            + [whole(w_up.shape), whole((1, hidden)), whole(w_down.shape)]
            + unread(earlier),
            out_specs=[
                whole((TILE, width)), whole((TILE, width)), packed(width), packed(hidden),
                packed(hidden), ordered, sent, ordered, sent, whole((8, hidden)),
            ],
            scratch_shapes=[pltpu.VMEM((4 * WIDTH, width), bf16)],
        ),
        out_shape=[
            out((TILE, width), f32), out((TILE, width), bf16), out((half, width), bf16),
            out((half, hidden), bf16), out((half, hidden), bf16),
        ]
        + [out((owners, TILE, width), bf16), out((2, TILE, width), bf16)] * 2
        + [out((8, hidden), f32)],
        compiler_params=params(LIMIT),
        cost_estimate=pl.CostEstimate(
            flops=20 * half * width * hidden, bytes_accessed=20 * MIB, transcendentals=0
        ),
        name="mlp",
    )(
        info, tokens, cotangent, *(part for part, _ in o_parts), w_all, b_out, gain, shift, w_up,
        b_up, w_down, *earlier
    )


def up_weights_kernel(left_a, left_b, right_a, right_b, out):
    left = jnp.concatenate([left_a[...], left_b[...]])
    right = jnp.concatenate([right_a[...], right_b[...]])
    out[...] = dot_tn(left, right).astype(bf16)


def up_weights(h2, du, earlier):
    half, width = h2[0].shape
    hidden = du[0].shape[1]
    return pl.pallas_call(
        in_order(up_weights_kernel, 4, len(earlier)),
        grid=(width // TILE,),
        in_specs=[pl.BlockSpec((half, TILE), lambda i: (0, i))] * 2
        + [whole((half, hidden))] * 2
        + unread(earlier),
        out_specs=pl.BlockSpec((TILE, hidden), lambda i: (i, 0)),
        out_shape=pltpu.HBM((width, hidden), bf16),
        compiler_params=params(LIMIT),
        cost_estimate=pl.CostEstimate(
            flops=8 * half * width * hidden, bytes_accessed=12 * MIB, transcendentals=0
        ),
        name="up_weights",
    )(*h2, *du, *earlier)


def down_weights_kernel(act_a, act_b, cot, out):
    owners = cot.shape[0] // (2 * TILE)
    rows = [cot[n * TILE : (n + 1) * TILE, :] for p in range(2) for n in range(p, 2 * owners, 2)]
    out[...] = dot_tn(
        jnp.concatenate([act_a[...], act_b[...]]), jnp.concatenate(rows)
    ).astype(bf16)


def down_weights(act, cotangent, earlier):
    half, hidden = act[0].shape
    length, width = cotangent.shape
    return pl.pallas_call(
        in_order(down_weights_kernel, 3, len(earlier)),
        grid=(hidden // TILE,),
        in_specs=[pl.BlockSpec((half, TILE), lambda i: (0, i))] * 2
        + [whole((length, width))]
        + unread(earlier),
        out_specs=pl.BlockSpec((TILE, width), lambda i: (i, 0)),
        out_shape=pltpu.HBM((hidden, width), bf16),
        compiler_params=params(LIMIT),
        cost_estimate=pl.CostEstimate(
            flops=8 * half * width * hidden, bytes_accessed=12 * MIB, transcendentals=0
        ),
        name="down_weights",
    )(*act, cotangent, *earlier)


def add_kernel(parts, other, out):
    out[...] = (parts[0].astype(f32) + other[0].astype(f32)).astype(bf16)


def to_give(parts, other, earlier):
    _, rows, width = parts.shape
    tile = min(rows, TILE)
    return pl.pallas_call(
        in_order(add_kernel, 2, len(earlier)),
        grid=(rows // tile,),
        in_specs=[
            pl.BlockSpec((1, tile, width), lambda i: (1, i, 0)),
            pl.BlockSpec((1, tile, width), lambda i: (1, i, 0)),
        ]
        + unread(earlier),
        out_specs=pl.BlockSpec((tile, width), lambda i: (i, 0)),
        out_shape=pltpu.HBM((rows, width), bf16),
        compiler_params=params(LIMIT),
        name="to_give",
    )(parts, other, *earlier)


def two_kernel(parts_a, parts_b, other_a, other_b, out):
    for n, (parts, other) in enumerate(((parts_a, other_a), (parts_b, other_b))):
        out[n] = (parts[0].astype(f32) + other[0].astype(f32)).astype(bf16)


def two_to_give(parts, others, earlier):
    _, rows, width = parts[0].shape
    tile = rows // 2
    return pl.pallas_call(
        in_order(two_kernel, 4, len(earlier)),
        grid=(rows // tile,),
        in_specs=[pl.BlockSpec((1, tile, width), lambda i: (1, i, 0))] * 4 + unread(earlier),
        out_specs=pl.BlockSpec((2, tile, width), lambda i: (0, i, 0)),
        out_shape=pltpu.HBM((2, rows, width), bf16),
        compiler_params=params(LIMIT),
        name="two_to_give",
    )(*parts, *others, *earlier)


def mixed_kernel(x2_a, x2_b, parts_a, parts_b, other_a, other_b, there, shift, out):
    for n, (x2, parts, other) in enumerate(
        ((x2_a, parts_a, other_a), (x2_b, parts_b, other_b))
    ):
        total = parts[0].astype(f32) + other[0].astype(f32) + there[n].astype(f32)
        out[n * TILE : (n + 1) * TILE, :] = (x2[...] + total + shift[...]).astype(bf16)


def mixed_rows(x2, parts, others, there, shift, earlier):
    rows, width = x2[0].shape
    first = pl.BlockSpec((1, rows, width), lambda i: (0, 0, 0))
    return pl.pallas_call(
        in_order(mixed_kernel, 8, len(earlier)),
        grid=(1,),
        in_specs=[whole((rows, width))] * 2
        + [first] * 4
        + [whole((2, rows, width)), whole((1, width))]
        + unread(earlier),
        out_specs=whole((2 * rows, width)),
        out_shape=jax.ShapeDtypeStruct((2 * rows, width), bf16),
        compiler_params=params(LIMIT),
        name="mixed_rows",
    )(*x2, *parts, *others, there, shift, *earlier)


def middle_kernel(info, *refs, me_at):
    halves, (gain, w_all, dx2, g, d_0, d_1, d_2, d_3, small) = (refs[0:5], refs[5:10]), refs[10:]
    small[...] = jnp.zeros_like(small)
    for part, (kept, other, there, x2, dy) in enumerate(halves):
        rows = slice(part * TILE, (part + 1) * TILE)
        grad = kept[0].astype(f32) + other[0].astype(f32) + there[...].astype(f32)
        hat, inverse = normalized(x2[...])
        dy = dy[...].astype(f32)
        full = dy + norm_back(hat, inverse, gain[...], grad)
        dx2[rows, :] = full
        low = full.astype(bf16)
        g[rows, :] = low
        small[0:1, :] += jnp.sum(grad * hat, axis=0, keepdims=True)
        small[1:2, :] += jnp.sum(grad, axis=0, keepdims=True)
        small[2:3, :] += jnp.sum(low.astype(f32), axis=0, keepdims=True)
        small[3:4, :] += jnp.sum(dy, axis=0, keepdims=True)
    low = g[...]
    for j, d_j in enumerate((d_0, d_1, d_2, d_3)):
        d_j[...] = dot_nt(low, w_all[jnp.bitwise_xor(info[me_at], j)]).astype(bf16)


def middle(info, me_at, half_a, half_b, gain, w_all, earlier):
    width = gain.shape[1]
    rows = 2 * TILE
    own = whole((TILE, width))
    first = pl.BlockSpec((1, TILE, width), lambda i, info: (0, 0, 0))
    return pl.pallas_call(
        in_order(functools.partial(middle_kernel, me_at=me_at), 13, len(earlier)),
        grid_spec=pltpu.PrefetchScalarGridSpec(
            num_scalar_prefetch=1,
            grid=(1,),
            in_specs=[first, first, own, own, own] * 2
            + [whole((1, width)), whole(w_all.shape)]
            + unread(earlier),
            out_specs=[whole((rows, width))] * 2
            + [whole((rows, WIDTH))] * 4
            + [whole((8, width))],
        ),
        out_shape=[pltpu.HBM((rows, width), f32), pltpu.HBM((rows, width), bf16)]
        + [pltpu.HBM((rows, WIDTH), bf16)] * 4
        + [pltpu.HBM((8, width), f32)],
        compiler_params=params(LIMIT),
        cost_estimate=pl.CostEstimate(
            flops=4 * TILE * width * width, bytes_accessed=12 * MIB, transcendentals=0
        ),
        name="middle",
    )(info, *half_a, *half_b, gain, w_all, *earlier)


def out_weights_kernel(info, *refs):
    parts_a, parts_b, (g, kept, sent) = refs[0:4], refs[4:8], refs[8:]
    for n in range(2):
        for out, j in ((kept, 2 * n), (sent, 2 * n + 1)):
            heads = jnp.concatenate([parts_a[j][...], parts_b[j][...]])
            out[n] = dot_tn(heads, g[...]).astype(bf16)


def out_weights(info, me_at, parts_a, parts_b, g):
    width = g.shape[1]

    def owner(i, info):
        return info[me_at]

    return pl.pallas_call(
        out_weights_kernel,
        grid_spec=pltpu.PrefetchScalarGridSpec(
            num_scalar_prefetch=1,
            grid=(1,),
            in_specs=[head_block(at, owner) for _, at in parts_a + parts_b]
            + [whole(g.shape)],
            out_specs=[whole((2, WIDTH, width))] * 2,
        ),
        out_shape=[pltpu.HBM((2, WIDTH, width), bf16)] * 2,
        compiler_params=params(LIMIT),
        cost_estimate=pl.CostEstimate(
            flops=4 * TILE * width * width, bytes_accessed=6 * MIB, transcendentals=0
        ),
        name="out_weights",
    )(info, *(part for part, _ in parts_a + parts_b), g)


def attend_back_kernel(
    info, k_aug, v_aug, k_t, q_aug_t, q, v_t, o_t, lse, pad, do_0, do_1, do_2, do_3, pos, table,
    *refs, part, me_at, first,
):
    if first:
        dk_in = dv_in = None
    else:
        dk_in, dv_in, *refs = refs
    dq_out, dk, dv, q_side, do_side, q_lanes, do_lanes, dq_t = refs
    i = pl.program_id(0)
    tile = 2 * jnp.bitwise_xor(info[me_at], i) + part

    @pl.when(i == 0)
    def _():
        if first:
            dk[...] = jnp.zeros_like(dk)
            dv[...] = jnp.zeros_like(dv)
        else:
            dk[...] = dk_in[...]
            dv[...] = dv_in[...]

    here = pl.ds(pl.multiple_of(tile * TILE, TILE), TILE)
    do_here = jnp.where(
        i == 0, do_0[...], jnp.where(i == 1, do_1[...], jnp.where(i == 2, do_2[...], do_3[...]))
    )
    q_here = q[...]
    do_t = do_here.astype(f32).T
    k_here = k_t[:, here].astype(f32)
    padded = jnp.where(pad[...] != 0, 1.0, 0.0)
    row = lax.broadcasted_iota(jnp.int32, (AUG - HEAD_DIM, TILE), 0)
    lane = lax.broadcasted_iota(jnp.int32, (TILE, WIDTH), 1) // HEAD_DIM
    dk_parts, dv_parts = [], []
    for h in range(HEADS):
        feat = slice(h * HEAD_DIM, (h + 1) * HEAD_DIM)
        at = h * AUG
        q_h = q_aug_t[at : at + HEAD_DIM, :]
        do_h = do_t[feat, :]
        delta = jnp.sum(do_h * o_t[feat, :].astype(f32), axis=0, keepdims=True)
        lse_h = lse[h : h + 1, :]
        one, two, three = three_parts(-lse_h)
        extra = q_aug_t[at + HEAD_DIM : at + AUG, :].astype(f32)
        extra = jnp.where(row == 4, one, jnp.where(row == 5, two, jnp.where(row == 6, three, extra)))
        q_side[at : at + HEAD_DIM, :] = q_h
        q_side[at + HEAD_DIM : at + AUG, :] = extra.astype(bf16)
        one, two, three = three_parts(-delta)
        extra = jnp.where(row == 0, one, jnp.where(row == 1, two, jnp.where(row == 2, three, 0.0)))
        do_side[at : at + HEAD_DIM, :] = do_h.astype(bf16)
        do_side[at + HEAD_DIM : at + AUG, :] = extra.astype(bf16)
        q_lanes[h] = jnp.where(lane == h, q_here, jnp.zeros_like(q_here))
        do_lanes[h] = jnp.where(lane == h, do_here, jnp.zeros_like(do_here))
        q_h = q_h.astype(f32)
        k_h = k_here[feat, :]
        p_own = padded * jnp.exp(jnp.sum(q_h * k_h, axis=0, keepdims=True) - lse_h)
        dp_own = jnp.sum(do_h * v_t[feat, :].astype(f32), axis=0, keepdims=True)
        ds_own = p_own * (dp_own - delta)
        dq_t[feat, :] = ds_own * k_h
        dk_parts.append(ds_own * q_h)
        dv_parts.append(p_own * do_h)
    dk[here, :] += jnp.concatenate(dk_parts, axis=0).T
    dv[here, :] += jnp.concatenate(dv_parts, axis=0).T

    begin, tiles = clip_range(info, tile, k_aug.shape[0])

    def step(j, _):
        keys = key_tiles(begin, j, 1)
        probs, grads = [], []
        for h in range(HEADS):
            wide = slice(h * AUG, (h + 1) * AUG)
            prob = jnp.exp(dot_nn(k_aug[keys, wide], q_side[wide, :]))
            grad = prob * dot_nn(v_aug[keys, wide], do_side[wide, :])
            probs.append(prob.astype(bf16))
            grads.append(grad.astype(bf16))
        deep = (HEADS * TILE, WIDTH)
        dv[keys, :] += dot_nn(jnp.concatenate(probs, axis=1), do_lanes[...].reshape(deep))
        dk[keys, :] += dot_nn(jnp.concatenate(grads, axis=1), q_lanes[...].reshape(deep))
        for h in range(HEADS):
            feat = slice(h * HEAD_DIM, (h + 1) * HEAD_DIM)
            dq_t[feat, :] += dot_nn(k_t[feat, keys], grads[h])
        return 0

    lax.fori_loop(0, tiles, step, 0)
    dq = dq_t[...].T * (1.0 / math.sqrt(HEAD_DIM))
    cos, low, high = rope_factors(pos, table)
    dq_out[...] = (dq * cos - turned(dq, low, high)).astype(bf16)


def attend_back(
    part, info, me_at, k_aug, v_aug, k_t, q_aug_t, q, v_t, o_t, lse, padding, do, positions, table,
    dk, dv, earlier,
):
    length = k_aug.shape[0]
    half = length // 2

    def owner(i, info):
        return jnp.bitwise_xor(info[me_at], i)

    def rows(columns):
        return pl.BlockSpec((TILE, columns), lambda i, info: (2 * owner(i, info) + part, 0))

    def columns(count):
        return pl.BlockSpec((count, TILE), lambda i, info: (0, 2 * owner(i, info) + part))

    def packed(count):
        return pl.BlockSpec((count, TILE), lambda i, info: (0, owner(i, info)))

    out = jax.ShapeDtypeStruct
    before = () if dk is None else (dk, dv)
    return pl.pallas_call(
        in_order(
            functools.partial(attend_back_kernel, part=part, me_at=me_at, first=dk is None),
            16 + len(before), len(earlier),
        ),
        grid_spec=pltpu.PrefetchScalarGridSpec(
            num_scalar_prefetch=1,
            grid=(half // TILE,),
            in_specs=[
                whole(k_aug.shape), whole(v_aug.shape), whole(k_t.shape), columns(HEADS * AUG),
                rows(WIDTH), columns(WIDTH), packed(WIDTH), packed(8), columns(1),
            ]
            + [pl.BlockSpec((TILE, WIDTH), lambda i, info: (part, 0))] * 4
            + [
                pl.BlockSpec(
                    (3, 1, TILE), lambda i, info: (0, 0, 2 * owner(i, info) + part)
                ),
                whole(table.shape),
            ]
            + [whole((length, WIDTH))] * len(before)
            + unread(earlier),
            out_specs=[
                pl.BlockSpec((TILE, WIDTH), lambda i, info: (owner(i, info), 0)),
                whole((length, WIDTH)), whole((length, WIDTH)),
            ],
            scratch_shapes=[
                pltpu.VMEM((HEADS * AUG, TILE), bf16), pltpu.VMEM((HEADS * AUG, TILE), bf16),
                pltpu.VMEM((HEADS, TILE, WIDTH), bf16), pltpu.VMEM((HEADS, TILE, WIDTH), bf16),
                pltpu.VMEM((WIDTH, TILE), f32),
            ],
        ),
        out_shape=[out((half, WIDTH), bf16), out((length, WIDTH), f32), out((length, WIDTH), f32)],
        compiler_params=params(LIMIT),
        cost_estimate=pl.CostEstimate(
            flops=72 * half * length * WIDTH, bytes_accessed=16 * MIB, transcendentals=0
        ),
        name="attend_back",
    )(
        info, k_aug, v_aug, k_t, q_aug_t, q, v_t, o_t, lse, padding, *do, positions, table, *before,
        *earlier,
    )


def pieces(begin, count, period):
    at, end, cuts = begin, begin + count, []
    while at < end:
        length = min(end - at, period - at % period)
        cuts.append((at, length))
        at += length
    return cuts


def stacked_pairs(rows, count):
    row = lax.broadcasted_iota(jnp.int32, (count, WIDTH), 0)
    out = jnp.zeros((count, WIDTH), f32)
    for m, value in enumerate(rows):
        one, two, _ = three_parts(value)
        out = jnp.where(row == 2 * m, one, jnp.where(row == 2 * m + 1, two, out))
    return out.astype(bf16)


def late_extra(width, blocks):
    vectors = -(-(3 + 7 * width // WIDTH) // blocks)
    return vectors, -(-vectors // 8) * 16


def project_back_kernel(
    info, tok, gain, shift, dq_a, dq_b, dk, dv, pos, table, w, out_kept, out_other, out_there, early,
    dh1, dh1_sent, sums, acc, grad_b, small, w_wide,
):
    i = pl.program_id(0)

    @pl.when(i == 0)
    def _():
        acc[...] = jnp.zeros_like(acc)
        grad_b[...] = jnp.zeros_like(grad_b)
        small[...] = jnp.zeros_like(small)
        for c in range(3):
            w_wide[:, c * WIDTH : (c + 1) * WIDTH] = w[c]

    dk_here = dk[...]
    cos, low, high = rope_factors(pos, table)
    dk_low = (dk_here * cos - turned(dk_here, low, high)).astype(bf16)
    dq = jnp.concatenate([dq_a[...], dq_b[...]])
    parts = jnp.concatenate([dq, dk_low, dv[...].astype(bf16)], axis=1)
    grad = dot_nt(parts, w_wide[...])
    hat, _ = normalized(tok[...].astype(f32))
    normed = (hat * gain[...] + shift[...]).astype(bf16)
    acc[...] += dot_tn(normed, parts)
    grad_b[0:1, :] += jnp.sum(parts.astype(f32), axis=0, keepdims=True)
    small[0:1, :] += jnp.sum(grad * hat, axis=0, keepdims=True)
    small[1:2, :] += jnp.sum(grad, axis=0, keepdims=True)
    low_grad = grad.astype(bf16)
    dh1[0] = low_grad
    dh1_sent[0] = low_grad

    @pl.when(i == pl.num_programs(0) - 1)
    def _():
        width = normed.shape[1]
        blocks = sums.shape[0]

        def cut(value, count):
            return [value[:, r * WIDTH : (r + 1) * WIDTH] for r in range(count)]

        rows = cut(grad_b[0:1, :], 3) + cut(early[4:5, :], width // WIDTH)
        for ref, count in ((small, 2), (early, 4)):
            for v in range(count):
                rows += cut(ref[v : v + 1, :], width // WIDTH)
        for n in range(blocks):
            for to, rows_here, c, begin in late_places(n, blocks, width):
                here = (slice(begin, begin + rows_here), slice(c * WIDTH, (c + 1) * WIDTH))
                sums[n, to : to + rows_here, :] = acc[here].astype(bf16)
            for to, rows_here, c, begin in late_places(n, blocks, width, True):
                here = (slice(begin, begin + rows_here), slice(c * WIDTH, (c + 1) * WIDTH))
                sums[n, to : to + rows_here, :] = (
                    out_kept[here].astype(f32)
                    + out_other[here].astype(f32)
                    + out_there[here].astype(f32)
                ).astype(bf16)
            extra_at = 4 * width // blocks
            sums[n, extra_at:, :] = stacked_pairs(rows[n::blocks], sums.shape[1] - extra_at)


def late_places(n, blocks, width, out=False):
    deep, period = (width // blocks, WIDTH) if out else (3 * width // blocks, width)
    first = 3 * width // blocks if out else 0
    return [
        (first + at - n * deep, length, at // period, at % period)
        for at, length in pieces(n * deep, deep, period)
    ]


def project_back(
    info, me_at, tokens, gain, shift, dq_a, dq_b, dk, dv, positions, table, w, kept, other, there,
    early, blocks, earlier,
):
    length, width = tokens.shape
    share = 2 * TILE

    def owner(i, info):
        return jnp.bitwise_xor(info[me_at], relative(i))

    def rows(count, columns):
        return pl.BlockSpec((count, columns), lambda i, info: (owner(i, info), 0))

    first = pl.BlockSpec((None, TILE, width), lambda i, info: (0, 0, 0))
    out = jax.ShapeDtypeStruct
    sums = (blocks, 4 * width // blocks + late_extra(width, blocks)[1], WIDTH)
    return pl.pallas_call(
        in_order(project_back_kernel, 15, len(earlier)),
        grid_spec=pltpu.PrefetchScalarGridSpec(
            num_scalar_prefetch=1,
            grid=(length // share,),
            in_specs=[
                rows(share, width), whole((1, width)), whole((1, width)), rows(TILE, WIDTH),
                rows(TILE, WIDTH), rows(share, WIDTH), rows(share, WIDTH),
                pl.BlockSpec((3, 1, share), lambda i, info: (0, 0, owner(i, info))),
                whole(table.shape), whole(w.shape), first, first, whole((TILE, width)),
                whole(early.shape),
            ]
            + unread(earlier),
            out_specs=[
                pl.BlockSpec((1, share, width), lambda i, info: (i, 0, 0)),
                pl.BlockSpec((1, share, width), lambda i, info: (jnp.maximum(i - 2, 0), 0, 0)),
                whole(sums),
            ],
            scratch_shapes=[
                pltpu.VMEM((width, 3 * WIDTH), f32), pltpu.VMEM((8, 3 * WIDTH), f32),
                pltpu.VMEM((8, width), f32),
                pltpu.VMEM((width, 3 * WIDTH), bf16),
            ],
        ),
        out_shape=[
            pltpu.HBM((4, share, width), bf16), pltpu.HBM((2, share, width), bf16),
            pltpu.HBM(sums, bf16),
        ],
        compiler_params=params(LIMIT),
        cost_estimate=pl.CostEstimate(
            flops=24 * length * width * WIDTH, bytes_accessed=20 * MIB, transcendentals=0
        ),
        name="project_back",
    )(
        info, tokens, gain, shift, dq_a, dq_b, dk, dv, positions, table, w, kept, other, there, early,
        *earlier,
    )


def vectors_kernel(extra, grad_b, vectors):
    blocks = extra.shape[0]
    width = vectors.shape[1]
    grad_b[...] = jnp.zeros_like(grad_b)
    vectors[...] = jnp.zeros_like(vectors)
    for v in range(3 + 7 * width // WIDTH):
        n, m = v % blocks, v // blocks
        pair = extra[n].astype(f32)
        row = pair[2 * m : 2 * m + 1, :] + pair[2 * m + 1 : 2 * m + 2, :]
        if v < 3:
            grad_b[v : v + 1, :] = row
        else:
            to, at = divmod((v - 3) * WIDTH, width)
            vectors[to : to + 1, at : at + WIDTH] = row


def unpack_vectors(sums, width, earlier):
    blocks = sums.shape[0]
    at, rows = 4 * width // blocks, late_extra(width, blocks)[1]
    return pl.pallas_call(
        in_order(vectors_kernel, 1, len(earlier)),
        grid=(1,),
        in_specs=[pl.BlockSpec((blocks, rows, WIDTH), lambda i: (0, at // rows, 0))]
        + unread(earlier),
        out_specs=[whole((8, WIDTH)), whole((8, width))],
        out_shape=[pltpu.HBM((8, WIDTH), f32), pltpu.HBM((8, width), f32)],
        compiler_params=params(LIMIT),
        name="unpack_vectors",
    )(sums, *earlier)


def unpack_kernel(sums, grad_qkv, grad_out):
    blocks = sums.shape[0]
    width = grad_out.shape[1]
    for n in range(blocks):
        for to, rows, c, begin in late_places(n, blocks, width):
            grad_qkv[c, begin : begin + rows, :] = sums[n, to : to + rows, :].astype(f32)
        for to, rows, c, begin in late_places(n, blocks, width, True):
            grad_out[begin : begin + rows, c * WIDTH : (c + 1) * WIDTH] = sums[
                n, to : to + rows, :
            ].astype(f32)


def unpack(sums, width, earlier):
    out = jax.ShapeDtypeStruct
    return pl.pallas_call(
        in_order(unpack_kernel, 1, len(earlier)),
        in_specs=[pl.BlockSpec(memory_space=pltpu.VMEM)] + unread(earlier),
        out_specs=[pl.BlockSpec(memory_space=pltpu.VMEM)] * 2,
        out_shape=[out((3, width, WIDTH), f32), out((WIDTH, width), f32)],
        compiler_params=pltpu.CompilerParams(vmem_limit_bytes=LIMIT * MIB),
        name="unpack",
    )(sums, *earlier)


def finish_kernel(info, parts, other, there, tok, gain, dx2, out):
    grad = parts[0].astype(f32) + other[0].astype(f32) + there[...].astype(f32)
    hat, inverse = normalized(tok[...].astype(f32))
    out[...] = dx2[...] + norm_back(hat, inverse, gain[...], grad)


def finish(info, me_at, parts, other, there, tokens, gain, dx2, earlier):
    width = tokens.shape[1]
    share = there.shape[0]
    rows = pl.BlockSpec((TILE, width), lambda i, info: (i, 0))
    return pl.pallas_call(
        in_order(finish_kernel, 7, len(earlier)),
        grid_spec=pltpu.PrefetchScalarGridSpec(
            num_scalar_prefetch=1,
            grid=(share // TILE,),
            in_specs=[
                pl.BlockSpec((1, TILE, width), lambda i, info: (0, i, 0)),
                pl.BlockSpec((1, TILE, width), lambda i, info: (0, i, 0)), rows,
                pl.BlockSpec((TILE, width), lambda i, info: (2 * info[me_at] + i, 0)),
                whole((1, width)), rows,
            ]
            + unread(earlier),
            out_specs=rows,
        ),
        out_shape=jax.ShapeDtypeStruct((share, width), f32),
        compiler_params=params(LIMIT),
        cost_estimate=pl.CostEstimate(
            flops=30 * share * width, bytes_accessed=10 * MIB, transcendentals=0
        ),
        name="finish",
    )(info, parts, other, there, tokens, gain, dx2, *earlier)


def total_of(blocks):
    total = blocks[0].astype(f32)
    for n in range(1, blocks.shape[0]):
        total += blocks[n].astype(f32)
    return total.astype(bf16)


def sums_kernel(blocks_a, blocks_b, out):
    rows = blocks_a.shape[1]
    out[:rows, :] = total_of(blocks_a)
    out[rows:, :] = total_of(blocks_b)


def two_sums(blocks_a, blocks_b, earlier):
    _, rows, width = blocks_a.shape
    return pl.pallas_call(
        in_order(sums_kernel, 2, len(earlier)),
        grid=(1,),
        in_specs=[whole(blocks_a.shape), whole(blocks_b.shape)] + unread(earlier),
        out_specs=whole((2 * rows, width)),
        out_shape=pltpu.HBM((2 * rows, width), bf16),
        compiler_params=params(LIMIT),
        name="two_sums",
    )(blocks_a, blocks_b, *earlier)


def sum_kernel(blocks, out):
    out[...] = total_of(blocks)


def summed(blocks, steps, earlier):
    count, rows, width = blocks.shape
    tile = rows // steps
    return pl.pallas_call(
        in_order(sum_kernel, 1, len(earlier)),
        grid=(steps,),
        in_specs=[pl.BlockSpec((count, tile, width), lambda i: (0, i, 0))] + unread(earlier),
        out_specs=pl.BlockSpec((tile, width), lambda i: (i, 0)),
        out_shape=pltpu.HBM((rows, width), bf16),
        compiler_params=params(LIMIT),
        name="summed",
    )(blocks, *earlier)


def copies_kernel(first, second, out):
    total = (first[...].astype(f32) + second[...].astype(f32)).astype(bf16)
    for n in range(out.shape[0]):
        out[n] = total


def sum_copies(first, second, count, earlier):
    rows, width = first.shape
    return pl.pallas_call(
        in_order(copies_kernel, 2, len(earlier)),
        grid=(1,),
        in_specs=[whole((rows, width))] * 2 + unread(earlier),
        out_specs=whole((count, rows, width)),
        out_shape=pltpu.HBM((count, rows, width), bf16),
        compiler_params=params(LIMIT),
        name="sum_copies",
    )(first, second, *earlier)


def swap(array, axis, bit=1):
    size = lax.axis_size(axis)
    if size == 1:
        return jnp.zeros_like(array)
    return lax.ppermute(array, axis, [(i, i ^ bit) for i in range(size)])


def swap_both(array):
    return lax.ppermute(array, MP, [(i, i ^ 3) for i in range(4)])


def scattered(rows, axes):
    group = lax.axis_size(axes)
    length, width = rows.shape
    return lax.all_to_all(
        rows.reshape(group, length // group, width), axes, 0, 0, tiled=True
    )


def both_sums(total):
    if lax.axis_size("zl") == 1:
        return total
    return (total.astype(f32) + swap(total, "zl").astype(f32)).astype(bf16)


def local(
    tokens, cotangent, segments, padding, positions, ln1_gain, ln1_bias, w_qkv, b_qkv, w_out, b_out,
    ln2_gain, ln2_bias, w_up, b_up, w_down, b_down,
):
    width, hidden = w_up.shape
    w_all = lax.all_gather(w_out, MP)
    gain_one, shift_one = ln1_gain[None], ln1_bias[None]
    gain_two, shift_two = ln2_gain[None], ln2_bias[None]
    ends = jnp.sum((segments <= jnp.arange(2)[:, None]).astype(jnp.int32), axis=1)
    info = jnp.concatenate([ends, lax.axis_index(MP)[None].astype(jnp.int32)])
    me_at = 2
    table = jnp.asarray(rope_constants())
    k_aug, v_aug, q_aug_t, q, k_t, v_t = project(
        tokens, w_qkv, b_qkv, gain_one, shift_one, positions, segments, padding, table
    )

    def exchanged(own, to_c, to_zh, to_both):
        return own, swap(to_c, "c"), swap(to_zh, "zh"), swap_both(to_both)

    o_0, o_t_0, lse_0 = attend(0, info, k_aug, v_t, q_aug_t, k_t, padding, ())
    o_zh_0, o_c_0 = swap(o_0, "zh"), swap(o_0, "c")
    o_1, o_t_1, lse_1 = attend(1, info, k_aug, v_t, q_aug_t, k_t, padding, (o_0, w_all))
    o_zh_1 = swap(o_1, "zh")
    o_zh_0 = after(o_zh_0, (o_1,))
    o_parts_0 = tuple((part, None) for part in (o_0, o_c_0, o_zh_0, swap(o_zh_0, "c")))

    def mlp_half(part, o_parts, earlier):
        return mlp(
            part, info, me_at, tokens, cotangent, o_parts, w_all, b_out[None], gain_two, shift_two,
            w_up, b_up[None], w_down, earlier,
        )

    x2_0, dy_0, h2_0, act_0, du_0, mlp_0, mlp_sent_0, dh2_0, sent, db_0 = mlp_half(
        0, o_parts_0, (o_1,)
    )
    pair = paired(o_1, o_zh_1, (x2_0,))
    pair_c = swap(pair, "c")
    o_parts_1 = ((pair, 0), (pair_c, 0), (pair, 1), (pair_c, 1))
    other_0 = swap(sent, "c")
    give_0 = to_give(dh2_0, other_0, ())
    there_0 = swap(give_0, "zh")
    x2_1, dy_1, h2_1, act_1, du_1, mlp_1, mlp_sent_1, dh2_1, sent, db_1 = mlp_half(
        1, o_parts_1, (give_0,)
    )
    other_1 = swap(sent, "c")
    grad_down = down_weights((act_0, act_1), cotangent, (there_0,))
    arrived_down = scattered(grad_down, ("y", "x"))
    give_1 = to_give(dh2_1, other_1, (grad_down,))
    there_1 = swap(give_1, "zh")
    grad_up = up_weights((h2_0, h2_1), (du_0, du_1), (give_1,))
    dx2, g, *d_parts, small = middle(
        info, me_at, (dh2_0, other_0, there_0, x2_0, dy_0), (dh2_1, other_1, there_1, x2_1, dy_1),
        gain_two, w_all, (grad_up,),
    )
    do = exchanged(*d_parts)
    arrived_up = scattered(after(grad_up, (g,)), ("y", "x"))
    grad_out, out_sent = out_weights(info, me_at, o_parts_0, o_parts_1, g)
    out_other = swap(out_sent, "c")
    mlp_parts = (mlp_0, mlp_1)
    mlp_others = (swap(mlp_sent_0, "c"), swap(mlp_sent_1, "c"))
    dq_0, dk, dv = attend_back(
        0, info, me_at, k_aug, v_aug, k_t, q_aug_t, q, v_t, o_t_0, lse_0, padding, do, positions,
        table, None, None, (grad_out, g),
    )
    give = to_give(grad_out, out_other, (dq_0,))
    out_there = swap(give, "zh")
    mlp_give = two_to_give(mlp_parts, mlp_others, (give,))
    mlp_there = swap(mlp_give, "zh")
    part_sum = both_sums(two_sums(arrived_up, arrived_down, (mlp_give,)))
    dq_1, dk, dv = attend_back(
        1, info, me_at, k_aug, v_aug, k_t, q_aug_t, q, v_t, o_t_1, lse_1, padding, do, positions,
        table, dk, dv, (give, part_sum),
    )
    grad_mlp = lax.all_gather(part_sum, ("y", "x"), axis=0, tiled=True)
    early = jnp.concatenate([small[0:4], (db_0 + db_1)[0:4]])
    dh1, sent, sums = project_back(
        info, me_at, tokens, gain_one, shift_one, dq_0, dq_1, dk, dv, positions, table, w_qkv,
        grad_out, out_other, out_there, early, lax.axis_size(("y", "x")), (mlp_there,),
    )
    other = swap(sent, "c")
    back = swap(to_give(dh1, other, (sums,)), "zh")
    arrived = scattered(sums.reshape(-1, WIDTH), ("y", "x"))
    total = summed(arrived, 1, (back,))
    copies = sum_copies(total, swap(total, "zl"), sums.shape[0], ())
    late = lax.all_to_all(copies, ("y", "x"), 0, 0, tiled=True)
    grad_inputs = finish(info, me_at, dh1, other, back, tokens, gain_one, dx2, (copies,))
    mixed = mixed_rows(
        (x2_0, x2_1), mlp_parts, mlp_others, mlp_there, b_down[None], (copies,)
    )
    count = lax.axis_size(("y", "x"))
    grad_mlp = grad_mlp.reshape(count, 2, width // count, hidden)
    grad_up = grad_mlp[:, 0].astype(f32).reshape(width, hidden)
    grad_down = grad_mlp[:, 1].astype(f32).reshape(hidden, width)
    grad_b, vectors = unpack_vectors(late, width, (grad_inputs, mixed, grad_up, grad_down))
    by_c, by_zh, by_both = swap(vectors, "c"), swap(vectors, "zh"), swap_both(vectors)
    grad_qkv, grad_w_out = unpack(late, width, (vectors,))
    group = (vectors + by_c) + (by_zh + by_both)
    return (
        mixed, grad_inputs, group[1], group[2], grad_qkv, grad_b[0:3], grad_w_out, group[5],
        group[3], group[4], grad_up, vectors[0], grad_down, group[6],
    )


def solution(mesh):
    packs = mesh.shape["dp"]
    if packs == 32:
        shape = (2, 4, 4, 2, 2)
    else:
        shape = (1, packs, 1, 2, 2)
    split = Mesh(mesh.devices.reshape(shape), EVERY)
    in_specs = (
        P(DP, None), P(DP, None), P(DP, None), P(DP, None), P(None, DP, None), P(), P(),
        P(None, None, MP), P(None, MP), P(MP, None), P(), P(), P(), P(None, MP), P(MP),
        P(MP, None), P(),
    )
    out_specs = (
        P(EVERY, None), P(EVERY, None), P(), P(), P(None, None, MP), P(None, MP), P(MP, None), P(),
        P(), P(), P(None, MP), P(MP), P(MP, None), P(),
    )
    return jax.shard_map(local, mesh=split, in_specs=in_specs, out_specs=out_specs, check_vma=False)
```

```python
import functools
import math

import jax
import jax.numpy as jnp
import ml_dtypes
import numpy as np
from jax import lax
from jax.experimental import pallas as pl
from jax.experimental.pallas import tpu as pltpu
from jax.sharding import Mesh
from jax.sharding import PartitionSpec as P

HEAD_DIM = 64
HEADS = 4
WIDTH = HEADS * HEAD_DIM
AUG = 128
TILE = 256
ROWS = 2 * TILE
PLACES = 64
LIMIT = 64
MIB = 1 << 20
DP = ("zl", "y", "x")
MP = ("zh", "c")
EVERY = ("zl", "y", "x", "zh", "c")

epsilon = 1e-06
NEG = -1e30
bf16 = jnp.bfloat16
f32 = jnp.float32


def dot_nn(a, b):
    return lax.dot_general(a, b, (((1,), (0,)), ((), ())), preferred_element_type=f32)


def dot_nt(a, b):
    return lax.dot_general(a, b, (((1,), (1,)), ((), ())), preferred_element_type=f32)


def dot_tn(a, b):
    return lax.dot_general(a, b, (((0,), (0,)), ((), ())), preferred_element_type=f32)


def normalized(values):
    center = jnp.mean(values, axis=-1, keepdims=True)
    shifted = values - center
    spread = jnp.mean(shifted * shifted, axis=-1, keepdims=True)
    inverse = lax.rsqrt(spread + epsilon)
    return shifted * inverse, inverse


def norm_back(hat, inverse, gain, grad):
    scaled = grad * gain
    return inverse * (
        scaled
        - jnp.mean(scaled, axis=-1, keepdims=True)
        - hat * jnp.mean(scaled * hat, axis=-1, keepdims=True)
    )


def turned(x, low, high):
    width = x.shape[1]
    pair = HEAD_DIM // 6
    return pltpu.roll(x, width - pair, 1) * low + pltpu.roll(x, pair, 1) * high


def three_parts(x):
    first = x.astype(bf16).astype(f32)
    rest = x - first
    second = rest.astype(bf16).astype(f32)
    return first, second, rest - second


def params(limit, axes=1):
    return pltpu.CompilerParams(
        dimension_semantics=("arbitrary",) * axes, vmem_limit_bytes=limit * MIB
    )


def in_order(kernel, inputs, earlier):
    def run(*refs):
        kernel(*refs[:inputs], *refs[inputs + earlier :])

    return run


def unread(arrays):
    return [pl.BlockSpec(memory_space=pl.ANY)] * len(arrays)


def whole(shape):
    return pl.BlockSpec(shape, lambda *_: (0,) * len(shape))


def clip_range(info, tile, length):
    half = TILE // 2
    first, second = info[0], info[1]
    at = tile * TILE
    begin = jnp.where(second <= at, second, jnp.where(first <= at, first, 0))
    end = jnp.where(
        first >= at + TILE, first, jnp.where(second >= at + TILE, second, length)
    )
    end = (end + half - 1) // half
    count = (end - begin // half + 1) // 2
    return jnp.maximum(end - 2 * count, 0), count


def key_tiles(begin, at, count):
    return pl.ds(pl.multiple_of(begin * (TILE // 2) + at * TILE, TILE // 2), count * TILE)


def rope_constants():
    pair = HEAD_DIM // 6
    feature = np.arange(WIDTH) % HEAD_DIM
    section, place = feature // (2 * pair), feature % (2 * pair)
    frequency = np.exp(-math.log(10000.0) * (place % pair) / pair)
    table = np.zeros((PLACES, 3, WIDTH))
    for s in range(3):
        for value in range(16):
            angle = value * frequency
            turns = section == s
            table[s * 16 + value, 0] = np.where(turns, np.cos(angle), 0.0)
            table[s * 16 + value, 1] = np.where(turns & (place < pair), -np.sin(angle), 0.0)
            table[s * 16 + value, 2] = np.where(turns & (place >= pair), np.sin(angle), 0.0)
    table[48, 0] = section == 3
    rest = table.reshape(PLACES, 3 * WIDTH).astype(np.float32)
    parts = []
    for _ in range(3):
        part = rest.astype(ml_dtypes.bfloat16)
        parts.append(part)
        rest = rest - part.astype(np.float32)
    return np.concatenate(parts)


def rope_factors(positions, table):
    row = lax.broadcasted_iota(jnp.int32, (PLACES, positions.shape[-1]), 0)
    where = jnp.where(
        row < 16, positions[0], jnp.where(row < 32, positions[1], positions[2])
    )
    hit = ((where == row % 16) & (row < 48)) | (row == 48)
    hit = jnp.where(hit, 1.0, 0.0)
    hits = jnp.concatenate([hit, hit, hit]).astype(bf16)
    factors = dot_tn(hits, table[...])
    return factors[:, :WIDTH], factors[:, WIDTH : 2 * WIDTH], factors[:, 2 * WIDTH :]


def qkv_kernel(
    tok, w, b, gain, shift, pos, seg, pad, table, k_aug, v_aug, q_aug_t, q_out, k_t, v_t, w_wide
):
    @pl.when(pl.program_id(0) == 0)
    def _():
        for c in range(3):
            w_wide[:, c * WIDTH : (c + 1) * WIDTH] = w[c]

    hat, _ = normalized(tok[...].astype(f32))
    normed = (hat * gain[...] + shift[...]).astype(bf16)
    cos, low, high = rope_factors(pos, table)
    all_three = dot_nn(normed, w_wide[...])
    q = all_three[:, :WIDTH] + b[0:1, :]
    k = all_three[:, WIDTH : 2 * WIDTH] + b[1:2, :]
    v = all_three[:, 2 * WIDTH :] + b[2:3, :]
    q = (q * cos + turned(q, low, high)) * (1.0 / math.sqrt(HEAD_DIM))
    k = k * cos + turned(k, low, high)
    q_out[...] = q.astype(bf16)
    q_t = q.T.astype(bf16)
    k_t[...] = k.T.astype(bf16)
    v_t[...] = v.T.astype(bf16)
    row = lax.broadcasted_iota(jnp.int32, (HEAD_DIM, ROWS), 0)
    clip = seg[...]
    same = (row >= 1) & (row < 4) & (clip == row - 1)
    mask = jnp.where((row >= 1) & (row < 4) & (clip != row - 1), NEG, 0.0)
    mask = jnp.where(row == 0, jnp.where(pad[...] != 0, NEG, 0.0), mask)
    k_extra = jnp.where((row >= 4) & (row < 7), 1.0, mask)
    q_extra = jnp.where(same | (row == 0), 1.0, 0.0).astype(bf16)
    k_side = jnp.concatenate([jnp.zeros((HEAD_DIM, ROWS), f32), k_extra]).T
    lane = lax.broadcasted_iota(jnp.int32, (ROWS, AUG), 1)
    ones = jnp.where((lane >= HEAD_DIM) & (lane < HEAD_DIM + 3), 1.0, 0.0)
    for h in range(HEADS):
        pair = slice(h // 2 * AUG, h // 2 * AUG + AUG)
        wide = slice(h * AUG, (h + 1) * AUG)
        k_pair, v_pair = k[:, pair], v[:, pair]
        if h % 2:
            k_pair, v_pair = pltpu.roll(k_pair, HEAD_DIM, 1), pltpu.roll(v_pair, HEAD_DIM, 1)
        k_aug[:, wide] = jnp.where(lane < HEAD_DIM, k_pair, k_side).astype(bf16)
        v_aug[:, wide] = jnp.where(lane < HEAD_DIM, v_pair, ones).astype(bf16)
        q_aug_t[h * AUG : h * AUG + HEAD_DIM, :] = q_t[h * HEAD_DIM : (h + 1) * HEAD_DIM, :]
        q_aug_t[h * AUG + HEAD_DIM : (h + 1) * AUG, :] = q_extra


def project(tokens, w, b, gain, shift, positions, segments, padding, table):
    length, width = tokens.shape
    tiles = length // ROWS

    def rows(columns):
        return pl.BlockSpec((ROWS, columns), lambda i: (i, 0))

    def columns(count):
        return pl.BlockSpec((count, ROWS), lambda i: (0, i))

    out = jax.ShapeDtypeStruct
    wide = out((length, HEADS * AUG), bf16)
    flat = out((WIDTH, length), bf16)
    return pl.pallas_call(
        qkv_kernel,
        grid=(tiles,),
        in_specs=[
            rows(width), whole(w.shape), whole(b.shape), whole((1, width)), whole((1, width)),
            pl.BlockSpec((3, 1, ROWS), lambda i: (0, 0, i)), columns(1), columns(1), whole(table.shape),
        ],
        out_specs=[
            rows(HEADS * AUG), rows(HEADS * AUG), columns(HEADS * AUG), rows(WIDTH), columns(WIDTH),
            columns(WIDTH),
        ],
        out_shape=[
            wide, wide, out((HEADS * AUG, length), bf16), out((length, WIDTH), bf16), flat, flat,
        ],
        scratch_shapes=[pltpu.VMEM((width, 3 * WIDTH), bf16)],
        compiler_params=params(LIMIT),
        cost_estimate=pl.CostEstimate(
            flops=6 * length * width * WIDTH, bytes_accessed=20 * MIB, transcendentals=0
        ),
        name="project",
    )(tokens, w, b, gain, shift, positions, segments, padding, table)


def attend_kernel(info, k_aug, v_t, q_aug_t, k_t, pad, o, o_t, lse, top, total, acc, *, part):
    tile = 2 * pl.program_id(0) + part
    padded = pad[...] != 0
    for h in range(HEADS):
        q_h = q_aug_t[h * AUG : h * AUG + HEAD_DIM, :].astype(f32)
        k_h = k_t[h * HEAD_DIM : (h + 1) * HEAD_DIM, :].astype(f32)
        own = jnp.sum(q_h * k_h, axis=0, keepdims=True)
        top[h : h + 1, :] = jnp.where(padded, own, -3e38)
        total[h : h + 1, :] = jnp.where(padded, 1.0, 0.0)
    here = pl.ds(pl.multiple_of(tile * TILE, TILE), TILE)
    acc[...] = jnp.where(padded, v_t[:, here].astype(f32), 0.0)
    feats = [slice(h * HEAD_DIM, (h + 1) * HEAD_DIM) for h in range(HEADS)]
    wides = [slice(h * AUG, (h + 1) * AUG) for h in range(HEADS)]

    begin, tiles = clip_range(info, tile, k_aug.shape[0])

    def step(j, count):
        keys = key_tiles(begin, j, count)
        scores = [dot_nn(k_aug[keys, wide], q_aug_t[wide, :]) for wide in wides]
        probs, fades = [], []
        for h in range(HEADS):
            old = top[h : h + 1, :]
            new = jnp.maximum(old, jnp.max(scores[h], axis=0, keepdims=True))
            prob = jnp.exp(scores[h] - new)
            fade = jnp.exp(old - new)
            top[h : h + 1, :] = new
            total[h : h + 1, :] = total[h : h + 1, :] * fade + jnp.sum(prob, axis=0, keepdims=True)
            probs.append(prob.astype(bf16))
            fades.append(fade)
        for h, feat in enumerate(feats):
            acc[feat, :] = acc[feat, :] * fades[h] + dot_nn(v_t[feat, keys], probs[h])

    pairs = tiles // 2

    def two(n, _):
        step(2 * n, 2)
        return 0

    lax.fori_loop(0, pairs, two, 0)

    @pl.when(2 * pairs < tiles)
    def _():
        step(tiles - 1, 1)

    for h, feat in enumerate(feats):
        acc[feat, :] = acc[feat, :] / total[h : h + 1, :]
    lse[...] = jnp.zeros_like(lse)
    lse[0:HEADS, :] = top[0:HEADS, :] + jnp.log(total[0:HEADS, :])
    turned_o = acc[...]
    o_t[...] = turned_o.astype(bf16)
    o[...] = turned_o.T.astype(bf16)


def attend(part, info, k_aug, v_t, q_aug_t, k_t, padding, earlier):
    length = k_aug.shape[0]
    half = length // 2

    def columns(count):
        return pl.BlockSpec((count, TILE), lambda i, *_: (0, 2 * i + part))

    def packed(count):
        return pl.BlockSpec((count, TILE), lambda i, *_: (0, i))

    out = jax.ShapeDtypeStruct
    return pl.pallas_call(
        in_order(functools.partial(attend_kernel, part=part), 6, len(earlier)),
        grid_spec=pltpu.PrefetchScalarGridSpec(
            num_scalar_prefetch=1,
            grid=(half // TILE,),
            in_specs=[
                whole(k_aug.shape), whole(v_t.shape), columns(HEADS * AUG), columns(WIDTH),
                columns(1),
            ]
            + unread(earlier),
            out_specs=[
                pl.BlockSpec((TILE, WIDTH), lambda i, *_: (i, 0)), packed(WIDTH), packed(8),
            ],
            scratch_shapes=[
                pltpu.VMEM((8, TILE), f32), pltpu.VMEM((8, TILE), f32), pltpu.VMEM((WIDTH, TILE), f32),
            ],
        ),
        out_shape=[out((half, WIDTH), bf16), out((WIDTH, half), bf16), out((8, half), f32)],
        compiler_params=params(LIMIT),
        cost_estimate=pl.CostEstimate(
            flops=24 * half * length * WIDTH, bytes_accessed=6 * MIB, transcendentals=0
        ),
        name="attend",
    )(info, k_aug, v_t, q_aug_t, k_t, padding, *earlier)


def nothing(*refs):
    del refs


def after(value, earlier):
    return pl.pallas_call(
        nothing,
        in_specs=unread((value,) + earlier),
        out_specs=pl.BlockSpec(memory_space=pl.ANY),
        out_shape=jax.ShapeDtypeStruct(value.shape, value.dtype),
        input_output_aliases={0: 0},
        name="after",
    )(value, *earlier)


def pair_kernel(first, second, out):
    out[0] = first[...]
    out[1] = second[...]


def paired(first, second, earlier):
    shape = (2,) + first.shape
    return pl.pallas_call(
        in_order(pair_kernel, 2, len(earlier)),
        in_specs=[pl.BlockSpec(memory_space=pltpu.VMEM)] * 2 + unread(earlier),
        out_specs=pl.BlockSpec(memory_space=pltpu.VMEM),
        out_shape=jax.ShapeDtypeStruct(shape, first.dtype),
        name="paired",
    )(first, second, *earlier)


def head_block(at, owner):
    if at is None:
        return pl.BlockSpec((TILE, WIDTH), lambda i, info: (owner(i, info), 0))
    return pl.BlockSpec((None, TILE, WIDTH), lambda i, info: (at, owner(i, info), 0))


def relative(i):
    return i % 2 * 2 + i // 2


def gelu_parts(u):
    size = jnp.abs(u)
    t = 1.0 / (1.0 + (0.3275911 / math.sqrt(2.0)) * size)
    bell = jnp.exp(-0.5 * (u * u))
    poly = 0.5 * 1.061405429
    for c in (-1.453152027, 1.421413741, -0.284496736, 0.254829592):
        poly = poly * t + 0.5 * c
    tail = poly * t * bell
    below = jnp.where(u >= 0, 1.0 - tail, tail)
    return u * below, below + u * bell * (1.0 / math.sqrt(2.0 * math.pi))


def mlp_kernel(
    info, tok, cot, o_0, o_1, o_2, o_3, w_all, b_out, gain, shift, w_up, b_up, w_down,
    x2, dy, h2, act, du, mlp, mlp_sent, dh2, dh2_sent, db_up, w_out, *, me_at,
):
    i = pl.program_id(0)

    @pl.when(i == 0)
    def _():
        for j in range(4):
            w_out[j * WIDTH : (j + 1) * WIDTH, :] = w_all[jnp.bitwise_xor(info[me_at], j)]
        db_up[...] = jnp.zeros_like(db_up)

    heads = jnp.concatenate([o_0[...], o_1[...], o_2[...], o_3[...]], axis=1)
    mid = tok[...].astype(f32) + b_out[...] + dot_nn(heads, w_out[...])

    @pl.when(i == 0)
    def _():
        x2[...] = mid
        dy[...] = cot[...]

    hat, _ = normalized(mid)
    normed = (hat * gain[...] + shift[...]).astype(bf16)
    h2[...] = normed
    u = dot_nn(normed, w_up[...]) + b_up[...]
    grad_act = dot_nt(cot[...], w_down[...])
    value, slope = gelu_parts(u)
    value = value.astype(bf16)
    grad = (grad_act * slope).astype(bf16)
    act[...] = value
    du[...] = grad
    db_up[0:1, :] += jnp.sum(grad.astype(f32), axis=0, keepdims=True)
    mlp_part = dot_nn(value, w_down[...]).astype(bf16)
    dh2_part = dot_nt(grad, w_up[...]).astype(bf16)
    mlp[0] = mlp_part
    mlp_sent[0] = mlp_part
    dh2[0] = dh2_part
    dh2_sent[0] = dh2_part


def mlp(
    part, info, me_at, tokens, cotangent, o_parts, w_all, b_out, gain, shift, w_up, b_up, w_down,
    earlier,
):
    length, width = tokens.shape
    half = length // 2
    hidden = w_up.shape[1]
    owners = half // TILE

    def owner(i, info):
        return jnp.bitwise_xor(info[me_at], relative(i))

    def rows(columns):
        return pl.BlockSpec((TILE, columns), lambda i, info: (2 * owner(i, info) + part, 0))

    def packed(columns):
        return pl.BlockSpec((TILE, columns), lambda i, info: (owner(i, info), 0))

    ordered = pl.BlockSpec((1, TILE, width), lambda i, info: (i, 0, 0))
    sent = pl.BlockSpec((1, TILE, width), lambda i, info: (jnp.maximum(i - 2, 0), 0, 0))

    out = jax.ShapeDtypeStruct
    return pl.pallas_call(
        in_order(functools.partial(mlp_kernel, me_at=me_at), 14, len(earlier)),
        grid_spec=pltpu.PrefetchScalarGridSpec(
            num_scalar_prefetch=1,
            grid=(owners,),
            in_specs=[rows(width), rows(width)]
            + [head_block(at, owner) for _, at in o_parts]
            + [whole(w_all.shape)]
            + [whole((1, width))] * 3
            + [whole(w_up.shape), whole((1, hidden)), whole(w_down.shape)]
            + unread(earlier),
            out_specs=[
                whole((TILE, width)), whole((TILE, width)), packed(width), packed(hidden),
                packed(hidden), ordered, sent, ordered, sent, whole((8, hidden)),
            ],
            scratch_shapes=[pltpu.VMEM((4 * WIDTH, width), bf16)],
        ),
        out_shape=[
            out((TILE, width), f32), out((TILE, width), bf16), out((half, width), bf16),
            out((half, hidden), bf16), out((half, hidden), bf16),
        ]
        + [out((owners, TILE, width), bf16), out((2, TILE, width), bf16)] * 2
        + [out((8, hidden), f32)],
        compiler_params=params(LIMIT),
        cost_estimate=pl.CostEstimate(
            flops=20 * half * width * hidden, bytes_accessed=20 * MIB, transcendentals=0
        ),
        name="mlp",
    )(
        info, tokens, cotangent, *(part for part, _ in o_parts), w_all, b_out, gain, shift, w_up,
        b_up, w_down, *earlier
    )


def up_weights_kernel(left_a, left_b, right_a, right_b, out):
    left = jnp.concatenate([left_a[...], left_b[...]])
    right = jnp.concatenate([right_a[...], right_b[...]])
    out[...] = dot_tn(left, right).astype(bf16)


def up_weights(h2, du, earlier):
    half, width = h2[0].shape
    hidden = du[0].shape[1]
    return pl.pallas_call(
        in_order(up_weights_kernel, 4, len(earlier)),
        grid=(width // TILE,),
        in_specs=[pl.BlockSpec((half, TILE), lambda i: (0, i))] * 2
        + [whole((half, hidden))] * 2
        + unread(earlier),
        out_specs=pl.BlockSpec((TILE, hidden), lambda i: (i, 0)),
        out_shape=pltpu.HBM((width, hidden), bf16),
        compiler_params=params(LIMIT),
        cost_estimate=pl.CostEstimate(
            flops=8 * half * width * hidden, bytes_accessed=12 * MIB, transcendentals=0
        ),
        name="up_weights",
    )(*h2, *du, *earlier)


def down_weights_kernel(act_a, act_b, cot, out):
    owners = cot.shape[0] // (2 * TILE)
    rows = [cot[n * TILE : (n + 1) * TILE, :] for p in range(2) for n in range(p, 2 * owners, 2)]
    out[...] = dot_tn(
        jnp.concatenate([act_a[...], act_b[...]]), jnp.concatenate(rows)
    ).astype(bf16)


def down_weights(act, cotangent, earlier):
    half, hidden = act[0].shape
    length, width = cotangent.shape
    return pl.pallas_call(
        in_order(down_weights_kernel, 3, len(earlier)),
        grid=(hidden // TILE,),
        in_specs=[pl.BlockSpec((half, TILE), lambda i: (0, i))] * 2
        + [whole((length, width))]
        + unread(earlier),
        out_specs=pl.BlockSpec((TILE, width), lambda i: (i, 0)),
        out_shape=pltpu.HBM((hidden, width), bf16),
        compiler_params=params(LIMIT),
        cost_estimate=pl.CostEstimate(
            flops=8 * half * width * hidden, bytes_accessed=12 * MIB, transcendentals=0
        ),
        name="down_weights",
    )(*act, cotangent, *earlier)


def add_kernel(parts, other, out):
    out[...] = (parts[0].astype(f32) + other[0].astype(f32)).astype(bf16)


def to_give(parts, other, earlier):
    _, rows, width = parts.shape
    tile = min(rows, TILE)
    return pl.pallas_call(
        in_order(add_kernel, 2, len(earlier)),
        grid=(rows // tile,),
        in_specs=[
            pl.BlockSpec((1, tile, width), lambda i: (1, i, 0)),
            pl.BlockSpec((1, tile, width), lambda i: (1, i, 0)),
        ]
        + unread(earlier),
        out_specs=pl.BlockSpec((tile, width), lambda i: (i, 0)),
        out_shape=pltpu.HBM((rows, width), bf16),
        compiler_params=params(LIMIT),
        name="to_give",
    )(parts, other, *earlier)


def two_kernel(parts_a, parts_b, other_a, other_b, out):
    for n, (parts, other) in enumerate(((parts_a, other_a), (parts_b, other_b))):
        out[n] = (parts[0].astype(f32) + other[0].astype(f32)).astype(bf16)


def two_to_give(parts, others, earlier):
    _, rows, width = parts[0].shape
    tile = rows // 2
    return pl.pallas_call(
        in_order(two_kernel, 4, len(earlier)),
        grid=(rows // tile,),
        in_specs=[pl.BlockSpec((1, tile, width), lambda i: (1, i, 0))] * 4 + unread(earlier),
        out_specs=pl.BlockSpec((2, tile, width), lambda i: (0, i, 0)),
        out_shape=pltpu.HBM((2, rows, width), bf16),
        compiler_params=params(LIMIT),
        name="two_to_give",
    )(*parts, *others, *earlier)


def mixed_kernel(x2_a, x2_b, parts_a, parts_b, other_a, other_b, there, shift, out):
    for n, (x2, parts, other) in enumerate(
        ((x2_a, parts_a, other_a), (x2_b, parts_b, other_b))
    ):
        total = parts[0].astype(f32) + other[0].astype(f32) + there[n].astype(f32)
        out[n * TILE : (n + 1) * TILE, :] = (x2[...] + total + shift[...]).astype(bf16)


def mixed_rows(x2, parts, others, there, shift, earlier):
    rows, width = x2[0].shape
    first = pl.BlockSpec((1, rows, width), lambda i: (0, 0, 0))
    return pl.pallas_call(
        in_order(mixed_kernel, 8, len(earlier)),
        grid=(1,),
        in_specs=[whole((rows, width))] * 2
        + [first] * 4
        + [whole((2, rows, width)), whole((1, width))]
        + unread(earlier),
        out_specs=whole((2 * rows, width)),
        out_shape=jax.ShapeDtypeStruct((2 * rows, width), bf16),
        compiler_params=params(LIMIT),
        name="mixed_rows",
    )(*x2, *parts, *others, there, shift, *earlier)


def middle_kernel(info, *refs, me_at):
    halves, (gain, w_all, dx2, g, d_0, d_1, d_2, d_3, small) = (refs[0:5], refs[5:10]), refs[10:]
    small[...] = jnp.zeros_like(small)
    for part, (kept, other, there, x2, dy) in enumerate(halves):
        rows = slice(part * TILE, (part + 1) * TILE)
        grad = kept[0].astype(f32) + other[0].astype(f32) + there[...].astype(f32)
        hat, inverse = normalized(x2[...])
        dy = dy[...].astype(f32)
        full = dy + norm_back(hat, inverse, gain[...], grad)
        dx2[rows, :] = full
        low = full.astype(bf16)
        g[rows, :] = low
        small[0:1, :] += jnp.sum(grad * hat, axis=0, keepdims=True)
        small[1:2, :] += jnp.sum(grad, axis=0, keepdims=True)
        small[2:3, :] += jnp.sum(low.astype(f32), axis=0, keepdims=True)
        small[3:4, :] += jnp.sum(dy, axis=0, keepdims=True)
    low = g[...]
    for j, d_j in enumerate((d_0, d_1, d_2, d_3)):
        d_j[...] = dot_nt(low, w_all[jnp.bitwise_xor(info[me_at], j)]).astype(bf16)


def middle(info, me_at, half_a, half_b, gain, w_all, earlier):
    width = gain.shape[1]
    rows = 2 * TILE
    own = whole((TILE, width))
    first = pl.BlockSpec((1, TILE, width), lambda i, info: (0, 0, 0))
    return pl.pallas_call(
        in_order(functools.partial(middle_kernel, me_at=me_at), 13, len(earlier)),
        grid_spec=pltpu.PrefetchScalarGridSpec(
            num_scalar_prefetch=1,
            grid=(1,),
            in_specs=[first, first, own, own, own] * 2
            + [whole((1, width)), whole(w_all.shape)]
            + unread(earlier),
            out_specs=[whole((rows, width))] * 2
            + [whole((rows, WIDTH))] * 4
            + [whole((8, width))],
        ),
        out_shape=[pltpu.HBM((rows, width), f32), pltpu.HBM((rows, width), bf16)]
        + [pltpu.HBM((rows, WIDTH), bf16)] * 4
        + [pltpu.HBM((8, width), f32)],
        compiler_params=params(LIMIT),
        cost_estimate=pl.CostEstimate(
            flops=4 * TILE * width * width, bytes_accessed=12 * MIB, transcendentals=0
        ),
        name="middle",
    )(info, *half_a, *half_b, gain, w_all, *earlier)


def out_weights_kernel(info, *refs):
    parts_a, parts_b, (g, kept, sent) = refs[0:4], refs[4:8], refs[8:]
    for n in range(2):
        for out, j in ((kept, 2 * n), (sent, 2 * n + 1)):
            heads = jnp.concatenate([parts_a[j][...], parts_b[j][...]])
            out[n] = dot_tn(heads, g[...]).astype(bf16)


def out_weights(info, me_at, parts_a, parts_b, g):
    width = g.shape[1]

    def owner(i, info):
        return info[me_at]

    return pl.pallas_call(
        out_weights_kernel,
        grid_spec=pltpu.PrefetchScalarGridSpec(
            num_scalar_prefetch=1,
            grid=(1,),
            in_specs=[head_block(at, owner) for _, at in parts_a + parts_b]
            + [whole(g.shape)],
            out_specs=[whole((2, WIDTH, width))] * 2,
        ),
        out_shape=[pltpu.HBM((2, WIDTH, width), bf16)] * 2,
        compiler_params=params(LIMIT),
        cost_estimate=pl.CostEstimate(
            flops=4 * TILE * width * width, bytes_accessed=6 * MIB, transcendentals=0
        ),
        name="out_weights",
    )(info, *(part for part, _ in parts_a + parts_b), g)


def attend_back_kernel(
    info, k_aug, v_aug, k_t, q_aug_t, q, v_t, o_t, lse, pad, do_0, do_1, do_2, do_3, pos, table,
    *refs, part, me_at, first,
):
    if first:
        dk_in = dv_in = None
    else:
        dk_in, dv_in, *refs = refs
    dq_out, dk, dv, q_side, do_side, q_lanes, do_lanes, dq_t = refs
    i = pl.program_id(0)
    tile = 2 * jnp.bitwise_xor(info[me_at], i) + part

    @pl.when(i == 0)
    def _():
        if first:
            dk[...] = jnp.zeros_like(dk)
            dv[...] = jnp.zeros_like(dv)
        else:
            dk[...] = dk_in[...]
            dv[...] = dv_in[...]

    here = pl.ds(pl.multiple_of(tile * TILE, TILE), TILE)
    do_here = jnp.where(
        i == 0, do_0[...], jnp.where(i == 1, do_1[...], jnp.where(i == 2, do_2[...], do_3[...]))
    )
    q_here = q[...]
    do_t = do_here.astype(f32).T
    k_here = k_t[:, here].astype(f32)
    padded = jnp.where(pad[...] != 0, 1.0, 0.0)
    row = lax.broadcasted_iota(jnp.int32, (AUG - HEAD_DIM, TILE), 0)
    lane = lax.broadcasted_iota(jnp.int32, (TILE, WIDTH), 1) // HEAD_DIM
    dk_parts, dv_parts = [], []
    for h in range(HEADS):
        feat = slice(h * HEAD_DIM, (h + 1) * HEAD_DIM)
        at = h * AUG
        q_h = q_aug_t[at : at + HEAD_DIM, :]
        do_h = do_t[feat, :]
        delta = jnp.sum(do_h * o_t[feat, :].astype(f32), axis=0, keepdims=True)
        lse_h = lse[h : h + 1, :]
        one, two, three = three_parts(-lse_h)
        extra = q_aug_t[at + HEAD_DIM : at + AUG, :].astype(f32)
        extra = jnp.where(row == 4, one, jnp.where(row == 5, two, jnp.where(row == 6, three, extra)))
        q_side[at : at + HEAD_DIM, :] = q_h
        q_side[at + HEAD_DIM : at + AUG, :] = extra.astype(bf16)
        one, two, three = three_parts(-delta)
        extra = jnp.where(row == 0, one, jnp.where(row == 1, two, jnp.where(row == 2, three, 0.0)))
        do_side[at : at + HEAD_DIM, :] = do_h.astype(bf16)
        do_side[at + HEAD_DIM : at + AUG, :] = extra.astype(bf16)
        q_lanes[h] = jnp.where(lane == h, q_here, jnp.zeros_like(q_here))
        do_lanes[h] = jnp.where(lane == h, do_here, jnp.zeros_like(do_here))
        q_h = q_h.astype(f32)
        k_h = k_here[feat, :]
        p_own = padded * jnp.exp(jnp.sum(q_h * k_h, axis=0, keepdims=True) - lse_h)
        dp_own = jnp.sum(do_h * v_t[feat, :].astype(f32), axis=0, keepdims=True)
        ds_own = p_own * (dp_own - delta)
        dq_t[feat, :] = ds_own * k_h
        dk_parts.append(ds_own * q_h)
        dv_parts.append(p_own * do_h)
    dk[here, :] += jnp.concatenate(dk_parts, axis=0).T
    dv[here, :] += jnp.concatenate(dv_parts, axis=0).T

    begin, tiles = clip_range(info, tile, k_aug.shape[0])

    def step(j, _):
        keys = key_tiles(begin, j, 1)
        probs, grads = [], []
        for h in range(HEADS):
            wide = slice(h * AUG, (h + 1) * AUG)
            prob = jnp.exp(dot_nn(k_aug[keys, wide], q_side[wide, :]))
            grad = prob * dot_nn(v_aug[keys, wide], do_side[wide, :])
            probs.append(prob.astype(bf16))
            grads.append(grad.astype(bf16))
        deep = (HEADS * TILE, WIDTH)
        dv[keys, :] += dot_nn(jnp.concatenate(probs, axis=1), do_lanes[...].reshape(deep))
        dk[keys, :] += dot_nn(jnp.concatenate(grads, axis=1), q_lanes[...].reshape(deep))
        for h in range(HEADS):
            feat = slice(h * HEAD_DIM, (h + 1) * HEAD_DIM)
            dq_t[feat, :] += dot_nn(k_t[feat, keys], grads[h])
        return 0

    lax.fori_loop(0, tiles, step, 0)
    dq = dq_t[...].T * (1.0 / math.sqrt(HEAD_DIM))
    cos, low, high = rope_factors(pos, table)
    dq_out[...] = (dq * cos - turned(dq, low, high)).astype(bf16)


def attend_back(
    part, info, me_at, k_aug, v_aug, k_t, q_aug_t, q, v_t, o_t, lse, padding, do, positions, table,
    dk, dv, earlier,
):
    length = k_aug.shape[0]
    half = length // 2

    def owner(i, info):
        return jnp.bitwise_xor(info[me_at], i)

    def rows(columns):
        return pl.BlockSpec((TILE, columns), lambda i, info: (2 * owner(i, info) + part, 0))

    def columns(count):
        return pl.BlockSpec((count, TILE), lambda i, info: (0, 2 * owner(i, info) + part))

    def packed(count):
        return pl.BlockSpec((count, TILE), lambda i, info: (0, owner(i, info)))

    out = jax.ShapeDtypeStruct
    before = () if dk is None else (dk, dv)
    return pl.pallas_call(
        in_order(
            functools.partial(attend_back_kernel, part=part, me_at=me_at, first=dk is None),
            16 + len(before), len(earlier),
        ),
        grid_spec=pltpu.PrefetchScalarGridSpec(
            num_scalar_prefetch=1,
            grid=(half // TILE,),
            in_specs=[
                whole(k_aug.shape), whole(v_aug.shape), whole(k_t.shape), columns(HEADS * AUG),
                rows(WIDTH), columns(WIDTH), packed(WIDTH), packed(8), columns(1),
            ]
            + [pl.BlockSpec((TILE, WIDTH), lambda i, info: (part, 0))] * 4
            + [
                pl.BlockSpec(
                    (3, 1, TILE), lambda i, info: (0, 0, 2 * owner(i, info) + part)
                ),
                whole(table.shape),
            ]
            + [whole((length, WIDTH))] * len(before)
            + unread(earlier),
            out_specs=[
                pl.BlockSpec((TILE, WIDTH), lambda i, info: (owner(i, info), 0)),
                whole((length, WIDTH)), whole((length, WIDTH)),
            ],
            scratch_shapes=[
                pltpu.VMEM((HEADS * AUG, TILE), bf16), pltpu.VMEM((HEADS * AUG, TILE), bf16),
                pltpu.VMEM((HEADS, TILE, WIDTH), bf16), pltpu.VMEM((HEADS, TILE, WIDTH), bf16),
                pltpu.VMEM((WIDTH, TILE), f32),
            ],
        ),
        out_shape=[out((half, WIDTH), bf16), out((length, WIDTH), f32), out((length, WIDTH), f32)],
        compiler_params=params(LIMIT),
        cost_estimate=pl.CostEstimate(
            flops=72 * half * length * WIDTH, bytes_accessed=16 * MIB, transcendentals=0
        ),
        name="attend_back",
    )(
        info, k_aug, v_aug, k_t, q_aug_t, q, v_t, o_t, lse, padding, *do, positions, table, *before,
        *earlier,
    )


def pieces(begin, count, period):
    at, end, cuts = begin, begin + count, []
    while at < end:
        length = min(end - at, period - at % period)
        cuts.append((at, length))
        at += length
    return cuts


def stacked_pairs(rows, count):
    row = lax.broadcasted_iota(jnp.int32, (count, WIDTH), 0)
    out = jnp.zeros((count, WIDTH), f32)
    for m, value in enumerate(rows):
        one, two, _ = three_parts(value)
        out = jnp.where(row == 2 * m, one, jnp.where(row == 2 * m + 1, two, out))
    return out.astype(bf16)


def late_extra(width, blocks):
    vectors = -(-(3 + 7 * width // WIDTH) // blocks)
    return vectors, -(-vectors // 8) * 16


def project_back_kernel(
    info, tok, gain, shift, dq_a, dq_b, dk, dv, pos, table, w, out_kept, out_other, out_there, early,
    dh1, dh1_sent, sums, acc, grad_b, small, w_wide,
):
    i = pl.program_id(0)

    @pl.when(i == 0)
    def _():
        acc[...] = jnp.zeros_like(acc)
        grad_b[...] = jnp.zeros_like(grad_b)
        small[...] = jnp.zeros_like(small)
        for c in range(3):
            w_wide[:, c * WIDTH : (c + 1) * WIDTH] = w[c]

    dk_here = dk[...]
    cos, low, high = rope_factors(pos, table)
    dk_low = (dk_here * cos - turned(dk_here, low, high)).astype(bf16)
    dq = jnp.concatenate([dq_a[...], dq_b[...]])
    parts = jnp.concatenate([dq, dk_low, dv[...].astype(bf16)], axis=1)
    grad = dot_nt(parts, w_wide[...])
    hat, _ = normalized(tok[...].astype(f32))
    normed = (hat * gain[...] + shift[...]).astype(bf16)
    acc[...] += dot_tn(normed, parts)
    grad_b[0:1, :] += jnp.sum(parts.astype(f32), axis=0, keepdims=True)
    small[0:1, :] += jnp.sum(grad * hat, axis=0, keepdims=True)
    small[1:2, :] += jnp.sum(grad, axis=0, keepdims=True)
    low_grad = grad.astype(bf16)
    dh1[0] = low_grad
    dh1_sent[0] = low_grad

    @pl.when(i == pl.num_programs(0) - 1)
    def _():
        width = normed.shape[1]
        blocks = sums.shape[0]

        def cut(value, count):
            return [value[:, r * WIDTH : (r + 1) * WIDTH] for r in range(count)]

        rows = cut(grad_b[0:1, :], 3) + cut(early[4:5, :], width // WIDTH)
        for ref, count in ((small, 2), (early, 4)):
            for v in range(count):
                rows += cut(ref[v : v + 1, :], width // WIDTH)
        for n in range(blocks):
            for to, rows_here, c, begin in late_places(n, blocks, width):
                here = (slice(begin, begin + rows_here), slice(c * WIDTH, (c + 1) * WIDTH))
                sums[n, to : to + rows_here, :] = acc[here].astype(bf16)
            for to, rows_here, c, begin in late_places(n, blocks, width, True):
                here = (slice(begin, begin + rows_here), slice(c * WIDTH, (c + 1) * WIDTH))
                sums[n, to : to + rows_here, :] = (
                    out_kept[here].astype(f32)
                    + out_other[here].astype(f32)
                    + out_there[here].astype(f32)
                ).astype(bf16)
            extra_at = 4 * width // blocks
            sums[n, extra_at:, :] = stacked_pairs(rows[n::blocks], sums.shape[1] - extra_at)


def late_places(n, blocks, width, out=False):
    deep, period = (width // blocks, WIDTH) if out else (3 * width // blocks, width)
    first = 3 * width // blocks if out else 0
    return [
        (first + at - n * deep, length, at // period, at % period)
        for at, length in pieces(n * deep, deep, period)
    ]


def project_back(
    info, me_at, tokens, gain, shift, dq_a, dq_b, dk, dv, positions, table, w, kept, other, there,
    early, blocks, earlier,
):
    length, width = tokens.shape
    share = 2 * TILE

    def owner(i, info):
        return jnp.bitwise_xor(info[me_at], relative(i))

    def rows(count, columns):
        return pl.BlockSpec((count, columns), lambda i, info: (owner(i, info), 0))

    first = pl.BlockSpec((None, TILE, width), lambda i, info: (0, 0, 0))
    out = jax.ShapeDtypeStruct
    sums = (blocks, 4 * width // blocks + late_extra(width, blocks)[1], WIDTH)
    return pl.pallas_call(
        in_order(project_back_kernel, 15, len(earlier)),
        grid_spec=pltpu.PrefetchScalarGridSpec(
            num_scalar_prefetch=1,
            grid=(length // share,),
            in_specs=[
                rows(share, width), whole((1, width)), whole((1, width)), rows(TILE, WIDTH),
                rows(TILE, WIDTH), rows(share, WIDTH), rows(share, WIDTH),
                pl.BlockSpec((3, 1, share), lambda i, info: (0, 0, owner(i, info))),
                whole(table.shape), whole(w.shape), first, first, whole((TILE, width)),
                whole(early.shape),
            ]
            + unread(earlier),
            out_specs=[
                pl.BlockSpec((1, share, width), lambda i, info: (i, 0, 0)),
                pl.BlockSpec((1, share, width), lambda i, info: (jnp.maximum(i - 2, 0), 0, 0)),
                whole(sums),
            ],
            scratch_shapes=[
                pltpu.VMEM((width, 3 * WIDTH), f32), pltpu.VMEM((8, 3 * WIDTH), f32),
                pltpu.VMEM((8, width), f32),
                pltpu.VMEM((width, 3 * WIDTH), bf16),
            ],
        ),
        out_shape=[
            pltpu.HBM((4, share, width), bf16), pltpu.HBM((2, share, width), bf16),
            pltpu.HBM(sums, bf16),
        ],
        compiler_params=params(LIMIT),
        cost_estimate=pl.CostEstimate(
            flops=24 * length * width * WIDTH, bytes_accessed=20 * MIB, transcendentals=0
        ),
        name="project_back",
    )(
        info, tokens, gain, shift, dq_a, dq_b, dk, dv, positions, table, w, kept, other, there, early,
        *earlier,
    )


def vectors_kernel(extra, grad_b, grad_up, vectors):
    blocks = extra.shape[0]
    width = vectors.shape[1]
    vectors[...] = jnp.zeros_like(vectors)
    for v in range(3 + 7 * width // WIDTH):
        n, m = v % blocks, v // blocks
        pair = extra[n].astype(f32)
        row = pair[2 * m : 2 * m + 1, :] + pair[2 * m + 1 : 2 * m + 2, :]
        to, at = divmod((v - 3) * WIDTH, width)
        if v < 3:
            grad_b[v : v + 1, :] = row
        elif to == 0:
            grad_up[:, at : at + WIDTH] = row
        else:
            vectors[to - 1 : to, at : at + WIDTH] = row


def unpack_vectors(sums, width, earlier):
    blocks = sums.shape[0]
    at, rows = 4 * width // blocks, late_extra(width, blocks)[1]
    out = jax.ShapeDtypeStruct
    return pl.pallas_call(
        in_order(vectors_kernel, 1, len(earlier)),
        grid=(1,),
        in_specs=[pl.BlockSpec((blocks, rows, WIDTH), lambda i: (0, at // rows, 0))]
        + unread(earlier),
        out_specs=[whole((3, WIDTH)), whole((1, width)), whole((8, width))],
        out_shape=[out((3, WIDTH), f32), out((1, width), f32), out((8, width), f32)],
        compiler_params=params(LIMIT),
        name="unpack_vectors",
    )(sums, *earlier)


def unpack_kernel(sums, grad_qkv, grad_out):
    blocks = sums.shape[0]
    width = grad_out.shape[1]
    for n in range(blocks):
        for to, rows, c, begin in late_places(n, blocks, width):
            grad_qkv[c, begin : begin + rows, :] = sums[n, to : to + rows, :].astype(f32)
        for to, rows, c, begin in late_places(n, blocks, width, True):
            grad_out[begin : begin + rows, c * WIDTH : (c + 1) * WIDTH] = sums[
                n, to : to + rows, :
            ].astype(f32)


def unpack(sums, width, earlier):
    out = jax.ShapeDtypeStruct
    return pl.pallas_call(
        in_order(unpack_kernel, 1, len(earlier)),
        in_specs=[pl.BlockSpec(memory_space=pltpu.VMEM)] + unread(earlier),
        out_specs=[pl.BlockSpec(memory_space=pltpu.VMEM)] * 2,
        out_shape=[out((3, width, WIDTH), f32), out((WIDTH, width), f32)],
        compiler_params=pltpu.CompilerParams(vmem_limit_bytes=LIMIT * MIB),
        name="unpack",
    )(sums, *earlier)


def finish_kernel(info, parts, other, there, tok, gain, dx2, out):
    grad = parts[0].astype(f32) + other[0].astype(f32) + there[...].astype(f32)
    hat, inverse = normalized(tok[...].astype(f32))
    out[...] = dx2[...] + norm_back(hat, inverse, gain[...], grad)


def finish(info, me_at, parts, other, there, tokens, gain, dx2, earlier):
    width = tokens.shape[1]
    share = there.shape[0]
    rows = pl.BlockSpec((TILE, width), lambda i, info: (i, 0))
    return pl.pallas_call(
        in_order(finish_kernel, 7, len(earlier)),
        grid_spec=pltpu.PrefetchScalarGridSpec(
            num_scalar_prefetch=1,
            grid=(share // TILE,),
            in_specs=[
                pl.BlockSpec((1, TILE, width), lambda i, info: (0, i, 0)),
                pl.BlockSpec((1, TILE, width), lambda i, info: (0, i, 0)), rows,
                pl.BlockSpec((TILE, width), lambda i, info: (2 * info[me_at] + i, 0)),
                whole((1, width)), rows,
            ]
            + unread(earlier),
            out_specs=rows,
        ),
        out_shape=jax.ShapeDtypeStruct((share, width), f32),
        compiler_params=params(LIMIT),
        cost_estimate=pl.CostEstimate(
            flops=30 * share * width, bytes_accessed=10 * MIB, transcendentals=0
        ),
        name="finish",
    )(info, parts, other, there, tokens, gain, dx2, *earlier)


def total_of(blocks):
    total = blocks[0].astype(f32)
    for n in range(1, blocks.shape[0]):
        total += blocks[n].astype(f32)
    return total.astype(bf16)


def sums_kernel(blocks_a, blocks_b, out):
    rows = blocks_a.shape[1]
    out[:rows, :] = total_of(blocks_a)
    out[rows:, :] = total_of(blocks_b)


def two_sums(blocks_a, blocks_b, earlier):
    _, rows, width = blocks_a.shape
    return pl.pallas_call(
        in_order(sums_kernel, 2, len(earlier)),
        grid=(1,),
        in_specs=[whole(blocks_a.shape), whole(blocks_b.shape)] + unread(earlier),
        out_specs=whole((2 * rows, width)),
        out_shape=pltpu.HBM((2 * rows, width), bf16),
        compiler_params=params(LIMIT),
        name="two_sums",
    )(blocks_a, blocks_b, *earlier)


def sum_kernel(blocks, out):
    out[...] = total_of(blocks)


def summed(blocks, steps, earlier):
    count, rows, width = blocks.shape
    tile = rows // steps
    return pl.pallas_call(
        in_order(sum_kernel, 1, len(earlier)),
        grid=(steps,),
        in_specs=[pl.BlockSpec((count, tile, width), lambda i: (0, i, 0))] + unread(earlier),
        out_specs=pl.BlockSpec((tile, width), lambda i: (i, 0)),
        out_shape=pltpu.HBM((rows, width), bf16),
        compiler_params=params(LIMIT),
        name="summed",
    )(blocks, *earlier)


def swap(array, axis, bit=1):
    size = lax.axis_size(axis)
    if size == 1:
        return jnp.zeros_like(array)
    return lax.ppermute(array, axis, [(i, i ^ bit) for i in range(size)])


def swap_both(array):
    return lax.ppermute(array, MP, [(i, i ^ 3) for i in range(4)])


def scattered(rows, axes):
    group = lax.axis_size(axes)
    length, width = rows.shape
    return lax.all_to_all(
        rows.reshape(group, length // group, width), axes, 0, 0, tiled=True
    )


def both_sums(total):
    if lax.axis_size("zl") == 1:
        return total
    return (total.astype(f32) + swap(total, "zl").astype(f32)).astype(bf16)


def local(
    tokens, cotangent, segments, padding, positions, ln1_gain, ln1_bias, w_qkv, b_qkv, w_out, b_out,
    ln2_gain, ln2_bias, w_up, b_up, w_down, b_down,
):
    width, hidden = w_up.shape
    w_all = lax.all_gather(w_out, MP)
    gain_one, shift_one = ln1_gain[None], ln1_bias[None]
    gain_two, shift_two = ln2_gain[None], ln2_bias[None]
    ends = jnp.sum((segments <= jnp.arange(2)[:, None]).astype(jnp.int32), axis=1)
    info = jnp.concatenate([ends, lax.axis_index(MP)[None].astype(jnp.int32)])
    me_at = 2
    table = jnp.asarray(rope_constants())
    k_aug, v_aug, q_aug_t, q, k_t, v_t = project(
        tokens, w_qkv, b_qkv, gain_one, shift_one, positions, segments, padding, table
    )

    def exchanged(own, to_c, to_zh, to_both):
        return own, swap(to_c, "c"), swap(to_zh, "zh"), swap_both(to_both)

    o_0, o_t_0, lse_0 = attend(0, info, k_aug, v_t, q_aug_t, k_t, padding, ())
    o_zh_0, o_c_0 = swap(o_0, "zh"), swap(o_0, "c")
    o_1, o_t_1, lse_1 = attend(1, info, k_aug, v_t, q_aug_t, k_t, padding, (o_0, w_all))
    o_zh_1 = swap(o_1, "zh")
    o_zh_0 = after(o_zh_0, (o_1,))
    o_parts_0 = tuple((part, None) for part in (o_0, o_c_0, o_zh_0, swap(o_zh_0, "c")))

    def mlp_half(part, o_parts, earlier):
        return mlp(
            part, info, me_at, tokens, cotangent, o_parts, w_all, b_out[None], gain_two, shift_two,
            w_up, b_up[None], w_down, earlier,
        )

    x2_0, dy_0, h2_0, act_0, du_0, mlp_0, mlp_sent_0, dh2_0, sent, db_0 = mlp_half(
        0, o_parts_0, (o_1,)
    )
    pair = paired(o_1, o_zh_1, (x2_0,))
    pair_c = swap(pair, "c")
    o_parts_1 = ((pair, 0), (pair_c, 0), (pair, 1), (pair_c, 1))
    other_0 = swap(sent, "c")
    give_0 = to_give(dh2_0, other_0, ())
    there_0 = swap(give_0, "zh")
    x2_1, dy_1, h2_1, act_1, du_1, mlp_1, mlp_sent_1, dh2_1, sent, db_1 = mlp_half(
        1, o_parts_1, (give_0,)
    )
    other_1 = swap(sent, "c")
    grad_down = down_weights((act_0, act_1), cotangent, (there_0,))
    arrived_down = scattered(grad_down, ("y", "x"))
    give_1 = to_give(dh2_1, other_1, (grad_down,))
    there_1 = swap(give_1, "zh")
    grad_up = up_weights((h2_0, h2_1), (du_0, du_1), (give_1,))
    dx2, g, *d_parts, small = middle(
        info, me_at, (dh2_0, other_0, there_0, x2_0, dy_0), (dh2_1, other_1, there_1, x2_1, dy_1),
        gain_two, w_all, (grad_up,),
    )
    do = exchanged(*d_parts)
    arrived_up = scattered(after(grad_up, (g,)), ("y", "x"))
    grad_out, out_sent = out_weights(info, me_at, o_parts_0, o_parts_1, g)
    out_other = swap(out_sent, "c")
    mlp_parts = (mlp_0, mlp_1)
    mlp_others = (swap(mlp_sent_0, "c"), swap(mlp_sent_1, "c"))
    dq_0, dk, dv = attend_back(
        0, info, me_at, k_aug, v_aug, k_t, q_aug_t, q, v_t, o_t_0, lse_0, padding, do, positions,
        table, None, None, (grad_out, g),
    )
    give = to_give(grad_out, out_other, (dq_0,))
    out_there = swap(give, "zh")
    mlp_give = two_to_give(mlp_parts, mlp_others, (give,))
    mlp_there = swap(mlp_give, "zh")
    part_sum = both_sums(two_sums(arrived_up, arrived_down, (mlp_give,)))
    dq_1, dk, dv = attend_back(
        1, info, me_at, k_aug, v_aug, k_t, q_aug_t, q, v_t, o_t_1, lse_1, padding, do, positions,
        table, dk, dv, (give, part_sum),
    )
    grad_mlp = lax.all_gather(part_sum, ("y", "x"), axis=0, tiled=True)
    early = jnp.concatenate([small[0:4], (db_0 + db_1)[0:4]])
    dh1, sent, sums = project_back(
        info, me_at, tokens, gain_one, shift_one, dq_0, dq_1, dk, dv, positions, table, w_qkv,
        grad_out, out_other, out_there, early, lax.axis_size(("y", "x")), (mlp_there,),
    )
    other = swap(sent, "c")
    back = swap(to_give(dh1, other, (sums,)), "zh")
    arrived = scattered(sums.reshape(-1, WIDTH), ("y", "x"))
    total = summed(arrived, 1, (back,))
    block = both_sums(total)
    late = lax.all_gather(block, ("y", "x"))
    grad_inputs = finish(info, me_at, dh1, other, back, tokens, gain_one, dx2, (block,))
    mixed = mixed_rows(
        (x2_0, x2_1), mlp_parts, mlp_others, mlp_there, b_down[None], (block,)
    )
    count = lax.axis_size(("y", "x"))
    grad_mlp = grad_mlp.reshape(count, 2, width // count, hidden)
    grad_up = grad_mlp[:, 0].astype(f32).reshape(width, hidden)
    grad_down = grad_mlp[:, 1].astype(f32).reshape(hidden, width)
    grad_b, grad_b_up, vectors = unpack_vectors(late, width, (grad_inputs, mixed, grad_up, grad_down))
    by_c, by_zh, by_both = swap(vectors, "c"), swap(vectors, "zh"), swap_both(vectors)
    grad_qkv, grad_w_out = unpack(late, width, (vectors,))
    group = (vectors + by_c) + (by_zh + by_both)
    return (
        mixed, grad_inputs, group[0], group[1], grad_qkv, grad_b, grad_w_out, group[4],
        group[2], group[3], grad_up, grad_b_up[0], grad_down, group[5],
    )


def solution(mesh):
    packs = mesh.shape["dp"]
    if packs == 32:
        shape = (2, 4, 4, 2, 2)
    else:
        shape = (1, packs, 1, 2, 2)
    split = Mesh(mesh.devices.reshape(shape), EVERY)
    in_specs = (
        P(DP, None), P(DP, None), P(DP, None), P(DP, None), P(None, DP, None), P(), P(),
        P(None, None, MP), P(None, MP), P(MP, None), P(), P(), P(), P(None, MP), P(MP),
        P(MP, None), P(),
    )
    out_specs = (
        P(EVERY, None), P(EVERY, None), P(), P(), P(None, None, MP), P(None, MP), P(MP, None), P(),
        P(), P(), P(None, MP), P(MP), P(MP, None), P(),
    )
    return jax.shard_map(local, mesh=split, in_specs=in_specs, out_specs=out_specs, check_vma=False)
```

```python
import functools
import math

import jax
import jax.numpy as jnp
import ml_dtypes
import numpy as np
from jax import lax
from jax.experimental import pallas as pl
from jax.experimental.pallas import tpu as pltpu
from jax.sharding import Mesh
from jax.sharding import PartitionSpec as P

HEAD_DIM = 64
HEADS = 4
WIDTH = HEADS * HEAD_DIM
AUG = 128
TILE = 256
ROWS = 2 * TILE
PLACES = 64
LIMIT = 64
MIB = 1 << 20
DP = ("zl", "y", "x")
MP = ("zh", "c")
EVERY = ("zl", "y", "x", "zh", "c")

epsilon = 1e-06
NEG = -1e30
bf16 = jnp.bfloat16
f32 = jnp.float32


def dot_nn(a, b):
    return lax.dot_general(a, b, (((1,), (0,)), ((), ())), preferred_element_type=f32)


def dot_nt(a, b):
    return lax.dot_general(a, b, (((1,), (1,)), ((), ())), preferred_element_type=f32)


def dot_tn(a, b):
    return lax.dot_general(a, b, (((0,), (0,)), ((), ())), preferred_element_type=f32)


def normalized(values):
    center = jnp.mean(values, axis=-1, keepdims=True)
    shifted = values - center
    spread = jnp.mean(shifted * shifted, axis=-1, keepdims=True)
    inverse = lax.rsqrt(spread + epsilon)
    return shifted * inverse, inverse


def norm_back(hat, inverse, gain, grad):
    scaled = grad * gain
    return inverse * (
        scaled
        - jnp.mean(scaled, axis=-1, keepdims=True)
        - hat * jnp.mean(scaled * hat, axis=-1, keepdims=True)
    )


def turned(x, low, high):
    width = x.shape[1]
    pair = HEAD_DIM // 6
    return pltpu.roll(x, width - pair, 1) * low + pltpu.roll(x, pair, 1) * high


def three_parts(x):
    first = x.astype(bf16).astype(f32)
    rest = x - first
    second = rest.astype(bf16).astype(f32)
    return first, second, rest - second


def params(limit, axes=1):
    return pltpu.CompilerParams(
        dimension_semantics=("arbitrary",) * axes, vmem_limit_bytes=limit * MIB
    )


def in_order(kernel, inputs, earlier):
    def run(*refs):
        kernel(*refs[:inputs], *refs[inputs + earlier :])

    return run


def unread(arrays):
    return [pl.BlockSpec(memory_space=pl.ANY)] * len(arrays)


def whole(shape):
    return pl.BlockSpec(shape, lambda *_: (0,) * len(shape))


def clip_range(info, tile, length):
    half = TILE // 2
    first, second = info[0], info[1]
    at = tile * TILE
    begin = jnp.where(second <= at, second, jnp.where(first <= at, first, 0))
    end = jnp.where(
        first >= at + TILE, first, jnp.where(second >= at + TILE, second, length)
    )
    end = (end + half - 1) // half
    count = (end - begin // half + 1) // 2
    return jnp.maximum(end - 2 * count, 0), count


def key_tiles(begin, at, count):
    return pl.ds(pl.multiple_of(begin * (TILE // 2) + at * TILE, TILE // 2), count * TILE)


def rope_constants():
    pair = HEAD_DIM // 6
    feature = np.arange(WIDTH) % HEAD_DIM
    section, place = feature // (2 * pair), feature % (2 * pair)
    frequency = np.exp(-math.log(10000.0) * (place % pair) / pair)
    table = np.zeros((PLACES, 3, WIDTH))
    for s in range(3):
        for value in range(16):
            angle = value * frequency
            turns = section == s
            table[s * 16 + value, 0] = np.where(turns, np.cos(angle), 0.0)
            table[s * 16 + value, 1] = np.where(turns & (place < pair), -np.sin(angle), 0.0)
            table[s * 16 + value, 2] = np.where(turns & (place >= pair), np.sin(angle), 0.0)
    table[48, 0] = section == 3
    rest = table.reshape(PLACES, 3 * WIDTH).astype(np.float32)
    parts = []
    for _ in range(3):
        part = rest.astype(ml_dtypes.bfloat16)
        parts.append(part)
        rest = rest - part.astype(np.float32)
    return np.concatenate(parts)


def rope_factors(positions, table):
    row = lax.broadcasted_iota(jnp.int32, (PLACES, positions.shape[-1]), 0)
    where = jnp.where(
        row < 16, positions[0], jnp.where(row < 32, positions[1], positions[2])
    )
    hit = ((where == row % 16) & (row < 48)) | (row == 48)
    hit = jnp.where(hit, 1.0, 0.0)
    hits = jnp.concatenate([hit, hit, hit]).astype(bf16)
    factors = dot_tn(hits, table[...])
    return factors[:, :WIDTH], factors[:, WIDTH : 2 * WIDTH], factors[:, 2 * WIDTH :]


def qkv_kernel(
    tok, w, b, gain, shift, pos, seg, pad, table, k_aug, v_aug, q_aug_t, q_out, k_t, v_t, w_wide
):
    @pl.when(pl.program_id(0) == 0)
    def _():
        for c in range(3):
            w_wide[:, c * WIDTH : (c + 1) * WIDTH] = w[c]

    hat, _ = normalized(tok[...].astype(f32))
    normed = (hat * gain[...] + shift[...]).astype(bf16)
    cos, low, high = rope_factors(pos, table)
    all_three = dot_nn(normed, w_wide[...])
    q = all_three[:, :WIDTH] + b[0:1, :]
    k = all_three[:, WIDTH : 2 * WIDTH] + b[1:2, :]
    v = all_three[:, 2 * WIDTH :] + b[2:3, :]
    q = (q * cos + turned(q, low, high)) * (1.0 / math.sqrt(HEAD_DIM))
    k = k * cos + turned(k, low, high)
    q_out[...] = q.astype(bf16)
    q_t = q.T.astype(bf16)
    k_t[...] = k.T.astype(bf16)
    v_t[...] = v.T.astype(bf16)
    row = lax.broadcasted_iota(jnp.int32, (HEAD_DIM, ROWS), 0)
    clip = seg[...]
    same = (row >= 1) & (row < 4) & (clip == row - 1)
    mask = jnp.where((row >= 1) & (row < 4) & (clip != row - 1), NEG, 0.0)
    mask = jnp.where(row == 0, jnp.where(pad[...] != 0, NEG, 0.0), mask)
    k_extra = jnp.where((row >= 4) & (row < 7), 1.0, mask)
    q_extra = jnp.where(same | (row == 0), 1.0, 0.0).astype(bf16)
    k_side = jnp.concatenate([jnp.zeros((HEAD_DIM, ROWS), f32), k_extra]).T
    lane = lax.broadcasted_iota(jnp.int32, (ROWS, AUG), 1)
    ones = jnp.where((lane >= HEAD_DIM) & (lane < HEAD_DIM + 3), 1.0, 0.0)
    for h in range(HEADS):
        pair = slice(h // 2 * AUG, h // 2 * AUG + AUG)
        wide = slice(h * AUG, (h + 1) * AUG)
        k_pair, v_pair = k[:, pair], v[:, pair]
        if h % 2:
            k_pair, v_pair = pltpu.roll(k_pair, HEAD_DIM, 1), pltpu.roll(v_pair, HEAD_DIM, 1)
        k_aug[:, wide] = jnp.where(lane < HEAD_DIM, k_pair, k_side).astype(bf16)
        v_aug[:, wide] = jnp.where(lane < HEAD_DIM, v_pair, ones).astype(bf16)
        q_aug_t[h * AUG : h * AUG + HEAD_DIM, :] = q_t[h * HEAD_DIM : (h + 1) * HEAD_DIM, :]
        q_aug_t[h * AUG + HEAD_DIM : (h + 1) * AUG, :] = q_extra


def project(tokens, w, b, gain, shift, positions, segments, padding, table):
    length, width = tokens.shape
    tiles = length // ROWS

    def rows(columns):
        return pl.BlockSpec((ROWS, columns), lambda i: (i, 0))

    def columns(count):
        return pl.BlockSpec((count, ROWS), lambda i: (0, i))

    out = jax.ShapeDtypeStruct
    wide = out((length, HEADS * AUG), bf16)
    flat = out((WIDTH, length), bf16)
    return pl.pallas_call(
        qkv_kernel,
        grid=(tiles,),
        in_specs=[
            rows(width), whole(w.shape), whole(b.shape), whole((1, width)), whole((1, width)),
            pl.BlockSpec((3, 1, ROWS), lambda i: (0, 0, i)), columns(1), columns(1), whole(table.shape),
        ],
        out_specs=[
            rows(HEADS * AUG), rows(HEADS * AUG), columns(HEADS * AUG), rows(WIDTH), columns(WIDTH),
            columns(WIDTH),
        ],
        out_shape=[
            wide, wide, out((HEADS * AUG, length), bf16), out((length, WIDTH), bf16), flat, flat,
        ],
        scratch_shapes=[pltpu.VMEM((width, 3 * WIDTH), bf16)],
        compiler_params=params(LIMIT),
        cost_estimate=pl.CostEstimate(
            flops=6 * length * width * WIDTH, bytes_accessed=20 * MIB, transcendentals=0
        ),
        name="project",
    )(tokens, w, b, gain, shift, positions, segments, padding, table)


def attend_kernel(info, k_aug, v_t, q_aug_t, k_t, pad, o, o_t, lse, top, total, acc, *, part):
    tile = 2 * pl.program_id(0) + part
    padded = pad[...] != 0
    for h in range(HEADS):
        q_h = q_aug_t[h * AUG : h * AUG + HEAD_DIM, :].astype(f32)
        k_h = k_t[h * HEAD_DIM : (h + 1) * HEAD_DIM, :].astype(f32)
        own = jnp.sum(q_h * k_h, axis=0, keepdims=True)
        top[h : h + 1, :] = jnp.where(padded, own, -3e38)
        total[h : h + 1, :] = jnp.where(padded, 1.0, 0.0)
    here = pl.ds(pl.multiple_of(tile * TILE, TILE), TILE)
    acc[...] = jnp.where(padded, v_t[:, here].astype(f32), 0.0)
    feats = [slice(h * HEAD_DIM, (h + 1) * HEAD_DIM) for h in range(HEADS)]
    wides = [slice(h * AUG, (h + 1) * AUG) for h in range(HEADS)]

    begin, tiles = clip_range(info, tile, k_aug.shape[0])

    def step(j, count):
        keys = key_tiles(begin, j, count)
        scores = [dot_nn(k_aug[keys, wide], q_aug_t[wide, :]) for wide in wides]
        probs, fades = [], []
        for h in range(HEADS):
            old = top[h : h + 1, :]
            new = jnp.maximum(old, jnp.max(scores[h], axis=0, keepdims=True))
            prob = jnp.exp(scores[h] - new)
            fade = jnp.exp(old - new)
            top[h : h + 1, :] = new
            total[h : h + 1, :] = total[h : h + 1, :] * fade + jnp.sum(prob, axis=0, keepdims=True)
            probs.append(prob.astype(bf16))
            fades.append(fade)
        for h, feat in enumerate(feats):
            acc[feat, :] = acc[feat, :] * fades[h] + dot_nn(v_t[feat, keys], probs[h])

    pairs = tiles // 2

    def two(n, _):
        step(2 * n, 2)
        return 0

    lax.fori_loop(0, pairs, two, 0)

    @pl.when(2 * pairs < tiles)
    def _():
        step(tiles - 1, 1)

    for h, feat in enumerate(feats):
        acc[feat, :] = acc[feat, :] / total[h : h + 1, :]
    lse[...] = jnp.zeros_like(lse)
    lse[0:HEADS, :] = top[0:HEADS, :] + jnp.log(total[0:HEADS, :])
    turned_o = acc[...]
    o_t[...] = turned_o.astype(bf16)
    o[...] = turned_o.T.astype(bf16)


def attend(part, info, k_aug, v_t, q_aug_t, k_t, padding, earlier):
    length = k_aug.shape[0]
    half = length // 2

    def columns(count):
        return pl.BlockSpec((count, TILE), lambda i, *_: (0, 2 * i + part))

    def packed(count):
        return pl.BlockSpec((count, TILE), lambda i, *_: (0, i))

    out = jax.ShapeDtypeStruct
    return pl.pallas_call(
        in_order(functools.partial(attend_kernel, part=part), 6, len(earlier)),
        grid_spec=pltpu.PrefetchScalarGridSpec(
            num_scalar_prefetch=1,
            grid=(half // TILE,),
            in_specs=[
                whole(k_aug.shape), whole(v_t.shape), columns(HEADS * AUG), columns(WIDTH),
                columns(1),
            ]
            + unread(earlier),
            out_specs=[
                pl.BlockSpec((TILE, WIDTH), lambda i, *_: (i, 0)), packed(WIDTH), packed(8),
            ],
            scratch_shapes=[
                pltpu.VMEM((8, TILE), f32), pltpu.VMEM((8, TILE), f32), pltpu.VMEM((WIDTH, TILE), f32),
            ],
        ),
        out_shape=[out((half, WIDTH), bf16), out((WIDTH, half), bf16), out((8, half), f32)],
        compiler_params=params(LIMIT),
        cost_estimate=pl.CostEstimate(
            flops=24 * half * length * WIDTH, bytes_accessed=6 * MIB, transcendentals=0
        ),
        name="attend",
    )(info, k_aug, v_t, q_aug_t, k_t, padding, *earlier)


def nothing(*refs):
    del refs


def after(value, earlier):
    return pl.pallas_call(
        nothing,
        in_specs=unread((value,) + earlier),
        out_specs=pl.BlockSpec(memory_space=pl.ANY),
        out_shape=jax.ShapeDtypeStruct(value.shape, value.dtype),
        input_output_aliases={0: 0},
        name="after",
    )(value, *earlier)


def pair_kernel(first, second, out):
    out[0] = first[...]
    out[1] = second[...]


def paired(first, second, earlier):
    shape = (2,) + first.shape
    return pl.pallas_call(
        in_order(pair_kernel, 2, len(earlier)),
        in_specs=[pl.BlockSpec(memory_space=pltpu.VMEM)] * 2 + unread(earlier),
        out_specs=pl.BlockSpec(memory_space=pltpu.VMEM),
        out_shape=jax.ShapeDtypeStruct(shape, first.dtype),
        name="paired",
    )(first, second, *earlier)


def head_block(at, owner):
    if at is None:
        return pl.BlockSpec((TILE, WIDTH), lambda i, info: (owner(i, info), 0))
    return pl.BlockSpec((None, TILE, WIDTH), lambda i, info: (at, owner(i, info), 0))


def relative(i):
    return i % 2 * 2 + i // 2


def gelu_parts(u):
    size = jnp.abs(u)
    t = 1.0 / (1.0 + (0.3275911 / math.sqrt(2.0)) * size)
    bell = jnp.exp(-0.5 * (u * u))
    poly = 0.5 * 1.061405429
    for c in (-1.453152027, 1.421413741, -0.284496736, 0.254829592):
        poly = poly * t + 0.5 * c
    tail = poly * t * bell
    below = jnp.where(u >= 0, 1.0 - tail, tail)
    return u * below, below + u * bell * (1.0 / math.sqrt(2.0 * math.pi))


def mlp_kernel(
    info, tok, cot, o_0, o_1, o_2, o_3, w_all, b_out, gain, shift, w_up, b_up, w_down,
    x2, dy, h2, act, du, mlp, mlp_sent, dh2, dh2_sent, db_up, w_out, *, me_at,
):
    i = pl.program_id(0)

    @pl.when(i == 0)
    def _():
        for j in range(4):
            w_out[j * WIDTH : (j + 1) * WIDTH, :] = w_all[jnp.bitwise_xor(info[me_at], j)]
        db_up[...] = jnp.zeros_like(db_up)

    heads = jnp.concatenate([o_0[...], o_1[...], o_2[...], o_3[...]], axis=1)
    mid = tok[...].astype(f32) + b_out[...] + dot_nn(heads, w_out[...])

    @pl.when(i == 0)
    def _():
        x2[...] = mid
        dy[...] = cot[...]

    hat, _ = normalized(mid)
    normed = (hat * gain[...] + shift[...]).astype(bf16)
    h2[...] = normed
    u = dot_nn(normed, w_up[...]) + b_up[...]
    grad_act = dot_nt(cot[...], w_down[...])
    value, slope = gelu_parts(u)
    value = value.astype(bf16)
    grad = (grad_act * slope).astype(bf16)
    act[...] = value
    du[...] = grad
    db_up[0:1, :] += jnp.sum(grad.astype(f32), axis=0, keepdims=True)
    mlp_part = dot_nn(value, w_down[...]).astype(bf16)
    dh2_part = dot_nt(grad, w_up[...]).astype(bf16)
    mlp[0] = mlp_part
    mlp_sent[0] = mlp_part
    dh2[0] = dh2_part
    dh2_sent[0] = dh2_part


def mlp(
    part, info, me_at, tokens, cotangent, o_parts, w_all, b_out, gain, shift, w_up, b_up, w_down,
    earlier,
):
    length, width = tokens.shape
    half = length // 2
    hidden = w_up.shape[1]
    owners = half // TILE

    def owner(i, info):
        return jnp.bitwise_xor(info[me_at], relative(i))

    def rows(columns):
        return pl.BlockSpec((TILE, columns), lambda i, info: (2 * owner(i, info) + part, 0))

    def packed(columns):
        return pl.BlockSpec((TILE, columns), lambda i, info: (owner(i, info), 0))

    ordered = pl.BlockSpec((1, TILE, width), lambda i, info: (i, 0, 0))
    sent = pl.BlockSpec((1, TILE, width), lambda i, info: (jnp.maximum(i - 2, 0), 0, 0))

    out = jax.ShapeDtypeStruct
    return pl.pallas_call(
        in_order(functools.partial(mlp_kernel, me_at=me_at), 14, len(earlier)),
        grid_spec=pltpu.PrefetchScalarGridSpec(
            num_scalar_prefetch=1,
            grid=(owners,),
            in_specs=[rows(width), rows(width)]
            + [head_block(at, owner) for _, at in o_parts]
            + [whole(w_all.shape)]
            + [whole((1, width))] * 3
            + [whole(w_up.shape), whole((1, hidden)), whole(w_down.shape)]
            + unread(earlier),
            out_specs=[
                whole((TILE, width)), whole((TILE, width)), packed(width), packed(hidden),
                packed(hidden), ordered, sent, ordered, sent, whole((8, hidden)),
            ],
            scratch_shapes=[pltpu.VMEM((4 * WIDTH, width), bf16)],
        ),
        out_shape=[
            out((TILE, width), f32), out((TILE, width), bf16), out((half, width), bf16),
            out((half, hidden), bf16), out((half, hidden), bf16),
        ]
        + [out((owners, TILE, width), bf16), out((2, TILE, width), bf16)] * 2
        + [out((8, hidden), f32)],
        compiler_params=params(LIMIT),
        cost_estimate=pl.CostEstimate(
            flops=20 * half * width * hidden, bytes_accessed=20 * MIB, transcendentals=0
        ),
        name="mlp",
    )(
        info, tokens, cotangent, *(part for part, _ in o_parts), w_all, b_out, gain, shift, w_up,
        b_up, w_down, *earlier
    )


def up_weights_kernel(left_a, left_b, right_a, right_b, out):
    left = jnp.concatenate([left_a[...], left_b[...]])
    right = jnp.concatenate([right_a[...], right_b[...]])
    out[...] = dot_tn(left, right).astype(bf16)


def up_weights(h2, du, earlier):
    half, width = h2[0].shape
    hidden = du[0].shape[1]
    return pl.pallas_call(
        in_order(up_weights_kernel, 4, len(earlier)),
        grid=(width // TILE,),
        in_specs=[pl.BlockSpec((half, TILE), lambda i: (0, i))] * 2
        + [whole((half, hidden))] * 2
        + unread(earlier),
        out_specs=pl.BlockSpec((TILE, hidden), lambda i: (i, 0)),
        out_shape=pltpu.HBM((width, hidden), bf16),
        compiler_params=params(LIMIT),
        cost_estimate=pl.CostEstimate(
            flops=8 * half * width * hidden, bytes_accessed=12 * MIB, transcendentals=0
        ),
        name="up_weights",
    )(*h2, *du, *earlier)


def down_weights_kernel(act_a, act_b, cot, out):
    owners = cot.shape[0] // (2 * TILE)
    rows = [cot[n * TILE : (n + 1) * TILE, :] for p in range(2) for n in range(p, 2 * owners, 2)]
    out[...] = dot_tn(
        jnp.concatenate([act_a[...], act_b[...]]), jnp.concatenate(rows)
    ).astype(bf16)


def down_weights(act, cotangent, earlier):
    half, hidden = act[0].shape
    length, width = cotangent.shape
    return pl.pallas_call(
        in_order(down_weights_kernel, 3, len(earlier)),
        grid=(hidden // TILE,),
        in_specs=[pl.BlockSpec((half, TILE), lambda i: (0, i))] * 2
        + [whole((length, width))]
        + unread(earlier),
        out_specs=pl.BlockSpec((TILE, width), lambda i: (i, 0)),
        out_shape=pltpu.HBM((hidden, width), bf16),
        compiler_params=params(LIMIT),
        cost_estimate=pl.CostEstimate(
            flops=8 * half * width * hidden, bytes_accessed=12 * MIB, transcendentals=0
        ),
        name="down_weights",
    )(*act, cotangent, *earlier)


def add_kernel(parts, other, out):
    out[...] = (parts[0].astype(f32) + other[0].astype(f32)).astype(bf16)


def to_give(parts, other, earlier):
    _, rows, width = parts.shape
    tile = min(rows, TILE)
    return pl.pallas_call(
        in_order(add_kernel, 2, len(earlier)),
        grid=(rows // tile,),
        in_specs=[
            pl.BlockSpec((1, tile, width), lambda i: (1, i, 0)),
            pl.BlockSpec((1, tile, width), lambda i: (1, i, 0)),
        ]
        + unread(earlier),
        out_specs=pl.BlockSpec((tile, width), lambda i: (i, 0)),
        out_shape=pltpu.HBM((rows, width), bf16),
        compiler_params=params(LIMIT),
        name="to_give",
    )(parts, other, *earlier)


def two_kernel(parts_a, parts_b, other_a, other_b, out):
    for n, (parts, other) in enumerate(((parts_a, other_a), (parts_b, other_b))):
        out[n] = (parts[0].astype(f32) + other[0].astype(f32)).astype(bf16)


def two_to_give(parts, others, earlier):
    _, rows, width = parts[0].shape
    tile = rows // 2
    return pl.pallas_call(
        in_order(two_kernel, 4, len(earlier)),
        grid=(rows // tile,),
        in_specs=[pl.BlockSpec((1, tile, width), lambda i: (1, i, 0))] * 4 + unread(earlier),
        out_specs=pl.BlockSpec((2, tile, width), lambda i: (0, i, 0)),
        out_shape=pltpu.HBM((2, rows, width), bf16),
        compiler_params=params(LIMIT),
        name="two_to_give",
    )(*parts, *others, *earlier)


def mixed_kernel(x2_a, x2_b, parts_a, parts_b, other_a, other_b, there, shift, out):
    for n, (x2, parts, other) in enumerate(
        ((x2_a, parts_a, other_a), (x2_b, parts_b, other_b))
    ):
        total = parts[0].astype(f32) + other[0].astype(f32) + there[n].astype(f32)
        out[n * TILE : (n + 1) * TILE, :] = (x2[...] + total + shift[...]).astype(bf16)


def mixed_rows(x2, parts, others, there, shift, earlier):
    rows, width = x2[0].shape
    first = pl.BlockSpec((1, rows, width), lambda i: (0, 0, 0))
    return pl.pallas_call(
        in_order(mixed_kernel, 8, len(earlier)),
        grid=(1,),
        in_specs=[whole((rows, width))] * 2
        + [first] * 4
        + [whole((2, rows, width)), whole((1, width))]
        + unread(earlier),
        out_specs=whole((2 * rows, width)),
        out_shape=jax.ShapeDtypeStruct((2 * rows, width), bf16),
        compiler_params=params(LIMIT),
        name="mixed_rows",
    )(*x2, *parts, *others, there, shift, *earlier)


def middle_kernel(info, *refs, me_at):
    halves, (gain, w_all, dx2, g, d_0, d_1, d_2, d_3, small) = (refs[0:5], refs[5:10]), refs[10:]
    small[...] = jnp.zeros_like(small)
    for part, (kept, other, there, x2, dy) in enumerate(halves):
        rows = slice(part * TILE, (part + 1) * TILE)
        grad = kept[0].astype(f32) + other[0].astype(f32) + there[...].astype(f32)
        hat, inverse = normalized(x2[...])
        dy = dy[...].astype(f32)
        full = dy + norm_back(hat, inverse, gain[...], grad)
        dx2[rows, :] = full
        low = full.astype(bf16)
        g[rows, :] = low
        small[0:1, :] += jnp.sum(grad * hat, axis=0, keepdims=True)
        small[1:2, :] += jnp.sum(grad, axis=0, keepdims=True)
        small[2:3, :] += jnp.sum(low.astype(f32), axis=0, keepdims=True)
        small[3:4, :] += jnp.sum(dy, axis=0, keepdims=True)
    low = g[...]
    for j, d_j in enumerate((d_0, d_1, d_2, d_3)):
        d_j[...] = dot_nt(low, w_all[jnp.bitwise_xor(info[me_at], j)]).astype(bf16)


def middle(info, me_at, half_a, half_b, gain, w_all, earlier):
    width = gain.shape[1]
    rows = 2 * TILE
    own = whole((TILE, width))
    first = pl.BlockSpec((1, TILE, width), lambda i, info: (0, 0, 0))
    return pl.pallas_call(
        in_order(functools.partial(middle_kernel, me_at=me_at), 13, len(earlier)),
        grid_spec=pltpu.PrefetchScalarGridSpec(
            num_scalar_prefetch=1,
            grid=(1,),
            in_specs=[first, first, own, own, own] * 2
            + [whole((1, width)), whole(w_all.shape)]
            + unread(earlier),
            out_specs=[whole((rows, width))] * 2
            + [whole((rows, WIDTH))] * 4
            + [whole((8, width))],
        ),
        out_shape=[pltpu.HBM((rows, width), f32), pltpu.HBM((rows, width), bf16)]
        + [pltpu.HBM((rows, WIDTH), bf16)] * 4
        + [pltpu.HBM((8, width), f32)],
        compiler_params=params(LIMIT),
        cost_estimate=pl.CostEstimate(
            flops=4 * TILE * width * width, bytes_accessed=12 * MIB, transcendentals=0
        ),
        name="middle",
    )(info, *half_a, *half_b, gain, w_all, *earlier)


def out_weights_kernel(info, *refs):
    parts_a, parts_b, (g, kept, sent) = refs[0:4], refs[4:8], refs[8:]
    for n in range(2):
        for out, j in ((kept, 2 * n), (sent, 2 * n + 1)):
            heads = jnp.concatenate([parts_a[j][...], parts_b[j][...]])
            out[n] = dot_tn(heads, g[...]).astype(bf16)


def out_weights(info, me_at, parts_a, parts_b, g):
    width = g.shape[1]

    def owner(i, info):
        return info[me_at]

    return pl.pallas_call(
        out_weights_kernel,
        grid_spec=pltpu.PrefetchScalarGridSpec(
            num_scalar_prefetch=1,
            grid=(1,),
            in_specs=[head_block(at, owner) for _, at in parts_a + parts_b]
            + [whole(g.shape)],
            out_specs=[whole((2, WIDTH, width))] * 2,
        ),
        out_shape=[pltpu.HBM((2, WIDTH, width), bf16)] * 2,
        compiler_params=params(LIMIT),
        cost_estimate=pl.CostEstimate(
            flops=4 * TILE * width * width, bytes_accessed=6 * MIB, transcendentals=0
        ),
        name="out_weights",
    )(info, *(part for part, _ in parts_a + parts_b), g)


def attend_back_kernel(
    info, k_aug, v_aug, k_t, q_aug_t, q, v_t, o_t, lse, pad, do_0, do_1, do_2, do_3, pos, table,
    *refs, part, me_at, first,
):
    if first:
        dk_in = dv_in = None
    else:
        dk_in, dv_in, *refs = refs
    dq_out, dk, dv, q_side, do_side, q_lanes, do_lanes, dq_t = refs
    i = pl.program_id(0)
    tile = 2 * jnp.bitwise_xor(info[me_at], i) + part

    @pl.when(i == 0)
    def _():
        if first:
            dk[...] = jnp.zeros_like(dk)
            dv[...] = jnp.zeros_like(dv)
        else:
            dk[...] = dk_in[...]
            dv[...] = dv_in[...]

    here = pl.ds(pl.multiple_of(tile * TILE, TILE), TILE)
    do_here = jnp.where(
        i == 0, do_0[...], jnp.where(i == 1, do_1[...], jnp.where(i == 2, do_2[...], do_3[...]))
    )
    q_here = q[...]
    do_t = do_here.astype(f32).T
    k_here = k_t[:, here].astype(f32)
    padded = jnp.where(pad[...] != 0, 1.0, 0.0)
    row = lax.broadcasted_iota(jnp.int32, (AUG - HEAD_DIM, TILE), 0)
    lane = lax.broadcasted_iota(jnp.int32, (TILE, WIDTH), 1) // HEAD_DIM
    dk_parts, dv_parts = [], []
    for h in range(HEADS):
        feat = slice(h * HEAD_DIM, (h + 1) * HEAD_DIM)
        at = h * AUG
        q_h = q_aug_t[at : at + HEAD_DIM, :]
        do_h = do_t[feat, :]
        delta = jnp.sum(do_h * o_t[feat, :].astype(f32), axis=0, keepdims=True)
        lse_h = lse[h : h + 1, :]
        one, two, three = three_parts(-lse_h)
        extra = q_aug_t[at + HEAD_DIM : at + AUG, :].astype(f32)
        extra = jnp.where(row == 4, one, jnp.where(row == 5, two, jnp.where(row == 6, three, extra)))
        q_side[at : at + HEAD_DIM, :] = q_h
        q_side[at + HEAD_DIM : at + AUG, :] = extra.astype(bf16)
        one, two, three = three_parts(-delta)
        extra = jnp.where(row == 0, one, jnp.where(row == 1, two, jnp.where(row == 2, three, 0.0)))
        do_side[at : at + HEAD_DIM, :] = do_h.astype(bf16)
        do_side[at + HEAD_DIM : at + AUG, :] = extra.astype(bf16)
        q_lanes[h] = jnp.where(lane == h, q_here, jnp.zeros_like(q_here))
        do_lanes[h] = jnp.where(lane == h, do_here, jnp.zeros_like(do_here))
        q_h = q_h.astype(f32)
        k_h = k_here[feat, :]
        p_own = padded * jnp.exp(jnp.sum(q_h * k_h, axis=0, keepdims=True) - lse_h)
        dp_own = jnp.sum(do_h * v_t[feat, :].astype(f32), axis=0, keepdims=True)
        ds_own = p_own * (dp_own - delta)
        dq_t[feat, :] = ds_own * k_h
        dk_parts.append(ds_own * q_h)
        dv_parts.append(p_own * do_h)
    dk[here, :] += jnp.concatenate(dk_parts, axis=0).T
    dv[here, :] += jnp.concatenate(dv_parts, axis=0).T

    begin, tiles = clip_range(info, tile, k_aug.shape[0])

    def step(j, _):
        keys = key_tiles(begin, j, 1)
        probs, grads = [], []
        for h in range(HEADS):
            wide = slice(h * AUG, (h + 1) * AUG)
            prob = jnp.exp(dot_nn(k_aug[keys, wide], q_side[wide, :]))
            grad = prob * dot_nn(v_aug[keys, wide], do_side[wide, :])
            probs.append(prob.astype(bf16))
            grads.append(grad.astype(bf16))
        deep = (HEADS * TILE, WIDTH)
        dv[keys, :] += dot_nn(jnp.concatenate(probs, axis=1), do_lanes[...].reshape(deep))
        dk[keys, :] += dot_nn(jnp.concatenate(grads, axis=1), q_lanes[...].reshape(deep))
        for h in range(HEADS):
            feat = slice(h * HEAD_DIM, (h + 1) * HEAD_DIM)
            dq_t[feat, :] += dot_nn(k_t[feat, keys], grads[h])
        return 0

    lax.fori_loop(0, tiles, step, 0)
    dq = dq_t[...].T * (1.0 / math.sqrt(HEAD_DIM))
    cos, low, high = rope_factors(pos, table)
    dq_out[...] = (dq * cos - turned(dq, low, high)).astype(bf16)


def attend_back(
    part, info, me_at, k_aug, v_aug, k_t, q_aug_t, q, v_t, o_t, lse, padding, do, positions, table,
    dk, dv, earlier,
):
    length = k_aug.shape[0]
    half = length // 2

    def owner(i, info):
        return jnp.bitwise_xor(info[me_at], i)

    def rows(columns):
        return pl.BlockSpec((TILE, columns), lambda i, info: (2 * owner(i, info) + part, 0))

    def columns(count):
        return pl.BlockSpec((count, TILE), lambda i, info: (0, 2 * owner(i, info) + part))

    def packed(count):
        return pl.BlockSpec((count, TILE), lambda i, info: (0, owner(i, info)))

    out = jax.ShapeDtypeStruct
    before = () if dk is None else (dk, dv)
    return pl.pallas_call(
        in_order(
            functools.partial(attend_back_kernel, part=part, me_at=me_at, first=dk is None),
            16 + len(before), len(earlier),
        ),
        grid_spec=pltpu.PrefetchScalarGridSpec(
            num_scalar_prefetch=1,
            grid=(half // TILE,),
            in_specs=[
                whole(k_aug.shape), whole(v_aug.shape), whole(k_t.shape), columns(HEADS * AUG),
                rows(WIDTH), columns(WIDTH), packed(WIDTH), packed(8), columns(1),
            ]
            + [pl.BlockSpec((TILE, WIDTH), lambda i, info: (part, 0))] * 4
            + [
                pl.BlockSpec(
                    (3, 1, TILE), lambda i, info: (0, 0, 2 * owner(i, info) + part)
                ),
                whole(table.shape),
            ]
            + [whole((length, WIDTH))] * len(before)
            + unread(earlier),
            out_specs=[
                pl.BlockSpec((TILE, WIDTH), lambda i, info: (owner(i, info), 0)),
                whole((length, WIDTH)), whole((length, WIDTH)),
            ],
            scratch_shapes=[
                pltpu.VMEM((HEADS * AUG, TILE), bf16), pltpu.VMEM((HEADS * AUG, TILE), bf16),
                pltpu.VMEM((HEADS, TILE, WIDTH), bf16), pltpu.VMEM((HEADS, TILE, WIDTH), bf16),
                pltpu.VMEM((WIDTH, TILE), f32),
            ],
        ),
        out_shape=[out((half, WIDTH), bf16), out((length, WIDTH), f32), out((length, WIDTH), f32)],
        compiler_params=params(LIMIT),
        cost_estimate=pl.CostEstimate(
            flops=72 * half * length * WIDTH, bytes_accessed=16 * MIB, transcendentals=0
        ),
        name="attend_back",
    )(
        info, k_aug, v_aug, k_t, q_aug_t, q, v_t, o_t, lse, padding, *do, positions, table, *before,
        *earlier,
    )


def pieces(begin, count, period):
    at, end, cuts = begin, begin + count, []
    while at < end:
        length = min(end - at, period - at % period)
        cuts.append((at, length))
        at += length
    return cuts


def stacked_pairs(rows, count):
    row = lax.broadcasted_iota(jnp.int32, (count, WIDTH), 0)
    out = jnp.zeros((count, WIDTH), f32)
    for m, value in enumerate(rows):
        one, two, _ = three_parts(value)
        out = jnp.where(row == 2 * m, one, jnp.where(row == 2 * m + 1, two, out))
    return out.astype(bf16)


def late_extra(width, blocks):
    vectors = -(-(3 + 7 * width // WIDTH) // blocks)
    return vectors, -(-vectors // 8) * 16


def project_back_kernel(
    info, tok, gain, shift, dq_a, dq_b, dk, dv, pos, table, w, out_kept, out_other, out_there, early,
    dh1, dh1_sent, sums, acc, grad_b, small, w_wide,
):
    i = pl.program_id(0)

    @pl.when(i == 0)
    def _():
        acc[...] = jnp.zeros_like(acc)
        grad_b[...] = jnp.zeros_like(grad_b)
        small[...] = jnp.zeros_like(small)
        for c in range(3):
            w_wide[:, c * WIDTH : (c + 1) * WIDTH] = w[c]

    dk_here = dk[...]
    cos, low, high = rope_factors(pos, table)
    dk_low = (dk_here * cos - turned(dk_here, low, high)).astype(bf16)
    dq = jnp.concatenate([dq_a[...], dq_b[...]])
    parts = jnp.concatenate([dq, dk_low, dv[...].astype(bf16)], axis=1)
    grad = dot_nt(parts, w_wide[...])
    hat, _ = normalized(tok[...].astype(f32))
    normed = (hat * gain[...] + shift[...]).astype(bf16)
    acc[...] += dot_tn(normed, parts)
    grad_b[0:1, :] += jnp.sum(parts.astype(f32), axis=0, keepdims=True)
    small[0:1, :] += jnp.sum(grad * hat, axis=0, keepdims=True)
    small[1:2, :] += jnp.sum(grad, axis=0, keepdims=True)
    low_grad = grad.astype(bf16)
    dh1[0] = low_grad
    dh1_sent[0] = low_grad

    @pl.when(i == pl.num_programs(0) - 1)
    def _():
        width = normed.shape[1]
        blocks = sums.shape[0]

        def cut(value, count):
            return [value[:, r * WIDTH : (r + 1) * WIDTH] for r in range(count)]

        rows = cut(grad_b[0:1, :], 3) + cut(early[4:5, :], width // WIDTH)
        for ref, count in ((small, 2), (early, 4)):
            for v in range(count):
                rows += cut(ref[v : v + 1, :], width // WIDTH)
        for n in range(blocks):
            for to, rows_here, c, begin in late_places(n, blocks, width):
                here = (slice(begin, begin + rows_here), slice(c * WIDTH, (c + 1) * WIDTH))
                sums[n, to : to + rows_here, :] = acc[here].astype(bf16)
            for to, rows_here, c, begin in late_places(n, blocks, width, True):
                here = (slice(begin, begin + rows_here), slice(c * WIDTH, (c + 1) * WIDTH))
                sums[n, to : to + rows_here, :] = (
                    out_kept[here].astype(f32)
                    + out_other[here].astype(f32)
                    + out_there[here].astype(f32)
                ).astype(bf16)
            extra_at = 4 * width // blocks
            sums[n, extra_at:, :] = stacked_pairs(rows[n::blocks], sums.shape[1] - extra_at)


def late_places(n, blocks, width, out=False):
    deep, period = (width // blocks, WIDTH) if out else (3 * width // blocks, width)
    first = 3 * width // blocks if out else 0
    return [
        (first + at - n * deep, length, at // period, at % period)
        for at, length in pieces(n * deep, deep, period)
    ]


def project_back(
    info, me_at, tokens, gain, shift, dq_a, dq_b, dk, dv, positions, table, w, kept, other, there,
    early, blocks, earlier,
):
    length, width = tokens.shape
    share = 2 * TILE

    def owner(i, info):
        return jnp.bitwise_xor(info[me_at], relative(i))

    def rows(count, columns):
        return pl.BlockSpec((count, columns), lambda i, info: (owner(i, info), 0))

    first = pl.BlockSpec((None, TILE, width), lambda i, info: (0, 0, 0))
    out = jax.ShapeDtypeStruct
    sums = (blocks, 4 * width // blocks + late_extra(width, blocks)[1], WIDTH)
    return pl.pallas_call(
        in_order(project_back_kernel, 15, len(earlier)),
        grid_spec=pltpu.PrefetchScalarGridSpec(
            num_scalar_prefetch=1,
            grid=(length // share,),
            in_specs=[
                rows(share, width), whole((1, width)), whole((1, width)), rows(TILE, WIDTH),
                rows(TILE, WIDTH), rows(share, WIDTH), rows(share, WIDTH),
                pl.BlockSpec((3, 1, share), lambda i, info: (0, 0, owner(i, info))),
                whole(table.shape), whole(w.shape), first, first, whole((TILE, width)),
                whole(early.shape),
            ]
            + unread(earlier),
            out_specs=[
                pl.BlockSpec((1, share, width), lambda i, info: (i, 0, 0)),
                pl.BlockSpec((1, share, width), lambda i, info: (jnp.maximum(i - 2, 0), 0, 0)),
                whole(sums),
            ],
            scratch_shapes=[
                pltpu.VMEM((width, 3 * WIDTH), f32), pltpu.VMEM((8, 3 * WIDTH), f32),
                pltpu.VMEM((8, width), f32),
                pltpu.VMEM((width, 3 * WIDTH), bf16),
            ],
        ),
        out_shape=[
            pltpu.HBM((4, share, width), bf16), pltpu.HBM((2, share, width), bf16),
            pltpu.HBM(sums, bf16),
        ],
        compiler_params=params(LIMIT),
        cost_estimate=pl.CostEstimate(
            flops=24 * length * width * WIDTH, bytes_accessed=20 * MIB, transcendentals=0
        ),
        name="project_back",
    )(
        info, tokens, gain, shift, dq_a, dq_b, dk, dv, positions, table, w, kept, other, there, early,
        *earlier,
    )


def vectors_kernel(extra, grad_b, grad_up, vectors):
    blocks = extra.shape[0]
    width = vectors.shape[1]
    vectors[...] = jnp.zeros_like(vectors)
    for v in range(3 + 7 * width // WIDTH):
        n, m = v % blocks, v // blocks
        pair = extra[n].astype(f32)
        row = pair[2 * m : 2 * m + 1, :] + pair[2 * m + 1 : 2 * m + 2, :]
        to, at = divmod((v - 3) * WIDTH, width)
        if v < 3:
            grad_b[v : v + 1, :] = row
        elif to == 0:
            grad_up[:, at : at + WIDTH] = row
        else:
            vectors[to - 1 : to, at : at + WIDTH] = row


def unpack_vectors(sums, width, earlier):
    blocks = sums.shape[0]
    at, rows = 4 * width // blocks, late_extra(width, blocks)[1]
    out = jax.ShapeDtypeStruct
    return pl.pallas_call(
        in_order(vectors_kernel, 1, len(earlier)),
        grid=(1,),
        in_specs=[pl.BlockSpec((blocks, rows, WIDTH), lambda i: (0, at // rows, 0))]
        + unread(earlier),
        out_specs=[whole((3, WIDTH)), whole((1, width)), whole((8, width))],
        out_shape=[out((3, WIDTH), f32), out((1, width), f32), out((8, width), f32)],
        compiler_params=params(LIMIT),
        name="unpack_vectors",
    )(sums, *earlier)


def unpack_kernel(sums, grad_qkv, grad_out):
    blocks = sums.shape[0]
    width = grad_out.shape[1]
    for n in range(blocks):
        for to, rows, c, begin in late_places(n, blocks, width):
            grad_qkv[c, begin : begin + rows, :] = sums[n, to : to + rows, :].astype(f32)
        for to, rows, c, begin in late_places(n, blocks, width, True):
            grad_out[begin : begin + rows, c * WIDTH : (c + 1) * WIDTH] = sums[
                n, to : to + rows, :
            ].astype(f32)


def unpack(sums, width, earlier):
    out = jax.ShapeDtypeStruct
    return pl.pallas_call(
        in_order(unpack_kernel, 1, len(earlier)),
        in_specs=[pl.BlockSpec(memory_space=pltpu.VMEM)] + unread(earlier),
        out_specs=[pl.BlockSpec(memory_space=pltpu.VMEM)] * 2,
        out_shape=[out((3, width, WIDTH), f32), out((WIDTH, width), f32)],
        compiler_params=pltpu.CompilerParams(vmem_limit_bytes=LIMIT * MIB),
        name="unpack",
    )(sums, *earlier)


def finish_kernel(info, parts, other, there, tok, gain, dx2, out):
    grad = parts[0].astype(f32) + other[0].astype(f32) + there[...].astype(f32)
    hat, inverse = normalized(tok[...].astype(f32))
    out[...] = dx2[...] + norm_back(hat, inverse, gain[...], grad)


def finish(info, me_at, parts, other, there, tokens, gain, dx2, earlier):
    width = tokens.shape[1]
    share = there.shape[0]
    rows = pl.BlockSpec((TILE, width), lambda i, info: (i, 0))
    return pl.pallas_call(
        in_order(finish_kernel, 7, len(earlier)),
        grid_spec=pltpu.PrefetchScalarGridSpec(
            num_scalar_prefetch=1,
            grid=(share // TILE,),
            in_specs=[
                pl.BlockSpec((1, TILE, width), lambda i, info: (0, i, 0)),
                pl.BlockSpec((1, TILE, width), lambda i, info: (0, i, 0)), rows,
                pl.BlockSpec((TILE, width), lambda i, info: (2 * info[me_at] + i, 0)),
                whole((1, width)), rows,
            ]
            + unread(earlier),
            out_specs=rows,
        ),
        out_shape=jax.ShapeDtypeStruct((share, width), f32),
        compiler_params=params(LIMIT),
        cost_estimate=pl.CostEstimate(
            flops=30 * share * width, bytes_accessed=10 * MIB, transcendentals=0
        ),
        name="finish",
    )(info, parts, other, there, tokens, gain, dx2, *earlier)


def total_of(blocks):
    total = blocks[0].astype(f32)
    for n in range(1, blocks.shape[0]):
        total += blocks[n].astype(f32)
    return total.astype(bf16)


def sums_kernel(blocks_a, blocks_b, out):
    rows = blocks_a.shape[1]
    out[:rows, :] = total_of(blocks_a)
    out[rows:, :] = total_of(blocks_b)


def two_sums(blocks_a, blocks_b, earlier):
    _, rows, width = blocks_a.shape
    return pl.pallas_call(
        in_order(sums_kernel, 2, len(earlier)),
        grid=(1,),
        in_specs=[whole(blocks_a.shape), whole(blocks_b.shape)] + unread(earlier),
        out_specs=whole((2 * rows, width)),
        out_shape=pltpu.HBM((2 * rows, width), bf16),
        compiler_params=params(LIMIT),
        name="two_sums",
    )(blocks_a, blocks_b, *earlier)


def sum_kernel(blocks, out):
    out[...] = total_of(blocks)


def summed(blocks, steps, earlier):
    count, rows, width = blocks.shape
    tile = rows // steps
    return pl.pallas_call(
        in_order(sum_kernel, 1, len(earlier)),
        grid=(steps,),
        in_specs=[pl.BlockSpec((count, tile, width), lambda i: (0, i, 0))] + unread(earlier),
        out_specs=pl.BlockSpec((tile, width), lambda i: (i, 0)),
        out_shape=pltpu.HBM((rows, width), bf16),
        compiler_params=params(LIMIT),
        name="summed",
    )(blocks, *earlier)


def copies_kernel(first, second, out):
    total = (first[...].astype(f32) + second[...].astype(f32)).astype(bf16)
    for n in range(out.shape[0]):
        out[n] = total


def sum_copies(first, second, count, earlier):
    rows, width = first.shape
    return pl.pallas_call(
        in_order(copies_kernel, 2, len(earlier)),
        grid=(1,),
        in_specs=[whole((rows, width))] * 2 + unread(earlier),
        out_specs=whole((count, rows, width)),
        out_shape=pltpu.HBM((count, rows, width), bf16),
        compiler_params=params(LIMIT),
        name="sum_copies",
    )(first, second, *earlier)


def swap(array, axis, bit=1):
    size = lax.axis_size(axis)
    if size == 1:
        return jnp.zeros_like(array)
    return lax.ppermute(array, axis, [(i, i ^ bit) for i in range(size)])


def swap_both(array):
    return lax.ppermute(array, MP, [(i, i ^ 3) for i in range(4)])


def scattered(rows, axes):
    group = lax.axis_size(axes)
    length, width = rows.shape
    return lax.all_to_all(
        rows.reshape(group, length // group, width), axes, 0, 0, tiled=True
    )


def both_sums(total):
    if lax.axis_size("zl") == 1:
        return total
    return (total.astype(f32) + swap(total, "zl").astype(f32)).astype(bf16)


def local(
    tokens, cotangent, segments, padding, positions, ln1_gain, ln1_bias, w_qkv, b_qkv, w_out, b_out,
    ln2_gain, ln2_bias, w_up, b_up, w_down, b_down,
):
    width, hidden = w_up.shape
    w_all = lax.all_gather(w_out, MP)
    gain_one, shift_one = ln1_gain[None], ln1_bias[None]
    gain_two, shift_two = ln2_gain[None], ln2_bias[None]
    ends = jnp.sum((segments <= jnp.arange(2)[:, None]).astype(jnp.int32), axis=1)
    info = jnp.concatenate([ends, lax.axis_index(MP)[None].astype(jnp.int32)])
    me_at = 2
    table = jnp.asarray(rope_constants())
    k_aug, v_aug, q_aug_t, q, k_t, v_t = project(
        tokens, w_qkv, b_qkv, gain_one, shift_one, positions, segments, padding, table
    )

    def exchanged(own, to_c, to_zh, to_both):
        return own, swap(to_c, "c"), swap(to_zh, "zh"), swap_both(to_both)

    o_0, o_t_0, lse_0 = attend(0, info, k_aug, v_t, q_aug_t, k_t, padding, ())
    o_zh_0, o_c_0 = swap(o_0, "zh"), swap(o_0, "c")
    o_1, o_t_1, lse_1 = attend(1, info, k_aug, v_t, q_aug_t, k_t, padding, (o_0, w_all))
    o_zh_1 = swap(o_1, "zh")
    o_zh_0 = after(o_zh_0, (o_1,))
    o_parts_0 = tuple((part, None) for part in (o_0, o_c_0, o_zh_0, swap(o_zh_0, "c")))

    def mlp_half(part, o_parts, earlier):
        return mlp(
            part, info, me_at, tokens, cotangent, o_parts, w_all, b_out[None], gain_two, shift_two,
            w_up, b_up[None], w_down, earlier,
        )

    x2_0, dy_0, h2_0, act_0, du_0, mlp_0, mlp_sent_0, dh2_0, sent, db_0 = mlp_half(
        0, o_parts_0, (o_1,)
    )
    pair = paired(o_1, o_zh_1, (x2_0,))
    pair_c = swap(pair, "c")
    o_parts_1 = ((pair, 0), (pair_c, 0), (pair, 1), (pair_c, 1))
    other_0 = swap(sent, "c")
    give_0 = to_give(dh2_0, other_0, ())
    there_0 = swap(give_0, "zh")
    x2_1, dy_1, h2_1, act_1, du_1, mlp_1, mlp_sent_1, dh2_1, sent, db_1 = mlp_half(
        1, o_parts_1, (give_0,)
    )
    other_1 = swap(sent, "c")
    grad_down = down_weights((act_0, act_1), cotangent, (there_0,))
    arrived_down = scattered(grad_down, ("y", "x"))
    give_1 = to_give(dh2_1, other_1, (grad_down,))
    there_1 = swap(give_1, "zh")
    grad_up = up_weights((h2_0, h2_1), (du_0, du_1), (give_1,))
    dx2, g, *d_parts, small = middle(
        info, me_at, (dh2_0, other_0, there_0, x2_0, dy_0), (dh2_1, other_1, there_1, x2_1, dy_1),
        gain_two, w_all, (grad_up,),
    )
    do = exchanged(*d_parts)
    arrived_up = scattered(after(grad_up, (g,)), ("y", "x"))
    grad_out, out_sent = out_weights(info, me_at, o_parts_0, o_parts_1, g)
    out_other = swap(out_sent, "c")
    mlp_parts = (mlp_0, mlp_1)
    mlp_others = (swap(mlp_sent_0, "c"), swap(mlp_sent_1, "c"))
    dq_0, dk, dv = attend_back(
        0, info, me_at, k_aug, v_aug, k_t, q_aug_t, q, v_t, o_t_0, lse_0, padding, do, positions,
        table, None, None, (grad_out, g),
    )
    give = to_give(grad_out, out_other, (dq_0,))
    out_there = swap(give, "zh")
    mlp_give = two_to_give(mlp_parts, mlp_others, (give,))
    mlp_there = swap(mlp_give, "zh")
    part_sum = both_sums(two_sums(arrived_up, arrived_down, (mlp_give,)))
    dq_1, dk, dv = attend_back(
        1, info, me_at, k_aug, v_aug, k_t, q_aug_t, q, v_t, o_t_1, lse_1, padding, do, positions,
        table, dk, dv, (give, part_sum),
    )
    grad_mlp = lax.all_gather(part_sum, ("y", "x"), axis=0, tiled=True)
    early = jnp.concatenate([small[0:4], (db_0 + db_1)[0:4]])
    dh1, sent, sums = project_back(
        info, me_at, tokens, gain_one, shift_one, dq_0, dq_1, dk, dv, positions, table, w_qkv,
        grad_out, out_other, out_there, early, lax.axis_size(("y", "x")), (mlp_there,),
    )
    other = swap(sent, "c")
    back = swap(to_give(dh1, other, (sums,)), "zh")
    arrived = scattered(sums.reshape(-1, WIDTH), ("y", "x"))
    total = summed(arrived, 1, (back,))
    block = sum_copies(total, swap(total, "zl"), sums.shape[0], ())
    late = lax.all_to_all(block, ("y", "x"), 0, 0, tiled=True)
    grad_inputs = finish(info, me_at, dh1, other, back, tokens, gain_one, dx2, (block,))
    mixed = mixed_rows(
        (x2_0, x2_1), mlp_parts, mlp_others, mlp_there, b_down[None], (block,)
    )
    count = lax.axis_size(("y", "x"))
    grad_mlp = grad_mlp.reshape(count, 2, width // count, hidden)
    grad_up = grad_mlp[:, 0].astype(f32).reshape(width, hidden)
    grad_down = grad_mlp[:, 1].astype(f32).reshape(hidden, width)
    grad_b, grad_b_up, vectors = unpack_vectors(late, width, (grad_inputs, mixed, grad_up, grad_down))
    by_c, by_zh, by_both = swap(vectors, "c"), swap(vectors, "zh"), swap_both(vectors)
    grad_qkv, grad_w_out = unpack(late, width, (vectors,))
    group = (vectors + by_c) + (by_zh + by_both)
    return (
        mixed, grad_inputs, group[0], group[1], grad_qkv, grad_b, grad_w_out, group[4],
        group[2], group[3], grad_up, grad_b_up[0], grad_down, group[5],
    )


def solution(mesh):
    packs = mesh.shape["dp"]
    if packs == 32:
        shape = (2, 4, 4, 2, 2)
    else:
        shape = (1, packs, 1, 2, 2)
    split = Mesh(mesh.devices.reshape(shape), EVERY)
    in_specs = (
        P(DP, None), P(DP, None), P(DP, None), P(DP, None), P(None, DP, None), P(), P(),
        P(None, None, MP), P(None, MP), P(MP, None), P(), P(), P(), P(None, MP), P(MP),
        P(MP, None), P(),
    )
    out_specs = (
        P(EVERY, None), P(EVERY, None), P(), P(), P(None, None, MP), P(None, MP), P(MP, None), P(),
        P(), P(), P(None, MP), P(MP), P(MP, None), P(),
    )
    return jax.shard_map(local, mesh=split, in_specs=in_specs, out_specs=out_specs, check_vma=False)
```

```python
import functools
import math

import jax
import jax.numpy as jnp
import ml_dtypes
import numpy as np
from jax import lax
from jax.experimental import pallas as pl
from jax.experimental.pallas import tpu as pltpu
from jax.sharding import Mesh
from jax.sharding import PartitionSpec as P

HEAD_DIM = 64
HEADS = 4
WIDTH = HEADS * HEAD_DIM
AUG = 128
TILE = 256
ROWS = 2 * TILE
PLACES = 64
LIMIT = 64
MIB = 1 << 20
DP = ("zl", "y", "x")
MP = ("zh", "c")
EVERY = ("zl", "y", "x", "zh", "c")

epsilon = 1e-06
NEG = -1e30
bf16 = jnp.bfloat16
f32 = jnp.float32


def dot_nn(a, b):
    return lax.dot_general(a, b, (((1,), (0,)), ((), ())), preferred_element_type=f32)


def dot_nt(a, b):
    return lax.dot_general(a, b, (((1,), (1,)), ((), ())), preferred_element_type=f32)


def dot_tn(a, b):
    return lax.dot_general(a, b, (((0,), (0,)), ((), ())), preferred_element_type=f32)


def normalized(values):
    center = jnp.mean(values, axis=-1, keepdims=True)
    shifted = values - center
    spread = jnp.mean(shifted * shifted, axis=-1, keepdims=True)
    inverse = lax.rsqrt(spread + epsilon)
    return shifted * inverse, inverse


def norm_back(hat, inverse, gain, grad):
    scaled = grad * gain
    return inverse * (
        scaled
        - jnp.mean(scaled, axis=-1, keepdims=True)
        - hat * jnp.mean(scaled * hat, axis=-1, keepdims=True)
    )


def turned(x, low, high):
    width = x.shape[1]
    pair = HEAD_DIM // 6
    return pltpu.roll(x, width - pair, 1) * low + pltpu.roll(x, pair, 1) * high


def three_parts(x):
    first = x.astype(bf16).astype(f32)
    rest = x - first
    second = rest.astype(bf16).astype(f32)
    return first, second, rest - second


def params(limit, axes=1):
    return pltpu.CompilerParams(
        dimension_semantics=("arbitrary",) * axes, vmem_limit_bytes=limit * MIB
    )


def in_order(kernel, inputs, earlier):
    def run(*refs):
        kernel(*refs[:inputs], *refs[inputs + earlier :])

    return run


def unread(arrays):
    return [pl.BlockSpec(memory_space=pl.ANY)] * len(arrays)


def whole(shape):
    return pl.BlockSpec(shape, lambda *_: (0,) * len(shape))


def clip_range(info, tile, length):
    half = TILE // 2
    first, second = info[0], info[1]
    at = tile * TILE
    begin = jnp.where(second <= at, second, jnp.where(first <= at, first, 0))
    end = jnp.where(
        first >= at + TILE, first, jnp.where(second >= at + TILE, second, length)
    )
    end = (end + half - 1) // half
    count = (end - begin // half + 1) // 2
    return jnp.maximum(end - 2 * count, 0), count


def key_tiles(begin, at, count):
    return pl.ds(pl.multiple_of(begin * (TILE // 2) + at * TILE, TILE // 2), count * TILE)


def rope_constants():
    pair = HEAD_DIM // 6
    feature = np.arange(WIDTH) % HEAD_DIM
    section, place = feature // (2 * pair), feature % (2 * pair)
    frequency = np.exp(-math.log(10000.0) * (place % pair) / pair)
    table = np.zeros((PLACES, 3, WIDTH))
    for s in range(3):
        for value in range(16):
            angle = value * frequency
            turns = section == s
            table[s * 16 + value, 0] = np.where(turns, np.cos(angle), 0.0)
            table[s * 16 + value, 1] = np.where(turns & (place < pair), -np.sin(angle), 0.0)
            table[s * 16 + value, 2] = np.where(turns & (place >= pair), np.sin(angle), 0.0)
    table[48, 0] = section == 3
    rest = table.reshape(PLACES, 3 * WIDTH).astype(np.float32)
    parts = []
    for _ in range(3):
        part = rest.astype(ml_dtypes.bfloat16)
        parts.append(part)
        rest = rest - part.astype(np.float32)
    return np.concatenate(parts)


def rope_factors(positions, table):
    row = lax.broadcasted_iota(jnp.int32, (PLACES, positions.shape[-1]), 0)
    where = jnp.where(
        row < 16, positions[0], jnp.where(row < 32, positions[1], positions[2])
    )
    hit = ((where == row % 16) & (row < 48)) | (row == 48)
    hit = jnp.where(hit, 1.0, 0.0)
    hits = jnp.concatenate([hit, hit, hit]).astype(bf16)
    factors = dot_tn(hits, table[...])
    return factors[:, :WIDTH], factors[:, WIDTH : 2 * WIDTH], factors[:, 2 * WIDTH :]


def qkv_kernel(
    tok, w, b, gain, shift, pos, seg, pad, table, k_aug, v_aug, q_aug_t, q_out, k_t, v_t, w_wide
):
    @pl.when(pl.program_id(0) == 0)
    def _():
        for c in range(3):
            w_wide[:, c * WIDTH : (c + 1) * WIDTH] = w[c]

    hat, _ = normalized(tok[...].astype(f32))
    normed = (hat * gain[...] + shift[...]).astype(bf16)
    cos, low, high = rope_factors(pos, table)
    all_three = dot_nn(normed, w_wide[...])
    q = all_three[:, :WIDTH] + b[0:1, :]
    k = all_three[:, WIDTH : 2 * WIDTH] + b[1:2, :]
    v = all_three[:, 2 * WIDTH :] + b[2:3, :]
    q = (q * cos + turned(q, low, high)) * (1.0 / math.sqrt(HEAD_DIM))
    k = k * cos + turned(k, low, high)
    q_out[...] = q.astype(bf16)
    q_t = q.T.astype(bf16)
    k_t[...] = k.T.astype(bf16)
    v_t[...] = v.T.astype(bf16)
    row = lax.broadcasted_iota(jnp.int32, (HEAD_DIM, ROWS), 0)
    clip = seg[...]
    same = (row >= 1) & (row < 4) & (clip == row - 1)
    mask = jnp.where((row >= 1) & (row < 4) & (clip != row - 1), NEG, 0.0)
    mask = jnp.where(row == 0, jnp.where(pad[...] != 0, NEG, 0.0), mask)
    k_extra = jnp.where((row >= 4) & (row < 7), 1.0, mask)
    q_extra = jnp.where(same | (row == 0), 1.0, 0.0).astype(bf16)
    k_side = jnp.concatenate([jnp.zeros((HEAD_DIM, ROWS), f32), k_extra]).T
    lane = lax.broadcasted_iota(jnp.int32, (ROWS, AUG), 1)
    ones = jnp.where((lane >= HEAD_DIM) & (lane < HEAD_DIM + 3), 1.0, 0.0)
    for h in range(HEADS):
        pair = slice(h // 2 * AUG, h // 2 * AUG + AUG)
        wide = slice(h * AUG, (h + 1) * AUG)
        k_pair, v_pair = k[:, pair], v[:, pair]
        if h % 2:
            k_pair, v_pair = pltpu.roll(k_pair, HEAD_DIM, 1), pltpu.roll(v_pair, HEAD_DIM, 1)
        k_aug[:, wide] = jnp.where(lane < HEAD_DIM, k_pair, k_side).astype(bf16)
        v_aug[:, wide] = jnp.where(lane < HEAD_DIM, v_pair, ones).astype(bf16)
        q_aug_t[h * AUG : h * AUG + HEAD_DIM, :] = q_t[h * HEAD_DIM : (h + 1) * HEAD_DIM, :]
        q_aug_t[h * AUG + HEAD_DIM : (h + 1) * AUG, :] = q_extra


def project(tokens, w, b, gain, shift, positions, segments, padding, table):
    length, width = tokens.shape
    tiles = length // ROWS

    def rows(columns):
        return pl.BlockSpec((ROWS, columns), lambda i: (i, 0))

    def columns(count):
        return pl.BlockSpec((count, ROWS), lambda i: (0, i))

    out = jax.ShapeDtypeStruct
    wide = out((length, HEADS * AUG), bf16)
    flat = out((WIDTH, length), bf16)
    return pl.pallas_call(
        qkv_kernel,
        grid=(tiles,),
        in_specs=[
            rows(width), whole(w.shape), whole(b.shape), whole((1, width)), whole((1, width)),
            pl.BlockSpec((3, 1, ROWS), lambda i: (0, 0, i)), columns(1), columns(1), whole(table.shape),
        ],
        out_specs=[
            rows(HEADS * AUG), rows(HEADS * AUG), columns(HEADS * AUG), rows(WIDTH), columns(WIDTH),
            columns(WIDTH),
        ],
        out_shape=[
            wide, wide, out((HEADS * AUG, length), bf16), out((length, WIDTH), bf16), flat, flat,
        ],
        scratch_shapes=[pltpu.VMEM((width, 3 * WIDTH), bf16)],
        compiler_params=params(LIMIT),
        cost_estimate=pl.CostEstimate(
            flops=6 * length * width * WIDTH, bytes_accessed=20 * MIB, transcendentals=0
        ),
        name="project",
    )(tokens, w, b, gain, shift, positions, segments, padding, table)


def attend_kernel(info, k_aug, v_t, q_aug_t, k_t, pad, o, o_t, lse, top, total, acc, *, part):
    tile = 2 * pl.program_id(0) + part
    padded = pad[...] != 0
    for h in range(HEADS):
        q_h = q_aug_t[h * AUG : h * AUG + HEAD_DIM, :].astype(f32)
        k_h = k_t[h * HEAD_DIM : (h + 1) * HEAD_DIM, :].astype(f32)
        own = jnp.sum(q_h * k_h, axis=0, keepdims=True)
        top[h : h + 1, :] = jnp.where(padded, own, -3e38)
        total[h : h + 1, :] = jnp.where(padded, 1.0, 0.0)
    here = pl.ds(pl.multiple_of(tile * TILE, TILE), TILE)
    acc[...] = jnp.where(padded, v_t[:, here].astype(f32), 0.0)
    feats = [slice(h * HEAD_DIM, (h + 1) * HEAD_DIM) for h in range(HEADS)]
    wides = [slice(h * AUG, (h + 1) * AUG) for h in range(HEADS)]

    begin, tiles = clip_range(info, tile, k_aug.shape[0])

    def step(j, count):
        keys = key_tiles(begin, j, count)
        scores = [dot_nn(k_aug[keys, wide], q_aug_t[wide, :]) for wide in wides]
        probs, fades = [], []
        for h in range(HEADS):
            old = top[h : h + 1, :]
            new = jnp.maximum(old, jnp.max(scores[h], axis=0, keepdims=True))
            prob = jnp.exp(scores[h] - new)
            fade = jnp.exp(old - new)
            top[h : h + 1, :] = new
            total[h : h + 1, :] = total[h : h + 1, :] * fade + jnp.sum(prob, axis=0, keepdims=True)
            probs.append(prob.astype(bf16))
            fades.append(fade)
        for h, feat in enumerate(feats):
            acc[feat, :] = acc[feat, :] * fades[h] + dot_nn(v_t[feat, keys], probs[h])

    pairs = tiles // 2

    def two(n, _):
        step(2 * n, 2)
        return 0

    lax.fori_loop(0, pairs, two, 0)

    @pl.when(2 * pairs < tiles)
    def _():
        step(tiles - 1, 1)

    for h, feat in enumerate(feats):
        acc[feat, :] = acc[feat, :] / total[h : h + 1, :]
    lse[...] = jnp.zeros_like(lse)
    lse[0:HEADS, :] = top[0:HEADS, :] + jnp.log(total[0:HEADS, :])
    turned_o = acc[...]
    o_t[...] = turned_o.astype(bf16)
    o[...] = turned_o.T.astype(bf16)


def attend(part, info, k_aug, v_t, q_aug_t, k_t, padding, earlier):
    length = k_aug.shape[0]
    half = length // 2

    def columns(count):
        return pl.BlockSpec((count, TILE), lambda i, *_: (0, 2 * i + part))

    def packed(count):
        return pl.BlockSpec((count, TILE), lambda i, *_: (0, i))

    out = jax.ShapeDtypeStruct
    return pl.pallas_call(
        in_order(functools.partial(attend_kernel, part=part), 6, len(earlier)),
        grid_spec=pltpu.PrefetchScalarGridSpec(
            num_scalar_prefetch=1,
            grid=(half // TILE,),
            in_specs=[
                whole(k_aug.shape), whole(v_t.shape), columns(HEADS * AUG), columns(WIDTH),
                columns(1),
            ]
            + unread(earlier),
            out_specs=[
                pl.BlockSpec((TILE, WIDTH), lambda i, *_: (i, 0)), packed(WIDTH), packed(8),
            ],
            scratch_shapes=[
                pltpu.VMEM((8, TILE), f32), pltpu.VMEM((8, TILE), f32), pltpu.VMEM((WIDTH, TILE), f32),
            ],
        ),
        out_shape=[out((half, WIDTH), bf16), out((WIDTH, half), bf16), out((8, half), f32)],
        compiler_params=params(LIMIT),
        cost_estimate=pl.CostEstimate(
            flops=24 * half * length * WIDTH, bytes_accessed=6 * MIB, transcendentals=0
        ),
        name="attend",
    )(info, k_aug, v_t, q_aug_t, k_t, padding, *earlier)


def nothing(*refs):
    del refs


def after(value, earlier):
    return pl.pallas_call(
        nothing,
        in_specs=unread((value,) + earlier),
        out_specs=pl.BlockSpec(memory_space=pl.ANY),
        out_shape=jax.ShapeDtypeStruct(value.shape, value.dtype),
        input_output_aliases={0: 0},
        name="after",
    )(value, *earlier)


def pair_kernel(first, second, out):
    out[0] = first[...]
    out[1] = second[...]


def paired(first, second, earlier):
    shape = (2,) + first.shape
    return pl.pallas_call(
        in_order(pair_kernel, 2, len(earlier)),
        in_specs=[pl.BlockSpec(memory_space=pltpu.VMEM)] * 2 + unread(earlier),
        out_specs=pl.BlockSpec(memory_space=pltpu.VMEM),
        out_shape=jax.ShapeDtypeStruct(shape, first.dtype),
        name="paired",
    )(first, second, *earlier)


def head_block(at, owner):
    if at is None:
        return pl.BlockSpec((TILE, WIDTH), lambda i, info: (owner(i, info), 0))
    return pl.BlockSpec((None, TILE, WIDTH), lambda i, info: (at, owner(i, info), 0))


def relative(i):
    return i % 2 * 2 + i // 2


def gelu_parts(u):
    size = jnp.abs(u)
    t = 1.0 / (1.0 + (0.3275911 / math.sqrt(2.0)) * size)
    bell = jnp.exp(-0.5 * (u * u))
    poly = 0.5 * 1.061405429
    for c in (-1.453152027, 1.421413741, -0.284496736, 0.254829592):
        poly = poly * t + 0.5 * c
    tail = poly * t * bell
    below = jnp.where(u >= 0, 1.0 - tail, tail)
    return u * below, below + u * bell * (1.0 / math.sqrt(2.0 * math.pi))


def mlp_kernel(
    info, tok, cot, o_0, o_1, o_2, o_3, w_all, b_out, gain, shift, w_up, b_up, w_down,
    x2, dy, h2, act, du, mlp, mlp_sent, dh2, dh2_sent, db_up, w_out, *, me_at,
):
    i = pl.program_id(0)

    @pl.when(i == 0)
    def _():
        for j in range(4):
            w_out[j * WIDTH : (j + 1) * WIDTH, :] = w_all[jnp.bitwise_xor(info[me_at], j)]
        db_up[...] = jnp.zeros_like(db_up)

    heads = jnp.concatenate([o_0[...], o_1[...], o_2[...], o_3[...]], axis=1)
    mid = tok[...].astype(f32) + b_out[...] + dot_nn(heads, w_out[...])

    @pl.when(i == 0)
    def _():
        x2[...] = mid
        dy[...] = cot[...]

    hat, _ = normalized(mid)
    normed = (hat * gain[...] + shift[...]).astype(bf16)
    h2[...] = normed
    u = dot_nn(normed, w_up[...]) + b_up[...]
    grad_act = dot_nt(cot[...], w_down[...])
    value, slope = gelu_parts(u)
    value = value.astype(bf16)
    grad = (grad_act * slope).astype(bf16)
    act[...] = value
    du[...] = grad
    db_up[0:1, :] += jnp.sum(grad.astype(f32), axis=0, keepdims=True)
    mlp_part = dot_nn(value, w_down[...]).astype(bf16)
    dh2_part = dot_nt(grad, w_up[...]).astype(bf16)
    mlp[0] = mlp_part
    mlp_sent[0] = mlp_part
    dh2[0] = dh2_part
    dh2_sent[0] = dh2_part


def mlp(
    part, info, me_at, tokens, cotangent, o_parts, w_all, b_out, gain, shift, w_up, b_up, w_down,
    earlier,
):
    length, width = tokens.shape
    half = length // 2
    hidden = w_up.shape[1]
    owners = half // TILE

    def owner(i, info):
        return jnp.bitwise_xor(info[me_at], relative(i))

    def rows(columns):
        return pl.BlockSpec((TILE, columns), lambda i, info: (2 * owner(i, info) + part, 0))

    def packed(columns):
        return pl.BlockSpec((TILE, columns), lambda i, info: (owner(i, info), 0))

    ordered = pl.BlockSpec((1, TILE, width), lambda i, info: (i, 0, 0))
    sent = pl.BlockSpec((1, TILE, width), lambda i, info: (jnp.maximum(i - 2, 0), 0, 0))

    out = jax.ShapeDtypeStruct
    return pl.pallas_call(
        in_order(functools.partial(mlp_kernel, me_at=me_at), 14, len(earlier)),
        grid_spec=pltpu.PrefetchScalarGridSpec(
            num_scalar_prefetch=1,
            grid=(owners,),
            in_specs=[rows(width), rows(width)]
            + [head_block(at, owner) for _, at in o_parts]
            + [whole(w_all.shape)]
            + [whole((1, width))] * 3
            + [whole(w_up.shape), whole((1, hidden)), whole(w_down.shape)]
            + unread(earlier),
            out_specs=[
                whole((TILE, width)), whole((TILE, width)), packed(width), packed(hidden),
                packed(hidden), ordered, sent, ordered, sent, whole((8, hidden)),
            ],
            scratch_shapes=[pltpu.VMEM((4 * WIDTH, width), bf16)],
        ),
        out_shape=[
            out((TILE, width), f32), out((TILE, width), bf16), out((half, width), bf16),
            out((half, hidden), bf16), out((half, hidden), bf16),
        ]
        + [out((owners, TILE, width), bf16), out((2, TILE, width), bf16)] * 2
        + [out((8, hidden), f32)],
        compiler_params=params(LIMIT),
        cost_estimate=pl.CostEstimate(
            flops=20 * half * width * hidden, bytes_accessed=20 * MIB, transcendentals=0
        ),
        name="mlp",
    )(
        info, tokens, cotangent, *(part for part, _ in o_parts), w_all, b_out, gain, shift, w_up,
        b_up, w_down, *earlier
    )


def up_weights_kernel(left_a, left_b, right_a, right_b, out):
    left = jnp.concatenate([left_a[...], left_b[...]])
    right = jnp.concatenate([right_a[...], right_b[...]])
    out[...] = dot_tn(left, right).astype(bf16)


def up_weights(h2, du, earlier):
    half, width = h2[0].shape
    hidden = du[0].shape[1]
    return pl.pallas_call(
        in_order(up_weights_kernel, 4, len(earlier)),
        grid=(width // TILE,),
        in_specs=[pl.BlockSpec((half, TILE), lambda i: (0, i))] * 2
        + [whole((half, hidden))] * 2
        + unread(earlier),
        out_specs=pl.BlockSpec((TILE, hidden), lambda i: (i, 0)),
        out_shape=pltpu.HBM((width, hidden), bf16),
        compiler_params=params(LIMIT),
        cost_estimate=pl.CostEstimate(
            flops=8 * half * width * hidden, bytes_accessed=12 * MIB, transcendentals=0
        ),
        name="up_weights",
    )(*h2, *du, *earlier)


def down_weights_kernel(act_a, act_b, cot, out):
    owners = cot.shape[0] // (2 * TILE)
    rows = [cot[n * TILE : (n + 1) * TILE, :] for p in range(2) for n in range(p, 2 * owners, 2)]
    out[...] = dot_tn(
        jnp.concatenate([act_a[...], act_b[...]]), jnp.concatenate(rows)
    ).astype(bf16)


def down_weights(act, cotangent, earlier):
    half, hidden = act[0].shape
    length, width = cotangent.shape
    return pl.pallas_call(
        in_order(down_weights_kernel, 3, len(earlier)),
        grid=(hidden // TILE,),
        in_specs=[pl.BlockSpec((half, TILE), lambda i: (0, i))] * 2
        + [whole((length, width))]
        + unread(earlier),
        out_specs=pl.BlockSpec((TILE, width), lambda i: (i, 0)),
        out_shape=pltpu.HBM((hidden, width), bf16),
        compiler_params=params(LIMIT),
        cost_estimate=pl.CostEstimate(
            flops=8 * half * width * hidden, bytes_accessed=12 * MIB, transcendentals=0
        ),
        name="down_weights",
    )(*act, cotangent, *earlier)


def add_kernel(parts, other, out):
    out[...] = (parts[0].astype(f32) + other[0].astype(f32)).astype(bf16)


def to_give(parts, other, earlier):
    _, rows, width = parts.shape
    tile = min(rows, TILE)
    return pl.pallas_call(
        in_order(add_kernel, 2, len(earlier)),
        grid=(rows // tile,),
        in_specs=[
            pl.BlockSpec((1, tile, width), lambda i: (1, i, 0)),
            pl.BlockSpec((1, tile, width), lambda i: (1, i, 0)),
        ]
        + unread(earlier),
        out_specs=pl.BlockSpec((tile, width), lambda i: (i, 0)),
        out_shape=pltpu.HBM((rows, width), bf16),
        compiler_params=params(LIMIT),
        name="to_give",
    )(parts, other, *earlier)


def gives_kernel(parts_0, parts_a, parts_b, other_0, other_a, other_b, first, out):
    first[...] = (parts_0[0].astype(f32) + other_0[0].astype(f32)).astype(bf16)
    for n, (parts, other) in enumerate(((parts_a, other_a), (parts_b, other_b))):
        out[n] = (parts[0].astype(f32) + other[0].astype(f32)).astype(bf16)


def three_to_give(parts, others, earlier):
    _, rows, width = parts[0].shape
    tile = rows // 2
    return pl.pallas_call(
        in_order(gives_kernel, 6, len(earlier)),
        grid=(rows // tile,),
        in_specs=[pl.BlockSpec((1, tile, width), lambda i: (1, i, 0))] * 6 + unread(earlier),
        out_specs=[
            pl.BlockSpec((tile, width), lambda i: (i, 0)),
            pl.BlockSpec((2, tile, width), lambda i: (0, i, 0)),
        ],
        out_shape=[pltpu.HBM((rows, width), bf16), pltpu.HBM((2, rows, width), bf16)],
        compiler_params=params(LIMIT),
        name="three_to_give",
    )(*parts, *others, *earlier)


def mixed_kernel(x2_a, x2_b, parts_a, parts_b, other_a, other_b, there, shift, out):
    for n, (x2, parts, other) in enumerate(
        ((x2_a, parts_a, other_a), (x2_b, parts_b, other_b))
    ):
        total = parts[0].astype(f32) + other[0].astype(f32) + there[n].astype(f32)
        out[n * TILE : (n + 1) * TILE, :] = (x2[...] + total + shift[...]).astype(bf16)


def mixed_rows(x2, parts, others, there, shift, earlier):
    rows, width = x2[0].shape
    first = pl.BlockSpec((1, rows, width), lambda i: (0, 0, 0))
    return pl.pallas_call(
        in_order(mixed_kernel, 8, len(earlier)),
        grid=(1,),
        in_specs=[whole((rows, width))] * 2
        + [first] * 4
        + [whole((2, rows, width)), whole((1, width))]
        + unread(earlier),
        out_specs=whole((2 * rows, width)),
        out_shape=jax.ShapeDtypeStruct((2 * rows, width), bf16),
        compiler_params=params(LIMIT),
        name="mixed_rows",
    )(*x2, *parts, *others, there, shift, *earlier)


def middle_kernel(info, *refs, me_at):
    halves, (gain, w_all, dx2, g, d_0, d_1, d_2, d_3, small) = (refs[0:5], refs[5:10]), refs[10:]
    small[...] = jnp.zeros_like(small)
    for part, (kept, other, there, x2, dy) in enumerate(halves):
        rows = slice(part * TILE, (part + 1) * TILE)
        grad = kept[0].astype(f32) + other[0].astype(f32) + there[...].astype(f32)
        hat, inverse = normalized(x2[...])
        dy = dy[...].astype(f32)
        full = dy + norm_back(hat, inverse, gain[...], grad)
        dx2[rows, :] = full
        low = full.astype(bf16)
        g[rows, :] = low
        small[0:1, :] += jnp.sum(grad * hat, axis=0, keepdims=True)
        small[1:2, :] += jnp.sum(grad, axis=0, keepdims=True)
        small[2:3, :] += jnp.sum(low.astype(f32), axis=0, keepdims=True)
        small[3:4, :] += jnp.sum(dy, axis=0, keepdims=True)
    low = g[...]
    for j, d_j in enumerate((d_0, d_1, d_2, d_3)):
        d_j[...] = dot_nt(low, w_all[jnp.bitwise_xor(info[me_at], j)]).astype(bf16)


def middle(info, me_at, half_a, half_b, gain, w_all, earlier):
    width = gain.shape[1]
    rows = 2 * TILE
    own = whole((TILE, width))
    first = pl.BlockSpec((1, TILE, width), lambda i, info: (0, 0, 0))
    return pl.pallas_call(
        in_order(functools.partial(middle_kernel, me_at=me_at), 13, len(earlier)),
        grid_spec=pltpu.PrefetchScalarGridSpec(
            num_scalar_prefetch=1,
            grid=(1,),
            in_specs=[first, first, own, own, own] * 2
            + [whole((1, width)), whole(w_all.shape)]
            + unread(earlier),
            out_specs=[whole((rows, width))] * 2
            + [whole((rows, WIDTH))] * 4
            + [whole((8, width))],
        ),
        out_shape=[pltpu.HBM((rows, width), f32), pltpu.HBM((rows, width), bf16)]
        + [pltpu.HBM((rows, WIDTH), bf16)] * 4
        + [pltpu.HBM((8, width), f32)],
        compiler_params=params(LIMIT),
        cost_estimate=pl.CostEstimate(
            flops=4 * TILE * width * width, bytes_accessed=12 * MIB, transcendentals=0
        ),
        name="middle",
    )(info, *half_a, *half_b, gain, w_all, *earlier)


def out_weights_kernel(info, *refs):
    parts_a, parts_b, (g, kept, sent) = refs[0:4], refs[4:8], refs[8:]
    for n in range(2):
        for out, j in ((kept, 2 * n), (sent, 2 * n + 1)):
            heads = jnp.concatenate([parts_a[j][...], parts_b[j][...]])
            out[n] = dot_tn(heads, g[...]).astype(bf16)


def out_weights(info, me_at, parts_a, parts_b, g):
    width = g.shape[1]

    def owner(i, info):
        return info[me_at]

    return pl.pallas_call(
        out_weights_kernel,
        grid_spec=pltpu.PrefetchScalarGridSpec(
            num_scalar_prefetch=1,
            grid=(1,),
            in_specs=[head_block(at, owner) for _, at in parts_a + parts_b]
            + [whole(g.shape)],
            out_specs=[whole((2, WIDTH, width))] * 2,
        ),
        out_shape=[pltpu.HBM((2, WIDTH, width), bf16)] * 2,
        compiler_params=params(LIMIT),
        cost_estimate=pl.CostEstimate(
            flops=4 * TILE * width * width, bytes_accessed=6 * MIB, transcendentals=0
        ),
        name="out_weights",
    )(info, *(part for part, _ in parts_a + parts_b), g)


def attend_back_kernel(
    info, k_aug, v_aug, k_t, q_aug_t, q, v_t, o_t, lse, pad, do_0, do_1, do_2, do_3, pos, table,
    *refs, part, me_at, first,
):
    if first:
        dk_in = dv_in = None
    else:
        dk_in, dv_in, *refs = refs
    dq_out, dk, dv, q_side, do_side, q_lanes, do_lanes, dq_t = refs
    i = pl.program_id(0)
    tile = 2 * jnp.bitwise_xor(info[me_at], i) + part

    @pl.when(i == 0)
    def _():
        if first:
            dk[...] = jnp.zeros_like(dk)
            dv[...] = jnp.zeros_like(dv)
        else:
            dk[...] = dk_in[...]
            dv[...] = dv_in[...]

    here = pl.ds(pl.multiple_of(tile * TILE, TILE), TILE)
    do_here = jnp.where(
        i == 0, do_0[...], jnp.where(i == 1, do_1[...], jnp.where(i == 2, do_2[...], do_3[...]))
    )
    q_here = q[...]
    do_t = do_here.astype(f32).T
    k_here = k_t[:, here].astype(f32)
    padded = jnp.where(pad[...] != 0, 1.0, 0.0)
    row = lax.broadcasted_iota(jnp.int32, (AUG - HEAD_DIM, TILE), 0)
    lane = lax.broadcasted_iota(jnp.int32, (TILE, WIDTH), 1) // HEAD_DIM
    dk_parts, dv_parts = [], []
    for h in range(HEADS):
        feat = slice(h * HEAD_DIM, (h + 1) * HEAD_DIM)
        at = h * AUG
        q_h = q_aug_t[at : at + HEAD_DIM, :]
        do_h = do_t[feat, :]
        delta = jnp.sum(do_h * o_t[feat, :].astype(f32), axis=0, keepdims=True)
        lse_h = lse[h : h + 1, :]
        one, two, three = three_parts(-lse_h)
        extra = q_aug_t[at + HEAD_DIM : at + AUG, :].astype(f32)
        extra = jnp.where(row == 4, one, jnp.where(row == 5, two, jnp.where(row == 6, three, extra)))
        q_side[at : at + HEAD_DIM, :] = q_h
        q_side[at + HEAD_DIM : at + AUG, :] = extra.astype(bf16)
        one, two, three = three_parts(-delta)
        extra = jnp.where(row == 0, one, jnp.where(row == 1, two, jnp.where(row == 2, three, 0.0)))
        do_side[at : at + HEAD_DIM, :] = do_h.astype(bf16)
        do_side[at + HEAD_DIM : at + AUG, :] = extra.astype(bf16)
        q_lanes[h] = jnp.where(lane == h, q_here, jnp.zeros_like(q_here))
        do_lanes[h] = jnp.where(lane == h, do_here, jnp.zeros_like(do_here))
        q_h = q_h.astype(f32)
        k_h = k_here[feat, :]
        p_own = padded * jnp.exp(jnp.sum(q_h * k_h, axis=0, keepdims=True) - lse_h)
        dp_own = jnp.sum(do_h * v_t[feat, :].astype(f32), axis=0, keepdims=True)
        ds_own = p_own * (dp_own - delta)
        dq_t[feat, :] = ds_own * k_h
        dk_parts.append(ds_own * q_h)
        dv_parts.append(p_own * do_h)
    dk[here, :] += jnp.concatenate(dk_parts, axis=0).T
    dv[here, :] += jnp.concatenate(dv_parts, axis=0).T

    begin, tiles = clip_range(info, tile, k_aug.shape[0])

    def step(j, _):
        keys = key_tiles(begin, j, 1)
        probs, grads = [], []
        for h in range(HEADS):
            wide = slice(h * AUG, (h + 1) * AUG)
            prob = jnp.exp(dot_nn(k_aug[keys, wide], q_side[wide, :]))
            grad = prob * dot_nn(v_aug[keys, wide], do_side[wide, :])
            probs.append(prob.astype(bf16))
            grads.append(grad.astype(bf16))
        deep = (HEADS * TILE, WIDTH)
        dv[keys, :] += dot_nn(jnp.concatenate(probs, axis=1), do_lanes[...].reshape(deep))
        dk[keys, :] += dot_nn(jnp.concatenate(grads, axis=1), q_lanes[...].reshape(deep))
        for h in range(HEADS):
            feat = slice(h * HEAD_DIM, (h + 1) * HEAD_DIM)
            dq_t[feat, :] += dot_nn(k_t[feat, keys], grads[h])
        return 0

    lax.fori_loop(0, tiles, step, 0)
    dq = dq_t[...].T * (1.0 / math.sqrt(HEAD_DIM))
    cos, low, high = rope_factors(pos, table)
    dq_out[...] = (dq * cos - turned(dq, low, high)).astype(bf16)


def attend_back(
    part, info, me_at, k_aug, v_aug, k_t, q_aug_t, q, v_t, o_t, lse, padding, do, positions, table,
    dk, dv, earlier,
):
    length = k_aug.shape[0]
    half = length // 2

    def owner(i, info):
        return jnp.bitwise_xor(info[me_at], i)

    def rows(columns):
        return pl.BlockSpec((TILE, columns), lambda i, info: (2 * owner(i, info) + part, 0))

    def columns(count):
        return pl.BlockSpec((count, TILE), lambda i, info: (0, 2 * owner(i, info) + part))

    def packed(count):
        return pl.BlockSpec((count, TILE), lambda i, info: (0, owner(i, info)))

    out = jax.ShapeDtypeStruct
    before = () if dk is None else (dk, dv)
    return pl.pallas_call(
        in_order(
            functools.partial(attend_back_kernel, part=part, me_at=me_at, first=dk is None),
            16 + len(before), len(earlier),
        ),
        grid_spec=pltpu.PrefetchScalarGridSpec(
            num_scalar_prefetch=1,
            grid=(half // TILE,),
            in_specs=[
                whole(k_aug.shape), whole(v_aug.shape), whole(k_t.shape), columns(HEADS * AUG),
                rows(WIDTH), columns(WIDTH), packed(WIDTH), packed(8), columns(1),
            ]
            + [pl.BlockSpec((TILE, WIDTH), lambda i, info: (part, 0))] * 4
            + [
                pl.BlockSpec(
                    (3, 1, TILE), lambda i, info: (0, 0, 2 * owner(i, info) + part)
                ),
                whole(table.shape),
            ]
            + [whole((length, WIDTH))] * len(before)
            + unread(earlier),
            out_specs=[
                pl.BlockSpec((TILE, WIDTH), lambda i, info: (owner(i, info), 0)),
                whole((length, WIDTH)), whole((length, WIDTH)),
            ],
            scratch_shapes=[
                pltpu.VMEM((HEADS * AUG, TILE), bf16), pltpu.VMEM((HEADS * AUG, TILE), bf16),
                pltpu.VMEM((HEADS, TILE, WIDTH), bf16), pltpu.VMEM((HEADS, TILE, WIDTH), bf16),
                pltpu.VMEM((WIDTH, TILE), f32),
            ],
        ),
        out_shape=[out((half, WIDTH), bf16), out((length, WIDTH), f32), out((length, WIDTH), f32)],
        compiler_params=params(LIMIT),
        cost_estimate=pl.CostEstimate(
            flops=72 * half * length * WIDTH, bytes_accessed=16 * MIB, transcendentals=0
        ),
        name="attend_back",
    )(
        info, k_aug, v_aug, k_t, q_aug_t, q, v_t, o_t, lse, padding, *do, positions, table, *before,
        *earlier,
    )


def pieces(begin, count, period):
    at, end, cuts = begin, begin + count, []
    while at < end:
        length = min(end - at, period - at % period)
        cuts.append((at, length))
        at += length
    return cuts


def stacked_pairs(rows, count):
    row = lax.broadcasted_iota(jnp.int32, (count, WIDTH), 0)
    out = jnp.zeros((count, WIDTH), f32)
    for m, value in enumerate(rows):
        one, two, _ = three_parts(value)
        out = jnp.where(row == 2 * m, one, jnp.where(row == 2 * m + 1, two, out))
    return out.astype(bf16)


def late_extra(width, blocks):
    vectors = -(-(3 + 7 * width // WIDTH) // blocks)
    return vectors, -(-vectors // 8) * 16


def project_back_kernel(
    info, tok, gain, shift, dq_a, dq_b, dk, dv, pos, table, w, out_kept, out_other, out_there, early,
    up_a, up_b,
    dh1, dh1_sent, sums, acc, grad_b, small, w_wide,
):
    i = pl.program_id(0)

    @pl.when(i == 0)
    def _():
        acc[...] = jnp.zeros_like(acc)
        grad_b[...] = jnp.zeros_like(grad_b)
        small[...] = jnp.zeros_like(small)
        for c in range(3):
            w_wide[:, c * WIDTH : (c + 1) * WIDTH] = w[c]

    dk_here = dk[...]
    cos, low, high = rope_factors(pos, table)
    dk_low = (dk_here * cos - turned(dk_here, low, high)).astype(bf16)
    dq = jnp.concatenate([dq_a[...], dq_b[...]])
    parts = jnp.concatenate([dq, dk_low, dv[...].astype(bf16)], axis=1)
    grad = dot_nt(parts, w_wide[...])
    hat, _ = normalized(tok[...].astype(f32))
    normed = (hat * gain[...] + shift[...]).astype(bf16)
    acc[...] += dot_tn(normed, parts)
    grad_b[0:1, :] += jnp.sum(parts.astype(f32), axis=0, keepdims=True)
    small[0:1, :] += jnp.sum(grad * hat, axis=0, keepdims=True)
    small[1:2, :] += jnp.sum(grad, axis=0, keepdims=True)
    low_grad = grad.astype(bf16)
    dh1[0] = low_grad
    dh1_sent[0] = low_grad

    @pl.when(i == pl.num_programs(0) - 1)
    def _():
        width = normed.shape[1]
        blocks = sums.shape[0]

        def cut(value, count):
            return [value[:, r * WIDTH : (r + 1) * WIDTH] for r in range(count)]

        rows = cut(grad_b[0:1, :], 3) + cut(up_a[0:1, :] + up_b[0:1, :], width // WIDTH)
        for ref, count in ((small, 2), (early, 4)):
            for v in range(count):
                rows += cut(ref[v : v + 1, :], width // WIDTH)
        for n in range(blocks):
            for to, rows_here, c, begin in late_places(n, blocks, width):
                here = (slice(begin, begin + rows_here), slice(c * WIDTH, (c + 1) * WIDTH))
                sums[n, to : to + rows_here, :] = acc[here].astype(bf16)
            for to, rows_here, c, begin in late_places(n, blocks, width, True):
                here = (slice(begin, begin + rows_here), slice(c * WIDTH, (c + 1) * WIDTH))
                sums[n, to : to + rows_here, :] = (
                    out_kept[here].astype(f32)
                    + out_other[here].astype(f32)
                    + out_there[here].astype(f32)
                ).astype(bf16)
            extra_at = 4 * width // blocks
            sums[n, extra_at:, :] = stacked_pairs(rows[n::blocks], sums.shape[1] - extra_at)


def late_places(n, blocks, width, out=False):
    deep, period = (width // blocks, WIDTH) if out else (3 * width // blocks, width)
    first = 3 * width // blocks if out else 0
    return [
        (first + at - n * deep, length, at // period, at % period)
        for at, length in pieces(n * deep, deep, period)
    ]


def project_back(
    info, me_at, tokens, gain, shift, dq_a, dq_b, dk, dv, positions, table, w, kept, other, there,
    early, up_a, up_b, blocks, earlier,
):
    length, width = tokens.shape
    share = 2 * TILE

    def owner(i, info):
        return jnp.bitwise_xor(info[me_at], relative(i))

    def rows(count, columns):
        return pl.BlockSpec((count, columns), lambda i, info: (owner(i, info), 0))

    first = pl.BlockSpec((None, TILE, width), lambda i, info: (0, 0, 0))
    out = jax.ShapeDtypeStruct
    sums = (blocks, 4 * width // blocks + late_extra(width, blocks)[1], WIDTH)
    return pl.pallas_call(
        in_order(project_back_kernel, 17, len(earlier)),
        grid_spec=pltpu.PrefetchScalarGridSpec(
            num_scalar_prefetch=1,
            grid=(length // share,),
            in_specs=[
                rows(share, width), whole((1, width)), whole((1, width)), rows(TILE, WIDTH),
                rows(TILE, WIDTH), rows(share, WIDTH), rows(share, WIDTH),
                pl.BlockSpec((3, 1, share), lambda i, info: (0, 0, owner(i, info))),
                whole(table.shape), whole(w.shape), first, first, whole((TILE, width)),
                whole(early.shape), whole(up_a.shape), whole(up_b.shape),
            ]
            + unread(earlier),
            out_specs=[
                pl.BlockSpec((1, share, width), lambda i, info: (i, 0, 0)),
                pl.BlockSpec((1, share, width), lambda i, info: (jnp.maximum(i - 2, 0), 0, 0)),
                whole(sums),
            ],
            scratch_shapes=[
                pltpu.VMEM((width, 3 * WIDTH), f32), pltpu.VMEM((8, 3 * WIDTH), f32),
                pltpu.VMEM((8, width), f32),
                pltpu.VMEM((width, 3 * WIDTH), bf16),
            ],
        ),
        out_shape=[
            pltpu.HBM((4, share, width), bf16), pltpu.HBM((2, share, width), bf16),
            pltpu.HBM(sums, bf16),
        ],
        compiler_params=params(LIMIT),
        cost_estimate=pl.CostEstimate(
            flops=24 * length * width * WIDTH, bytes_accessed=20 * MIB, transcendentals=0
        ),
        name="project_back",
    )(
        info, tokens, gain, shift, dq_a, dq_b, dk, dv, positions, table, w, kept, other, there, early,
        up_a, up_b, *earlier,
    )


def vectors_kernel(extra, grad_b, grad_up, vectors):
    blocks = extra.shape[0]
    width = vectors.shape[1]
    vectors[...] = jnp.zeros_like(vectors)
    for v in range(3 + 7 * width // WIDTH):
        n, m = v % blocks, v // blocks
        pair = extra[n].astype(f32)
        row = pair[2 * m : 2 * m + 1, :] + pair[2 * m + 1 : 2 * m + 2, :]
        to, at = divmod((v - 3) * WIDTH, width)
        if v < 3:
            grad_b[v : v + 1, :] = row
        elif to == 0:
            grad_up[:, at : at + WIDTH] = row
        else:
            vectors[to - 1 : to, at : at + WIDTH] = row


def unpack_vectors(sums, width, earlier):
    blocks = sums.shape[0]
    at, rows = 4 * width // blocks, late_extra(width, blocks)[1]
    out = jax.ShapeDtypeStruct
    return pl.pallas_call(
        in_order(vectors_kernel, 1, len(earlier)),
        grid=(1,),
        in_specs=[pl.BlockSpec((blocks, rows, WIDTH), lambda i: (0, at // rows, 0))]
        + unread(earlier),
        out_specs=[whole((3, WIDTH)), whole((1, width)), whole((8, width))],
        out_shape=[out((3, WIDTH), f32), out((1, width), f32), out((8, width), f32)],
        compiler_params=params(LIMIT),
        name="unpack_vectors",
    )(sums, *earlier)


def unpack_kernel(sums, grad_qkv, grad_out):
    blocks = sums.shape[0]
    width = grad_out.shape[1]
    for n in range(blocks):
        for to, rows, c, begin in late_places(n, blocks, width):
            grad_qkv[c, begin : begin + rows, :] = sums[n, to : to + rows, :].astype(f32)
        for to, rows, c, begin in late_places(n, blocks, width, True):
            grad_out[begin : begin + rows, c * WIDTH : (c + 1) * WIDTH] = sums[
                n, to : to + rows, :
            ].astype(f32)


def unpack(sums, width, earlier):
    out = jax.ShapeDtypeStruct
    return pl.pallas_call(
        in_order(unpack_kernel, 1, len(earlier)),
        in_specs=[pl.BlockSpec(memory_space=pltpu.VMEM)] + unread(earlier),
        out_specs=[pl.BlockSpec(memory_space=pltpu.VMEM)] * 2,
        out_shape=[out((3, width, WIDTH), f32), out((WIDTH, width), f32)],
        compiler_params=pltpu.CompilerParams(vmem_limit_bytes=LIMIT * MIB),
        name="unpack",
    )(sums, *earlier)


def finish_kernel(info, parts, other, there, tok, gain, dx2, out):
    grad = parts[0].astype(f32) + other[0].astype(f32) + there[...].astype(f32)
    hat, inverse = normalized(tok[...].astype(f32))
    out[...] = dx2[...] + norm_back(hat, inverse, gain[...], grad)


def finish(info, me_at, parts, other, there, tokens, gain, dx2, earlier):
    width = tokens.shape[1]
    share = there.shape[0]
    rows = pl.BlockSpec((TILE, width), lambda i, info: (i, 0))
    return pl.pallas_call(
        in_order(finish_kernel, 7, len(earlier)),
        grid_spec=pltpu.PrefetchScalarGridSpec(
            num_scalar_prefetch=1,
            grid=(share // TILE,),
            in_specs=[
                pl.BlockSpec((1, TILE, width), lambda i, info: (0, i, 0)),
                pl.BlockSpec((1, TILE, width), lambda i, info: (0, i, 0)), rows,
                pl.BlockSpec((TILE, width), lambda i, info: (2 * info[me_at] + i, 0)),
                whole((1, width)), rows,
            ]
            + unread(earlier),
            out_specs=rows,
        ),
        out_shape=jax.ShapeDtypeStruct((share, width), f32),
        compiler_params=params(LIMIT),
        cost_estimate=pl.CostEstimate(
            flops=30 * share * width, bytes_accessed=10 * MIB, transcendentals=0
        ),
        name="finish",
    )(info, parts, other, there, tokens, gain, dx2, *earlier)


def total_of(blocks):
    total = blocks[0].astype(f32)
    for n in range(1, blocks.shape[0]):
        total += blocks[n].astype(f32)
    return total.astype(bf16)


def sums_kernel(blocks_a, blocks_b, out):
    rows = blocks_a.shape[1]
    out[:rows, :] = total_of(blocks_a)
    out[rows:, :] = total_of(blocks_b)


def two_sums(blocks_a, blocks_b, earlier):
    _, rows, width = blocks_a.shape
    return pl.pallas_call(
        in_order(sums_kernel, 2, len(earlier)),
        grid=(1,),
        in_specs=[whole(blocks_a.shape), whole(blocks_b.shape)] + unread(earlier),
        out_specs=whole((2 * rows, width)),
        out_shape=pltpu.HBM((2 * rows, width), bf16),
        compiler_params=params(LIMIT),
        name="two_sums",
    )(blocks_a, blocks_b, *earlier)


def sum_kernel(blocks, out):
    out[...] = total_of(blocks)


def summed(blocks, steps, earlier):
    count, rows, width = blocks.shape
    tile = rows // steps
    return pl.pallas_call(
        in_order(sum_kernel, 1, len(earlier)),
        grid=(steps,),
        in_specs=[pl.BlockSpec((count, tile, width), lambda i: (0, i, 0))] + unread(earlier),
        out_specs=pl.BlockSpec((tile, width), lambda i: (i, 0)),
        out_shape=pltpu.HBM((rows, width), bf16),
        compiler_params=params(LIMIT),
        name="summed",
    )(blocks, *earlier)


def copies_kernel(first, second, out):
    total = (first[...].astype(f32) + second[...].astype(f32)).astype(bf16)
    for n in range(out.shape[0]):
        out[n] = total


def sum_copies(first, second, count, earlier):
    rows, width = first.shape
    return pl.pallas_call(
        in_order(copies_kernel, 2, len(earlier)),
        grid=(1,),
        in_specs=[whole((rows, width))] * 2 + unread(earlier),
        out_specs=whole((count, rows, width)),
        out_shape=pltpu.HBM((count, rows, width), bf16),
        compiler_params=params(LIMIT),
        name="sum_copies",
    )(first, second, *earlier)


def swap(array, axis, bit=1):
    size = lax.axis_size(axis)
    if size == 1:
        return jnp.zeros_like(array)
    return lax.ppermute(array, axis, [(i, i ^ bit) for i in range(size)])


def swap_both(array):
    return lax.ppermute(array, MP, [(i, i ^ 3) for i in range(4)])


def scattered(rows, axes):
    group = lax.axis_size(axes)
    length, width = rows.shape
    return lax.all_to_all(
        rows.reshape(group, length // group, width), axes, 0, 0, tiled=True
    )


def both_sums(total):
    if lax.axis_size("zl") == 1:
        return total
    return (total.astype(f32) + swap(total, "zl").astype(f32)).astype(bf16)


def local(
    tokens, cotangent, segments, padding, positions, ln1_gain, ln1_bias, w_qkv, b_qkv, w_out, b_out,
    ln2_gain, ln2_bias, w_up, b_up, w_down, b_down,
):
    width, hidden = w_up.shape
    w_all = lax.all_gather(w_out, MP)
    gain_one, shift_one = ln1_gain[None], ln1_bias[None]
    gain_two, shift_two = ln2_gain[None], ln2_bias[None]
    ends = jnp.sum((segments <= jnp.arange(2)[:, None]).astype(jnp.int32), axis=1)
    info = jnp.concatenate([ends, lax.axis_index(MP)[None].astype(jnp.int32)])
    me_at = 2
    table = jnp.asarray(rope_constants())
    k_aug, v_aug, q_aug_t, q, k_t, v_t = project(
        tokens, w_qkv, b_qkv, gain_one, shift_one, positions, segments, padding, table
    )

    def exchanged(own, to_c, to_zh, to_both):
        return own, swap(to_c, "c"), swap(to_zh, "zh"), swap_both(to_both)

    o_0, o_t_0, lse_0 = attend(0, info, k_aug, v_t, q_aug_t, k_t, padding, ())
    o_zh_0, o_c_0 = swap(o_0, "zh"), swap(o_0, "c")
    o_1, o_t_1, lse_1 = attend(1, info, k_aug, v_t, q_aug_t, k_t, padding, (o_0, w_all))
    o_zh_1 = swap(o_1, "zh")
    o_zh_0 = after(o_zh_0, (o_1,))
    o_parts_0 = tuple((part, None) for part in (o_0, o_c_0, o_zh_0, swap(o_zh_0, "c")))

    def mlp_half(part, o_parts, earlier):
        return mlp(
            part, info, me_at, tokens, cotangent, o_parts, w_all, b_out[None], gain_two, shift_two,
            w_up, b_up[None], w_down, earlier,
        )

    x2_0, dy_0, h2_0, act_0, du_0, mlp_0, mlp_sent_0, dh2_0, sent, db_0 = mlp_half(
        0, o_parts_0, (o_1,)
    )
    pair = paired(o_1, o_zh_1, (x2_0,))
    pair_c = swap(pair, "c")
    o_parts_1 = ((pair, 0), (pair_c, 0), (pair, 1), (pair_c, 1))
    other_0 = swap(sent, "c")
    give_0 = to_give(dh2_0, other_0, ())
    there_0 = swap(give_0, "zh")
    x2_1, dy_1, h2_1, act_1, du_1, mlp_1, mlp_sent_1, dh2_1, sent, db_1 = mlp_half(
        1, o_parts_1, (give_0,)
    )
    other_1 = swap(sent, "c")
    grad_down = down_weights((act_0, act_1), cotangent, (there_0,))
    arrived_down = scattered(grad_down, ("y", "x"))
    give_1 = to_give(dh2_1, other_1, (grad_down,))
    there_1 = swap(give_1, "zh")
    grad_up = up_weights((h2_0, h2_1), (du_0, du_1), (give_1,))
    dx2, g, *d_parts, small = middle(
        info, me_at, (dh2_0, other_0, there_0, x2_0, dy_0), (dh2_1, other_1, there_1, x2_1, dy_1),
        gain_two, w_all, (grad_up,),
    )
    do = exchanged(*d_parts)
    arrived_up = scattered(after(grad_up, (g,)), ("y", "x"))
    grad_out, out_sent = out_weights(info, me_at, o_parts_0, o_parts_1, g)
    out_other = swap(out_sent, "c")
    mlp_parts = (mlp_0, mlp_1)
    mlp_others = (swap(mlp_sent_0, "c"), swap(mlp_sent_1, "c"))
    dq_0, dk, dv = attend_back(
        0, info, me_at, k_aug, v_aug, k_t, q_aug_t, q, v_t, o_t_0, lse_0, padding, do, positions,
        table, None, None, (grad_out, g),
    )
    give, mlp_give = three_to_give(
        (grad_out,) + mlp_parts, (out_other,) + mlp_others, (dq_0,)
    )
    out_there = swap(give, "zh")
    mlp_there = swap(mlp_give, "zh")
    part_sum = both_sums(two_sums(arrived_up, arrived_down, (mlp_give,)))
    dq_1, dk, dv = attend_back(
        1, info, me_at, k_aug, v_aug, k_t, q_aug_t, q, v_t, o_t_1, lse_1, padding, do, positions,
        table, dk, dv, (give, part_sum),
    )
    grad_mlp = lax.all_gather(part_sum, ("y", "x"), axis=0, tiled=True)
    dh1, sent, sums = project_back(
        info, me_at, tokens, gain_one, shift_one, dq_0, dq_1, dk, dv, positions, table, w_qkv,
        grad_out, out_other, out_there, small, db_0, db_1, lax.axis_size(("y", "x")), (mlp_there,),
    )
    other = swap(sent, "c")
    back = swap(to_give(dh1, other, (sums,)), "zh")
    arrived = scattered(sums.reshape(-1, WIDTH), ("y", "x"))
    total = summed(arrived, 1, (back,))
    block = sum_copies(total, swap(total, "zl"), sums.shape[0], ())
    late = lax.all_to_all(block, ("y", "x"), 0, 0, tiled=True)
    grad_inputs = finish(info, me_at, dh1, other, back, tokens, gain_one, dx2, (block,))
    mixed = mixed_rows(
        (x2_0, x2_1), mlp_parts, mlp_others, mlp_there, b_down[None], (block,)
    )
    count = lax.axis_size(("y", "x"))
    grad_mlp = grad_mlp.reshape(count, 2, width // count, hidden)
    grad_up = grad_mlp[:, 0].astype(f32).reshape(width, hidden)
    grad_down = grad_mlp[:, 1].astype(f32).reshape(hidden, width)
    grad_b, grad_b_up, vectors = unpack_vectors(late, width, (grad_inputs, mixed, grad_up, grad_down))
    by_c, by_zh, by_both = swap(vectors, "c"), swap(vectors, "zh"), swap_both(vectors)
    grad_qkv, grad_w_out = unpack(late, width, (vectors,))
    group = (vectors + by_c) + (by_zh + by_both)
    return (
        mixed, grad_inputs, group[0], group[1], grad_qkv, grad_b, grad_w_out, group[4],
        group[2], group[3], grad_up, grad_b_up[0], grad_down, group[5],
    )


def solution(mesh):
    packs = mesh.shape["dp"]
    if packs == 32:
        shape = (2, 4, 4, 2, 2)
    else:
        shape = (1, packs, 1, 2, 2)
    split = Mesh(mesh.devices.reshape(shape), EVERY)
    in_specs = (
        P(DP, None), P(DP, None), P(DP, None), P(DP, None), P(None, DP, None), P(), P(),
        P(None, None, MP), P(None, MP), P(MP, None), P(), P(), P(), P(None, MP), P(MP),
        P(MP, None), P(),
    )
    out_specs = (
        P(EVERY, None), P(EVERY, None), P(), P(), P(None, None, MP), P(None, MP), P(MP, None), P(),
        P(), P(), P(None, MP), P(MP), P(MP, None), P(),
    )
    return jax.shard_map(local, mesh=split, in_specs=in_specs, out_specs=out_specs, check_vma=False)
```
